32 devices in a mesh: lat: 4 (over y, x), lon: 8 (over z, core).
Axes of the slice: x: 2, y: 2, z: 4, core: 2. Of those that a mesh axis runs over, the one named last changes fastest.
Arguments:
- residual: float32 [524288], P(('lat', 'lon')), may hold values from -6 to 6
- star_pixel: int32 [524288], P(('lat', 'lon')), may hold values from 0 to 63
- star_bin: int32 [524288], P(('lat', 'lon')), may hold values from 0 to 511
- send_counts: int32 [32, 32], P(('lat', 'lon')), may hold values from 64 to 512, as said below
- send_offsets: int32 [32, 32], P(('lat', 'lon')), may hold values from 0 to 10112, as said below
- latent: float32 [32, 64, 512], P('lat', 'lon'), may hold values from -6 to 6
- stencils: float32 [2, 27, 512], replicated
Outputs:
- gradient: float32 [32, 64, 512], P('lat', 'lon')
The draws below stay inside these ranges and needn't reach their ends.
Inputs may be any that keep to these rules, and one draw needn't show every extreme that they name: `send_counts`: each entry is at most 512; for one owner of the latitude tiles 4 // 4 to 2, drawn from the seed, every catalog shard holds exactly 512 stars. Owners of those latitude tiles get 512 // 2 to 512 from a shard, the others 512 // 8 to 128; one catalog shard, drawn from the seed, holds that most for every owner. `send_offsets`: each row is the running sum of the same row of send_counts before each entry, starting at 0. `star_pixel`: equals row * 8 + column within the owner's tile.
All inputs are finite; a program needn't handle non-finite values.
Results may differ from the reference program's by a relative error of at most 0.0003.
Values sent between devices are 32-bit elements; how exact they have to be, the bound alone decides.
No kernel may reach another device: no remote copies, remote signals or barrier semaphores. Data moves between devices by JAX's collectives and lax.ppermute only.
A program may use at most 64 MiB of HBM per device.

```python
import jax
import jax.numpy as jnp

R = 512
TLAT = 8
TLON = 8
CAP = 512
S_DEV = 16384
STARS = 524288
NLAT = 32
NLON = 64
N_LAT = 4
N_LON = 8


def star_loads(key):
    shards = N_LAT * N_LON
    dest = jnp.arange(shards, dtype=jnp.int32)
    lat_of = dest // N_LON
    plane = (lat_of >= N_LAT // 4) & (lat_of < N_LAT - N_LAT // 4)
    top = jnp.where(plane, CAP, CAP // 4).astype(jnp.int32)
    least = top // 2
    loads = jax.random.randint(key, (shards, shards), least[None, :], top[None, :] + 1, dtype=jnp.int32)
    full_shard = jax.random.randint(jax.random.fold_in(key, 5), (), 0, shards, dtype=jnp.int32)
    loads = jnp.where(dest[:, None] == full_shard, top[None, :], loads)
    owner_lat = jax.random.randint(jax.random.fold_in(key, 7), (), N_LAT // 4, N_LAT - N_LAT // 4, dtype=jnp.int32)
    owner_lon = jax.random.randint(jax.random.fold_in(key, 9), (), 0, N_LON, dtype=jnp.int32)
    full_owner = owner_lat * N_LON + owner_lon
    loads = jnp.where(dest[None, :] == full_owner, CAP, loads)
    return loads.astype(jnp.int32)


def draw_send_counts(key, part):
    return star_loads(key)


def draw_send_offsets(key, part):
    loads = star_loads(key)
    return (jnp.cumsum(loads, axis=1) - loads).astype(jnp.int32)


def draw_stencils(key, part):
    key = jax.random.fold_in(key, 11)
    side_key, middle_key = jax.random.split(key)
    side = jax.random.uniform(side_key, (2, 27, R), jnp.float32, -0.05, 0.05) + 0.01
    middle = jax.random.uniform(middle_key, (2, 1, R), jnp.float32, 0.5, 0.9)
    taps = jnp.arange(27, dtype=jnp.int32)[None, :, None]
    return jnp.where(taps == 13, middle, side).astype(jnp.float32)


def set_ends(result, stream_key, low, high):
    shape = result.shape
    index_at = [jax.random.randint(jax.random.fold_in(stream_key, axis), (), 0, shape[axis]) for axis in range(len(shape))]
    result = result.at[tuple(index_at)].set(low)
    longest = shape.index(max(shape))
    index_at[longest] = (index_at[longest] + 1) % shape[longest]
    return result.at[tuple(index_at)].set(high)


def levels(own_key, extent, cuts, low, largest):
    factor_of = 1.0
    for axis_at, blocks in cuts:
        draws = jax.random.uniform(jax.random.fold_in(jax.random.fold_in(own_key, 6), axis_at), (blocks,), jnp.float32, low / len(cuts), largest / len(cuts))
        factor_of = factor_of * jnp.repeat(jnp.exp(draws), extent[axis_at] // blocks).reshape((-1,) + (1,) * (len(extent) - 1 - axis_at))
    return factor_of


def normal_values(own_key, extent, scale, reach, cuts=(), kind=jnp.bfloat16):
    drawn = scale * jax.random.normal(own_key, extent, jnp.float32)
    if cuts:
        drawn = drawn * levels(own_key, extent, cuts, -0.22, 0.18)
    return jnp.clip(drawn, -reach, reach).astype(kind)


def setup_inputs(seed: int = 0) -> dict:
    key_of = jax.random.split(jax.random.key(seed), 8)
    return {
        "residual": normal_values(key_of[0], (STARS,), 1.0, 6.0, ((0, 32),), jnp.float32),
        "star_pixel": set_ends(jax.random.randint(key_of[1], (STARS,), 0, TLAT * TLON), jax.random.fold_in(key_of[1], 1), 0, (TLAT * TLON) - 1).astype(jnp.int32),
        "star_bin": set_ends(jax.random.randint(key_of[2], (STARS,), 0, R), jax.random.fold_in(key_of[2], 1), 0, R - 1).astype(jnp.int32),
        "send_counts": draw_send_counts(jax.random.fold_in(key_of[7], 71), 0),
        "send_offsets": draw_send_offsets(jax.random.fold_in(key_of[7], 71), 0),
        "latent": normal_values(key_of[5], (NLAT, NLON, R), 1.0, 6.0, ((0, 4), (1, 8)), jnp.float32),
        "stencils": draw_stencils(jax.random.fold_in(key_of[7], 71), 0),
    }


bin_width = 0.0625


def shift_radial(values, step):
    if step == 1:
        return jnp.concatenate([values[..., 1:], jnp.zeros_like(values[..., :1])], axis=-1)
    if step == -1:
        return jnp.concatenate([jnp.zeros_like(values[..., :1]), values[..., :-1]], axis=-1)
    return values


def widen(field):
    wrapped = jnp.concatenate([field[:, -1:], field, field[:, :1]], axis=1)
    return jnp.pad(wrapped, ((1, 1), (0, 0), (0, 0)))


def refine(ext, coef):
    height = ext.shape[0] - 2
    width = ext.shape[1] - 2
    total = jnp.zeros((height, width, ext.shape[2]), jnp.float32)
    for radial in (-1, 0, 1):
        shifted = shift_radial(ext, radial)
        for above in (-1, 0, 1):
            for beside in (-1, 0, 1):
                tap = (above + 1) * 9 + (beside + 1) * 3 + radial + 1
                window = shifted[1 + above:1 + above + height, 1 + beside:1 + beside + width]
                total = total + coef[tap] * window
    return total


def adjoint(ext, coef):
    height = ext.shape[0] - 2
    width = ext.shape[1] - 2
    total = jnp.zeros((height, width, ext.shape[2]), jnp.float32)
    for radial in (-1, 0, 1):
        partial_sum = jnp.zeros((height, width, ext.shape[2]), jnp.float32)
        for above in (-1, 0, 1):
            for beside in (-1, 0, 1):
                tap = (above + 1) * 9 + (beside + 1) * 3 + radial + 1
                window = ext[1 - above:1 - above + height, 1 - beside:1 - beside + width]
                partial_sum = partial_sum + coef[tap] * window
        total = total + shift_radial(partial_sum, -radial)
    return total


def reference(residual, star_pixel, star_bin, send_counts, send_offsets, latent, stencils):
    shards = N_LAT * N_LON
    slots = jnp.arange(S_DEV, dtype=jnp.int32)
    owner = jax.vmap(lambda row: jnp.searchsorted(row, slots, side="right"))(send_offsets).astype(jnp.int32) - 1
    totals = send_offsets[:, -1] + send_counts[:, -1]
    live = slots[None, :] < totals[:, None]
    owner_lat = owner // N_LON
    owner_lon = owner % N_LON
    pixel = star_pixel.reshape(shards, S_DEV)
    rows = owner_lat * TLAT + pixel // TLON
    cols = owner_lon * TLON + pixel % TLON
    cells = ((rows * NLON + cols) * R + star_bin.reshape(shards, S_DEV)).astype(jnp.int32)
    values = jnp.where(live, residual.reshape(shards, S_DEV), jnp.float32(0.0))
    binned = jnp.zeros((NLAT * NLON * R,), jnp.float32).at[cells.reshape(-1)].add(values.reshape(-1))
    binned = binned.reshape(NLAT, NLON, R)
    behind = bin_width * jnp.flip(jnp.cumsum(jnp.flip(binned, -1), axis=-1), -1)
    coarse = refine(widen(latent), stencils[0])
    fine = refine(widen(coarse), stencils[1])
    upstream = jnp.exp(fine) * behind
    middle = adjoint(widen(upstream), stencils[1])
    back = adjoint(widen(middle), stencils[0])
    return latent + back
```

```python
import functools

import jax
import jax.numpy as jnp
from jax import lax
from jax.experimental import pallas as pl
from jax.experimental.pallas import tpu as pltpu
from jax.sharding import PartitionSpec as P

CAP = 512
LANES = 128
SUBLANES = 8
RUNS = CAP // LANES
bin_width = 0.0625


def lane_roll(values, shift):
    return pltpu.roll(values, shift % values.shape[-1], values.ndim - 1)


def compact_kernel(counts, offsets, residual, pixel, bins, out, cells, *, radial):
    cells[...] = (pixel[...] * radial + bins[...]).astype(jnp.float32)
    lane = lax.broadcasted_iota(jnp.int32, (SUBLANES, LANES), 1)
    row = lax.broadcasted_iota(jnp.int32, (SUBLANES, LANES), 0)
    slot = row * LANES + lane
    for owner in range(out.shape[0]):
        start = offsets[0, owner]
        first = lax.shift_right_logical(start, 7)
        part = lax.bitwise_and(start, LANES - 1)
        live = slot < counts[0, owner]

        def window(ref):
            rows = ref[pl.ds(first, SUBLANES), :]
            turned = pltpu.roll(rows, lax.bitwise_and(LANES - part, LANES - 1), 1)
            joined = jnp.where(lane < LANES - part, turned, pltpu.roll(turned, SUBLANES - 1, 0))
            return jnp.where(live, joined, 0.0)

        out[owner] = jnp.where(row < RUNS, window(residual), pltpu.roll(window(cells), RUNS, 0))


def behind_of(got, left, right, *, radial, pixels):
    half = radial // 2
    classes = 2 * pixels
    shards = got.shape[0]
    group = 4
    column = lax.broadcasted_iota(jnp.int32, (classes, LANES), 0).astype(jnp.float32).astype(jnp.bfloat16)
    place = lax.broadcasted_iota(jnp.int32, (half, LANES), 0).astype(jnp.float32).astype(jnp.bfloat16)
    zero = jnp.zeros((), jnp.bfloat16)
    one = jnp.ones((), jnp.bfloat16)

    def tall(row, height):
        return jnp.concatenate([jnp.broadcast_to(row, (16, LANES)).astype(jnp.bfloat16)] * (height // 16), axis=0)

    def step(turn, total):
        for member in range(group):
            tile = got[turn * group + member]
            cell = tile.astype(jnp.int32)
            pixel = lax.shift_right_logical(cell, radial.bit_length() - 1)
            bins = lax.bitwise_and(cell, radial - 1)
            upper = (bins >= half).astype(jnp.int32)
            label = (upper * pixels + pixel).astype(jnp.float32)
            low = (bins - upper * half).astype(jnp.float32)
            coarse = tile.astype(jnp.bfloat16).astype(jnp.float32)
            rest = tile - coarse
            for run in range(RUNS):
                at = slice((member * RUNS + run) * LANES, (member * RUNS + run + 1) * LANES)
                mine = tall(label[RUNS + run:RUNS + run + 1], classes) == column
                left[:classes, at] = jnp.where(mine, tall(coarse[run:run + 1], classes), zero)
                left[classes:, at] = jnp.where(mine, tall(rest[run:run + 1], classes), zero)
                right[:, at] = jnp.where(tall(low[RUNS + run:RUNS + run + 1], half) >= place, one, zero)
        return total + lax.dot_general(
            left[...], right[...], (((1,), (1,)), ((), ())), preferred_element_type=jnp.float32
        )

    total = lax.fori_loop(0, shards // group, step, jnp.zeros((2 * classes, half), jnp.float32))
    both = (total[:classes] + total[classes:]) * bin_width
    near, far = both[:pixels], both[pixels:]
    return near + far[:, :1], far


def bin_kernel(got, latent, behind, to_left, to_right, left, right):
    height, width, radial = latent.shape
    near, far = behind_of(got, left, right, radial=radial, pixels=height * width)
    half = radial // 2
    sub = lax.broadcasted_iota(jnp.int32, (width, radial), 0)
    for row in range(height):
        at = slice(row * width, (row + 1) * width)
        mine = jnp.concatenate([near[at], far[at]], axis=1)
        behind[row] = mine
        turned = pltpu.roll(mine, width // 2, 0)
        field = latent[row]
        to_left[row] = jnp.where(sub < width // 2, field, turned)
        to_right[row] = jnp.where(sub < width // 2, turned, field)


def lon_halos(from_left, from_right, sub, width):
    field = jnp.where(sub < width // 2, from_right, from_left)
    behind = pltpu.roll(jnp.where(sub < width // 2, from_left, from_right), width // 2, 0)
    return field, behind


def pack_kernel(latent, behind, from_left, from_right, to_up, to_down):
    height, width, radial = latent.shape
    sub = lax.broadcasted_iota(jnp.int32, (width, radial), 0)
    wide = slice(width, 2 * width)
    for out, rows in ((to_up, range(4)), (to_down, range(height - 4, height))):
        for place, row in enumerate(rows):
            field, _ = lon_halos(from_left[row], from_right[row], sub, width)
            out[place, :width] = latent[row]
            out[place, wide] = field
    for out, rows in ((to_up, range(2)), (to_down, range(height - 2, height))):
        for place, row in enumerate(rows):
            _, mass = lon_halos(from_left[row], from_right[row], sub, width)
            out[4 + place, :width] = behind[row]
            out[4 + place, wide] = mass


def level(source, shifted, coef, first, last, write):
    cols, radial = source.shape[1], source.shape[2]
    lane = lax.broadcasted_iota(jnp.int32, (cols, radial), 1)

    def shift(row, _):
        field = source[row]
        shifted[0, row] = jnp.where(lane == 0, 0.0, lane_roll(field, 1))
        shifted[1, row] = jnp.where(lane == radial - 1, 0.0, lane_roll(field, -1))
        return 0

    lax.fori_loop(first - 1, last + 2, shift, 0, unroll=2)

    for tile in range(radial // LANES):
        at = slice(tile * LANES, (tile + 1) * LANES)
        taps = [jnp.broadcast_to(coef[k:k + 1, at], (cols, LANES)) for k in range(27)]

        def line(row, _, taps=taps, at=at):
            sums = [None, None, None]
            for above in (-1, 0, 1):
                window = (shifted[0, row + above, :, at], source[row + above, :, at], shifted[1, row + above, :, at])
                for beside in (-1, 0, 1):
                    for radial_step in (-1, 0, 1):
                        tap = (above + 1) * 9 + (beside + 1) * 3 + radial_step + 1
                        term = taps[tap] * window[radial_step + 1]
                        old = sums[beside + 1]
                        sums[beside + 1] = term if old is None else old + term
            write(row, at, sums[1] + pltpu.roll(sums[0], 1, 0) + pltpu.roll(sums[2], cols - 1, 0))
            return 0

        lax.fori_loop(first, last + 1, line, 0, unroll=2)


def field_kernel(
    inside, latent, behind, from_left, from_right, from_up, from_down, stencils, mirrored, out,
    field, mass, other, shifted,
):
    height, width, radial = latent.shape
    sub = lax.broadcasted_iota(jnp.int32, (width, radial), 0)
    cols = 2 * width
    field[:4] = from_up[:4]
    field[height + 4:] = from_down[:4]
    mass[2:4] = from_up[4:]
    mass[height + 4:height + 6] = from_down[4:]

    def fill(row, _):
        near, dust = lon_halos(from_left[row], from_right[row], sub, width)
        field[row + 4, :width] = latent[row]
        field[row + 4, width:] = near
        mass[row + 4, :width] = behind[row]
        mass[row + 4, width:] = dust
        return 0

    lax.fori_loop(0, height, fill, 0)

    def kept(row, values):
        real = jnp.where(row < 4, inside[0], jnp.where(row >= height + 4, inside[1], 1))
        return jnp.where(jnp.full(values.shape, real, jnp.int32) > 0, values, 0.0)

    def to_coarse(row, at, values):
        other[row, :, at] = kept(row, values)

    def to_upstream(row, at, values):
        mass[row, :, at] = kept(row, jnp.exp(values) * mass[row, :, at])

    def to_middle(row, at, values):
        other[row, :, at] = kept(row, values)

    def to_out(row, at, values):
        out[row - 4, :, at] = latent[row - 4, :, at] + values[:width]

    level(field, shifted, stencils.at[0], 1, height + 6, to_coarse)
    level(other, shifted, stencils.at[1], 2, height + 5, to_upstream)
    level(mass, shifted, mirrored.at[1], 3, height + 4, to_middle)
    level(other, shifted, mirrored.at[0], 4, height + 3, to_out)


def mirror(stencils):
    turned = jnp.flip(stencils, axis=1).reshape(stencils.shape[0], 9, 3, stencils.shape[2])
    edge = jnp.zeros_like(turned[:, :, 0, :1])
    back = jnp.concatenate([edge, turned[:, :, 0, :-1]], axis=-1)
    ahead = jnp.concatenate([turned[:, :, 2, 1:], edge], axis=-1)
    return jnp.stack([back, turned[:, :, 1], ahead], axis=2).reshape(stencils.shape)


def exchange(first, last, axis, closed):
    count = lax.axis_size(axis)
    ends = count if closed else count - 1
    return (
        lax.ppermute(last, axis, [(i, (i + 1) % count) for i in range(ends)]),
        lax.ppermute(first, axis, [((i + 1) % count, i) for i in range(ends)]),
    )


VMEM = pl.BlockSpec(memory_space=pltpu.VMEM)
SMEM = pl.BlockSpec(memory_space=pltpu.SMEM)
LIMIT = pltpu.CompilerParams(vmem_limit_bytes=32 * 1024 * 1024)


def on_device(residual, star_pixel, star_bin, send_counts, send_offsets, latent, stencils):
    height, width, radial = latent.shape
    shards = send_counts.shape[1]
    slots = residual.shape[0]
    f32 = jnp.float32

    def rows(values):
        return values.reshape(slots // LANES, LANES)

    packed = pl.pallas_call(
        functools.partial(compact_kernel, radial=radial),
        out_shape=jax.ShapeDtypeStruct((shards, 2 * RUNS, LANES), f32),
        in_specs=[SMEM, SMEM, VMEM, VMEM, VMEM],
        out_specs=VMEM,
        scratch_shapes=[pltpu.VMEM((slots // LANES, LANES), f32)],
        compiler_params=LIMIT,
        name="compact",
    )(send_counts, send_offsets, rows(residual), rows(star_pixel), rows(star_bin))
    got = lax.all_to_all(packed, ("lat", "lon"), split_axis=0, concat_axis=0, tiled=True)

    tile = jax.ShapeDtypeStruct((height, width, radial), f32)
    behind, to_left, to_right = pl.pallas_call(
        bin_kernel,
        out_shape=(tile, tile, tile),
        in_specs=[VMEM, VMEM],
        out_specs=(VMEM, VMEM, VMEM),
        scratch_shapes=[
            pltpu.VMEM((4 * height * width, 4 * CAP), jnp.bfloat16),
            pltpu.VMEM((radial // 2, 4 * CAP), jnp.bfloat16),
        ],
        compiler_params=LIMIT,
        name="binning",
    )(got, latent)
    from_left, from_right = exchange(to_left, to_right, "lon", True)

    band = jax.ShapeDtypeStruct((6, 2 * width, radial), f32)
    to_up, to_down = pl.pallas_call(
        pack_kernel,
        out_shape=(band, band),
        in_specs=[VMEM] * 4,
        out_specs=(VMEM, VMEM),
        compiler_params=LIMIT,
        name="pack",
    )(latent, behind, from_left, from_right)
    from_up, from_down = exchange(to_up, to_down, "lat", False)

    row = lax.axis_index("lat")
    inside = jnp.stack([row > 0, row < lax.axis_size("lat") - 1]).astype(jnp.int32)
    wide = (height + 8, 2 * width, radial)
    return pl.pallas_call(
        field_kernel,
        out_shape=tile,
        in_specs=[SMEM] + [VMEM] * 8,
        out_specs=VMEM,
        scratch_shapes=[pltpu.VMEM(wide, f32)] * 3 + [pltpu.VMEM((2,) + wide, f32)],
        compiler_params=LIMIT,
        name="field",
    )(inside, latent, behind, from_left, from_right, from_up, from_down, stencils, mirror(stencils))


def solution(mesh):
    return jax.shard_map(
        on_device,
        mesh=mesh,
        in_specs=(
            P(("lat", "lon")),
            P(("lat", "lon")),
            P(("lat", "lon")),
            P(("lat", "lon"), None),
            P(("lat", "lon"), None),
            P("lat", "lon", None),
            P(),
        ),
        out_specs=P("lat", "lon", None),
        check_vma=False,
    )
```

```python
import functools

import jax
import jax.numpy as jnp
from jax import lax
from jax.experimental import pallas as pl
from jax.experimental.pallas import tpu as pltpu
from jax.sharding import PartitionSpec as P

CAP = 512
LANES = 128
SUBLANES = 8
RUNS = CAP // LANES
bin_width = 0.0625


def position(axis):
    index = lax.axis_index(axis)
    return index, lax.bitwise_and(index, 1)


def either(flag, if_set, if_clear):
    return jnp.where(jnp.full(if_set.shape, flag, jnp.int32) > 0, if_set, if_clear)


def sublane(radial):
    return lax.broadcasted_iota(jnp.int32, (SUBLANES, radial), 0)


def pack_sides(rows, to_partner, to_outer):
    _, odd = position("lon")
    sub = sublane(rows[0].shape[1])
    for group in range(len(rows) // 4):
        before, after = rows[4 * group], rows[4 * group]
        for k in range(1, 4):
            row = rows[4 * group + k]
            pair = lax.shift_right_logical(sub, 1)
            before = jnp.where(pair == k, pltpu.roll(row, 2 * k, 0), before)
            after = jnp.where(pair == 3 - k, pltpu.roll(row, SUBLANES - 2 * k, 0), after)
        to_partner[group] = either(odd, before, after)
        to_outer[group] = either(odd, after, before)


def unpack_sides(from_partner, from_outer, height):
    _, odd = position("lon")
    sub = sublane(from_partner.shape[2])
    tiles = []
    for group in range(height // 4):
        partner, outer = from_partner[group], from_outer[group]
        before, after = either(odd, partner, outer), either(odd, outer, partner)
        for k in range(4):
            if k:
                tiles.append(jnp.where(sub < 4, pltpu.roll(after, SUBLANES - 2 * k, 0), pltpu.roll(before, 2 * k, 0)))
            else:
                tiles.append(jnp.where(sub < 4, after, before))
    return tiles


def pack_ends_kernel(field, from_partner, from_outer, to_partner, to_outer):
    height, _, radial = field.shape
    _, odd = position("lat")
    sub = sublane(radial)
    outside = (sub < 2) | (sub >= 6)
    tiles = unpack_sides(from_partner, from_outer, height)

    def ends(first):
        return (
            field[first],
            field[first + 1],
            jnp.where(outside, tiles[first], pltpu.roll(tiles[first + 1], 4, 0)),
        )

    for place, (top, bottom) in enumerate(zip(ends(0), ends(height - 2))):
        to_partner[place] = either(odd, top, bottom)
        to_outer[place] = either(odd, bottom, top)


def fill_wide(wide, rows, sides, ends):
    height = len(rows)
    tiles = unpack_sides(*sides, height)
    for row in range(height):
        wide[row + 2, :SUBLANES] = rows[row]
        wide[row + 2, SUBLANES:] = tiles[row]
    _, odd = position("lat")
    from_partner, from_outer = ends
    packs = [(from_partner[place], from_outer[place]) for place in range(3)]
    above = [either(odd, partner, outer) for partner, outer in packs]
    below = [either(odd, outer, partner) for partner, outer in packs]
    for first, (one, two, corners) in ((0, above), (height + 2, below)):
        wide[first, :SUBLANES] = one
        wide[first + 1, :SUBLANES] = two
        wide[first, SUBLANES:] = corners
        wide[first + 1, SUBLANES:] = pltpu.roll(corners, 4, 0)


def radial_shifts(field):
    radial = field.shape[-1]
    lane = lax.broadcasted_iota(jnp.int32, field.shape, field.ndim - 1)
    return (
        jnp.where(lane == 0, 0.0, pltpu.roll(field, 1, field.ndim - 1)),
        jnp.where(lane == radial - 1, 0.0, pltpu.roll(field, radial - 1, field.ndim - 1)),
    )


def two_levels(wide, first_coef, second_coef, shifted, middle, write):
    reach, cols, radial = wide.shape
    height = reach - 4
    lat, _ = position("lat")
    bounds = (lat > 0).astype(jnp.int32), (lat < lax.axis_size("lat") - 1).astype(jnp.int32)

    for row in range(reach):
        for place, moved in enumerate(radial_shifts(wide[row])):
            shifted[place, row] = moved

    def taps_of(coef, at):
        return [jnp.broadcast_to(coef[k:k + 1, at], (SUBLANES, LANES)) for k in range(27)]

    def first_level(tile, _):
        at = pl.ds(pl.multiple_of(tile * LANES, LANES), LANES)
        taps = taps_of(first_coef, at)
        for row in range(1, reach - 1):
            parts = []
            for side in (slice(0, SUBLANES), slice(SUBLANES, cols)):
                sums = [None, None, None]
                for above in (-1, 0, 1):
                    window = (shifted[0, row + above, side, at], wide[row + above, side, at], shifted[1, row + above, side, at])
                    for beside in range(3):
                        for step in range(3):
                            term = taps[(above + 1) * 9 + beside * 3 + step] * window[step]
                            sums[beside] = term if sums[beside] is None else sums[beside] + term
                parts.append(sums)
            whole = [jnp.concatenate([parts[0][b], parts[1][b]], axis=0) for b in range(3)]
            value = whole[1] + pltpu.roll(whole[0], 1, 0) + pltpu.roll(whole[2], cols - 1, 0)
            if row in (1, reach - 2):
                value = either(bounds[row != 1], value, jnp.zeros_like(value))
            middle[0, 0, row - 1, :, at] = pltpu.roll(value, 1, 0)[:SUBLANES]
            middle[1, 0, row - 1, :, at] = value[:SUBLANES]
            middle[2, 0, row - 1, :, at] = pltpu.roll(value, cols - 1, 0)[:SUBLANES]
        return 0

    lax.fori_loop(0, radial // LANES, first_level, 0)

    for row in range(reach - 2):
        for beside in range(3):
            for place, moved in enumerate(radial_shifts(middle[beside, 0, row])):
                middle[beside, place + 1, row] = moved

    order = (1, 0, 2)

    def second_level(tile, _):
        at = pl.ds(pl.multiple_of(tile * LANES, LANES), LANES)
        taps = taps_of(second_coef, at)
        for row in range(height):
            total = None
            for above in range(3):
                for beside in range(3):
                    for step in range(3):
                        term = taps[above * 9 + beside * 3 + step] * middle[beside, order[step], row + above, :, at]
                        total = term if total is None else total + term
            write(row, at, total)
        return 0

    lax.fori_loop(0, radial // LANES, second_level, 0)


def open_kernel(
    counts_in, offsets_in, residual_in, pixel_in, bins_in, latent_in, out, to_partner, to_outer,
    counts, offsets, residual, pixel, bins, latent, arrived,
):
    pairs = (
        (latent_in, latent), (counts_in, counts), (offsets_in, offsets),
        (residual_in, residual), (pixel_in, pixel), (bins_in, bins),
    )
    copies = [pltpu.make_async_copy(source, target, arrived.at[i]) for i, (source, target) in enumerate(pairs)]
    for copy in copies:
        copy.start()
    copies[0].wait()
    height, _, radial = latent.shape
    pack_sides([latent[row] for row in range(height)], to_partner, to_outer)
    for copy in copies[1:]:
        copy.wait()

    lane = lax.broadcasted_iota(jnp.int32, (SUBLANES, LANES), 1)
    row = lax.broadcasted_iota(jnp.int32, (SUBLANES, LANES), 0)
    slot = row * LANES + lane
    for owner in range(out.shape[0]):
        start = offsets[0, owner]
        first = lax.shift_right_logical(start, 7)
        part = lax.bitwise_and(start, LANES - 1)
        live = slot < counts[0, owner]

        def window(values):
            turned = pltpu.roll(values, lax.bitwise_and(LANES - part, LANES - 1), 1)
            joined = jnp.where(lane < LANES - part, turned, pltpu.roll(turned, SUBLANES - 1, 0))
            return jnp.where(live, joined, 0.0)

        at = pl.ds(first, SUBLANES)
        cell = (pixel[at, :] * radial + bins[at, :]).astype(jnp.float32)
        out[owner] = jnp.where(row < RUNS, window(residual[at, :]), pltpu.roll(window(cell), RUNS, 0))


def behind_of(got, lefts, rights, *, radial, pixels):
    half = radial // 2
    classes = 2 * pixels
    shards = got.shape[0]
    group = lefts[0].shape[1] // CAP
    column = lax.broadcasted_iota(jnp.int32, (classes, LANES), 0).astype(jnp.float32).astype(jnp.bfloat16)
    place = lax.broadcasted_iota(jnp.int32, (half, LANES), 0).astype(jnp.float32).astype(jnp.bfloat16)
    zero = jnp.zeros((), jnp.bfloat16)
    one = jnp.ones((), jnp.bfloat16)

    def tall(row, height):
        return jnp.concatenate([jnp.broadcast_to(row, (16, LANES)).astype(jnp.bfloat16)] * (height // 16), axis=0)

    def build(turn, left, right):
        for member in range(group):
            tile = got[turn * group + member]
            cell = tile.astype(jnp.int32)
            pixel = lax.shift_right_logical(cell, radial.bit_length() - 1)
            bins = lax.bitwise_and(cell, radial - 1)
            upper = (bins >= half).astype(jnp.int32)
            label = (upper * pixels + pixel).astype(jnp.float32)
            low = (bins - upper * half).astype(jnp.float32)
            coarse = tile.astype(jnp.bfloat16).astype(jnp.float32)
            rest = tile - coarse
            for run in range(RUNS):
                at = slice((member * RUNS + run) * LANES, (member * RUNS + run + 1) * LANES)
                mine = tall(label[RUNS + run:RUNS + run + 1], classes) == column
                left[:classes, at] = jnp.where(mine, tall(coarse[run:run + 1], classes), zero)
                left[classes:, at] = jnp.where(mine, tall(rest[run:run + 1], classes), zero)
                right[:, at] = jnp.where(tall(low[RUNS + run:RUNS + run + 1], half) >= place, one, zero)

    def product(left, right):
        return lax.dot_general(left[...], right[...], (((1,), (1,)), ((), ())), preferred_element_type=jnp.float32)

    def step(pair, total):
        build(2 * pair + 1, lefts[1], rights[1])
        total = total + product(lefts[0], rights[0])
        build(jnp.minimum(2 * pair + 2, shards // group - 1), lefts[0], rights[0])
        return total + product(lefts[1], rights[1])

    build(0, lefts[0], rights[0])
    total = lax.fori_loop(0, shards // group // 2, step, jnp.zeros((2 * classes, half), jnp.float32))
    both = (total[:classes] + total[classes:]) * bin_width
    near, far = both[:pixels], both[pixels:]
    return near + far[:, :1], far


def bin_kernel(got, density, upstream, to_partner, to_outer, left_0, left_1, right_0, right_1):
    height, width, radial = density.shape
    near, far = behind_of(got, (left_0, left_1), (right_0, right_1), radial=radial, pixels=height * width)
    rows = []
    for row in range(height):
        at = slice(row * width, (row + 1) * width)
        rows.append(density[row] * jnp.concatenate([near[at], far[at]], axis=1))
        upstream[row] = rows[row]
    pack_sides(rows, to_partner, to_outer)


def density_kernel(latent, side_0, side_1, end_0, end_1, stencils, out, wide, shifted, middle):
    fill_wide(wide, [latent[row] for row in range(latent.shape[0])], (side_0, side_1), (end_0, end_1))

    def write(row, at, value):
        out[row, :, at] = jnp.exp(value)

    two_levels(wide, stencils.at[0], stencils.at[1], shifted, middle, write)


def back_kernel(latent, upstream, side_0, side_1, end_0, end_1, mirrored, out, wide, shifted, middle):
    fill_wide(wide, [upstream[row] for row in range(upstream.shape[0])], (side_0, side_1), (end_0, end_1))

    def write(row, at, value):
        out[row, :, at] = latent[row, :, at] + value

    two_levels(wide, mirrored.at[1], mirrored.at[0], shifted, middle, write)


def mirror(stencils):
    turned = jnp.flip(stencils, axis=1).reshape(stencils.shape[0], 9, 3, stencils.shape[2])
    edge = jnp.zeros_like(turned[:, :, 0, :1])
    back = jnp.concatenate([edge, turned[:, :, 0, :-1]], axis=-1)
    ahead = jnp.concatenate([turned[:, :, 2, 1:], edge], axis=-1)
    return jnp.stack([back, turned[:, :, 1], ahead], axis=2).reshape(stencils.shape)


def swap(to_partner, to_outer, axis, closed):
    count = lax.axis_size(axis)
    outer = [(i, (i + 1) % count) for i in range(1, count, 2) if closed or i + 1 < count]
    inner = [(i, i + 1) for i in range(0, count - 1, 2)]

    def both_ways(pairs):
        return pairs + [(j, i) for i, j in pairs]

    from_outer = lax.ppermute(to_outer, axis, both_ways(outer))
    return lax.ppermute(to_partner, axis, both_ways(inner)), from_outer


VMEM = pl.BlockSpec(memory_space=pltpu.VMEM)
HBM = pl.BlockSpec(memory_space=pl.ANY)
LIMIT = pltpu.CompilerParams(vmem_limit_bytes=32 * 1024 * 1024)


def on_device(residual, star_pixel, star_bin, send_counts, send_offsets, latent, stencils):
    height, width, radial = latent.shape
    shards = send_counts.shape[1]
    slots = residual.shape[0]
    f32 = jnp.float32
    i32 = jnp.int32
    tile = jax.ShapeDtypeStruct((height, width, radial), f32)
    sides = jax.ShapeDtypeStruct((height // 4, SUBLANES, radial), f32)
    ends = jax.ShapeDtypeStruct((3, SUBLANES, radial), f32)
    reach, cols = height + 4, 2 * width
    level_scratch = [
        pltpu.VMEM((reach, cols, radial), f32),
        pltpu.VMEM((2, reach, cols, radial), f32),
        pltpu.VMEM((3, 3, reach - 2, width, radial), f32),
    ]

    def table(values):
        return values.reshape(slots // LANES, LANES)

    packed, to_partner, to_outer = pl.pallas_call(
        open_kernel,
        out_shape=(jax.ShapeDtypeStruct((shards, 2 * RUNS, LANES), f32), sides, sides),
        in_specs=[HBM] * 6,
        out_specs=(VMEM, VMEM, VMEM),
        scratch_shapes=[pltpu.SMEM((1, shards), i32)] * 2
        + [pltpu.VMEM((slots // LANES, LANES), kind) for kind in (f32, i32, i32)]
        + [pltpu.VMEM((height, width, radial), f32), pltpu.SemaphoreType.DMA((6,))],
        compiler_params=LIMIT,
        name="opening",
    )(send_counts, send_offsets, table(residual), table(star_pixel), table(star_bin), latent)
    got = lax.all_to_all(packed, ("lat", "lon"), split_axis=0, concat_axis=0, tiled=True)

    def pack_ends(field, beside):
        return pl.pallas_call(
            pack_ends_kernel,
            out_shape=(ends, ends),
            in_specs=[VMEM] * 3,
            out_specs=(VMEM, VMEM),
            compiler_params=LIMIT,
            name="pack_ends",
        )(field, *beside)

    beside = swap(to_partner, to_outer, "lon", True)
    above = swap(*pack_ends(latent, beside), "lat", False)
    density = pl.pallas_call(
        density_kernel,
        out_shape=tile,
        in_specs=[VMEM] * 6,
        out_specs=VMEM,
        scratch_shapes=level_scratch,
        compiler_params=LIMIT,
        name="density",
    )(latent, *beside, *above, stencils)

    pieces = 2 * CAP
    upstream, to_partner, to_outer = pl.pallas_call(
        bin_kernel,
        out_shape=(tile, sides, sides),
        in_specs=[VMEM, VMEM],
        out_specs=(VMEM, VMEM, VMEM),
        scratch_shapes=[pltpu.VMEM((4 * height * width, pieces), jnp.bfloat16)] * 2
        + [pltpu.VMEM((radial // 2, pieces), jnp.bfloat16)] * 2,
        compiler_params=LIMIT,
        name="binning",
    )(got, density)
    beside = swap(to_partner, to_outer, "lon", True)
    above = swap(*pack_ends(upstream, beside), "lat", False)
    return pl.pallas_call(
        back_kernel,
        out_shape=tile,
        in_specs=[VMEM] * 7,
        out_specs=VMEM,
        scratch_shapes=level_scratch,
        compiler_params=LIMIT,
        name="back",
    )(latent, upstream, *beside, *above, mirror(stencils))


def solution(mesh):
    return jax.shard_map(
        on_device,
        mesh=mesh,
        in_specs=(
            P(("lat", "lon")),
            P(("lat", "lon")),
            P(("lat", "lon")),
            P(("lat", "lon"), None),
            P(("lat", "lon"), None),
            P("lat", "lon", None),
            P(),
        ),
        out_specs=P("lat", "lon", None),
        check_vma=False,
    )
```

```python
import functools

import jax
import jax.numpy as jnp
from jax import lax
from jax.experimental import pallas as pl
from jax.experimental.pallas import tpu as pltpu
from jax.sharding import PartitionSpec as P

CAP = 512
LANES = 128
SUBLANES = 8
RUNS = CAP // LANES
bin_width = 0.0625


def position(axis):
    index = lax.axis_index(axis)
    return index, lax.bitwise_and(index, 1)


def either(flag, if_set, if_clear):
    return jnp.where(jnp.full(if_set.shape, flag, jnp.int32) > 0, if_set, if_clear)


def sublane(radial):
    return lax.broadcasted_iota(jnp.int32, (SUBLANES, radial), 0)


def pack_sides(rows, to_partner, to_outer):
    _, odd = position("lon")
    sub = sublane(rows[0].shape[1])
    for group in range(len(rows) // 4):
        before, after = rows[4 * group], rows[4 * group]
        for k in range(1, 4):
            row = rows[4 * group + k]
            pair = lax.shift_right_logical(sub, 1)
            before = jnp.where(pair == k, pltpu.roll(row, 2 * k, 0), before)
            after = jnp.where(pair == 3 - k, pltpu.roll(row, SUBLANES - 2 * k, 0), after)
        to_partner[group] = either(odd, before, after)
        to_outer[group] = either(odd, after, before)


def unpack_sides(from_partner, from_outer, height):
    _, odd = position("lon")
    sub = sublane(from_partner.shape[2])
    tiles = []
    for group in range(height // 4):
        partner, outer = from_partner[group], from_outer[group]
        before, after = either(odd, partner, outer), either(odd, outer, partner)
        for k in range(4):
            if k:
                tiles.append(jnp.where(sub < 4, pltpu.roll(after, SUBLANES - 2 * k, 0), pltpu.roll(before, 2 * k, 0)))
            else:
                tiles.append(jnp.where(sub < 4, after, before))
    return tiles


def pack_ends_kernel(field, from_partner, from_outer, to_partner, to_outer):
    height, _, radial = field.shape
    _, odd = position("lat")
    sub = sublane(radial)
    outside = (sub < 2) | (sub >= 6)
    tiles = unpack_sides(from_partner, from_outer, height)

    def ends(first):
        return (
            field[first],
            field[first + 1],
            jnp.where(outside, tiles[first], pltpu.roll(tiles[first + 1], 4, 0)),
        )

    for place, (top, bottom) in enumerate(zip(ends(0), ends(height - 2))):
        to_partner[place] = either(odd, top, bottom)
        to_outer[place] = either(odd, bottom, top)


def fill_wide(wide, rows, sides, ends):
    height = len(rows)
    tiles = unpack_sides(*sides, height)
    for row in range(height):
        wide[row + 2, :SUBLANES] = rows[row]
        wide[row + 2, SUBLANES:] = tiles[row]
    _, odd = position("lat")
    from_partner, from_outer = ends
    packs = [(from_partner[place], from_outer[place]) for place in range(3)]
    above = [either(odd, partner, outer) for partner, outer in packs]
    below = [either(odd, outer, partner) for partner, outer in packs]
    for first, (one, two, corners) in ((0, above), (height + 2, below)):
        wide[first, :SUBLANES] = one
        wide[first + 1, :SUBLANES] = two
        wide[first, SUBLANES:] = corners
        wide[first + 1, SUBLANES:] = pltpu.roll(corners, 4, 0)


def radial_shifts(field):
    radial = field.shape[-1]
    lane = lax.broadcasted_iota(jnp.int32, field.shape, field.ndim - 1)
    return (
        jnp.where(lane == 0, 0.0, pltpu.roll(field, 1, field.ndim - 1)),
        jnp.where(lane == radial - 1, 0.0, pltpu.roll(field, radial - 1, field.ndim - 1)),
    )


def two_levels(wide, first_coef, second_coef, shifted, middle, write):
    reach, cols, radial = wide.shape
    height = reach - 4
    lat, _ = position("lat")
    bounds = (lat > 0).astype(jnp.int32), (lat < lax.axis_size("lat") - 1).astype(jnp.int32)

    for row in range(reach):
        for place, moved in enumerate(radial_shifts(wide[row])):
            shifted[place, row] = moved

    def taps_of(coef, at):
        return [jnp.broadcast_to(coef[k:k + 1, at], (SUBLANES, LANES)) for k in range(27)]

    def first_level(tile, _):
        at = pl.ds(pl.multiple_of(tile * LANES, LANES), LANES)
        taps = taps_of(first_coef, at)
        for row in range(1, reach - 1):
            parts = []
            for side in (slice(0, SUBLANES), slice(SUBLANES, cols)):
                sums = [None, None, None]
                for above in (-1, 0, 1):
                    window = (shifted[0, row + above, side, at], wide[row + above, side, at], shifted[1, row + above, side, at])
                    for beside in range(3):
                        for step in range(3):
                            term = taps[(above + 1) * 9 + beside * 3 + step] * window[step]
                            sums[beside] = term if sums[beside] is None else sums[beside] + term
                parts.append(sums)
            whole = [jnp.concatenate([parts[0][b], parts[1][b]], axis=0) for b in range(3)]
            value = whole[1] + pltpu.roll(whole[0], 1, 0) + pltpu.roll(whole[2], cols - 1, 0)
            if row in (1, reach - 2):
                value = either(bounds[row != 1], value, jnp.zeros_like(value))
            middle[0, 0, row - 1, :, at] = pltpu.roll(value, 1, 0)[:SUBLANES]
            middle[1, 0, row - 1, :, at] = value[:SUBLANES]
            middle[2, 0, row - 1, :, at] = pltpu.roll(value, cols - 1, 0)[:SUBLANES]
        return 0

    lax.fori_loop(0, radial // LANES, first_level, 0)

    for row in range(reach - 2):
        for beside in range(3):
            for place, moved in enumerate(radial_shifts(middle[beside, 0, row])):
                middle[beside, place + 1, row] = moved

    order = (1, 0, 2)

    def second_level(tile, _):
        at = pl.ds(pl.multiple_of(tile * LANES, LANES), LANES)
        taps = taps_of(second_coef, at)
        for row in range(height):
            total = None
            for above in range(3):
                for beside in range(3):
                    for step in range(3):
                        term = taps[above * 9 + beside * 3 + step] * middle[beside, order[step], row + above, :, at]
                        total = term if total is None else total + term
            write(row, at, total)
        return 0

    lax.fori_loop(0, radial // LANES, second_level, 0)


def open_kernel(
    counts_in, offsets_in, residual_in, pixel_in, bins_in, latent_in, out, latent, to_partner, to_outer,
    counts, offsets, residual, pixel, bins, arrived,
):
    pairs = (
        (latent_in, latent), (counts_in, counts), (offsets_in, offsets),
        (residual_in, residual), (pixel_in, pixel), (bins_in, bins),
    )
    copies = [pltpu.make_async_copy(source, target, arrived.at[i]) for i, (source, target) in enumerate(pairs)]
    for copy in copies:
        copy.start()
    copies[0].wait()
    height, _, radial = latent.shape
    pack_sides([latent[row] for row in range(height)], to_partner, to_outer)
    for copy in copies[1:]:
        copy.wait()

    lane = lax.broadcasted_iota(jnp.int32, (SUBLANES, LANES), 1)
    row = lax.broadcasted_iota(jnp.int32, (SUBLANES, LANES), 0)
    slot = row * LANES + lane
    for owner in range(out.shape[0]):
        start = offsets[0, owner]
        first = lax.shift_right_logical(start, 7)
        part = lax.bitwise_and(start, LANES - 1)
        live = slot < counts[0, owner]

        def window(values):
            turned = pltpu.roll(values, lax.bitwise_and(LANES - part, LANES - 1), 1)
            joined = jnp.where(lane < LANES - part, turned, pltpu.roll(turned, SUBLANES - 1, 0))
            return jnp.where(live, joined, 0.0)

        at = pl.ds(first, SUBLANES)
        cell = (pixel[at, :] * radial + bins[at, :]).astype(jnp.float32)
        out[owner] = jnp.where(row < RUNS, window(residual[at, :]), pltpu.roll(window(cell), RUNS, 0))


def behind_of(got, *, radial, pixels):
    half = radial // 2
    classes = 2 * pixels
    shards = got.shape[0]
    column = lax.broadcasted_iota(jnp.int32, (classes, LANES), 0).astype(jnp.float32).astype(jnp.bfloat16)
    place = lax.broadcasted_iota(jnp.int32, (half, LANES), 0).astype(jnp.float32).astype(jnp.bfloat16)
    zero = jnp.zeros((), jnp.bfloat16)
    one = jnp.ones((), jnp.bfloat16)

    def tall(row, height):
        return jnp.concatenate([jnp.broadcast_to(row, (16, LANES)).astype(jnp.bfloat16)] * (height // 16), axis=0)

    def product(shard):
        tile = got[shard]
        cell = tile.astype(jnp.int32)
        pixel = lax.shift_right_logical(cell, radial.bit_length() - 1)
        bins = lax.bitwise_and(cell, radial - 1)
        upper = (bins >= half).astype(jnp.int32)
        label = (upper * pixels + pixel).astype(jnp.float32)
        low = (bins - upper * half).astype(jnp.float32)
        coarse = tile.astype(jnp.bfloat16).astype(jnp.float32)
        rest = tile - coarse
        left, right = [], []
        for run in range(RUNS):
            mine = tall(label[RUNS + run:RUNS + run + 1], classes) == column
            left.append(jnp.concatenate([
                jnp.where(mine, tall(coarse[run:run + 1], classes), zero),
                jnp.where(mine, tall(rest[run:run + 1], classes), zero),
            ], axis=0))
            right.append(jnp.where(tall(low[RUNS + run:RUNS + run + 1], half) >= place, one, zero))
        return lax.dot_general(
            jnp.concatenate(left, axis=1), jnp.concatenate(right, axis=1),
            (((1,), (1,)), ((), ())), preferred_element_type=jnp.float32,
        )

    def step(turn, total):
        for member in range(4):
            total = total + product(4 * turn + member)
        return total

    total = lax.fori_loop(0, shards // 4, step, jnp.zeros((2 * classes, half), jnp.float32))
    both = (total[:classes] + total[classes:]) * bin_width
    near, far = both[:pixels], both[pixels:]
    return near + far[:, :1], far


def bin_kernel(got, density, upstream, to_partner, to_outer):
    height, width, radial = density.shape
    near, far = behind_of(got, radial=radial, pixels=height * width)
    rows = []
    for row in range(height):
        at = slice(row * width, (row + 1) * width)
        rows.append(density[row] * jnp.concatenate([near[at], far[at]], axis=1))
        upstream[row] = rows[row]
    pack_sides(rows, to_partner, to_outer)


def density_kernel(latent, side_0, side_1, end_0, end_1, stencils, out, wide, shifted, middle):
    fill_wide(wide, [latent[row] for row in range(latent.shape[0])], (side_0, side_1), (end_0, end_1))

    def write(row, at, value):
        out[row, :, at] = jnp.exp(value)

    two_levels(wide, stencils.at[0], stencils.at[1], shifted, middle, write)


def back_kernel(latent, upstream, side_0, side_1, end_0, end_1, mirrored, out, wide, shifted, middle):
    fill_wide(wide, [upstream[row] for row in range(upstream.shape[0])], (side_0, side_1), (end_0, end_1))

    def write(row, at, value):
        out[row, :, at] = latent[row, :, at] + value

    two_levels(wide, mirrored.at[1], mirrored.at[0], shifted, middle, write)


def mirror(stencils):
    turned = jnp.flip(stencils, axis=1).reshape(stencils.shape[0], 9, 3, stencils.shape[2])
    edge = jnp.zeros_like(turned[:, :, 0, :1])
    back = jnp.concatenate([edge, turned[:, :, 0, :-1]], axis=-1)
    ahead = jnp.concatenate([turned[:, :, 2, 1:], edge], axis=-1)
    return jnp.stack([back, turned[:, :, 1], ahead], axis=2).reshape(stencils.shape)


def swap(to_partner, to_outer, axis, closed):
    count = lax.axis_size(axis)
    outer = [(i, (i + 1) % count) for i in range(1, count, 2) if closed or i + 1 < count]
    inner = [(i, i + 1) for i in range(0, count - 1, 2)]

    def both_ways(pairs):
        return pairs + [(j, i) for i, j in pairs]

    from_outer = lax.ppermute(to_outer, axis, both_ways(outer))
    return lax.ppermute(to_partner, axis, both_ways(inner)), from_outer


VMEM = pl.BlockSpec(memory_space=pltpu.VMEM)
HBM = pl.BlockSpec(memory_space=pltpu.HBM)
LIMIT = pltpu.CompilerParams(vmem_limit_bytes=32 * 1024 * 1024)


def on_device(residual, star_pixel, star_bin, send_counts, send_offsets, latent, stencils):
    height, width, radial = latent.shape
    shards = send_counts.shape[1]
    slots = residual.shape[0]
    f32 = jnp.float32
    i32 = jnp.int32
    tile = jax.ShapeDtypeStruct((height, width, radial), f32)
    sides = jax.ShapeDtypeStruct((height // 4, SUBLANES, radial), f32)
    ends = jax.ShapeDtypeStruct((3, SUBLANES, radial), f32)
    reach, cols = height + 4, 2 * width
    level_scratch = [
        pltpu.VMEM((reach, cols, radial), f32),
        pltpu.VMEM((2, reach, cols, radial), f32),
        pltpu.VMEM((3, 3, reach - 2, width, radial), f32),
    ]

    def table(values):
        return values.reshape(slots // LANES, LANES)

    packed, latent, to_partner, to_outer = pl.pallas_call(
        open_kernel,
        out_shape=(jax.ShapeDtypeStruct((shards, 2 * RUNS, LANES), f32), tile, sides, sides),
        in_specs=[HBM] * 6,
        out_specs=(VMEM, VMEM, VMEM, VMEM),
        scratch_shapes=[pltpu.SMEM((1, shards), i32)] * 2
        + [pltpu.VMEM((slots // LANES, LANES), kind) for kind in (f32, i32, i32)]
        + [pltpu.SemaphoreType.DMA((6,))],
        compiler_params=LIMIT,
        name="opening",
    )(*[
        pltpu.with_memory_space_constraint(values, pltpu.HBM)
        for values in (send_counts, send_offsets, table(residual), table(star_pixel), table(star_bin), latent)
    ])
    got = lax.all_to_all(packed, ("lat", "lon"), split_axis=0, concat_axis=0, tiled=True)

    def pack_ends(field, beside):
        return pl.pallas_call(
            pack_ends_kernel,
            out_shape=(ends, ends),
            in_specs=[VMEM] * 3,
            out_specs=(VMEM, VMEM),
            compiler_params=LIMIT,
            name="pack_ends",
        )(field, *beside)

    beside = swap(to_partner, to_outer, "lon", True)
    above = swap(*pack_ends(latent, beside), "lat", False)
    density = pl.pallas_call(
        density_kernel,
        out_shape=tile,
        in_specs=[VMEM] * 6,
        out_specs=VMEM,
        scratch_shapes=level_scratch,
        compiler_params=LIMIT,
        name="density",
    )(latent, *beside, *above, stencils)

    upstream, to_partner, to_outer = pl.pallas_call(
        bin_kernel,
        out_shape=(tile, sides, sides),
        in_specs=[VMEM, VMEM],
        out_specs=(VMEM, VMEM, VMEM),
        compiler_params=LIMIT,
        name="binning",
    )(got, density)
    beside = swap(to_partner, to_outer, "lon", True)
    above = swap(*pack_ends(upstream, beside), "lat", False)
    return pl.pallas_call(
        back_kernel,
        out_shape=tile,
        in_specs=[VMEM] * 7,
        out_specs=VMEM,
        scratch_shapes=level_scratch,
        compiler_params=LIMIT,
        name="back",
    )(latent, upstream, *beside, *above, mirror(stencils))


def solution(mesh):
    return jax.shard_map(
        on_device,
        mesh=mesh,
        in_specs=(
            P(("lat", "lon")),
            P(("lat", "lon")),
            P(("lat", "lon")),
            P(("lat", "lon"), None),
            P(("lat", "lon"), None),
            P("lat", "lon", None),
            P(),
        ),
        out_specs=P("lat", "lon", None),
        check_vma=False,
    )
```

```python
import functools

import jax
import jax.numpy as jnp
from jax import lax
from jax.experimental import pallas as pl
from jax.experimental.pallas import tpu as pltpu
from jax.sharding import PartitionSpec as P

CAP = 512
LANES = 128
SUBLANES = 8
RUNS = CAP // LANES
bin_width = 0.0625


def position(axis):
    index = lax.axis_index(axis)
    return index, lax.bitwise_and(index, 1)


def either(flag, if_set, if_clear):
    return jnp.where(jnp.full(if_set.shape, flag, jnp.int32) > 0, if_set, if_clear)


def sublane(radial):
    return lax.broadcasted_iota(jnp.int32, (SUBLANES, radial), 0)


def pack_sides(rows, to_partner, to_outer):
    _, odd = position("lon")
    sub = sublane(rows[0].shape[1])
    for group in range(len(rows) // 4):
        before, after = rows[4 * group], rows[4 * group]
        for k in range(1, 4):
            row = rows[4 * group + k]
            pair = lax.shift_right_logical(sub, 1)
            before = jnp.where(pair == k, pltpu.roll(row, 2 * k, 0), before)
            after = jnp.where(pair == 3 - k, pltpu.roll(row, SUBLANES - 2 * k, 0), after)
        to_partner[group] = either(odd, before, after)
        to_outer[group] = either(odd, after, before)


def unpack_sides(from_partner, from_outer, height):
    _, odd = position("lon")
    sub = sublane(from_partner.shape[2])
    tiles = []
    for group in range(height // 4):
        partner, outer = from_partner[group], from_outer[group]
        before, after = either(odd, partner, outer), either(odd, outer, partner)
        for k in range(4):
            if k:
                tiles.append(jnp.where(sub < 4, pltpu.roll(after, SUBLANES - 2 * k, 0), pltpu.roll(before, 2 * k, 0)))
            else:
                tiles.append(jnp.where(sub < 4, after, before))
    return tiles


def pack_ends_kernel(field, from_partner, from_outer, to_partner, to_outer):
    height, _, radial = field.shape
    _, odd = position("lat")
    sub = sublane(radial)
    outside = (sub < 2) | (sub >= 6)
    tiles = unpack_sides(from_partner, from_outer, height)

    def ends(first):
        return (
            field[first],
            field[first + 1],
            jnp.where(outside, tiles[first], pltpu.roll(tiles[first + 1], 4, 0)),
        )

    for place, (top, bottom) in enumerate(zip(ends(0), ends(height - 2))):
        to_partner[place] = either(odd, top, bottom)
        to_outer[place] = either(odd, bottom, top)


def radial_shifts(field):
    radial = field.shape[-1]
    lane = lax.broadcasted_iota(jnp.int32, field.shape, field.ndim - 1)
    return (
        jnp.where(lane == 0, 0.0, pltpu.roll(field, 1, field.ndim - 1)),
        jnp.where(lane == radial - 1, 0.0, pltpu.roll(field, radial - 1, field.ndim - 1)),
    )


def taps_of(coef, at):
    return [jnp.broadcast_to(coef[k:k + 1, at], (SUBLANES, LANES)) for k in range(27)]


def tiles_of_bins(radial, body):
    def step(tile, _):
        body(pl.ds(pl.multiple_of(tile * LANES, LANES), LANES))
        return 0

    lax.fori_loop(0, radial // LANES, step, 0)


def first_level(wide, shifted, coef, centers, middle, real):
    reach, cols, radial = wide.shape
    for row in range(reach):
        for place, moved in enumerate(radial_shifts(wide[row])):
            shifted[place, row] = moved

    def body(at):
        taps = taps_of(coef, at)
        for place, row in enumerate(centers):
            parts = []
            for side in (slice(0, SUBLANES), slice(SUBLANES, cols)):
                sums = [None, None, None]
                for above in (-1, 0, 1):
                    window = (shifted[0, row + above, side, at], wide[row + above, side, at], shifted[1, row + above, side, at])
                    for beside in range(3):
                        for step in range(3):
                            term = taps[(above + 1) * 9 + beside * 3 + step] * window[step]
                            sums[beside] = term if sums[beside] is None else sums[beside] + term
                parts.append(sums)
            whole = [jnp.concatenate([parts[0][b], parts[1][b]], axis=0) for b in range(3)]
            value = whole[1] + pltpu.roll(whole[0], 1, 0) + pltpu.roll(whole[2], cols - 1, 0)
            if real[place] is not None:
                value = either(real[place], value, jnp.zeros_like(value))
            middle[0, 1, place, :, at] = pltpu.roll(value, 1, 0)[:SUBLANES]
            middle[1, 1, place, :, at] = value[:SUBLANES]
            middle[2, 1, place, :, at] = pltpu.roll(value, cols - 1, 0)[:SUBLANES]

    tiles_of_bins(radial, body)
    for place in range(len(centers)):
        for beside in range(3):
            for step, moved in zip((0, 2), radial_shifts(middle[beside, 1, place])):
                middle[beside, step, place] = moved


def second_level(coef, windows, radial, write):
    def body(at):
        taps = taps_of(coef, at)
        for row, around in windows.items():
            total = None
            for above, (buffer, place) in enumerate(around):
                for beside in range(3):
                    for step in range(3):
                        term = taps[above * 9 + beside * 3 + step] * buffer[beside, step, place, :, at]
                        total = term if total is None else total + term
            write(row, at, total)

    tiles_of_bins(radial, body)


def refine_inside_kernel(coefs, finish, field, side_0, side_1, stencils, extra, out, middle, wide, shifted):
    height, width, radial = field.shape
    tiles = unpack_sides(side_0, side_1, height)
    for row in range(height):
        wide[row, :width] = field[row]
        wide[row, width:] = tiles[row]
    first_level(wide, shifted, stencils.at[coefs[0]], range(1, height - 1), middle, [None] * (height - 2))

    def write(row, at, value):
        out[row - 2, :, at] = finish(value, extra[row, :, at])

    windows = {row: [(middle, row - 2 + k) for k in range(3)] for row in range(2, height - 2)}
    second_level(stencils.at[coefs[1]], windows, radial, write)


def refine_ends_kernel(
    coefs, finish, field, side_0, side_1, end_0, end_1, stencils, extra, inside, inner, out, middle, wide, shifted
):
    height, width, radial = field.shape
    tiles = unpack_sides(side_0, side_1, height)
    lat, odd = position("lat")
    for place in range(3):
        partner, outer = end_0[place], end_1[place]
        for first, pack in ((0, either(odd, partner, outer)), (6, either(odd, outer, partner))):
            if place < 2:
                wide[first + place, :width] = pack
            else:
                wide[first, width:] = pack
                wide[first + 1, width:] = pltpu.roll(pack, 4, 0)
    for place, row in ((2, 0), (3, 1), (4, height - 2), (5, height - 1)):
        wide[place, :width] = field[row]
        wide[place, width:] = tiles[row]
    above = (lat > 0).astype(jnp.int32)
    below = (lat < lax.axis_size("lat") - 1).astype(jnp.int32)
    first_level(wide, shifted, stencils.at[coefs[0]], (1, 2, 5, 6), middle, [above, None, None, below])

    def write(row, at, value):
        out[row, :, at] = finish(value, extra[row, :, at])

    last = height - 3
    top = [(middle, 0), (middle, 1), (inside, 0), (inside, 1)]
    bottom = [(inside, last - 1), (inside, last), (middle, 2), (middle, 3)]
    windows = {0: top[:3], 1: top[1:], height - 2: bottom[:3], height - 1: bottom[1:]}
    second_level(stencils.at[coefs[1]], windows, radial, write)
    for row in range(2, height - 2):
        out[row] = inner[row - 2]


def open_kernel(
    counts_in, offsets_in, residual_in, pixel_in, bins_in, latent_in, out, latent, to_partner, to_outer,
    counts, offsets, residual, pixel, bins, arrived,
):
    pairs = (
        (latent_in, latent), (counts_in, counts), (offsets_in, offsets),
        (residual_in, residual), (pixel_in, pixel), (bins_in, bins),
    )
    copies = [pltpu.make_async_copy(source, target, arrived.at[i]) for i, (source, target) in enumerate(pairs)]
    for copy in copies:
        copy.start()
    copies[0].wait()
    height, _, radial = latent.shape
    pack_sides([latent[row] for row in range(height)], to_partner, to_outer)
    for copy in copies[1:]:
        copy.wait()

    lane = lax.broadcasted_iota(jnp.int32, (SUBLANES, LANES), 1)
    row = lax.broadcasted_iota(jnp.int32, (SUBLANES, LANES), 0)
    slot = row * LANES + lane
    for owner in range(out.shape[0]):
        start = offsets[0, owner]
        first = lax.shift_right_logical(start, 7)
        part = lax.bitwise_and(start, LANES - 1)
        live = slot < counts[0, owner]

        def window(values):
            turned = pltpu.roll(values, lax.bitwise_and(LANES - part, LANES - 1), 1)
            joined = jnp.where(lane < LANES - part, turned, pltpu.roll(turned, SUBLANES - 1, 0))
            return jnp.where(live, joined, 0.0)

        at = pl.ds(first, SUBLANES)
        cell = (pixel[at, :] * radial + bins[at, :]).astype(jnp.float32)
        out[owner] = jnp.where(row < RUNS, window(residual[at, :]), pltpu.roll(window(cell), RUNS, 0))


def behind_of(got, *, radial, pixels):
    half = radial // 2
    classes = 2 * pixels
    shards = got.shape[0]
    bf16 = jnp.bfloat16
    column = lax.broadcasted_iota(jnp.int32, (classes, LANES), 0).astype(jnp.float32).astype(bf16)
    place = (lax.broadcasted_iota(jnp.int32, (half, LANES), 0) + 1).astype(jnp.float32).astype(bf16)
    zero = jnp.zeros((), bf16)
    one = jnp.ones((), bf16)

    def tall(row, height):
        return jnp.concatenate([jnp.broadcast_to(row, (16, LANES)).astype(bf16)] * (height // 16), axis=0)

    def product(shard):
        tile = got[shard]
        cell = tile.astype(jnp.int32)
        pixel = lax.shift_right_logical(cell, radial.bit_length() - 1)
        bins = lax.bitwise_and(cell, radial - 1)
        upper = (bins >= half).astype(jnp.int32)
        label = (upper * pixels + pixel).astype(jnp.float32)
        low = (bins - upper * half + 1).astype(jnp.float32)
        coarse = tile.astype(bf16).astype(jnp.float32)
        rest = tile - coarse
        left, right = [], []
        for run in range(RUNS):
            away = tall(label[RUNS + run:RUNS + run + 1], classes) - column
            mine = jnp.maximum(one - away * away, zero)
            left.append(jnp.concatenate([
                mine * tall(coarse[run:run + 1], classes),
                mine * tall(rest[run:run + 1], classes),
            ], axis=0))
            right.append(jnp.maximum(tall(low[RUNS + run:RUNS + run + 1], half), place))
        return lax.dot_general(
            jnp.concatenate(left, axis=1), jnp.concatenate(right, axis=1),
            (((1,), (1,)), ((), ())), preferred_element_type=jnp.float32,
        )

    def step(turn, total):
        for member in range(4):
            total = total + product(4 * turn + member)
        return total

    total = lax.fori_loop(0, shards // 4, step, jnp.zeros((2 * classes, half), jnp.float32))
    both = (total[:classes] + total[classes:]) * bin_width
    every = both[:, half - 1:] * (1.0 / half)
    lane = lax.broadcasted_iota(jnp.int32, both.shape, 1)
    at_least = jnp.where(lane == 0, every, pltpu.roll(both, 1, 1) - both + every)
    near, far = at_least[:pixels], at_least[pixels:]
    return near + far[:, :1], far


def bin_kernel(got, density, upstream, to_partner, to_outer):
    height, width, radial = density.shape
    near, far = behind_of(got, radial=radial, pixels=height * width)
    rows = []
    for row in range(height):
        at = slice(row * width, (row + 1) * width)
        rows.append(density[row] * jnp.concatenate([near[at], far[at]], axis=1))
        upstream[row] = rows[row]
    pack_sides(rows, to_partner, to_outer)


def mirror(stencils):
    turned = jnp.flip(stencils, axis=1).reshape(stencils.shape[0], 9, 3, stencils.shape[2])
    edge = jnp.zeros_like(turned[:, :, 0, :1])
    back = jnp.concatenate([edge, turned[:, :, 0, :-1]], axis=-1)
    ahead = jnp.concatenate([turned[:, :, 2, 1:], edge], axis=-1)
    return jnp.stack([back, turned[:, :, 1], ahead], axis=2).reshape(stencils.shape)


def swap(to_partner, to_outer, axis, closed):
    count = lax.axis_size(axis)
    outer = [(i, (i + 1) % count) for i in range(1, count, 2) if closed or i + 1 < count]
    inner = [(i, i + 1) for i in range(0, count - 1, 2)]

    def both_ways(pairs):
        return pairs + [(j, i) for i, j in pairs]

    from_outer = lax.ppermute(to_outer, axis, both_ways(outer))
    return lax.ppermute(to_partner, axis, both_ways(inner)), from_outer


VMEM = pl.BlockSpec(memory_space=pltpu.VMEM)
HBM = pl.BlockSpec(memory_space=pltpu.HBM)
LIMIT = pltpu.CompilerParams(vmem_limit_bytes=32 * 1024 * 1024)


def on_device(residual, star_pixel, star_bin, send_counts, send_offsets, latent, stencils):
    height, width, radial = latent.shape
    shards = send_counts.shape[1]
    slots = residual.shape[0]
    f32 = jnp.float32
    i32 = jnp.int32
    tile = jax.ShapeDtypeStruct((height, width, radial), f32)
    sides = jax.ShapeDtypeStruct((height // 4, SUBLANES, radial), f32)
    ends = jax.ShapeDtypeStruct((3, SUBLANES, radial), f32)

    def table(values):
        return values.reshape(slots // LANES, LANES)

    packed, latent, *to_sides = pl.pallas_call(
        open_kernel,
        out_shape=(jax.ShapeDtypeStruct((shards, 2 * RUNS, LANES), f32), tile, sides, sides),
        in_specs=[HBM] * 6,
        out_specs=(VMEM, VMEM, VMEM, VMEM),
        scratch_shapes=[pltpu.SMEM((1, shards), i32)] * 2
        + [pltpu.VMEM((slots // LANES, LANES), kind) for kind in (f32, i32, i32)]
        + [pltpu.SemaphoreType.DMA((6,))],
        compiler_params=LIMIT,
        name="opening",
    )(*[
        pltpu.with_memory_space_constraint(values, pltpu.HBM)
        for values in (send_counts, send_offsets, table(residual), table(star_pixel), table(star_bin), latent)
    ])
    got = lax.all_to_all(packed, ("lat", "lon"), split_axis=0, concat_axis=0, tiled=True)

    def refined(field, to_sides, coefs, table, extra, finish, name):
        beside = swap(*to_sides, "lon", True)
        to_ends = pl.pallas_call(
            pack_ends_kernel,
            out_shape=(ends, ends),
            in_specs=[VMEM] * 3,
            out_specs=(VMEM, VMEM),
            compiler_params=LIMIT,
            name=name + "_pack",
        )(field, *beside)
        above = swap(*to_ends, "lat", False)
        rows = pltpu.VMEM((height, 2 * width, radial), f32)
        moved = pltpu.VMEM((2, height, 2 * width, radial), f32)
        inner, middle = pl.pallas_call(
            functools.partial(refine_inside_kernel, coefs, finish),
            out_shape=(
                jax.ShapeDtypeStruct((height - 4, width, radial), f32),
                jax.ShapeDtypeStruct((3, 3, height - 2, width, radial), f32),
            ),
            in_specs=[VMEM] * 5,
            out_specs=(VMEM, VMEM),
            scratch_shapes=[rows, moved],
            compiler_params=LIMIT,
            name=name + "_inside",
        )(field, *beside, table, extra)
        return pl.pallas_call(
            functools.partial(refine_ends_kernel, coefs, finish),
            out_shape=tile,
            in_specs=[VMEM] * 9,
            out_specs=VMEM,
            scratch_shapes=[pltpu.VMEM((3, 3, 4, width, radial), f32), rows, moved],
            compiler_params=LIMIT,
            name=name + "_ends",
        )(field, *beside, *above, table, extra, middle, inner)

    density = refined(latent, to_sides, (0, 1), stencils, latent, lambda value, _: jnp.exp(value), "density")
    upstream, *to_sides = pl.pallas_call(
        bin_kernel,
        out_shape=(tile, sides, sides),
        in_specs=[VMEM, VMEM],
        out_specs=(VMEM, VMEM, VMEM),
        compiler_params=LIMIT,
        name="binning",
    )(got, density)
    return refined(upstream, to_sides, (1, 0), mirror(stencils), latent, lambda value, field: field + value, "back")


def solution(mesh):
    return jax.shard_map(
        on_device,
        mesh=mesh,
        in_specs=(
            P(("lat", "lon")),
            P(("lat", "lon")),
            P(("lat", "lon")),
            P(("lat", "lon"), None),
            P(("lat", "lon"), None),
            P("lat", "lon", None),
            P(),
        ),
        out_specs=P("lat", "lon", None),
        check_vma=False,
    )
```

```python
import functools

import jax
import jax.numpy as jnp
from jax import lax
from jax.experimental import pallas as pl
from jax.experimental.pallas import tpu as pltpu
from jax.sharding import PartitionSpec as P

CAP = 512
LANES = 128
SUBLANES = 8
RUNS = CAP // LANES
bin_width = 0.0625


def position(axis):
    index = lax.axis_index(axis)
    return index, lax.bitwise_and(index, 1)


def either(flag, if_set, if_clear):
    return jnp.where(jnp.full(if_set.shape, flag, jnp.int32) > 0, if_set, if_clear)


def sublane(radial):
    return lax.broadcasted_iota(jnp.int32, (SUBLANES, radial), 0)


def pack_sides(rows, to_partner, to_outer):
    _, odd = position("lon")
    sub = sublane(rows[0].shape[1])
    for group in range(len(rows) // 4):
        before, after = rows[4 * group], rows[4 * group]
        for k in range(1, 4):
            row = rows[4 * group + k]
            pair = lax.shift_right_logical(sub, 1)
            before = jnp.where(pair == k, pltpu.roll(row, 2 * k, 0), before)
            after = jnp.where(pair == 3 - k, pltpu.roll(row, SUBLANES - 2 * k, 0), after)
        to_partner[group] = either(odd, before, after)
        to_outer[group] = either(odd, after, before)


def unpack_sides(from_partner, from_outer, height):
    _, odd = position("lon")
    sub = sublane(from_partner.shape[2])
    tiles = []
    for group in range(height // 4):
        partner, outer = from_partner[group], from_outer[group]
        before, after = either(odd, partner, outer), either(odd, outer, partner)
        for k in range(4):
            if k:
                tiles.append(jnp.where(sub < 4, pltpu.roll(after, SUBLANES - 2 * k, 0), pltpu.roll(before, 2 * k, 0)))
            else:
                tiles.append(jnp.where(sub < 4, after, before))
    return tiles


def pack_ends_kernel(field, from_partner, from_outer, to_partner, to_outer):
    height, _, radial = field.shape
    _, odd = position("lat")
    sub = sublane(radial)
    outside = (sub < 2) | (sub >= 6)
    tiles = unpack_sides(from_partner, from_outer, height)

    def ends(first):
        return (
            field[first],
            field[first + 1],
            jnp.where(outside, tiles[first], pltpu.roll(tiles[first + 1], 4, 0)),
        )

    for place, (top, bottom) in enumerate(zip(ends(0), ends(height - 2))):
        to_partner[place] = either(odd, top, bottom)
        to_outer[place] = either(odd, bottom, top)


def radial_shifts(field):
    radial = field.shape[-1]
    lane = lax.broadcasted_iota(jnp.int32, field.shape, field.ndim - 1)
    return (
        jnp.where(lane == 0, 0.0, pltpu.roll(field, 1, field.ndim - 1)),
        jnp.where(lane == radial - 1, 0.0, pltpu.roll(field, radial - 1, field.ndim - 1)),
    )


def taps_of(coef, at):
    return [jnp.broadcast_to(coef[k:k + 1, at], (SUBLANES, LANES)) for k in range(27)]


def tiles_of_bins(radial, body):
    def step(tile, _):
        body(pl.ds(pl.multiple_of(tile * LANES, LANES), LANES))
        return 0

    lax.fori_loop(0, radial // LANES, step, 0)


def first_level(wide, shifted, coef, centers, middle, real):
    reach, cols, radial = wide.shape
    for row in range(reach):
        for place, moved in enumerate(radial_shifts(wide[row])):
            shifted[place, row] = moved

    def body(at):
        taps = taps_of(coef, at)
        for place, row in enumerate(centers):
            parts = []
            for side in (slice(0, SUBLANES), slice(SUBLANES, cols)):
                sums = [None, None, None]
                for above in (-1, 0, 1):
                    window = (shifted[0, row + above, side, at], wide[row + above, side, at], shifted[1, row + above, side, at])
                    for beside in range(3):
                        for step in range(3):
                            term = taps[(above + 1) * 9 + beside * 3 + step] * window[step]
                            sums[beside] = term if sums[beside] is None else sums[beside] + term
                parts.append(sums)
            whole = [jnp.concatenate([parts[0][b], parts[1][b]], axis=0) for b in range(3)]
            value = whole[1] + pltpu.roll(whole[0], 1, 0) + pltpu.roll(whole[2], cols - 1, 0)
            if real[place] is not None:
                value = either(real[place], value, jnp.zeros_like(value))
            middle[0, 1, place, :, at] = pltpu.roll(value, 1, 0)[:SUBLANES]
            middle[1, 1, place, :, at] = value[:SUBLANES]
            middle[2, 1, place, :, at] = pltpu.roll(value, cols - 1, 0)[:SUBLANES]

    tiles_of_bins(radial, body)
    for place in range(len(centers)):
        for beside in range(3):
            for step, moved in zip((0, 2), radial_shifts(middle[beside, 1, place])):
                middle[beside, step, place] = moved


def second_level(coef, windows, radial, write):
    def body(at):
        taps = taps_of(coef, at)
        for row, around in windows.items():
            total = None
            for above, (buffer, place) in enumerate(around):
                for beside in range(3):
                    for step in range(3):
                        term = taps[above * 9 + beside * 3 + step] * buffer[beside, step, place, :, at]
                        total = term if total is None else total + term
            write(row, at, total)

    tiles_of_bins(radial, body)


def refine_inside_kernel(coefs, finish, field, side_0, side_1, stencils, extra, out, middle, wide, shifted):
    height, width, radial = field.shape
    tiles = unpack_sides(side_0, side_1, height)
    for row in range(height):
        wide[row, :width] = field[row]
        wide[row, width:] = tiles[row]
    first_level(wide, shifted, stencils.at[coefs[0]], range(1, height - 1), middle, [None] * (height - 2))

    def write(row, at, value):
        out[row - 2, :, at] = finish(value, extra[row, :, at])

    windows = {row: [(middle, row - 2 + k) for k in range(3)] for row in range(2, height - 2)}
    second_level(stencils.at[coefs[1]], windows, radial, write)


def refine_ends_kernel(
    coefs, finish, finish_inner, packs, field, side_0, side_1, end_0, end_1, stencils, extra, inside, inner, *rest
):
    out, *to_sides, middle, wide, shifted = rest
    height, width, radial = field.shape
    tiles = unpack_sides(side_0, side_1, height)
    lat, odd = position("lat")
    for place in range(3):
        partner, outer = end_0[place], end_1[place]
        for first, pack in ((0, either(odd, partner, outer)), (6, either(odd, outer, partner))):
            if place < 2:
                wide[first + place, :width] = pack
            else:
                wide[first, width:] = pack
                wide[first + 1, width:] = pltpu.roll(pack, 4, 0)
    for place, row in ((2, 0), (3, 1), (4, height - 2), (5, height - 1)):
        wide[place, :width] = field[row]
        wide[place, width:] = tiles[row]
    above = (lat > 0).astype(jnp.int32)
    below = (lat < lax.axis_size("lat") - 1).astype(jnp.int32)
    first_level(wide, shifted, stencils.at[coefs[0]], (1, 2, 5, 6), middle, [above, None, None, below])

    def write(row, at, value):
        out[row, :, at] = finish(value, extra[row, :, at])

    last = height - 3
    top = [(middle, 0), (middle, 1), (inside, 0), (inside, 1)]
    bottom = [(inside, last - 1), (inside, last), (middle, 2), (middle, 3)]
    windows = {0: top[:3], 1: top[1:], height - 2: bottom[:3], height - 1: bottom[1:]}
    second_level(stencils.at[coefs[1]], windows, radial, write)
    for row in range(2, height - 2):
        out[row] = finish_inner(inner[row - 2], extra[row])
    if packs:
        pack_sides([out[row] for row in range(height)], *to_sides)


def open_kernel(
    counts_in, offsets_in, residual_in, pixel_in, bins_in, latent_in, out, latent, to_partner, to_outer,
    counts, offsets, residual, pixel, bins, arrived,
):
    pairs = (
        (latent_in, latent), (counts_in, counts), (offsets_in, offsets),
        (residual_in, residual), (pixel_in, pixel), (bins_in, bins),
    )
    copies = [pltpu.make_async_copy(source, target, arrived.at[i]) for i, (source, target) in enumerate(pairs)]
    for copy in copies:
        copy.start()
    copies[0].wait()
    height, _, radial = latent.shape
    pack_sides([latent[row] for row in range(height)], to_partner, to_outer)
    for copy in copies[1:]:
        copy.wait()

    lane = lax.broadcasted_iota(jnp.int32, (SUBLANES, LANES), 1)
    row = lax.broadcasted_iota(jnp.int32, (SUBLANES, LANES), 0)
    slot = row * LANES + lane
    for owner in range(out.shape[0]):
        start = offsets[0, owner]
        first = lax.shift_right_logical(start, 7)
        part = lax.bitwise_and(start, LANES - 1)
        live = slot < counts[0, owner]

        def window(values):
            turned = pltpu.roll(values, lax.bitwise_and(LANES - part, LANES - 1), 1)
            joined = jnp.where(lane < LANES - part, turned, pltpu.roll(turned, SUBLANES - 1, 0))
            return jnp.where(live, joined, 0.0)

        at = pl.ds(first, SUBLANES)
        cell = (pixel[at, :] * radial + bins[at, :]).astype(jnp.float32)
        out[owner] = jnp.where(row < RUNS, window(residual[at, :]), pltpu.roll(window(cell), RUNS, 0))


def behind_of(got, *, radial, pixels):
    half = radial // 2
    classes = 2 * pixels
    shards, rows, _ = got.shape
    bf16 = jnp.bfloat16
    column = lax.broadcasted_iota(jnp.int32, (classes, LANES), 0).astype(jnp.float32).astype(bf16)
    places = [
        (lax.broadcasted_iota(jnp.int32, (LANES, LANES), 1) + (first + 1)).astype(jnp.float32).astype(bf16)
        for first in range(0, half, LANES)
    ]
    zero = jnp.zeros((), bf16)
    one = jnp.ones((), bf16)

    def tall(row):
        return jnp.concatenate([jnp.broadcast_to(row, (16, LANES)).astype(bf16)] * (classes // 16), axis=0)

    tiles = got[...].reshape(shards * rows, LANES)
    cell = tiles.astype(jnp.int32)
    pixel = lax.shift_right_logical(cell, radial.bit_length() - 1)
    bins = lax.bitwise_and(cell, radial - 1)
    upper = (bins >= half).astype(jnp.int32)
    label = (upper * pixels + pixel).astype(jnp.float32)
    lows = jnp.transpose((bins - upper * half + 1).astype(jnp.float32))
    coarse = tiles.astype(bf16).astype(jnp.float32)
    rest = tiles - coarse

    total = jnp.zeros((2 * classes, half), jnp.float32)
    for first in range(0, shards, 2):
        left, right = [], []
        for run in range(2 * RUNS):
            row = (first + run // RUNS) * rows + run % RUNS
            away = tall(label[row + RUNS:row + RUNS + 1]) - column
            mine = jnp.maximum(one - away * away, zero)
            left.append(jnp.concatenate([mine * tall(coarse[row:row + 1]), mine * tall(rest[row:row + 1])], axis=0))
            low = jnp.broadcast_to(lows[:, row + RUNS:row + RUNS + 1], (LANES, LANES)).astype(bf16)
            right.append(jnp.concatenate([jnp.maximum(low, place) for place in places], axis=1))
        total = total + jnp.dot(
            jnp.concatenate(left, axis=1), jnp.concatenate(right, axis=0), preferred_element_type=jnp.float32
        )
    both = (total[:classes] + total[classes:]) * bin_width
    every = both[:, half - 1:] * (1.0 / half)
    lane = lax.broadcasted_iota(jnp.int32, both.shape, 1)
    at_least = jnp.where(lane == 0, every, pltpu.roll(both, 1, 1) - both + every)
    near, far = at_least[:pixels], at_least[pixels:]
    return near + far[:, :1], far


def bin_kernel(got, _, behind):
    height, width, radial = behind.shape
    near, far = behind_of(got, radial=radial, pixels=height * width)
    for row in range(height):
        at = slice(row * width, (row + 1) * width)
        behind[row] = jnp.concatenate([near[at], far[at]], axis=1)


def mirror(stencils):
    turned = jnp.flip(stencils, axis=1).reshape(stencils.shape[0], 9, 3, stencils.shape[2])
    edge = jnp.zeros_like(turned[:, :, 0, :1])
    back = jnp.concatenate([edge, turned[:, :, 0, :-1]], axis=-1)
    ahead = jnp.concatenate([turned[:, :, 2, 1:], edge], axis=-1)
    return jnp.stack([back, turned[:, :, 1], ahead], axis=2).reshape(stencils.shape)


def swap(to_partner, to_outer, axis, closed):
    count = lax.axis_size(axis)
    outer = [(i, (i + 1) % count) for i in range(1, count, 2) if closed or i + 1 < count]
    inner = [(i, i + 1) for i in range(0, count - 1, 2)]

    def both_ways(pairs):
        return pairs + [(j, i) for i, j in pairs]

    from_partner = lax.ppermute(to_partner, axis, both_ways(inner))
    return from_partner, lax.ppermute(to_outer, axis, both_ways(outer))


VMEM = pl.BlockSpec(memory_space=pltpu.VMEM)
HBM = pl.BlockSpec(memory_space=pltpu.HBM)
LIMIT = pltpu.CompilerParams(vmem_limit_bytes=32 * 1024 * 1024)


def on_device(residual, star_pixel, star_bin, send_counts, send_offsets, latent, stencils):
    height, width, radial = latent.shape
    shards = send_counts.shape[1]
    slots = residual.shape[0]
    f32 = jnp.float32
    i32 = jnp.int32
    tile = jax.ShapeDtypeStruct((height, width, radial), f32)
    sides = jax.ShapeDtypeStruct((height // 4, SUBLANES, radial), f32)
    ends = jax.ShapeDtypeStruct((3, SUBLANES, radial), f32)

    def table(values):
        return values.reshape(slots // LANES, LANES)

    packed, latent, *to_sides = pl.pallas_call(
        open_kernel,
        out_shape=(jax.ShapeDtypeStruct((shards, 2 * RUNS, LANES), f32), tile, sides, sides),
        in_specs=[HBM] * 6,
        out_specs=(VMEM, VMEM, VMEM, VMEM),
        scratch_shapes=[pltpu.SMEM((1, shards), i32)] * 2
        + [pltpu.VMEM((slots // LANES, LANES), kind) for kind in (f32, i32, i32)]
        + [pltpu.SemaphoreType.DMA((6,))],
        compiler_params=LIMIT,
        name="opening",
    )(*[
        pltpu.with_memory_space_constraint(values, pltpu.HBM)
        for values in (send_counts, send_offsets, table(residual), table(star_pixel), table(star_bin), latent)
    ])
    got = lax.all_to_all(packed, ("lat", "lon"), split_axis=0, concat_axis=0, tiled=True)

    def spread(field, to_sides, name):
        beside = swap(*to_sides, "lon", True)
        to_ends = pl.pallas_call(
            pack_ends_kernel,
            out_shape=(ends, ends),
            in_specs=[VMEM] * 3,
            out_specs=(VMEM, VMEM),
            compiler_params=LIMIT,
            name=name + "_pack",
        )(field, *beside)
        return beside, swap(*to_ends, "lat", False)

    rows = pltpu.VMEM((height, 2 * width, radial), f32)
    moved = pltpu.VMEM((2, height, 2 * width, radial), f32)

    def refined_inside(coefs, finish, field, beside, table, extra, name):
        return pl.pallas_call(
            functools.partial(refine_inside_kernel, coefs, finish),
            out_shape=(
                jax.ShapeDtypeStruct((height - 4, width, radial), f32),
                jax.ShapeDtypeStruct((3, 3, height - 2, width, radial), f32),
            ),
            in_specs=[VMEM] * 5,
            out_specs=(VMEM, VMEM),
            scratch_shapes=[rows, moved],
            compiler_params=LIMIT,
            name=name + "_inside",
        )(field, *beside, table, extra)

    def refined_ends(coefs, finish, finish_inner, field, beside, above, table, extra, inner, middle, name, packs):
        return pl.pallas_call(
            functools.partial(refine_ends_kernel, coefs, finish, finish_inner, packs),
            out_shape=(tile, sides, sides) if packs else tile,
            in_specs=[VMEM] * 9,
            out_specs=(VMEM,) * 3 if packs else VMEM,
            scratch_shapes=[pltpu.VMEM((3, 3, 4, width, radial), f32), rows, moved],
            compiler_params=LIMIT,
            name=name + "_ends",
        )(field, *beside, *above, table, extra, middle, inner)

    beside, above = spread(latent, to_sides, "density")
    inner, middle = refined_inside(
        (0, 1), lambda value, _: jnp.exp(value), latent, beside, stencils, latent, "density"
    )
    behind = pl.pallas_call(
        bin_kernel,
        out_shape=tile,
        in_specs=[VMEM, VMEM],
        out_specs=VMEM,
        compiler_params=LIMIT,
        name="binning",
    )(got, inner)
    upstream, *to_sides = refined_ends(
        (0, 1), lambda value, mass: jnp.exp(value) * mass, lambda value, mass: value * mass,
        latent, beside, above, stencils, behind, inner, middle, "density", True,
    )

    mirrored = mirror(stencils)
    beside, above = spread(upstream, to_sides, "back")
    inner, middle = refined_inside(
        (1, 0), lambda value, field: field + value, upstream, beside, mirrored, latent, "back"
    )
    return refined_ends(
        (1, 0), lambda value, field: field + value, lambda value, _: value,
        upstream, beside, above, mirrored, latent, inner, middle, "back", False,
    )


def solution(mesh):
    return jax.shard_map(
        on_device,
        mesh=mesh,
        in_specs=(
            P(("lat", "lon")),
            P(("lat", "lon")),
            P(("lat", "lon")),
            P(("lat", "lon"), None),
            P(("lat", "lon"), None),
            P("lat", "lon", None),
            P(),
        ),
        out_specs=P("lat", "lon", None),
        check_vma=False,
    )
```

```python
import functools

import jax
import jax.numpy as jnp
from jax import lax
from jax.experimental import pallas as pl
from jax.experimental.pallas import tpu as pltpu
from jax.sharding import PartitionSpec as P

CAP = 512
LANES = 128
SUBLANES = 8
RUNS = CAP // LANES
bin_width = 0.0625


def position(axis):
    index = lax.axis_index(axis)
    return index, lax.bitwise_and(index, 1)


def either(flag, if_set, if_clear):
    return jnp.where(jnp.full(if_set.shape, flag, jnp.int32) > 0, if_set, if_clear)


def sublane(radial):
    return lax.broadcasted_iota(jnp.int32, (SUBLANES, radial), 0)


def pack_sides(rows, to_partner, to_outer):
    _, odd = position("lon")
    sub = sublane(rows[0].shape[1])
    for group in range(len(rows) // 4):
        before, after = rows[4 * group], rows[4 * group]
        for k in range(1, 4):
            row = rows[4 * group + k]
            pair = lax.shift_right_logical(sub, 1)
            before = jnp.where(pair == k, pltpu.roll(row, 2 * k, 0), before)
            after = jnp.where(pair == 3 - k, pltpu.roll(row, SUBLANES - 2 * k, 0), after)
        to_partner[group] = either(odd, before, after)
        to_outer[group] = either(odd, after, before)


def unpack_sides(from_partner, from_outer, height):
    _, odd = position("lon")
    sub = sublane(from_partner.shape[2])
    tiles = []
    for group in range(height // 4):
        partner, outer = from_partner[group], from_outer[group]
        before, after = either(odd, partner, outer), either(odd, outer, partner)
        for k in range(4):
            if k:
                tiles.append(jnp.where(sub < 4, pltpu.roll(after, SUBLANES - 2 * k, 0), pltpu.roll(before, 2 * k, 0)))
            else:
                tiles.append(jnp.where(sub < 4, after, before))
    return tiles


def pack_ends_kernel(field, from_partner, from_outer, to_partner, to_outer):
    height, _, radial = field.shape
    _, odd = position("lat")
    sub = sublane(radial)
    outside = (sub < 2) | (sub >= 6)
    tiles = unpack_sides(from_partner, from_outer, height)

    def ends(first):
        return (
            field[first],
            field[first + 1],
            jnp.where(outside, tiles[first], pltpu.roll(tiles[first + 1], 4, 0)),
        )

    for place, (top, bottom) in enumerate(zip(ends(0), ends(height - 2))):
        to_partner[place] = either(odd, top, bottom)
        to_outer[place] = either(odd, bottom, top)


def radial_shifts(field):
    radial = field.shape[-1]
    lane = lax.broadcasted_iota(jnp.int32, field.shape, field.ndim - 1)
    return (
        jnp.where(lane == 0, 0.0, pltpu.roll(field, 1, field.ndim - 1)),
        jnp.where(lane == radial - 1, 0.0, pltpu.roll(field, radial - 1, field.ndim - 1)),
    )


def taps_of(coef, at):
    return [jnp.broadcast_to(coef[k:k + 1, at], (SUBLANES, LANES)) for k in range(27)]


def tiles_of_bins(radial, body):
    def step(tile, _):
        body(pl.ds(pl.multiple_of(tile * LANES, LANES), LANES))
        return 0

    lax.fori_loop(0, radial // LANES, step, 0)


def first_level(wide, shifted, coef, centers, middle, real):
    reach, cols, radial = wide.shape
    for row in range(reach):
        for place, moved in enumerate(radial_shifts(wide[row])):
            shifted[place, row] = moved

    def body(at):
        taps = taps_of(coef, at)
        for place, row in enumerate(centers):
            parts = []
            for side in (slice(0, SUBLANES), slice(SUBLANES, cols)):
                sums = [None, None, None]
                for above in (-1, 0, 1):
                    window = (shifted[0, row + above, side, at], wide[row + above, side, at], shifted[1, row + above, side, at])
                    for beside in range(3):
                        for step in range(3):
                            term = taps[(above + 1) * 9 + beside * 3 + step] * window[step]
                            sums[beside] = term if sums[beside] is None else sums[beside] + term
                parts.append(sums)
            whole = [jnp.concatenate([parts[0][b], parts[1][b]], axis=0) for b in range(3)]
            value = whole[1] + pltpu.roll(whole[0], 1, 0) + pltpu.roll(whole[2], cols - 1, 0)
            if real[place] is not None:
                value = either(real[place], value, jnp.zeros_like(value))
            middle[0, 1, place, :, at] = pltpu.roll(value, 1, 0)[:SUBLANES]
            middle[1, 1, place, :, at] = value[:SUBLANES]
            middle[2, 1, place, :, at] = pltpu.roll(value, cols - 1, 0)[:SUBLANES]

    tiles_of_bins(radial, body)
    for place in range(len(centers)):
        for beside in range(3):
            for step, moved in zip((0, 2), radial_shifts(middle[beside, 1, place])):
                middle[beside, step, place] = moved


def second_level(coef, windows, radial, write):
    def body(at):
        taps = taps_of(coef, at)
        for row, around in windows.items():
            total = None
            for above, (buffer, place) in enumerate(around):
                for beside in range(3):
                    for step in range(3):
                        term = taps[above * 9 + beside * 3 + step] * buffer[beside, step, place, :, at]
                        total = term if total is None else total + term
            write(row, at, total)

    tiles_of_bins(radial, body)


def refine_inside_kernel(coefs, finish, field, side_0, side_1, stencils, extra, out, middle, wide, shifted):
    height, width, radial = field.shape
    tiles = unpack_sides(side_0, side_1, height)
    for row in range(height):
        wide[row, :width] = field[row]
        wide[row, width:] = tiles[row]
    first_level(wide, shifted, stencils.at[coefs[0]], range(1, height - 1), middle, [None] * (height - 2))

    def write(row, at, value):
        out[row - 2, :, at] = finish(value, extra[row, :, at])

    windows = {row: [(middle, row - 2 + k) for k in range(3)] for row in range(2, height - 2)}
    second_level(stencils.at[coefs[1]], windows, radial, write)


def refine_ends_kernel(
    coefs, finish, finish_inner, packs, field, side_0, side_1, end_0, end_1, stencils, extra, inside, inner, *rest
):
    out, *to_sides, middle, wide, shifted = rest
    height, width, radial = field.shape
    tiles = unpack_sides(side_0, side_1, height)
    lat, odd = position("lat")
    for place in range(3):
        partner, outer = end_0[place], end_1[place]
        for first, pack in ((0, either(odd, partner, outer)), (6, either(odd, outer, partner))):
            if place < 2:
                wide[first + place, :width] = pack
            else:
                wide[first, width:] = pack
                wide[first + 1, width:] = pltpu.roll(pack, 4, 0)
    for place, row in ((2, 0), (3, 1), (4, height - 2), (5, height - 1)):
        wide[place, :width] = field[row]
        wide[place, width:] = tiles[row]
    above = (lat > 0).astype(jnp.int32)
    below = (lat < lax.axis_size("lat") - 1).astype(jnp.int32)
    first_level(wide, shifted, stencils.at[coefs[0]], (1, 2, 5, 6), middle, [above, None, None, below])

    def write(row, at, value):
        out[row, :, at] = finish(value, extra[row, :, at])

    last = height - 3
    top = [(middle, 0), (middle, 1), (inside, 0), (inside, 1)]
    bottom = [(inside, last - 1), (inside, last), (middle, 2), (middle, 3)]
    windows = {0: top[:3], 1: top[1:], height - 2: bottom[:3], height - 1: bottom[1:]}
    second_level(stencils.at[coefs[1]], windows, radial, write)
    for row in range(2, height - 2):
        out[row] = finish_inner(inner[row - 2], extra[row])
    if packs:
        pack_sides([out[row] for row in range(height)], *to_sides)


def open_kernel(
    counts_in, offsets_in, residual_in, pixel_in, bins_in, latent_in, out, latent, to_partner, to_outer,
    counts, offsets, residual, pixel, bins, arrived,
):
    pairs = (
        (latent_in, latent), (counts_in, counts), (offsets_in, offsets),
        (residual_in, residual), (pixel_in, pixel), (bins_in, bins),
    )
    copies = [pltpu.make_async_copy(source, target, arrived.at[i]) for i, (source, target) in enumerate(pairs)]
    for copy in copies:
        copy.start()
    copies[0].wait()
    height, _, radial = latent.shape
    pack_sides([latent[row] for row in range(height)], to_partner, to_outer)
    for copy in copies[1:]:
        copy.wait()

    lane = lax.broadcasted_iota(jnp.int32, (SUBLANES, LANES), 1)
    row = lax.broadcasted_iota(jnp.int32, (SUBLANES, LANES), 0)
    slot = row * LANES + lane
    for owner in range(out.shape[0]):
        start = offsets[0, owner]
        first = lax.shift_right_logical(start, 7)
        part = lax.bitwise_and(start, LANES - 1)
        live = slot < counts[0, owner]

        def window(values):
            turned = pltpu.roll(values, lax.bitwise_and(LANES - part, LANES - 1), 1)
            joined = jnp.where(lane < LANES - part, turned, pltpu.roll(turned, SUBLANES - 1, 0))
            return jnp.where(live, joined, 0.0)

        at = pl.ds(first, SUBLANES)
        cell = (pixel[at, :] * radial + bins[at, :]).astype(jnp.float32)
        out[owner] = jnp.where(row < RUNS, window(residual[at, :]), pltpu.roll(window(cell), RUNS, 0))


def behind_of(got, *, radial, pixels):
    half = radial // 2
    classes = 2 * pixels
    shards, rows, _ = got.shape
    bf16 = jnp.bfloat16
    column = lax.broadcasted_iota(jnp.int32, (classes, LANES), 0).astype(jnp.float32).astype(bf16)
    places = [
        (lax.broadcasted_iota(jnp.int32, (LANES, LANES), 1) + (first + 1)).astype(jnp.float32).astype(bf16)
        for first in range(0, half, LANES)
    ]
    zero = jnp.zeros((), bf16)

    def tall(row):
        return jnp.concatenate([jnp.broadcast_to(row, (16, LANES)).astype(bf16)] * (classes // 16), axis=0)

    tiles = got[...].reshape(shards * rows, LANES)
    cell = tiles.astype(jnp.int32)
    pixel = lax.shift_right_logical(cell, radial.bit_length() - 1)
    bins = lax.bitwise_and(cell, radial - 1)
    upper = (bins >= half).astype(jnp.int32)
    label = (upper * pixels + pixel).astype(jnp.float32)
    lows = jnp.transpose((bins - upper * half + 1).astype(jnp.float32))
    coarse = tiles.astype(bf16).astype(jnp.float32)
    rest = tiles - coarse

    total = jnp.zeros((2 * classes, half), jnp.float32)
    for first in range(0, shards, 2):
        left, right = [], []
        for run in range(2 * RUNS):
            row = (first + run // RUNS) * rows + run % RUNS
            mine = tall(label[row + RUNS:row + RUNS + 1]) == column
            left.append(jnp.concatenate([
                jnp.where(mine, tall(coarse[row:row + 1]), zero), jnp.where(mine, tall(rest[row:row + 1]), zero)
            ], axis=0))
            low = jnp.broadcast_to(lows[:, row + RUNS:row + RUNS + 1], (LANES, LANES)).astype(bf16)
            right.append(jnp.concatenate([jnp.maximum(low, place) for place in places], axis=1))
        total = total + jnp.dot(
            jnp.concatenate(left, axis=1), jnp.concatenate(right, axis=0), preferred_element_type=jnp.float32
        )
    both = (total[:classes] + total[classes:]) * bin_width
    every = both[:, half - 1:] * (1.0 / half)
    lane = lax.broadcasted_iota(jnp.int32, both.shape, 1)
    at_least = jnp.where(lane == 0, every, pltpu.roll(both, 1, 1) - both + every)
    near, far = at_least[:pixels], at_least[pixels:]
    return near + far[:, :1], far


def bin_kernel(got, _, behind):
    height, width, radial = behind.shape
    near, far = behind_of(got, radial=radial, pixels=height * width)
    for row in range(height):
        at = slice(row * width, (row + 1) * width)
        behind[row] = jnp.concatenate([near[at], far[at]], axis=1)


def mirror(stencils):
    turned = jnp.flip(stencils, axis=1).reshape(stencils.shape[0], 9, 3, stencils.shape[2])
    edge = jnp.zeros_like(turned[:, :, 0, :1])
    back = jnp.concatenate([edge, turned[:, :, 0, :-1]], axis=-1)
    ahead = jnp.concatenate([turned[:, :, 2, 1:], edge], axis=-1)
    return jnp.stack([back, turned[:, :, 1], ahead], axis=2).reshape(stencils.shape)


def gathered_ends(to_partner, to_outer):
    every = lax.all_gather(jnp.stack([to_partner, to_outer]), "lat")
    lat = lax.axis_index("lat")
    outer = lat + 2 * lax.rem(lat, 2) - 1
    inside = (outer >= 0) & (outer < lax.axis_size("lat"))
    from_partner = lax.dynamic_index_in_dim(every, lat + 1 - 2 * lax.rem(lat, 2), keepdims=False)[0]
    from_outer = lax.dynamic_index_in_dim(every, jnp.clip(outer, 0, lax.axis_size("lat") - 1), keepdims=False)[1]
    return from_partner, jnp.where(inside, from_outer, 0.0)


def swap(to_partner, to_outer, axis, closed):
    count = lax.axis_size(axis)
    outer = [(i, (i + 1) % count) for i in range(1, count, 2) if closed or i + 1 < count]
    inner = [(i, i + 1) for i in range(0, count - 1, 2)]

    def both_ways(pairs):
        return pairs + [(j, i) for i, j in pairs]

    from_partner = lax.ppermute(to_partner, axis, both_ways(inner))
    return from_partner, lax.ppermute(to_outer, axis, both_ways(outer))


VMEM = pl.BlockSpec(memory_space=pltpu.VMEM)
HBM = pl.BlockSpec(memory_space=pltpu.HBM)
LIMIT = pltpu.CompilerParams(vmem_limit_bytes=32 * 1024 * 1024)


def on_device(residual, star_pixel, star_bin, send_counts, send_offsets, latent, stencils):
    height, width, radial = latent.shape
    shards = send_counts.shape[1]
    slots = residual.shape[0]
    f32 = jnp.float32
    i32 = jnp.int32
    tile = jax.ShapeDtypeStruct((height, width, radial), f32)
    sides = jax.ShapeDtypeStruct((height // 4, SUBLANES, radial), f32)
    ends = jax.ShapeDtypeStruct((3, SUBLANES, radial), f32)

    def table(values):
        return values.reshape(slots // LANES, LANES)

    packed, latent, *to_sides = pl.pallas_call(
        open_kernel,
        out_shape=(jax.ShapeDtypeStruct((shards, 2 * RUNS, LANES), f32), tile, sides, sides),
        in_specs=[HBM] * 6,
        out_specs=(VMEM, VMEM, VMEM, VMEM),
        scratch_shapes=[pltpu.SMEM((1, shards), i32)] * 2
        + [pltpu.VMEM((slots // LANES, LANES), kind) for kind in (f32, i32, i32)]
        + [pltpu.SemaphoreType.DMA((6,))],
        compiler_params=LIMIT,
        name="opening",
    )(*[
        pltpu.with_memory_space_constraint(values, pltpu.HBM)
        for values in (send_counts, send_offsets, table(residual), table(star_pixel), table(star_bin), latent)
    ])
    got = lax.all_to_all(packed, ("lat", "lon"), split_axis=0, concat_axis=0, tiled=True)

    def spread(field, to_sides, name, gathers):
        beside = swap(*to_sides, "lon", True)
        to_ends = pl.pallas_call(
            pack_ends_kernel,
            out_shape=(ends, ends),
            in_specs=[VMEM] * 3,
            out_specs=(VMEM, VMEM),
            compiler_params=LIMIT,
            name=name + "_pack",
        )(field, *beside)
        return beside, gathered_ends(*to_ends) if gathers else swap(*to_ends, "lat", False)

    rows = pltpu.VMEM((height, 2 * width, radial), f32)
    moved = pltpu.VMEM((2, height, 2 * width, radial), f32)

    def refined_inside(coefs, finish, field, beside, table, extra, name):
        return pl.pallas_call(
            functools.partial(refine_inside_kernel, coefs, finish),
            out_shape=(
                jax.ShapeDtypeStruct((height - 4, width, radial), f32),
                jax.ShapeDtypeStruct((3, 3, height - 2, width, radial), f32),
            ),
            in_specs=[VMEM] * 5,
            out_specs=(VMEM, VMEM),
            scratch_shapes=[rows, moved],
            compiler_params=LIMIT,
            name=name + "_inside",
        )(field, *beside, table, extra)

    def refined_ends(coefs, finish, finish_inner, field, beside, above, table, extra, inner, middle, name, packs):
        return pl.pallas_call(
            functools.partial(refine_ends_kernel, coefs, finish, finish_inner, packs),
            out_shape=(tile, sides, sides) if packs else tile,
            in_specs=[VMEM] * 9,
            out_specs=(VMEM,) * 3 if packs else VMEM,
            scratch_shapes=[pltpu.VMEM((3, 3, 4, width, radial), f32), rows, moved],
            compiler_params=LIMIT,
            name=name + "_ends",
        )(field, *beside, *above, table, extra, middle, inner)

    beside, above = spread(latent, to_sides, "density", False)
    inner, middle = refined_inside(
        (0, 1), lambda value, _: jnp.exp(value), latent, beside, stencils, latent, "density"
    )
    behind = pl.pallas_call(
        bin_kernel,
        out_shape=tile,
        in_specs=[VMEM, VMEM],
        out_specs=VMEM,
        compiler_params=LIMIT,
        name="binning",
    )(got, inner)
    upstream, *to_sides = refined_ends(
        (0, 1), lambda value, mass: jnp.exp(value) * mass, lambda value, mass: value * mass,
        latent, beside, above, stencils, behind, inner, middle, "density", True,
    )

    mirrored = mirror(stencils)
    beside, above = spread(upstream, to_sides, "back", True)
    inner, middle = refined_inside(
        (1, 0), lambda value, field: field + value, upstream, beside, mirrored, latent, "back"
    )
    return refined_ends(
        (1, 0), lambda value, field: field + value, lambda value, _: value,
        upstream, beside, above, mirrored, latent, inner, middle, "back", False,
    )


def solution(mesh):
    return jax.shard_map(
        on_device,
        mesh=mesh,
        in_specs=(
            P(("lat", "lon")),
            P(("lat", "lon")),
            P(("lat", "lon")),
            P(("lat", "lon"), None),
            P(("lat", "lon"), None),
            P("lat", "lon", None),
            P(),
        ),
        out_specs=P("lat", "lon", None),
        check_vma=False,
    )
```

```python
import functools

import jax
import jax.numpy as jnp
from jax import lax
from jax.experimental import pallas as pl
from jax.experimental.pallas import tpu as pltpu
from jax.sharding import PartitionSpec as P

CAP = 512
LANES = 128
SUBLANES = 8
RUNS = CAP // LANES
bin_width = 0.0625


def position(axis):
    index = lax.axis_index(axis)
    return index, lax.bitwise_and(index, 1)


def either(flag, if_set, if_clear):
    return jnp.where(jnp.full(if_set.shape, flag, jnp.int32) > 0, if_set, if_clear)


def sublane(radial):
    return lax.broadcasted_iota(jnp.int32, (SUBLANES, radial), 0)


def pack_sides(rows, to_partner, to_outer):
    _, odd = position("lon")
    sub = sublane(rows[0].shape[1])
    for group in range(len(rows) // 4):
        before, after = rows[4 * group], rows[4 * group]
        for k in range(1, 4):
            row = rows[4 * group + k]
            pair = lax.shift_right_logical(sub, 1)
            before = jnp.where(pair == k, pltpu.roll(row, 2 * k, 0), before)
            after = jnp.where(pair == 3 - k, pltpu.roll(row, SUBLANES - 2 * k, 0), after)
        to_partner[group] = either(odd, before, after)
        to_outer[group] = either(odd, after, before)


def unpack_sides(from_partner, from_outer, height):
    _, odd = position("lon")
    sub = sublane(from_partner.shape[2])
    tiles = []
    for group in range(height // 4):
        partner, outer = from_partner[group], from_outer[group]
        before, after = either(odd, partner, outer), either(odd, outer, partner)
        for k in range(4):
            if k:
                tiles.append(jnp.where(sub < 4, pltpu.roll(after, SUBLANES - 2 * k, 0), pltpu.roll(before, 2 * k, 0)))
            else:
                tiles.append(jnp.where(sub < 4, after, before))
    return tiles


def pack_ends_kernel(field, from_partner, from_outer, to_partner, to_outer):
    height, _, radial = field.shape
    _, odd = position("lat")
    sub = sublane(radial)
    outside = (sub < 2) | (sub >= 6)
    tiles = unpack_sides(from_partner, from_outer, height)

    def ends(first):
        return (
            field[first],
            field[first + 1],
            jnp.where(outside, tiles[first], pltpu.roll(tiles[first + 1], 4, 0)),
        )

    for place, (top, bottom) in enumerate(zip(ends(0), ends(height - 2))):
        to_partner[place] = either(odd, top, bottom)
        to_outer[place] = either(odd, bottom, top)


def radial_shifts(field):
    radial = field.shape[-1]
    lane = lax.broadcasted_iota(jnp.int32, field.shape, field.ndim - 1)
    return (
        jnp.where(lane == 0, 0.0, pltpu.roll(field, 1, field.ndim - 1)),
        jnp.where(lane == radial - 1, 0.0, pltpu.roll(field, radial - 1, field.ndim - 1)),
    )


def taps_of(coef, at):
    return [jnp.broadcast_to(coef[k:k + 1, at], (SUBLANES, LANES)) for k in range(27)]


def tiles_of_bins(radial, body):
    def step(tile, _):
        body(pl.ds(pl.multiple_of(tile * LANES, LANES), LANES))
        return 0

    lax.fori_loop(0, radial // LANES, step, 0)


def first_level(wide, shifted, coef, centers, middle, real):
    reach, cols, radial = wide.shape
    for row in range(reach):
        for place, moved in enumerate(radial_shifts(wide[row])):
            shifted[place, row] = moved

    def body(at):
        taps = taps_of(coef, at)
        for place, row in enumerate(centers):
            parts = []
            for side in (slice(0, SUBLANES), slice(SUBLANES, cols)):
                sums = [None, None, None]
                for above in (-1, 0, 1):
                    window = (shifted[0, row + above, side, at], wide[row + above, side, at], shifted[1, row + above, side, at])
                    for beside in range(3):
                        for step in range(3):
                            term = taps[(above + 1) * 9 + beside * 3 + step] * window[step]
                            sums[beside] = term if sums[beside] is None else sums[beside] + term
                parts.append(sums)
            whole = [jnp.concatenate([parts[0][b], parts[1][b]], axis=0) for b in range(3)]
            value = whole[1] + pltpu.roll(whole[0], 1, 0) + pltpu.roll(whole[2], cols - 1, 0)
            if real[place] is not None:
                value = either(real[place], value, jnp.zeros_like(value))
            middle[0, 1, place, :, at] = pltpu.roll(value, 1, 0)[:SUBLANES]
            middle[1, 1, place, :, at] = value[:SUBLANES]
            middle[2, 1, place, :, at] = pltpu.roll(value, cols - 1, 0)[:SUBLANES]

    tiles_of_bins(radial, body)
    for place in range(len(centers)):
        for beside in range(3):
            for step, moved in zip((0, 2), radial_shifts(middle[beside, 1, place])):
                middle[beside, step, place] = moved


def second_level(coef, windows, radial, write):
    def body(at):
        taps = taps_of(coef, at)
        for row, around in windows.items():
            total = None
            for above, (buffer, place) in enumerate(around):
                for beside in range(3):
                    for step in range(3):
                        term = taps[above * 9 + beside * 3 + step] * buffer[beside, step, place, :, at]
                        total = term if total is None else total + term
            write(row, at, total)

    tiles_of_bins(radial, body)


def refine_inside_kernel(coefs, finish, field, side_0, side_1, stencils, extra, out, middle, wide, shifted):
    height, width, radial = field.shape
    tiles = unpack_sides(side_0, side_1, height)
    for row in range(height):
        wide[row, :width] = field[row]
        wide[row, width:] = tiles[row]
    first_level(wide, shifted, stencils.at[coefs[0]], range(1, height - 1), middle, [None] * (height - 2))

    def write(row, at, value):
        out[row - 2, :, at] = finish(value, extra[row, :, at])

    windows = {row: [(middle, row - 2 + k) for k in range(3)] for row in range(2, height - 2)}
    second_level(stencils.at[coefs[1]], windows, radial, write)


def refine_ends_kernel(
    coefs, finish, finish_inner, packs, field, side_0, side_1, end_1, end_0, stencils, extra, inside, inner, *rest
):
    out, *to_sides, middle, wide, shifted = rest
    height, width, radial = field.shape
    tiles = unpack_sides(side_0, side_1, height)
    lat, odd = position("lat")
    for place in range(3):
        partner, outer = end_0[place], end_1[place]
        for first, pack in ((0, either(odd, partner, outer)), (6, either(odd, outer, partner))):
            if place < 2:
                wide[first + place, :width] = pack
            else:
                wide[first, width:] = pack
                wide[first + 1, width:] = pltpu.roll(pack, 4, 0)
    for place, row in ((2, 0), (3, 1), (4, height - 2), (5, height - 1)):
        wide[place, :width] = field[row]
        wide[place, width:] = tiles[row]
    above = (lat > 0).astype(jnp.int32)
    below = (lat < lax.axis_size("lat") - 1).astype(jnp.int32)
    first_level(wide, shifted, stencils.at[coefs[0]], (1, 2, 5, 6), middle, [above, None, None, below])

    def write(row, at, value):
        out[row, :, at] = finish(value, extra[row, :, at])

    last = height - 3
    top = [(middle, 0), (middle, 1), (inside, 0), (inside, 1)]
    bottom = [(inside, last - 1), (inside, last), (middle, 2), (middle, 3)]
    windows = {0: top[:3], 1: top[1:], height - 2: bottom[:3], height - 1: bottom[1:]}
    second_level(stencils.at[coefs[1]], windows, radial, write)
    for row in range(2, height - 2):
        out[row] = finish_inner(inner[row - 2], extra[row])
    if packs:
        pack_sides([out[row] for row in range(height)], *to_sides)


def open_kernel(
    counts_in, offsets_in, residual_in, pixel_in, bins_in, latent_in, out, latent, to_partner, to_outer,
    counts, offsets, residual, pixel, bins, arrived,
):
    pairs = (
        (latent_in, latent), (counts_in, counts), (offsets_in, offsets),
        (residual_in, residual), (pixel_in, pixel), (bins_in, bins),
    )
    copies = [pltpu.make_async_copy(source, target, arrived.at[i]) for i, (source, target) in enumerate(pairs)]
    for copy in copies:
        copy.start()
    copies[0].wait()
    height, _, radial = latent.shape
    pack_sides([latent[row] for row in range(height)], to_partner, to_outer)
    for copy in copies[1:]:
        copy.wait()

    lane = lax.broadcasted_iota(jnp.int32, (SUBLANES, LANES), 1)
    row = lax.broadcasted_iota(jnp.int32, (SUBLANES, LANES), 0)
    slot = row * LANES + lane
    for owner in range(out.shape[0]):
        start = offsets[0, owner]
        first = lax.shift_right_logical(start, 7)
        part = lax.bitwise_and(start, LANES - 1)
        live = slot < counts[0, owner]

        def window(values):
            turned = pltpu.roll(values, lax.bitwise_and(LANES - part, LANES - 1), 1)
            joined = jnp.where(lane < LANES - part, turned, pltpu.roll(turned, SUBLANES - 1, 0))
            return jnp.where(live, joined, 0.0)

        at = pl.ds(first, SUBLANES)
        cell = (pixel[at, :] * radial + bins[at, :]).astype(jnp.float32)
        out[owner] = jnp.where(row < RUNS, window(residual[at, :]), pltpu.roll(window(cell), RUNS, 0))


def behind_of(got, *, radial, pixels):
    half = radial // 2
    classes = 2 * pixels
    shards, rows, _ = got.shape
    group = 4
    bf16 = jnp.bfloat16
    column = lax.broadcasted_iota(jnp.int32, (classes, LANES), 0).astype(jnp.float32).astype(bf16)
    places = [
        (lax.broadcasted_iota(jnp.int32, (LANES, LANES), 1) + (first + 1)).astype(jnp.float32).astype(bf16)
        for first in range(0, half, LANES)
    ]
    zero = jnp.zeros((), bf16)

    def tall(row):
        return jnp.concatenate([jnp.broadcast_to(row, (16, LANES)).astype(bf16)] * (classes // 16), axis=0)

    def step(turn, total):
        tiles = got[pl.ds(group * turn, group)].reshape(group * rows, LANES)
        cell = tiles.astype(jnp.int32)
        pixel = lax.shift_right_logical(cell, radial.bit_length() - 1)
        bins = lax.bitwise_and(cell, radial - 1)
        upper = (bins >= half).astype(jnp.int32)
        label = (upper * pixels + pixel).astype(jnp.float32)
        lows = jnp.transpose((bins - upper * half + 1).astype(jnp.float32))
        coarse = tiles.astype(bf16).astype(jnp.float32)
        rest = tiles - coarse
        left, right = [], []
        for run in range(group * RUNS):
            row = run // RUNS * rows + run % RUNS
            mine = tall(label[row + RUNS:row + RUNS + 1]) == column
            left.append(jnp.concatenate([
                jnp.where(mine, tall(coarse[row:row + 1]), zero), jnp.where(mine, tall(rest[row:row + 1]), zero)
            ], axis=0))
            low = jnp.broadcast_to(lows[:, row + RUNS:row + RUNS + 1], (LANES, LANES)).astype(bf16)
            right.append(jnp.concatenate([jnp.maximum(low, place) for place in places], axis=1))
        return total + jnp.dot(
            jnp.concatenate(left, axis=1), jnp.concatenate(right, axis=0), preferred_element_type=jnp.float32
        )

    total = lax.fori_loop(0, shards // group, step, jnp.zeros((2 * classes, half), jnp.float32))
    both = (total[:classes] + total[classes:]) * bin_width
    every = both[:, half - 1:] * (1.0 / half)
    lane = lax.broadcasted_iota(jnp.int32, both.shape, 1)
    at_least = jnp.where(lane == 0, every, pltpu.roll(both, 1, 1) - both + every)
    near, far = at_least[:pixels], at_least[pixels:]
    return near + far[:, :1], far


def bin_kernel(got, _, behind):
    height, width, radial = behind.shape
    near, far = behind_of(got, radial=radial, pixels=height * width)
    for row in range(height):
        at = slice(row * width, (row + 1) * width)
        behind[row] = jnp.concatenate([near[at], far[at]], axis=1)


def mirror(stencils):
    turned = jnp.flip(stencils, axis=1).reshape(stencils.shape[0], 9, 3, stencils.shape[2])
    edge = jnp.zeros_like(turned[:, :, 0, :1])
    back = jnp.concatenate([edge, turned[:, :, 0, :-1]], axis=-1)
    ahead = jnp.concatenate([turned[:, :, 2, 1:], edge], axis=-1)
    return jnp.stack([back, turned[:, :, 1], ahead], axis=2).reshape(stencils.shape)


def swap(to_partner, to_outer, axis, closed, outer_first=False):
    count = lax.axis_size(axis)
    outer = [(i, (i + 1) % count) for i in range(1, count, 2) if closed or i + 1 < count]
    inner = [(i, i + 1) for i in range(0, count - 1, 2)]

    def both_ways(pairs):
        return pairs + [(j, i) for i, j in pairs]

    moves = [(to_partner, inner), (to_outer, outer)]
    return tuple(lax.ppermute(values, axis, both_ways(pairs)) for values, pairs in moves[::-1 if outer_first else 1])


VMEM = pl.BlockSpec(memory_space=pltpu.VMEM)
HBM = pl.BlockSpec(memory_space=pltpu.HBM)
LIMIT = pltpu.CompilerParams(vmem_limit_bytes=32 * 1024 * 1024)


def on_device(residual, star_pixel, star_bin, send_counts, send_offsets, latent, stencils):
    height, width, radial = latent.shape
    shards = send_counts.shape[1]
    slots = residual.shape[0]
    f32 = jnp.float32
    i32 = jnp.int32
    tile = jax.ShapeDtypeStruct((height, width, radial), f32)
    sides = jax.ShapeDtypeStruct((height // 4, SUBLANES, radial), f32)
    ends = jax.ShapeDtypeStruct((3, SUBLANES, radial), f32)

    def table(values):
        return values.reshape(slots // LANES, LANES)

    packed, latent, *to_sides = pl.pallas_call(
        open_kernel,
        out_shape=(jax.ShapeDtypeStruct((shards, 2 * RUNS, LANES), f32), tile, sides, sides),
        in_specs=[HBM] * 6,
        out_specs=(VMEM, VMEM, VMEM, VMEM),
        scratch_shapes=[pltpu.SMEM((1, shards), i32)] * 2
        + [pltpu.VMEM((slots // LANES, LANES), kind) for kind in (f32, i32, i32)]
        + [pltpu.SemaphoreType.DMA((6,))],
        compiler_params=LIMIT,
        name="opening",
    )(*[
        pltpu.with_memory_space_constraint(values, pltpu.HBM)
        for values in (send_counts, send_offsets, table(residual), table(star_pixel), table(star_bin), latent)
    ])
    got = lax.all_to_all(packed, ("lat", "lon"), split_axis=0, concat_axis=0, tiled=True)

    def spread(field, to_sides, name):
        beside = swap(*to_sides, "lon", True)
        to_ends = pl.pallas_call(
            pack_ends_kernel,
            out_shape=(ends, ends),
            in_specs=[VMEM] * 3,
            out_specs=(VMEM, VMEM),
            compiler_params=LIMIT,
            name=name + "_pack",
        )(field, *beside)
        return beside, swap(*to_ends, "lat", False, outer_first=True)

    rows = pltpu.VMEM((height, 2 * width, radial), f32)
    moved = pltpu.VMEM((2, height, 2 * width, radial), f32)

    def refined_inside(coefs, finish, field, beside, table, extra, name):
        return pl.pallas_call(
            functools.partial(refine_inside_kernel, coefs, finish),
            out_shape=(
                jax.ShapeDtypeStruct((height - 4, width, radial), f32),
                jax.ShapeDtypeStruct((3, 3, height - 2, width, radial), f32),
            ),
            in_specs=[VMEM] * 5,
            out_specs=(VMEM, VMEM),
            scratch_shapes=[rows, moved],
            compiler_params=LIMIT,
            name=name + "_inside",
        )(field, *beside, table, extra)

    def refined_ends(coefs, finish, finish_inner, field, beside, above, table, extra, inner, middle, name, packs):
        return pl.pallas_call(
            functools.partial(refine_ends_kernel, coefs, finish, finish_inner, packs),
            out_shape=(tile, sides, sides) if packs else tile,
            in_specs=[VMEM] * 9,
            out_specs=(VMEM,) * 3 if packs else VMEM,
            scratch_shapes=[pltpu.VMEM((3, 3, 4, width, radial), f32), rows, moved],
            compiler_params=LIMIT,
            name=name + "_ends",
        )(field, *beside, *above, table, extra, middle, inner)

    beside, above = spread(latent, to_sides, "density")
    inner, middle = refined_inside(
        (0, 1), lambda value, _: jnp.exp(value), latent, beside, stencils, latent, "density"
    )
    behind = pl.pallas_call(
        bin_kernel,
        out_shape=tile,
        in_specs=[VMEM, VMEM],
        out_specs=VMEM,
        compiler_params=LIMIT,
        name="binning",
    )(got, inner)
    upstream, *to_sides = refined_ends(
        (0, 1), lambda value, mass: jnp.exp(value) * mass, lambda value, mass: value * mass,
        latent, beside, above, stencils, behind, inner, middle, "density", True,
    )

    mirrored = mirror(stencils)
    beside, above = spread(upstream, to_sides, "back")
    inner, middle = refined_inside(
        (1, 0), lambda value, field: field + value, upstream, beside, mirrored, latent, "back"
    )
    return refined_ends(
        (1, 0), lambda value, field: field + value, lambda value, _: value,
        upstream, beside, above, mirrored, latent, inner, middle, "back", False,
    )


def solution(mesh):
    return jax.shard_map(
        on_device,
        mesh=mesh,
        in_specs=(
            P(("lat", "lon")),
            P(("lat", "lon")),
            P(("lat", "lon")),
            P(("lat", "lon"), None),
            P(("lat", "lon"), None),
            P("lat", "lon", None),
            P(),
        ),
        out_specs=P("lat", "lon", None),
        check_vma=False,
    )
```

```python
import functools

import jax
import jax.numpy as jnp
from jax import lax
from jax.experimental import pallas as pl
from jax.experimental.pallas import tpu as pltpu
from jax.sharding import PartitionSpec as P

CAP = 512
LANES = 128
SUBLANES = 8
RUNS = CAP // LANES
bin_width = 0.0625


def position(axis):
    index = lax.axis_index(axis)
    return index, lax.bitwise_and(index, 1)


def either(flag, if_set, if_clear):
    return jnp.where(jnp.full(if_set.shape, flag, jnp.int32) > 0, if_set, if_clear)


def sublane(radial):
    return lax.broadcasted_iota(jnp.int32, (SUBLANES, radial), 0)


def pack_sides(rows, to_partner, to_outer):
    _, odd = position("lon")
    sub = sublane(rows[0].shape[1])
    for group in range(len(rows) // 4):
        before, after = rows[4 * group], rows[4 * group]
        for k in range(1, 4):
            row = rows[4 * group + k]
            pair = lax.shift_right_logical(sub, 1)
            before = jnp.where(pair == k, pltpu.roll(row, 2 * k, 0), before)
            after = jnp.where(pair == 3 - k, pltpu.roll(row, SUBLANES - 2 * k, 0), after)
        to_partner[group] = either(odd, before, after)
        to_outer[group] = either(odd, after, before)


def unpack_sides(from_partner, from_outer, height):
    _, odd = position("lon")
    sub = sublane(from_partner.shape[2])
    tiles = []
    for group in range(height // 4):
        partner, outer = from_partner[group], from_outer[group]
        before, after = either(odd, partner, outer), either(odd, outer, partner)
        for k in range(4):
            if k:
                tiles.append(jnp.where(sub < 4, pltpu.roll(after, SUBLANES - 2 * k, 0), pltpu.roll(before, 2 * k, 0)))
            else:
                tiles.append(jnp.where(sub < 4, after, before))
    return tiles


def pack_ends_kernel(field, from_partner, from_outer, to_partner, to_outer):
    height, _, radial = field.shape
    _, odd = position("lat")
    sub = sublane(radial)
    outside = (sub < 2) | (sub >= 6)
    tiles = unpack_sides(from_partner, from_outer, height)

    def ends(first):
        return (
            field[first],
            field[first + 1],
            jnp.where(outside, tiles[first], pltpu.roll(tiles[first + 1], 4, 0)),
        )

    for place, (top, bottom) in enumerate(zip(ends(0), ends(height - 2))):
        to_partner[place] = either(odd, top, bottom)
        to_outer[place] = either(odd, bottom, top)


def radial_shifts(field):
    radial = field.shape[-1]
    lane = lax.broadcasted_iota(jnp.int32, field.shape, field.ndim - 1)
    return (
        jnp.where(lane == 0, 0.0, pltpu.roll(field, 1, field.ndim - 1)),
        jnp.where(lane == radial - 1, 0.0, pltpu.roll(field, radial - 1, field.ndim - 1)),
    )


def taps_of(coef, at):
    return [jnp.broadcast_to(coef[k:k + 1, at], (SUBLANES, LANES)) for k in range(27)]


def tiles_of_bins(radial, body):
    def step(tile, _):
        body(pl.ds(pl.multiple_of(tile * LANES, LANES), LANES))
        return 0

    lax.fori_loop(0, radial // LANES, step, 0)


def first_level(wide, shifted, coef, centers, middle, real):
    reach, cols, radial = wide.shape
    for row in range(reach):
        for place, moved in enumerate(radial_shifts(wide[row])):
            shifted[place, row] = moved

    def body(at):
        taps = taps_of(coef, at)
        for place, row in enumerate(centers):
            parts = []
            for side in (slice(0, SUBLANES), slice(SUBLANES, cols)):
                sums = [None, None, None]
                for above in (-1, 0, 1):
                    window = (shifted[0, row + above, side, at], wide[row + above, side, at], shifted[1, row + above, side, at])
                    for beside in range(3):
                        for step in range(3):
                            term = taps[(above + 1) * 9 + beside * 3 + step] * window[step]
                            sums[beside] = term if sums[beside] is None else sums[beside] + term
                parts.append(sums)
            whole = [jnp.concatenate([parts[0][b], parts[1][b]], axis=0) for b in range(3)]
            value = whole[1] + pltpu.roll(whole[0], 1, 0) + pltpu.roll(whole[2], cols - 1, 0)
            if real[place] is not None:
                value = either(real[place], value, jnp.zeros_like(value))
            middle[0, 1, place, :, at] = pltpu.roll(value, 1, 0)[:SUBLANES]
            middle[1, 1, place, :, at] = value[:SUBLANES]
            middle[2, 1, place, :, at] = pltpu.roll(value, cols - 1, 0)[:SUBLANES]

    tiles_of_bins(radial, body)
    for place in range(len(centers)):
        for beside in range(3):
            for step, moved in zip((0, 2), radial_shifts(middle[beside, 1, place])):
                middle[beside, step, place] = moved


def second_level(coef, windows, radial, write):
    def body(at):
        taps = taps_of(coef, at)
        for row, around in windows.items():
            total = None
            for above, (buffer, place) in enumerate(around):
                for beside in range(3):
                    for step in range(3):
                        term = taps[above * 9 + beside * 3 + step] * buffer[beside, step, place, :, at]
                        total = term if total is None else total + term
            write(row, at, total)

    tiles_of_bins(radial, body)


def refine_inside_kernel(coefs, finish, field, side_0, side_1, stencils, extra, out, middle, wide, shifted):
    height, width, radial = field.shape
    tiles = unpack_sides(side_0, side_1, height)
    for row in range(height):
        wide[row, :width] = field[row]
        wide[row, width:] = tiles[row]
    first_level(wide, shifted, stencils.at[coefs[0]], range(1, height - 1), middle, [None] * (height - 2))

    def write(row, at, value):
        out[row - 2, :, at] = finish(value, extra[row, :, at])

    windows = {row: [(middle, row - 2 + k) for k in range(3)] for row in range(2, height - 2)}
    second_level(stencils.at[coefs[1]], windows, radial, write)


def refine_ends_kernel(
    coefs, finish, packs, field, side_0, side_1, end_1, end_0, stencils, extra, inside, inner, *rest
):
    out, *to_sides, middle, wide, shifted = rest
    height, width, radial = field.shape
    tiles = unpack_sides(side_0, side_1, height)
    lat, odd = position("lat")
    for place in range(3):
        partner, outer = end_0[place], end_1[place]
        for first, pack in ((0, either(odd, partner, outer)), (6, either(odd, outer, partner))):
            if place < 2:
                wide[first + place, :width] = pack
            else:
                wide[first, width:] = pack
                wide[first + 1, width:] = pltpu.roll(pack, 4, 0)
    for place, row in ((2, 0), (3, 1), (4, height - 2), (5, height - 1)):
        wide[place, :width] = field[row]
        wide[place, width:] = tiles[row]
    above = (lat > 0).astype(jnp.int32)
    below = (lat < lax.axis_size("lat") - 1).astype(jnp.int32)
    first_level(wide, shifted, stencils.at[coefs[0]], (1, 2, 5, 6), middle, [above, None, None, below])

    def write(row, at, value):
        out[row, :, at] = finish(value, extra[row, :, at])

    last = height - 3
    top = [(middle, 0), (middle, 1), (inside, 0), (inside, 1)]
    bottom = [(inside, last - 1), (inside, last), (middle, 2), (middle, 3)]
    windows = {0: top[:3], 1: top[1:], height - 2: bottom[:3], height - 1: bottom[1:]}
    second_level(stencils.at[coefs[1]], windows, radial, write)
    for row in range(2, height - 2):
        out[row] = inner[row - 2]
    if packs:
        pack_sides([out[row] * extra[row] for row in range(height)], *to_sides)


def open_kernel(
    counts_in, offsets_in, residual_in, pixel_in, bins_in, latent_in, out, latent, to_partner, to_outer,
    counts, offsets, residual, pixel, bins, arrived,
):
    pairs = (
        (latent_in, latent), (counts_in, counts), (offsets_in, offsets),
        (residual_in, residual), (pixel_in, pixel), (bins_in, bins),
    )
    copies = [pltpu.make_async_copy(source, target, arrived.at[i]) for i, (source, target) in enumerate(pairs)]
    for copy in copies:
        copy.start()
    copies[0].wait()
    height, _, radial = latent.shape
    pack_sides([latent[row] for row in range(height)], to_partner, to_outer)
    for copy in copies[1:]:
        copy.wait()

    lane = lax.broadcasted_iota(jnp.int32, (SUBLANES, LANES), 1)
    row = lax.broadcasted_iota(jnp.int32, (SUBLANES, LANES), 0)
    slot = row * LANES + lane
    for owner in range(out.shape[0]):
        start = offsets[0, owner]
        first = lax.shift_right_logical(start, 7)
        part = lax.bitwise_and(start, LANES - 1)
        live = slot < counts[0, owner]

        def window(values):
            turned = pltpu.roll(values, lax.bitwise_and(LANES - part, LANES - 1), 1)
            joined = jnp.where(lane < LANES - part, turned, pltpu.roll(turned, SUBLANES - 1, 0))
            return jnp.where(live, joined, 0.0)

        at = pl.ds(first, SUBLANES)
        cell = (pixel[at, :] * radial + bins[at, :]).astype(jnp.float32)
        out[owner] = jnp.where(row < RUNS, window(residual[at, :]), pltpu.roll(window(cell), RUNS, 0))


def behind_of(got, part, *, height, width, radial):
    half = radial // 2
    pixels = height * width // 2
    classes = 2 * pixels
    shards, rows, _ = got.shape
    bf16 = jnp.bfloat16
    column = lax.broadcasted_iota(jnp.int32, (classes, LANES), 0).astype(jnp.float32).astype(bf16)
    places = [
        (lax.broadcasted_iota(jnp.int32, (LANES, LANES), 1) + (first + 1)).astype(jnp.float32).astype(bf16)
        for first in range(0, half, LANES)
    ]
    zero = jnp.zeros((), bf16)

    def tall(row):
        return jnp.concatenate([jnp.broadcast_to(row, (16, LANES)).astype(bf16)] * (classes // 16), axis=0)

    tiles = got[...].reshape(shards * rows, LANES)
    cell = tiles.astype(jnp.int32)
    pixel = lax.shift_right_logical(cell, radial.bit_length() - 1)
    bins = lax.bitwise_and(cell, radial - 1)
    upper = (bins >= half).astype(jnp.int32)
    place = lax.bitwise_and(pixel + 2, width - 1)
    own = upper * pixels + lax.shift_right_logical(pixel, 3) * 4 + lax.bitwise_and(place, 3)
    label = jnp.where(lax.shift_right_logical(place, 2) == part, own, classes).astype(jnp.float32)
    lows = jnp.transpose((bins - upper * half + 1).astype(jnp.float32))
    coarse = tiles.astype(bf16).astype(jnp.float32)
    rest = tiles - coarse

    total = jnp.zeros((2 * classes, half), jnp.float32)
    for first in range(0, shards, 2):
        left, right = [], []
        for run in range(2 * RUNS):
            row = (first + run // RUNS) * rows + run % RUNS
            mine = tall(label[row + RUNS:row + RUNS + 1]) == column
            left.append(jnp.concatenate([
                jnp.where(mine, tall(coarse[row:row + 1]), zero), jnp.where(mine, tall(rest[row:row + 1]), zero)
            ], axis=0))
            low = jnp.broadcast_to(lows[:, row + RUNS:row + RUNS + 1], (LANES, LANES)).astype(bf16)
            right.append(jnp.concatenate([jnp.maximum(low, place) for place in places], axis=1))
        total = total + jnp.dot(
            jnp.concatenate(left, axis=1), jnp.concatenate(right, axis=0), preferred_element_type=jnp.float32
        )
    both = (total[:classes] + total[classes:]) * bin_width
    every = both[:, half - 1:] * (1.0 / half)
    lane = lax.broadcasted_iota(jnp.int32, both.shape, 1)
    at_least = jnp.where(lane == 0, every, pltpu.roll(both, 1, 1) - both + every)
    near, far = at_least[:pixels], at_least[pixels:]
    return jnp.concatenate([near + far[:, :1], far], axis=1)


def column_rows(packed, part, height):
    rows = []
    for row in range(height):
        tile = packed[row // 2 * SUBLANES:(row // 2 + 1) * SUBLANES]
        turn = row % 2 * 4 + (2 if part == 0 else SUBLANES - 2)
        rows.append(pltpu.roll(tile, (SUBLANES - turn) % SUBLANES, 0))
    return rows


def bin_sides_kernel(got, _, behind):
    height, width, radial = behind.shape
    packed = behind_of(got, 0, height=height, width=width, radial=radial)
    for row, values in enumerate(column_rows(packed, 0, height)):
        behind[row] = values


def bin_rest_kernel(got, density, behind, upstream):
    height, width, radial = behind.shape
    sub = sublane(radial)
    packed = behind_of(got, 1, height=height, width=width, radial=radial)
    for row, values in enumerate(column_rows(packed, 1, height)):
        upstream[row] = density[row] * jnp.where((sub < 2) | (sub >= 6), behind[row], values)


def mirror(stencils):
    turned = jnp.flip(stencils, axis=1).reshape(stencils.shape[0], 9, 3, stencils.shape[2])
    edge = jnp.zeros_like(turned[:, :, 0, :1])
    back = jnp.concatenate([edge, turned[:, :, 0, :-1]], axis=-1)
    ahead = jnp.concatenate([turned[:, :, 2, 1:], edge], axis=-1)
    return jnp.stack([back, turned[:, :, 1], ahead], axis=2).reshape(stencils.shape)


def swap(to_partner, to_outer, axis, closed, outer_first=False):
    count = lax.axis_size(axis)
    outer = [(i, (i + 1) % count) for i in range(1, count, 2) if closed or i + 1 < count]
    inner = [(i, i + 1) for i in range(0, count - 1, 2)]

    def both_ways(pairs):
        return pairs + [(j, i) for i, j in pairs]

    moves = [(to_partner, inner), (to_outer, outer)]
    return tuple(lax.ppermute(values, axis, both_ways(pairs)) for values, pairs in moves[::-1 if outer_first else 1])


VMEM = pl.BlockSpec(memory_space=pltpu.VMEM)
HBM = pl.BlockSpec(memory_space=pltpu.HBM)
LIMIT = pltpu.CompilerParams(vmem_limit_bytes=32 * 1024 * 1024)


def on_device(residual, star_pixel, star_bin, send_counts, send_offsets, latent, stencils):
    height, width, radial = latent.shape
    shards = send_counts.shape[1]
    slots = residual.shape[0]
    f32 = jnp.float32
    i32 = jnp.int32
    tile = jax.ShapeDtypeStruct((height, width, radial), f32)
    sides = jax.ShapeDtypeStruct((height // 4, SUBLANES, radial), f32)
    ends = jax.ShapeDtypeStruct((3, SUBLANES, radial), f32)

    def table(values):
        return values.reshape(slots // LANES, LANES)

    packed, latent, *to_sides = pl.pallas_call(
        open_kernel,
        out_shape=(jax.ShapeDtypeStruct((shards, 2 * RUNS, LANES), f32), tile, sides, sides),
        in_specs=[HBM] * 6,
        out_specs=(VMEM, VMEM, VMEM, VMEM),
        scratch_shapes=[pltpu.SMEM((1, shards), i32)] * 2
        + [pltpu.VMEM((slots // LANES, LANES), kind) for kind in (f32, i32, i32)]
        + [pltpu.SemaphoreType.DMA((6,))],
        compiler_params=LIMIT,
        name="opening",
    )(*[
        pltpu.with_memory_space_constraint(values, pltpu.HBM)
        for values in (send_counts, send_offsets, table(residual), table(star_pixel), table(star_bin), latent)
    ])
    got = lax.all_to_all(packed, ("lat", "lon"), split_axis=0, concat_axis=0, tiled=True)

    def spread(field, to_sides, name):
        beside = swap(*to_sides, "lon", True)
        to_ends = pl.pallas_call(
            pack_ends_kernel,
            out_shape=(ends, ends),
            in_specs=[VMEM] * 3,
            out_specs=(VMEM, VMEM),
            compiler_params=LIMIT,
            name=name + "_pack",
        )(field, *beside)
        return beside, swap(*to_ends, "lat", False, outer_first=True)

    rows = pltpu.VMEM((height, 2 * width, radial), f32)
    moved = pltpu.VMEM((2, height, 2 * width, radial), f32)

    def refined_inside(coefs, finish, field, beside, table, extra, name):
        return pl.pallas_call(
            functools.partial(refine_inside_kernel, coefs, finish),
            out_shape=(
                jax.ShapeDtypeStruct((height - 4, width, radial), f32),
                jax.ShapeDtypeStruct((3, 3, height - 2, width, radial), f32),
            ),
            in_specs=[VMEM] * 5,
            out_specs=(VMEM, VMEM),
            scratch_shapes=[rows, moved],
            compiler_params=LIMIT,
            name=name + "_inside",
        )(field, *beside, table, extra)

    def refined_ends(coefs, finish, field, beside, above, table, extra, inner, middle, name, packs):
        return pl.pallas_call(
            functools.partial(refine_ends_kernel, coefs, finish, packs),
            out_shape=(tile, sides, sides) if packs else tile,
            in_specs=[VMEM] * 9,
            out_specs=(VMEM,) * 3 if packs else VMEM,
            scratch_shapes=[pltpu.VMEM((3, 3, 4, width, radial), f32), rows, moved],
            compiler_params=LIMIT,
            name=name + "_ends",
        )(field, *beside, *above, table, extra, middle, inner)

    beside, above = spread(latent, to_sides, "density")
    inner, middle = refined_inside(
        (0, 1), lambda value, _: jnp.exp(value), latent, beside, stencils, latent, "density"
    )
    behind = pl.pallas_call(
        bin_sides_kernel,
        out_shape=tile,
        in_specs=[VMEM, VMEM],
        out_specs=VMEM,
        compiler_params=LIMIT,
        name="bin_sides",
    )(got, inner)
    density, *to_sides = refined_ends(
        (0, 1), lambda value, _: jnp.exp(value), latent, beside, above, stencils, behind, inner, middle, "density", True,
    )
    upstream = pl.pallas_call(
        bin_rest_kernel,
        out_shape=tile,
        in_specs=[VMEM] * 3,
        out_specs=VMEM,
        compiler_params=LIMIT,
        name="bin_rest",
    )(got, density, behind)

    mirrored = mirror(stencils)
    beside, above = spread(upstream, to_sides, "back")
    inner, middle = refined_inside(
        (1, 0), lambda value, field: field + value, upstream, beside, mirrored, latent, "back"
    )
    return refined_ends(
        (1, 0), lambda value, field: field + value, upstream, beside, above, mirrored, latent, inner, middle, "back", False,
    )


def solution(mesh):
    return jax.shard_map(
        on_device,
        mesh=mesh,
        in_specs=(
            P(("lat", "lon")),
            P(("lat", "lon")),
            P(("lat", "lon")),
            P(("lat", "lon"), None),
            P(("lat", "lon"), None),
            P("lat", "lon", None),
            P(),
        ),
        out_specs=P("lat", "lon", None),
        check_vma=False,
    )
```

```python
import functools

import jax
import jax.numpy as jnp
from jax import lax
from jax.experimental import pallas as pl
from jax.experimental.pallas import tpu as pltpu
from jax.sharding import PartitionSpec as P

CAP = 512
LANES = 128
SUBLANES = 8
RUNS = CAP // LANES
bin_width = 0.0625


def position(axis):
    index = lax.axis_index(axis)
    return index, lax.bitwise_and(index, 1)


def either(flag, if_set, if_clear):
    return jnp.where(jnp.full(if_set.shape, flag, jnp.int32) > 0, if_set, if_clear)


def sublane(radial):
    return lax.broadcasted_iota(jnp.int32, (SUBLANES, radial), 0)


def pack_sides(rows, to_partner, to_outer):
    _, odd = position("lon")
    sub = sublane(rows[0].shape[1])
    for group in range(len(rows) // 4):
        before, after = rows[4 * group], rows[4 * group]
        for k in range(1, 4):
            row = rows[4 * group + k]
            pair = lax.shift_right_logical(sub, 1)
            before = jnp.where(pair == k, pltpu.roll(row, 2 * k, 0), before)
            after = jnp.where(pair == 3 - k, pltpu.roll(row, SUBLANES - 2 * k, 0), after)
        to_partner[group] = either(odd, before, after)
        to_outer[group] = either(odd, after, before)


def unpack_sides(from_partner, from_outer, height):
    _, odd = position("lon")
    sub = sublane(from_partner.shape[2])
    tiles = []
    for group in range(height // 4):
        partner, outer = from_partner[group], from_outer[group]
        before, after = either(odd, partner, outer), either(odd, outer, partner)
        for k in range(4):
            if k:
                tiles.append(jnp.where(sub < 4, pltpu.roll(after, SUBLANES - 2 * k, 0), pltpu.roll(before, 2 * k, 0)))
            else:
                tiles.append(jnp.where(sub < 4, after, before))
    return tiles


def in_order(turned, first, second):
    return (second, first) if turned else (first, second)


def pack_ends_kernel(turned, field, side_0, side_1, to_partner, to_outer):
    height, _, radial = field.shape
    _, odd = position("lat")
    sub = sublane(radial)
    outside = (sub < 2) | (sub >= 6)
    tiles = unpack_sides(*in_order(turned, side_0, side_1), height)

    def ends(first):
        return (
            field[first],
            field[first + 1],
            jnp.where(outside, tiles[first], pltpu.roll(tiles[first + 1], 4, 0)),
        )

    for place, (top, bottom) in enumerate(zip(ends(0), ends(height - 2))):
        to_partner[place] = either(odd, top, bottom)
        to_outer[place] = either(odd, bottom, top)


def radial_shifts(field):
    radial = field.shape[-1]
    lane = lax.broadcasted_iota(jnp.int32, field.shape, field.ndim - 1)
    return (
        jnp.where(lane == 0, 0.0, pltpu.roll(field, 1, field.ndim - 1)),
        jnp.where(lane == radial - 1, 0.0, pltpu.roll(field, radial - 1, field.ndim - 1)),
    )


def taps_of(coef, at):
    return [jnp.broadcast_to(coef[k:k + 1, at], (SUBLANES, LANES)) for k in range(27)]


def tiles_of_bins(radial, body):
    def step(tile, _):
        body(pl.ds(pl.multiple_of(tile * LANES, LANES), LANES))
        return 0

    lax.fori_loop(0, radial // LANES, step, 0)


def first_level(wide, shifted, coef, centers, middle, real):
    reach, cols, radial = wide.shape
    for row in range(reach):
        for place, moved in enumerate(radial_shifts(wide[row])):
            shifted[place, row] = moved

    def body(at):
        taps = taps_of(coef, at)
        for place, row in enumerate(centers):
            parts = []
            for side in (slice(0, SUBLANES), slice(SUBLANES, cols)):
                sums = [None, None, None]
                for above in (-1, 0, 1):
                    window = (shifted[0, row + above, side, at], wide[row + above, side, at], shifted[1, row + above, side, at])
                    for beside in range(3):
                        for step in range(3):
                            term = taps[(above + 1) * 9 + beside * 3 + step] * window[step]
                            sums[beside] = term if sums[beside] is None else sums[beside] + term
                parts.append(sums)
            whole = [jnp.concatenate([parts[0][b], parts[1][b]], axis=0) for b in range(3)]
            value = whole[1] + pltpu.roll(whole[0], 1, 0) + pltpu.roll(whole[2], cols - 1, 0)
            if real[place] is not None:
                value = either(real[place], value, jnp.zeros_like(value))
            middle[0, 1, place, :, at] = pltpu.roll(value, 1, 0)[:SUBLANES]
            middle[1, 1, place, :, at] = value[:SUBLANES]
            middle[2, 1, place, :, at] = pltpu.roll(value, cols - 1, 0)[:SUBLANES]

    tiles_of_bins(radial, body)
    for place in range(len(centers)):
        for beside in range(3):
            for step, moved in zip((0, 2), radial_shifts(middle[beside, 1, place])):
                middle[beside, step, place] = moved


def second_level(coef, windows, radial, write):
    def body(at):
        taps = taps_of(coef, at)
        for row, around in windows.items():
            total = None
            for above, (buffer, place) in enumerate(around):
                for beside in range(3):
                    for step in range(3):
                        term = taps[above * 9 + beside * 3 + step] * buffer[beside, step, place, :, at]
                        total = term if total is None else total + term
            write(row, at, total)

    tiles_of_bins(radial, body)


def refine_inside_kernel(turned, coefs, finish, field, side_0, side_1, stencils, extra, out, middle, wide, shifted):
    height, width, radial = field.shape
    tiles = unpack_sides(*in_order(turned, side_0, side_1), height)
    for row in range(height):
        wide[row, :width] = field[row]
        wide[row, width:] = tiles[row]
    first_level(wide, shifted, stencils.at[coefs[0]], range(1, height - 1), middle, [None] * (height - 2))

    def write(row, at, value):
        out[row - 2, :, at] = finish(value, extra[row, :, at])

    windows = {row: [(middle, row - 2 + k) for k in range(3)] for row in range(2, height - 2)}
    second_level(stencils.at[coefs[1]], windows, radial, write)


def refine_ends_kernel(
    turned, coefs, finish, packs, field, side_0, side_1, end_0, end_1, stencils, extra, inside, inner, *rest
):
    out, *to_sides, middle, wide, shifted = rest
    height, width, radial = field.shape
    tiles = unpack_sides(*in_order(turned[0], side_0, side_1), height)
    end_0, end_1 = in_order(turned[1], end_0, end_1)
    lat, odd = position("lat")
    for place in range(3):
        partner, outer = end_0[place], end_1[place]
        for first, pack in ((0, either(odd, partner, outer)), (6, either(odd, outer, partner))):
            if place < 2:
                wide[first + place, :width] = pack
            else:
                wide[first, width:] = pack
                wide[first + 1, width:] = pltpu.roll(pack, 4, 0)
    for place, row in ((2, 0), (3, 1), (4, height - 2), (5, height - 1)):
        wide[place, :width] = field[row]
        wide[place, width:] = tiles[row]
    above = (lat > 0).astype(jnp.int32)
    below = (lat < lax.axis_size("lat") - 1).astype(jnp.int32)
    first_level(wide, shifted, stencils.at[coefs[0]], (1, 2, 5, 6), middle, [above, None, None, below])

    def write(row, at, value):
        out[row, :, at] = finish(value, extra[row, :, at])

    last = height - 3
    top = [(middle, 0), (middle, 1), (inside, 0), (inside, 1)]
    bottom = [(inside, last - 1), (inside, last), (middle, 2), (middle, 3)]
    windows = {0: top[:3], 1: top[1:], height - 2: bottom[:3], height - 1: bottom[1:]}
    second_level(stencils.at[coefs[1]], windows, radial, write)
    for row in range(2, height - 2):
        out[row] = inner[row - 2]
    if packs:
        pack_sides([out[row] * extra[row] for row in range(height)], *to_sides)


def open_kernel(
    counts_in, offsets_in, residual_in, pixel_in, bins_in, latent_in, out, latent, to_partner, to_outer,
    counts, offsets, residual, pixel, bins, arrived,
):
    pairs = (
        (latent_in, latent), (counts_in, counts), (offsets_in, offsets),
        (residual_in, residual), (pixel_in, pixel), (bins_in, bins),
    )
    copies = [pltpu.make_async_copy(source, target, arrived.at[i]) for i, (source, target) in enumerate(pairs)]
    for copy in copies:
        copy.start()
    copies[0].wait()
    height, _, radial = latent.shape
    pack_sides([latent[row] for row in range(height)], to_partner, to_outer)
    for copy in copies[1:]:
        copy.wait()

    lane = lax.broadcasted_iota(jnp.int32, (SUBLANES, LANES), 1)
    row = lax.broadcasted_iota(jnp.int32, (SUBLANES, LANES), 0)
    slot = row * LANES + lane
    for owner in range(out.shape[0]):
        start = offsets[0, owner]
        first = lax.shift_right_logical(start, 7)
        part = lax.bitwise_and(start, LANES - 1)
        live = slot < counts[0, owner]

        def window(values):
            turned = pltpu.roll(values, lax.bitwise_and(LANES - part, LANES - 1), 1)
            joined = jnp.where(lane < LANES - part, turned, pltpu.roll(turned, SUBLANES - 1, 0))
            return jnp.where(live, joined, 0.0)

        at = pl.ds(first, SUBLANES)
        cell = (pixel[at, :] * radial + bins[at, :]).astype(jnp.float32)
        out[owner] = jnp.where(row < RUNS, window(residual[at, :]), pltpu.roll(window(cell), RUNS, 0))


def behind_of(got, part, *, height, width, radial):
    half = radial // 2
    pixels = height * width // 2
    classes = 2 * pixels
    shards, rows, _ = got.shape
    bf16 = jnp.bfloat16
    column = lax.broadcasted_iota(jnp.int32, (classes, LANES), 0).astype(jnp.float32).astype(bf16)
    places = [
        (lax.broadcasted_iota(jnp.int32, (LANES, LANES), 1) + (first + 1)).astype(jnp.float32).astype(bf16)
        for first in range(0, half, LANES)
    ]
    zero = jnp.zeros((), bf16)

    def tall(row):
        return jnp.concatenate([jnp.broadcast_to(row, (16, LANES)).astype(bf16)] * (classes // 16), axis=0)

    tiles = got[...].reshape(shards * rows, LANES)
    cell = tiles.astype(jnp.int32)
    pixel = lax.shift_right_logical(cell, radial.bit_length() - 1)
    bins = lax.bitwise_and(cell, radial - 1)
    upper = (bins >= half).astype(jnp.int32)
    place = lax.bitwise_and(pixel + 2, width - 1)
    own = upper * pixels + lax.shift_right_logical(pixel, 3) * 4 + lax.bitwise_and(place, 3)
    label = jnp.where(lax.shift_right_logical(place, 2) == part, own, classes).astype(jnp.float32)
    lows = jnp.transpose((bins - upper * half + 1).astype(jnp.float32)).astype(bf16)
    coarse = tiles.astype(bf16).astype(jnp.float32)
    rest = tiles - coarse

    total = jnp.zeros((2 * classes, half), jnp.float32)
    for first in range(0, shards, 2):
        left, right = [], []
        for run in range(2 * RUNS):
            row = (first + run // RUNS) * rows + run % RUNS
            mine = tall(label[row + RUNS:row + RUNS + 1]) == column
            left.append(jnp.concatenate([
                jnp.where(mine, tall(coarse[row:row + 1]), zero), jnp.where(mine, tall(rest[row:row + 1]), zero)
            ], axis=0))
            low = jnp.broadcast_to(lows[:, row + RUNS:row + RUNS + 1], (LANES, LANES))
            right.append(jnp.concatenate([jnp.maximum(low, place) for place in places], axis=1))
        total = total + jnp.dot(
            jnp.concatenate(left, axis=1), jnp.concatenate(right, axis=0), preferred_element_type=jnp.float32
        )
    both = (total[:classes] + total[classes:]) * bin_width
    every = both[:, half - 1:] * (1.0 / half)
    lane = lax.broadcasted_iota(jnp.int32, both.shape, 1)
    at_least = jnp.where(lane == 0, every, pltpu.roll(both, 1, 1) - both + every)
    near, far = at_least[:pixels], at_least[pixels:]
    return jnp.concatenate([near + far[:, :1], far], axis=1)


def column_rows(packed, part, height):
    rows = []
    for row in range(height):
        tile = packed[row // 2 * SUBLANES:(row // 2 + 1) * SUBLANES]
        turn = row % 2 * 4 + (2 if part == 0 else SUBLANES - 2)
        rows.append(pltpu.roll(tile, (SUBLANES - turn) % SUBLANES, 0))
    return rows


def bin_sides_kernel(got, _, behind):
    height, width, radial = behind.shape
    packed = behind_of(got, 0, height=height, width=width, radial=radial)
    for row, values in enumerate(column_rows(packed, 0, height)):
        behind[row] = values


def bin_rest_kernel(got, density, behind, upstream):
    height, width, radial = behind.shape
    sub = sublane(radial)
    packed = behind_of(got, 1, height=height, width=width, radial=radial)
    for row, values in enumerate(column_rows(packed, 1, height)):
        upstream[row] = density[row] * jnp.where((sub < 2) | (sub >= 6), behind[row], values)


def mirror(stencils):
    turned = jnp.flip(stencils, axis=1).reshape(stencils.shape[0], 9, 3, stencils.shape[2])
    edge = jnp.zeros_like(turned[:, :, 0, :1])
    back = jnp.concatenate([edge, turned[:, :, 0, :-1]], axis=-1)
    ahead = jnp.concatenate([turned[:, :, 2, 1:], edge], axis=-1)
    return jnp.stack([back, turned[:, :, 1], ahead], axis=2).reshape(stencils.shape)


def swap(to_partner, to_outer, axis, closed, outer_first=False):
    count = lax.axis_size(axis)
    outer = [(i, (i + 1) % count) for i in range(1, count, 2) if closed or i + 1 < count]
    inner = [(i, i + 1) for i in range(0, count - 1, 2)]

    def both_ways(pairs):
        return pairs + [(j, i) for i, j in pairs]

    moves = [(to_partner, inner), (to_outer, outer)]
    return tuple(lax.ppermute(values, axis, both_ways(pairs)) for values, pairs in moves[::-1 if outer_first else 1])


VMEM = pl.BlockSpec(memory_space=pltpu.VMEM)
HBM = pl.BlockSpec(memory_space=pltpu.HBM)
LIMIT = pltpu.CompilerParams(vmem_limit_bytes=32 * 1024 * 1024)


def on_device(residual, star_pixel, star_bin, send_counts, send_offsets, latent, stencils):
    height, width, radial = latent.shape
    shards = send_counts.shape[1]
    slots = residual.shape[0]
    f32 = jnp.float32
    i32 = jnp.int32
    tile = jax.ShapeDtypeStruct((height, width, radial), f32)
    sides = jax.ShapeDtypeStruct((height // 4, SUBLANES, radial), f32)
    ends = jax.ShapeDtypeStruct((3, SUBLANES, radial), f32)

    def table(values):
        return values.reshape(slots // LANES, LANES)

    packed, latent, *to_sides = pl.pallas_call(
        open_kernel,
        out_shape=(jax.ShapeDtypeStruct((shards, 2 * RUNS, LANES), f32), tile, sides, sides),
        in_specs=[HBM] * 6,
        out_specs=(VMEM, VMEM, VMEM, VMEM),
        scratch_shapes=[pltpu.SMEM((1, shards), i32)] * 2
        + [pltpu.VMEM((slots // LANES, LANES), kind) for kind in (f32, i32, i32)]
        + [pltpu.SemaphoreType.DMA((6,))],
        compiler_params=LIMIT,
        name="opening",
    )(*[
        pltpu.with_memory_space_constraint(values, pltpu.HBM)
        for values in (send_counts, send_offsets, table(residual), table(star_pixel), table(star_bin), latent)
    ])
    got = lax.all_to_all(packed, ("lat", "lon"), split_axis=0, concat_axis=0, tiled=True)

    def spread(field, to_sides, name, turned):
        beside = swap(*to_sides, "lon", True, turned[0])
        to_ends = pl.pallas_call(
            functools.partial(pack_ends_kernel, turned[0]),
            out_shape=(ends, ends),
            in_specs=[VMEM] * 3,
            out_specs=(VMEM, VMEM),
            compiler_params=LIMIT,
            name=name + "_pack",
        )(field, *beside)
        return beside, swap(*to_ends, "lat", False, turned[1])

    rows = pltpu.VMEM((height, 2 * width, radial), f32)
    moved = pltpu.VMEM((2, height, 2 * width, radial), f32)

    def refined_inside(turned, coefs, finish, field, beside, table, extra, name):
        return pl.pallas_call(
            functools.partial(refine_inside_kernel, turned[0], coefs, finish),
            out_shape=(
                jax.ShapeDtypeStruct((height - 4, width, radial), f32),
                jax.ShapeDtypeStruct((3, 3, height - 2, width, radial), f32),
            ),
            in_specs=[VMEM] * 5,
            out_specs=(VMEM, VMEM),
            scratch_shapes=[rows, moved],
            compiler_params=LIMIT,
            name=name + "_inside",
        )(field, *beside, table, extra)

    def refined_ends(turned, coefs, finish, field, beside, above, table, extra, inner, middle, name, packs):
        return pl.pallas_call(
            functools.partial(refine_ends_kernel, turned, coefs, finish, packs),
            out_shape=(tile, sides, sides) if packs else tile,
            in_specs=[VMEM] * 9,
            out_specs=(VMEM,) * 3 if packs else VMEM,
            scratch_shapes=[pltpu.VMEM((3, 3, 4, width, radial), f32), rows, moved],
            compiler_params=LIMIT,
            name=name + "_ends",
        )(field, *beside, *above, table, extra, middle, inner)

    first_turned, last_turned = (False, True), (True, False)
    beside, above = spread(latent, to_sides, "density", first_turned)
    inner, middle = refined_inside(
        first_turned, (0, 1), lambda value, _: jnp.exp(value), latent, beside, stencils, latent, "density"
    )
    behind = pl.pallas_call(
        bin_sides_kernel,
        out_shape=tile,
        in_specs=[VMEM, VMEM],
        out_specs=VMEM,
        compiler_params=LIMIT,
        name="bin_sides",
    )(got, inner)
    density, *to_sides = refined_ends(
        first_turned, (0, 1), lambda value, _: jnp.exp(value), latent, beside, above, stencils, behind, inner, middle,
        "density", True,
    )
    upstream = pl.pallas_call(
        bin_rest_kernel,
        out_shape=tile,
        in_specs=[VMEM] * 3,
        out_specs=VMEM,
        compiler_params=LIMIT,
        name="bin_rest",
    )(got, density, behind)

    mirrored = mirror(stencils)
    beside, above = spread(upstream, to_sides, "back", last_turned)
    inner, middle = refined_inside(
        last_turned, (1, 0), lambda value, field: field + value, upstream, beside, mirrored, latent, "back"
    )
    return refined_ends(
        last_turned, (1, 0), lambda value, field: field + value, upstream, beside, above, mirrored, latent, inner, middle,
        "back", False,
    )


def solution(mesh):
    return jax.shard_map(
        on_device,
        mesh=mesh,
        in_specs=(
            P(("lat", "lon")),
            P(("lat", "lon")),
            P(("lat", "lon")),
            P(("lat", "lon"), None),
            P(("lat", "lon"), None),
            P("lat", "lon", None),
            P(),
        ),
        out_specs=P("lat", "lon", None),
        check_vma=False,
    )
```

```python
import functools

import jax
import jax.numpy as jnp
from jax import lax
from jax.experimental import pallas as pl
from jax.experimental.pallas import tpu as pltpu
from jax.sharding import PartitionSpec as P

CAP = 512
LANES = 128
SUBLANES = 8
RUNS = CAP // LANES
bin_width = 0.0625


def position(axis):
    index = lax.axis_index(axis)
    return index, lax.bitwise_and(index, 1)


def either(flag, if_set, if_clear):
    return jnp.where(jnp.full(if_set.shape, flag, jnp.int32) > 0, if_set, if_clear)


def sublane(radial):
    return lax.broadcasted_iota(jnp.int32, (SUBLANES, radial), 0)


def pack_sides(rows, to_partner, to_outer):
    _, odd = position("lon")
    sub = sublane(rows[0].shape[1])
    for group in range(len(rows) // 4):
        before, after = rows[4 * group], rows[4 * group]
        for k in range(1, 4):
            row = rows[4 * group + k]
            pair = lax.shift_right_logical(sub, 1)
            before = jnp.where(pair == k, pltpu.roll(row, 2 * k, 0), before)
            after = jnp.where(pair == 3 - k, pltpu.roll(row, SUBLANES - 2 * k, 0), after)
        to_partner[group] = either(odd, before, after)
        to_outer[group] = either(odd, after, before)


def unpack_sides(from_partner, from_outer, height):
    _, odd = position("lon")
    sub = sublane(from_partner.shape[2])
    tiles = []
    for group in range(height // 4):
        partner, outer = from_partner[group], from_outer[group]
        before, after = either(odd, partner, outer), either(odd, outer, partner)
        for k in range(4):
            if k:
                tiles.append(jnp.where(sub < 4, pltpu.roll(after, SUBLANES - 2 * k, 0), pltpu.roll(before, 2 * k, 0)))
            else:
                tiles.append(jnp.where(sub < 4, after, before))
    return tiles


def in_order(turned, first, second):
    return (second, first) if turned else (first, second)


def pack_ends_kernel(turned, field, side_0, side_1, to_partner, to_outer):
    height, _, radial = field.shape
    _, odd = position("lat")
    sub = sublane(radial)
    outside = (sub < 2) | (sub >= 6)
    tiles = unpack_sides(*in_order(turned, side_0, side_1), height)

    def ends(first):
        return (
            field[first],
            field[first + 1],
            jnp.where(outside, tiles[first], pltpu.roll(tiles[first + 1], 4, 0)),
        )

    for place, (top, bottom) in enumerate(zip(ends(0), ends(height - 2))):
        to_partner[place] = either(odd, top, bottom)
        to_outer[place] = either(odd, bottom, top)


def radial_shifts(field):
    radial = field.shape[-1]
    lane = lax.broadcasted_iota(jnp.int32, field.shape, field.ndim - 1)
    return (
        jnp.where(lane == 0, 0.0, pltpu.roll(field, 1, field.ndim - 1)),
        jnp.where(lane == radial - 1, 0.0, pltpu.roll(field, radial - 1, field.ndim - 1)),
    )


def taps_of(coef, at):
    return [jnp.broadcast_to(coef[k:k + 1, at], (SUBLANES, LANES)) for k in range(27)]


def tiles_of_bins(radial, body):
    def step(tile, _):
        body(pl.ds(pl.multiple_of(tile * LANES, LANES), LANES))
        return 0

    lax.fori_loop(0, radial // LANES, step, 0)


def first_level(wide, shifted, coef, centers, middle, real):
    reach, cols, radial = wide.shape
    for row in range(reach):
        for place, moved in enumerate(radial_shifts(wide[row])):
            shifted[place, row] = moved

    def body(at):
        taps = taps_of(coef, at)
        for place, row in enumerate(centers):
            parts = []
            for side in (slice(0, SUBLANES), slice(SUBLANES, cols)):
                sums = [None, None, None]
                for above in (-1, 0, 1):
                    window = (shifted[0, row + above, side, at], wide[row + above, side, at], shifted[1, row + above, side, at])
                    for beside in range(3):
                        for step in range(3):
                            term = taps[(above + 1) * 9 + beside * 3 + step] * window[step]
                            sums[beside] = term if sums[beside] is None else sums[beside] + term
                parts.append(sums)
            whole = [jnp.concatenate([parts[0][b], parts[1][b]], axis=0) for b in range(3)]
            value = whole[1] + pltpu.roll(whole[0], 1, 0) + pltpu.roll(whole[2], cols - 1, 0)
            if real[place] is not None:
                value = either(real[place], value, jnp.zeros_like(value))
            middle[0, 1, place, :, at] = pltpu.roll(value, 1, 0)[:SUBLANES]
            middle[1, 1, place, :, at] = value[:SUBLANES]
            middle[2, 1, place, :, at] = pltpu.roll(value, cols - 1, 0)[:SUBLANES]

    tiles_of_bins(radial, body)
    for place in range(len(centers)):
        for beside in range(3):
            for step, moved in zip((0, 2), radial_shifts(middle[beside, 1, place])):
                middle[beside, step, place] = moved


def second_level(coef, windows, radial, write):
    def body(at):
        taps = taps_of(coef, at)
        for row, around in windows.items():
            total = None
            for above, (buffer, place) in enumerate(around):
                for beside in range(3):
                    for step in range(3):
                        term = taps[above * 9 + beside * 3 + step] * buffer[beside, step, place, :, at]
                        total = term if total is None else total + term
            write(row, at, total)

    tiles_of_bins(radial, body)


def refine_inside_kernel(turned, coefs, finish, field, side_0, side_1, stencils, extra, _, out, middle, wide, shifted):
    height, width, radial = field.shape
    tiles = unpack_sides(*in_order(turned, side_0, side_1), height)
    for row in range(height):
        wide[row, :width] = field[row]
        wide[row, width:] = tiles[row]
    first_level(wide, shifted, stencils.at[coefs[0]], range(1, height - 1), middle, [None] * (height - 2))

    def write(row, at, value):
        out[row - 2, :, at] = finish(value, extra[row, :, at])

    windows = {row: [(middle, row - 2 + k) for k in range(3)] for row in range(2, height - 2)}
    second_level(stencils.at[coefs[1]], windows, radial, write)


def refine_ends_kernel(
    turned, coefs, finish, field, side_0, side_1, end_0, end_1, stencils, extra, inside, inner,
    out, middle, wide, shifted,
):
    height, width, radial = field.shape
    tiles = unpack_sides(*in_order(turned, side_0, side_1), height)
    lat, odd = position("lat")
    for place in range(3):
        partner, outer = end_0[place], end_1[place]
        for first, pack in ((0, either(odd, partner, outer)), (6, either(odd, outer, partner))):
            if place < 2:
                wide[first + place, :width] = pack
            else:
                wide[first, width:] = pack
                wide[first + 1, width:] = pltpu.roll(pack, 4, 0)
    for place, row in ((2, 0), (3, 1), (4, height - 2), (5, height - 1)):
        wide[place, :width] = field[row]
        wide[place, width:] = tiles[row]
    above = (lat > 0).astype(jnp.int32)
    below = (lat < lax.axis_size("lat") - 1).astype(jnp.int32)
    first_level(wide, shifted, stencils.at[coefs[0]], (1, 2, 5, 6), middle, [above, None, None, below])

    def write(row, at, value):
        out[row, :, at] = finish(value, extra[row, :, at])

    last = height - 3
    top = [(middle, 0), (middle, 1), (inside, 0), (inside, 1)]
    bottom = [(inside, last - 1), (inside, last), (middle, 2), (middle, 3)]
    windows = {0: top[:3], 1: top[1:], height - 2: bottom[:3], height - 1: bottom[1:]}
    second_level(stencils.at[coefs[1]], windows, radial, write)
    for row in range(2, height - 2):
        out[row] = inner[row - 2]


def open_kernel(
    counts_in, offsets_in, residual_in, pixel_in, bins_in, latent_in, out, latent, to_partner, to_outer,
    counts, offsets, residual, pixel, bins, arrived,
):
    pairs = (
        (latent_in, latent), (counts_in, counts), (offsets_in, offsets),
        (residual_in, residual), (pixel_in, pixel), (bins_in, bins),
    )
    copies = [pltpu.make_async_copy(source, target, arrived.at[i]) for i, (source, target) in enumerate(pairs)]
    for copy in copies:
        copy.start()
    copies[0].wait()
    height, _, radial = latent.shape
    pack_sides([latent[row] for row in range(height)], to_partner, to_outer)
    for copy in copies[1:]:
        copy.wait()

    lane = lax.broadcasted_iota(jnp.int32, (SUBLANES, LANES), 1)
    row = lax.broadcasted_iota(jnp.int32, (SUBLANES, LANES), 0)
    slot = row * LANES + lane
    for owner in range(out.shape[0]):
        start = offsets[0, owner]
        first = lax.shift_right_logical(start, 7)
        part = lax.bitwise_and(start, LANES - 1)
        live = slot < counts[0, owner]

        def window(values):
            turned = pltpu.roll(values, lax.bitwise_and(LANES - part, LANES - 1), 1)
            joined = jnp.where(lane < LANES - part, turned, pltpu.roll(turned, SUBLANES - 1, 0))
            return jnp.where(live, joined, 0.0)

        at = pl.ds(first, SUBLANES)
        cell = (pixel[at, :] * radial + bins[at, :]).astype(jnp.float32)
        out[owner] = jnp.where(row < RUNS, window(residual[at, :]), pltpu.roll(window(cell), RUNS, 0))


def behind_of(got, part, *, height, width, radial):
    half = radial // 2
    pixels = height * width // 2
    classes = 2 * pixels
    shards, rows, _ = got.shape
    bf16 = jnp.bfloat16
    column = lax.broadcasted_iota(jnp.int32, (classes, LANES), 0).astype(jnp.float32).astype(bf16)
    places = [
        (lax.broadcasted_iota(jnp.int32, (LANES, LANES), 1) + (first + 1)).astype(jnp.float32).astype(bf16)
        for first in range(0, half, LANES)
    ]
    zero = jnp.zeros((), bf16)

    def tall(row):
        return jnp.concatenate([jnp.broadcast_to(row, (16, LANES)).astype(bf16)] * (classes // 16), axis=0)

    tiles = got[...].reshape(shards * rows, LANES)
    cell = tiles.astype(jnp.int32)
    pixel = lax.shift_right_logical(cell, radial.bit_length() - 1)
    bins = lax.bitwise_and(cell, radial - 1)
    upper = (bins >= half).astype(jnp.int32)
    place = lax.bitwise_and(pixel + 2, width - 1)
    own = upper * pixels + lax.shift_right_logical(pixel, 3) * 4 + lax.bitwise_and(place, 3)
    label = jnp.where(lax.shift_right_logical(place, 2) == part, own, classes).astype(jnp.float32)
    lows = jnp.transpose((bins - upper * half + 1).astype(jnp.float32)).astype(bf16)
    coarse = tiles.astype(bf16).astype(jnp.float32)
    rest = tiles - coarse

    total = jnp.zeros((2 * classes, half), jnp.float32)
    for first in range(0, shards, 2):
        left, right = [], []
        for run in range(2 * RUNS):
            row = (first + run // RUNS) * rows + run % RUNS
            mine = tall(label[row + RUNS:row + RUNS + 1]) == column
            left.append(jnp.concatenate([
                jnp.where(mine, tall(coarse[row:row + 1]), zero), jnp.where(mine, tall(rest[row:row + 1]), zero)
            ], axis=0))
            low = jnp.broadcast_to(lows[:, row + RUNS:row + RUNS + 1], (LANES, LANES))
            right.append(jnp.concatenate([jnp.maximum(low, place) for place in places], axis=1))
        total = total + jnp.dot(
            jnp.concatenate(left, axis=1), jnp.concatenate(right, axis=0), preferred_element_type=jnp.float32
        )
    both = (total[:classes] + total[classes:]) * bin_width
    every = both[:, half - 1:] * (1.0 / half)
    lane = lax.broadcasted_iota(jnp.int32, both.shape, 1)
    at_least = jnp.where(lane == 0, every, pltpu.roll(both, 1, 1) - both + every)
    near, far = at_least[:pixels], at_least[pixels:]
    return jnp.concatenate([near + far[:, :1], far], axis=1)


def column_rows(packed, part, height):
    rows = []
    for row in range(height):
        tile = packed[row // 2 * SUBLANES:(row // 2 + 1) * SUBLANES]
        turn = row % 2 * 4 + (2 if part == 0 else SUBLANES - 2)
        rows.append(pltpu.roll(tile, (SUBLANES - turn) % SUBLANES, 0))
    return rows


def bin_sides_kernel(got, density, behind, to_partner, to_outer):
    height, width, radial = behind.shape
    packed = behind_of(got, 0, height=height, width=width, radial=radial)
    rows = column_rows(packed, 0, height)
    for row, values in enumerate(rows):
        behind[row] = values
    pack_sides([density[row] * values for row, values in enumerate(rows)], to_partner, to_outer)


def bin_rest_kernel(got, density, behind, upstream):
    height, width, radial = behind.shape
    sub = sublane(radial)
    packed = behind_of(got, 1, height=height, width=width, radial=radial)
    for row, values in enumerate(column_rows(packed, 1, height)):
        upstream[row] = density[row] * jnp.where((sub < 2) | (sub >= 6), behind[row], values)


def mirror(stencils):
    turned = jnp.flip(stencils, axis=1).reshape(stencils.shape[0], 9, 3, stencils.shape[2])
    edge = jnp.zeros_like(turned[:, :, 0, :1])
    back = jnp.concatenate([edge, turned[:, :, 0, :-1]], axis=-1)
    ahead = jnp.concatenate([turned[:, :, 2, 1:], edge], axis=-1)
    return jnp.stack([back, turned[:, :, 1], ahead], axis=2).reshape(stencils.shape)


def swap(to_partner, to_outer, axis, closed, outer_first=False):
    count = lax.axis_size(axis)
    outer = [(i, (i + 1) % count) for i in range(1, count, 2) if closed or i + 1 < count]
    inner = [(i, i + 1) for i in range(0, count - 1, 2)]

    def both_ways(pairs):
        return pairs + [(j, i) for i, j in pairs]

    moves = [(to_partner, inner), (to_outer, outer)]
    return tuple(lax.ppermute(values, axis, both_ways(pairs)) for values, pairs in moves[::-1 if outer_first else 1])


def relay(to_partner, to_outer):
    if lax.axis_size("lat") != 4:
        ends = swap(to_partner, to_outer, "lat", False)
        return *ends, ends[0]
    passing = lax.ppermute(to_outer, "lat", [(1, 3), (2, 0)])
    from_partner = lax.ppermute(to_partner, "lat", [(0, 1), (1, 0), (2, 3), (3, 2)])
    return from_partner, lax.ppermute(passing, "lat", [(0, 1), (3, 2)]), passing


VMEM = pl.BlockSpec(memory_space=pltpu.VMEM)
HBM = pl.BlockSpec(memory_space=pltpu.HBM)
LIMIT = pltpu.CompilerParams(vmem_limit_bytes=32 * 1024 * 1024)


def on_device(residual, star_pixel, star_bin, send_counts, send_offsets, latent, stencils):
    height, width, radial = latent.shape
    shards = send_counts.shape[1]
    slots = residual.shape[0]
    f32 = jnp.float32
    i32 = jnp.int32
    tile = jax.ShapeDtypeStruct((height, width, radial), f32)
    sides = jax.ShapeDtypeStruct((height // 4, SUBLANES, radial), f32)
    ends = jax.ShapeDtypeStruct((3, SUBLANES, radial), f32)

    def table(values):
        return values.reshape(slots // LANES, LANES)

    packed, latent, *to_sides = pl.pallas_call(
        open_kernel,
        out_shape=(jax.ShapeDtypeStruct((shards, 2 * RUNS, LANES), f32), tile, sides, sides),
        in_specs=[HBM] * 6,
        out_specs=(VMEM, VMEM, VMEM, VMEM),
        scratch_shapes=[pltpu.SMEM((1, shards), i32)] * 2
        + [pltpu.VMEM((slots // LANES, LANES), kind) for kind in (f32, i32, i32)]
        + [pltpu.SemaphoreType.DMA((6,))],
        compiler_params=LIMIT,
        name="opening",
    )(*[
        pltpu.with_memory_space_constraint(values, pltpu.HBM)
        for values in (send_counts, send_offsets, table(residual), table(star_pixel), table(star_bin), latent)
    ])
    got = lax.all_to_all(packed, ("lat", "lon"), split_axis=0, concat_axis=0, tiled=True)

    def spread(field, to_sides, name, turned):
        beside = swap(*to_sides, "lon", True, turned)
        to_ends = pl.pallas_call(
            functools.partial(pack_ends_kernel, turned),
            out_shape=(ends, ends),
            in_specs=[VMEM] * 3,
            out_specs=(VMEM, VMEM),
            compiler_params=LIMIT,
            name=name + "_pack",
        )(field, *beside)
        return beside, relay(*to_ends)

    rows = pltpu.VMEM((height, 2 * width, radial), f32)
    moved = pltpu.VMEM((2, height, 2 * width, radial), f32)

    def refined(field, to_sides, turned, coefs, table, extra, finish, name):
        beside, (*above, passing) = spread(field, to_sides, name, turned)
        inner, middle = pl.pallas_call(
            functools.partial(refine_inside_kernel, turned, coefs, finish),
            out_shape=(
                jax.ShapeDtypeStruct((height - 4, width, radial), f32),
                jax.ShapeDtypeStruct((3, 3, height - 2, width, radial), f32),
            ),
            in_specs=[VMEM] * 6,
            out_specs=(VMEM, VMEM),
            scratch_shapes=[rows, moved],
            compiler_params=LIMIT,
            name=name + "_inside",
        )(field, *beside, table, extra, passing)
        return pl.pallas_call(
            functools.partial(refine_ends_kernel, turned, coefs, finish),
            out_shape=tile,
            in_specs=[VMEM] * 9,
            out_specs=VMEM,
            scratch_shapes=[pltpu.VMEM((3, 3, 4, width, radial), f32), rows, moved],
            compiler_params=LIMIT,
            name=name + "_ends",
        )(field, *beside, *above, table, extra, middle, inner)

    density = refined(latent, to_sides, False, (0, 1), stencils, latent, lambda value, _: jnp.exp(value), "density")
    behind, *to_sides = pl.pallas_call(
        bin_sides_kernel,
        out_shape=(tile, sides, sides),
        in_specs=[VMEM, VMEM],
        out_specs=(VMEM,) * 3,
        compiler_params=LIMIT,
        name="bin_sides",
    )(got, density)
    upstream = pl.pallas_call(
        bin_rest_kernel,
        out_shape=tile,
        in_specs=[VMEM] * 3,
        out_specs=VMEM,
        compiler_params=LIMIT,
        name="bin_rest",
    )(got, density, behind)
    return refined(
        upstream, to_sides, True, (1, 0), mirror(stencils), latent, lambda value, field: field + value, "back"
    )


def solution(mesh):
    return jax.shard_map(
        on_device,
        mesh=mesh,
        in_specs=(
            P(("lat", "lon")),
            P(("lat", "lon")),
            P(("lat", "lon")),
            P(("lat", "lon"), None),
            P(("lat", "lon"), None),
            P("lat", "lon", None),
            P(),
        ),
        out_specs=P("lat", "lon", None),
        check_vma=False,
    )
```

```python
import functools

import jax
import jax.numpy as jnp
from jax import lax
from jax.experimental import pallas as pl
from jax.experimental.pallas import tpu as pltpu
from jax.sharding import PartitionSpec as P

CAP = 512
LANES = 128
SUBLANES = 8
RUNS = CAP // LANES
bin_width = 0.0625


def position(axis):
    index = lax.axis_index(axis)
    return index, lax.bitwise_and(index, 1)


def either(flag, if_set, if_clear):
    return jnp.where(jnp.full(if_set.shape, flag, jnp.int32) > 0, if_set, if_clear)


def sublane(radial):
    return lax.broadcasted_iota(jnp.int32, (SUBLANES, radial), 0)


def pack_sides(rows, to_partner, to_outer):
    _, odd = position("lon")
    sub = sublane(rows[0].shape[1])
    for group in range(len(rows) // 4):
        before, after = rows[4 * group], rows[4 * group]
        for k in range(1, 4):
            row = rows[4 * group + k]
            pair = lax.shift_right_logical(sub, 1)
            before = jnp.where(pair == k, pltpu.roll(row, 2 * k, 0), before)
            after = jnp.where(pair == 3 - k, pltpu.roll(row, SUBLANES - 2 * k, 0), after)
        to_partner[group] = either(odd, before, after)
        to_outer[group] = either(odd, after, before)


def unpack_sides(from_partner, from_outer, height):
    _, odd = position("lon")
    sub = sublane(from_partner.shape[2])
    tiles = []
    for group in range(height // 4):
        partner, outer = from_partner[group], from_outer[group]
        before, after = either(odd, partner, outer), either(odd, outer, partner)
        for k in range(4):
            if k:
                tiles.append(jnp.where(sub < 4, pltpu.roll(after, SUBLANES - 2 * k, 0), pltpu.roll(before, 2 * k, 0)))
            else:
                tiles.append(jnp.where(sub < 4, after, before))
    return tiles


def pack_ends_kernel(field, side_0, side_1, to_partner, to_outer):
    height, _, radial = field.shape
    _, odd = position("lat")
    sub = sublane(radial)
    outside = (sub < 2) | (sub >= 6)
    tiles = unpack_sides(side_0, side_1, height)

    def ends(first):
        return (
            field[first],
            field[first + 1],
            jnp.where(outside, tiles[first], pltpu.roll(tiles[first + 1], 4, 0)),
        )

    for place, (top, bottom) in enumerate(zip(ends(0), ends(height - 2))):
        to_partner[place] = either(odd, top, bottom)
        to_outer[place] = either(odd, bottom, top)


def radial_shifts(field):
    radial = field.shape[-1]
    lane = lax.broadcasted_iota(jnp.int32, field.shape, field.ndim - 1)
    return (
        jnp.where(lane == 0, 0.0, pltpu.roll(field, 1, field.ndim - 1)),
        jnp.where(lane == radial - 1, 0.0, pltpu.roll(field, radial - 1, field.ndim - 1)),
    )


def taps_of(coef, at):
    return [jnp.broadcast_to(coef[k:k + 1, at], (SUBLANES, LANES)) for k in range(27)]


def tiles_of_bins(radial, body):
    def step(tile, _):
        body(pl.ds(pl.multiple_of(tile * LANES, LANES), LANES))
        return 0

    lax.fori_loop(0, radial // LANES, step, 0)


ALL = (-1, 0, 1)


def first_level(wide, shifted, coef, centers, middle, real):
    _, cols, radial = wide.shape
    for row in sorted({row + above for row, around in centers for above in around}):
        for place, moved in enumerate(radial_shifts(wide[row])):
            shifted[place, row] = moved

    def body(at):
        taps = taps_of(coef, at)
        for place, (row, around) in enumerate(centers):
            parts = []
            for side in (slice(0, SUBLANES), slice(SUBLANES, cols)):
                sums = [None, None, None]
                for above in around:
                    window = (shifted[0, row + above, side, at], wide[row + above, side, at], shifted[1, row + above, side, at])
                    for beside in range(3):
                        for step in range(3):
                            term = taps[(above + 1) * 9 + beside * 3 + step] * window[step]
                            sums[beside] = term if sums[beside] is None else sums[beside] + term
                parts.append(sums)
            whole = [jnp.concatenate([parts[0][b], parts[1][b]], axis=0) for b in range(3)]
            value = whole[1] + pltpu.roll(whole[0], 1, 0) + pltpu.roll(whole[2], cols - 1, 0)
            if real[place] is not None:
                value = either(real[place], value, jnp.zeros_like(value))
            middle[0, 1, place, :, at] = pltpu.roll(value, 1, 0)[:SUBLANES]
            middle[1, 1, place, :, at] = value[:SUBLANES]
            middle[2, 1, place, :, at] = pltpu.roll(value, cols - 1, 0)[:SUBLANES]

    tiles_of_bins(radial, body)
    for place in range(len(centers)):
        for beside in range(3):
            for step, moved in zip((0, 2), radial_shifts(middle[beside, 1, place])):
                middle[beside, step, place] = moved


def second_level(coef, windows, radial, write):
    def body(at):
        taps = taps_of(coef, at)
        for row, around in windows.items():
            total = None
            for above, at_row in enumerate(around):
                if at_row is None:
                    continue
                buffer, place = at_row
                for beside in range(3):
                    for step in range(3):
                        term = taps[above * 9 + beside * 3 + step] * buffer[beside, step, place, :, at]
                        total = term if total is None else total + term
            write(row, at, total)

    tiles_of_bins(radial, body)


def fill_wide(wide, field, side_0, side_1, rows):
    height, width, _ = field.shape
    tiles = unpack_sides(side_0, side_1, height)
    for row in rows:
        wide[row, :width] = field[row]
        wide[row, width:] = tiles[row]


def density_inside_kernel(field, side_0, side_1, stencils, out, middle, wide, shifted):
    height, width, radial = field.shape
    fill_wide(wide, field, side_0, side_1, range(height))
    centers = [(row, ALL) for row in range(1, height - 1)]
    first_level(wide, shifted, stencils.at[0], centers, middle, [None] * len(centers))

    def write(row, at, value):
        out[row - 2, :, at] = jnp.exp(value)

    windows = {row: [(middle, row - 2 + k) for k in range(3)] for row in range(2, height - 2)}
    second_level(stencils.at[1], windows, radial, write)


def density_ends_kernel(
    field, side_0, side_1, end_1, end_0, stencils, inside, inner, behind, out, to_partner, to_outer, middle, wide, shifted
):
    height, width, radial = field.shape
    tiles = unpack_sides(side_0, side_1, height)
    lat, odd = position("lat")
    for place in range(3):
        partner, outer = end_0[place], end_1[place]
        for first, pack in ((0, either(odd, partner, outer)), (6, either(odd, outer, partner))):
            if place < 2:
                wide[first + place, :width] = pack
            else:
                wide[first, width:] = pack
                wide[first + 1, width:] = pltpu.roll(pack, 4, 0)
    for place, row in ((2, 0), (3, 1), (4, height - 2), (5, height - 1)):
        wide[place, :width] = field[row]
        wide[place, width:] = tiles[row]
    above = (lat > 0).astype(jnp.int32)
    below = (lat < lax.axis_size("lat") - 1).astype(jnp.int32)
    centers = [(row, ALL) for row in (1, 2, 5, 6)]
    first_level(wide, shifted, stencils.at[0], centers, middle, [above, None, None, below])

    def write(row, at, value):
        out[row, :, at] = jnp.exp(value)

    last = height - 3
    top = [(middle, 0), (middle, 1), (inside, 0), (inside, 1)]
    bottom = [(inside, last - 1), (inside, last), (middle, 2), (middle, 3)]
    windows = {0: top[:3], 1: top[1:], height - 2: bottom[:3], height - 1: bottom[1:]}
    second_level(stencils.at[1], windows, radial, write)
    for row in range(2, height - 2):
        out[row] = inner[row - 2]
    pack_sides([out[row] * behind[row] for row in range(height)], to_partner, to_outer)


def back_reach_kernel(field, side_1, side_0, stencils, to_partner, to_outer, middle, wide, shifted, reach):
    height, _, radial = field.shape
    last = height - 1
    fill_wide(wide, field, side_0, side_1, (0, 1, last - 1, last))
    lat, odd = position("lat")
    above = (lat > 0).astype(jnp.int32)
    below = (lat < lax.axis_size("lat") - 1).astype(jnp.int32)
    centers = [(-1, (1,)), (0, (0, 1)), (last, (-1, 0)), (last + 1, (-1,))]
    first_level(wide, shifted, stencils.at[0], centers, middle, [above, None, None, below])

    def write(row, at, value):
        reach[row, :, at] = value

    windows = {
        0: [None, None, (middle, 0)],
        1: [None, (middle, 0), (middle, 1)],
        2: [(middle, 2), (middle, 3), None],
        3: [(middle, 3), None, None],
    }
    second_level(stencils.at[1], windows, radial, write)
    for place in range(2):
        to_partner[place] = either(odd, reach[place], reach[2 + place])
        to_outer[place] = either(odd, reach[2 + place], reach[place])


def back_own_kernel(field, side_1, side_0, stencils, latent, edge, out, wide, shifted, middle):
    height, _, radial = field.shape
    fill_wide(wide, field, side_0, side_1, range(height))
    centers = [(row, ALL) for row in range(1, height - 1)]
    first_level(wide, shifted, stencils.at[0], centers, middle, [None] * len(centers))

    def write(row, at, value):
        out[row, :, at] = latent[row, :, at] + value

    line = [(edge, 0), (edge, 1)] + [(middle, place) for place in range(height - 2)] + [(edge, 2), (edge, 3)]
    second_level(stencils.at[1], {row: line[row:row + 3] for row in range(height)}, radial, write)


def close_kernel(own, end_0, end_1, out):
    height = own.shape[0]
    _, odd = position("lat")
    for row in range(2, height - 2):
        out[row] = own[row]
    for place in range(2):
        partner, outer = end_0[place], end_1[place]
        out[place] = own[place] + either(odd, partner, outer)
        out[height - 2 + place] = own[height - 2 + place] + either(odd, outer, partner)


def open_kernel(
    counts_in, offsets_in, residual_in, pixel_in, bins_in, latent_in, out, latent, to_partner, to_outer,
    counts, offsets, residual, pixel, bins, arrived,
):
    pairs = (
        (counts_in, counts), (offsets_in, offsets), (residual_in, residual), (pixel_in, pixel), (bins_in, bins),
        (latent_in, latent),
    )
    copies = [pltpu.make_async_copy(source, target, arrived.at[i]) for i, (source, target) in enumerate(pairs)]
    for copy in copies:
        copy.start()
    for copy in copies[:-1]:
        copy.wait()
    height, _, radial = latent.shape
    lane = lax.broadcasted_iota(jnp.int32, (SUBLANES, LANES), 1)
    row = lax.broadcasted_iota(jnp.int32, (SUBLANES, LANES), 0)
    slot = row * LANES + lane
    for owner in range(out.shape[0]):
        start = offsets[0, owner]
        first = lax.shift_right_logical(start, 7)
        part = lax.bitwise_and(start, LANES - 1)
        live = slot < counts[0, owner]

        def window(values):
            turned = pltpu.roll(values, lax.bitwise_and(LANES - part, LANES - 1), 1)
            joined = jnp.where(lane < LANES - part, turned, pltpu.roll(turned, SUBLANES - 1, 0))
            return jnp.where(live, joined, 0.0)

        at = pl.ds(first, SUBLANES)
        cell = (pixel[at, :] * radial + bins[at, :]).astype(jnp.float32)
        out[owner] = jnp.where(row < RUNS, window(residual[at, :]), pltpu.roll(window(cell), RUNS, 0))

    copies[-1].wait()
    pack_sides([latent[row] for row in range(height)], to_partner, to_outer)


def behind_of(got, part, *, height, width, radial):
    half = radial // 2
    pixels = height * width // 2
    classes = 2 * pixels
    shards, rows, _ = got.shape
    bf16 = jnp.bfloat16
    column = lax.broadcasted_iota(jnp.int32, (classes, LANES), 0).astype(jnp.float32).astype(bf16)
    places = [
        (lax.broadcasted_iota(jnp.int32, (LANES, LANES), 1) + (first + 1)).astype(jnp.float32).astype(bf16)
        for first in range(0, half, LANES)
    ]
    zero = jnp.zeros((), bf16)

    def tall(row):
        return jnp.concatenate([jnp.broadcast_to(row, (16, LANES)).astype(bf16)] * (classes // 16), axis=0)

    tiles = got[...].reshape(shards * rows, LANES)
    cell = tiles.astype(jnp.int32)
    pixel = lax.shift_right_logical(cell, radial.bit_length() - 1)
    bins = lax.bitwise_and(cell, radial - 1)
    upper = (bins >= half).astype(jnp.int32)
    place = lax.bitwise_and(pixel + 2, width - 1)
    own = upper * pixels + lax.shift_right_logical(pixel, 3) * 4 + lax.bitwise_and(place, 3)
    label = jnp.where(lax.shift_right_logical(place, 2) == part, own, classes).astype(jnp.float32)
    lows = jnp.transpose((bins - upper * half + 1).astype(jnp.float32)).astype(bf16)
    coarse = tiles.astype(bf16).astype(jnp.float32)
    rest = tiles - coarse

    total = jnp.zeros((2 * classes, half), jnp.float32)
    for first in range(0, shards, 2):
        left, right = [], []
        for run in range(2 * RUNS):
            row = (first + run // RUNS) * rows + run % RUNS
            mine = tall(label[row + RUNS:row + RUNS + 1]) == column
            left.append(jnp.concatenate([
                jnp.where(mine, tall(coarse[row:row + 1]), zero), jnp.where(mine, tall(rest[row:row + 1]), zero)
            ], axis=0))
            low = jnp.broadcast_to(lows[:, row + RUNS:row + RUNS + 1], (LANES, LANES))
            right.append(jnp.concatenate([jnp.maximum(low, place) for place in places], axis=1))
        total = total + jnp.dot(
            jnp.concatenate(left, axis=1), jnp.concatenate(right, axis=0), preferred_element_type=jnp.float32
        )
    both = (total[:classes] + total[classes:]) * bin_width
    every = both[:, half - 1:] * (1.0 / half)
    lane = lax.broadcasted_iota(jnp.int32, both.shape, 1)
    at_least = jnp.where(lane == 0, every, pltpu.roll(both, 1, 1) - both + every)
    near, far = at_least[:pixels], at_least[pixels:]
    return jnp.concatenate([near + far[:, :1], far], axis=1)


def column_rows(packed, part, height):
    rows = []
    for row in range(height):
        tile = packed[row // 2 * SUBLANES:(row // 2 + 1) * SUBLANES]
        turn = row % 2 * 4 + (2 if part == 0 else SUBLANES - 2)
        rows.append(pltpu.roll(tile, (SUBLANES - turn) % SUBLANES, 0))
    return rows


def bin_sides_kernel(got, _, behind):
    height, width, radial = behind.shape
    packed = behind_of(got, 0, height=height, width=width, radial=radial)
    for row, values in enumerate(column_rows(packed, 0, height)):
        behind[row] = values


def bin_rest_kernel(got, density, behind, upstream):
    height, width, radial = behind.shape
    sub = sublane(radial)
    packed = behind_of(got, 1, height=height, width=width, radial=radial)
    for row, values in enumerate(column_rows(packed, 1, height)):
        upstream[row] = density[row] * jnp.where((sub < 2) | (sub >= 6), behind[row], values)


def mirror(stencils):
    turned = jnp.flip(stencils, axis=1).reshape(stencils.shape[0], 9, 3, stencils.shape[2])
    edge = jnp.zeros_like(turned[:, :, 0, :1])
    back = jnp.concatenate([edge, turned[:, :, 0, :-1]], axis=-1)
    ahead = jnp.concatenate([turned[:, :, 2, 1:], edge], axis=-1)
    return jnp.stack([back, turned[:, :, 1], ahead], axis=2).reshape(stencils.shape)


def swap(to_partner, to_outer, axis, closed, outer_first=False):
    count = lax.axis_size(axis)
    outer = [(i, (i + 1) % count) for i in range(1, count, 2) if closed or i + 1 < count]
    inner = [(i, i + 1) for i in range(0, count - 1, 2)]

    def both_ways(pairs):
        return pairs + [(j, i) for i, j in pairs]

    moves = [(to_partner, inner), (to_outer, outer)]
    got = [lax.ppermute(values, axis, both_ways(pairs)) for values, pairs in moves[::-1 if outer_first else 1]]
    return tuple(got[::-1 if outer_first else 1])


VMEM = pl.BlockSpec(memory_space=pltpu.VMEM)
HBM = pl.BlockSpec(memory_space=pltpu.HBM)
LIMIT = pltpu.CompilerParams(vmem_limit_bytes=32 * 1024 * 1024)


def on_device(residual, star_pixel, star_bin, send_counts, send_offsets, latent, stencils):
    height, width, radial = latent.shape
    shards = send_counts.shape[1]
    slots = residual.shape[0]
    f32 = jnp.float32
    i32 = jnp.int32
    tile = jax.ShapeDtypeStruct((height, width, radial), f32)
    sides = jax.ShapeDtypeStruct((height // 4, SUBLANES, radial), f32)
    ends = jax.ShapeDtypeStruct((3, SUBLANES, radial), f32)

    def table(values):
        return values.reshape(slots // LANES, LANES)

    packed, latent, *to_sides = pl.pallas_call(
        open_kernel,
        out_shape=(jax.ShapeDtypeStruct((shards, 2 * RUNS, LANES), f32), tile, sides, sides),
        in_specs=[HBM] * 6,
        out_specs=(VMEM, VMEM, VMEM, VMEM),
        scratch_shapes=[pltpu.SMEM((1, shards), i32)] * 2
        + [pltpu.VMEM((slots // LANES, LANES), kind) for kind in (f32, i32, i32)]
        + [pltpu.SemaphoreType.DMA((6,))],
        compiler_params=LIMIT,
        name="opening",
    )(*[
        pltpu.with_memory_space_constraint(values, pltpu.HBM)
        for values in (send_counts, send_offsets, table(residual), table(star_pixel), table(star_bin), latent)
    ])
    got = lax.all_to_all(packed, ("lat", "lon"), split_axis=0, concat_axis=0, tiled=True)

    rows = pltpu.VMEM((height, 2 * width, radial), f32)
    moved = pltpu.VMEM((2, height, 2 * width, radial), f32)
    edge = (3, 3, 4, width, radial)
    inner_rows = (3, 3, height - 2, width, radial)

    def call(kernel, name, outs, scratch, *operands):
        return pl.pallas_call(
            kernel,
            out_shape=outs,
            in_specs=[VMEM] * len(operands),
            out_specs=jax.tree.map(lambda _: VMEM, outs),
            scratch_shapes=scratch,
            compiler_params=LIMIT,
            name=name,
        )(*operands)

    def shape(*sizes):
        return jax.ShapeDtypeStruct(sizes, f32)

    beside = swap(*to_sides, "lon", True)
    to_ends = call(pack_ends_kernel, "density_pack", (ends, ends), [], latent, *beside)
    above = swap(*to_ends, "lat", False, outer_first=True)
    inner, middle = call(
        density_inside_kernel, "density_inside", (shape(height - 4, width, radial), shape(*inner_rows)), [rows, moved],
        latent, *beside, stencils,
    )
    behind = call(bin_sides_kernel, "bin_sides", tile, [], got, inner)
    density, *to_sides = call(
        density_ends_kernel, "density_ends", (tile, sides, sides), [pltpu.VMEM(edge, f32), rows, moved],
        latent, *beside, *above[::-1], stencils, middle, inner, behind,
    )
    upstream = call(bin_rest_kernel, "bin_rest", tile, [], got, density, behind)

    mirrored = mirror(stencils)[::-1]
    beside = swap(*to_sides, "lon", True, outer_first=True)
    *to_ends, middle = call(
        back_reach_kernel, "back_reach", (shape(2, width, radial), shape(2, width, radial), shape(*edge)),
        [rows, moved, pltpu.VMEM((4, width, radial), f32)], upstream, *beside[::-1], mirrored,
    )
    above = swap(*to_ends, "lat", False)
    own = call(
        back_own_kernel, "back_own", tile, [rows, moved, pltpu.VMEM(inner_rows, f32)],
        upstream, *beside[::-1], mirrored, latent, middle,
    )
    return call(close_kernel, "close", tile, [], own, *above)


def solution(mesh):
    return jax.shard_map(
        on_device,
        mesh=mesh,
        in_specs=(
            P(("lat", "lon")),
            P(("lat", "lon")),
            P(("lat", "lon")),
            P(("lat", "lon"), None),
            P(("lat", "lon"), None),
            P("lat", "lon", None),
            P(),
        ),
        out_specs=P("lat", "lon", None),
        check_vma=False,
    )
```

```python
import functools

import jax
import jax.numpy as jnp
from jax import lax
from jax.experimental import pallas as pl
from jax.experimental.pallas import tpu as pltpu
from jax.sharding import PartitionSpec as P

CAP = 512
LANES = 128
SUBLANES = 8
RUNS = CAP // LANES
bin_width = 0.0625


def position(axis):
    index = lax.axis_index(axis)
    return index, lax.bitwise_and(index, 1)


def either(flag, if_set, if_clear):
    return jnp.where(jnp.full(if_set.shape, flag, jnp.int32) > 0, if_set, if_clear)


def sublane(radial):
    return lax.broadcasted_iota(jnp.int32, (SUBLANES, radial), 0)


def pack_sides(rows, to_partner, to_outer):
    _, odd = position("lon")
    sub = sublane(rows[0].shape[1])
    for group in range(len(rows) // 4):
        before, after = rows[4 * group], rows[4 * group]
        for k in range(1, 4):
            row = rows[4 * group + k]
            pair = lax.shift_right_logical(sub, 1)
            before = jnp.where(pair == k, pltpu.roll(row, 2 * k, 0), before)
            after = jnp.where(pair == 3 - k, pltpu.roll(row, SUBLANES - 2 * k, 0), after)
        to_partner[group] = either(odd, before, after)
        to_outer[group] = either(odd, after, before)


def unpack_sides(from_partner, from_outer, height):
    _, odd = position("lon")
    sub = sublane(from_partner.shape[2])
    tiles = []
    for group in range(height // 4):
        partner, outer = from_partner[group], from_outer[group]
        before, after = either(odd, partner, outer), either(odd, outer, partner)
        for k in range(4):
            if k:
                tiles.append(jnp.where(sub < 4, pltpu.roll(after, SUBLANES - 2 * k, 0), pltpu.roll(before, 2 * k, 0)))
            else:
                tiles.append(jnp.where(sub < 4, after, before))
    return tiles


def pack_ends_kernel(field, side_0, side_1, to_partner, to_outer):
    height, _, radial = field.shape
    _, odd = position("lat")
    sub = sublane(radial)
    outside = (sub < 2) | (sub >= 6)
    tiles = unpack_sides(side_0, side_1, height)

    def ends(first):
        return (
            field[first],
            field[first + 1],
            jnp.where(outside, tiles[first], pltpu.roll(tiles[first + 1], 4, 0)),
        )

    for place, (top, bottom) in enumerate(zip(ends(0), ends(height - 2))):
        to_partner[place] = either(odd, top, bottom)
        to_outer[place] = either(odd, bottom, top)


def radial_shifts(field):
    radial = field.shape[-1]
    lane = lax.broadcasted_iota(jnp.int32, field.shape, field.ndim - 1)
    return (
        jnp.where(lane == 0, 0.0, pltpu.roll(field, 1, field.ndim - 1)),
        jnp.where(lane == radial - 1, 0.0, pltpu.roll(field, radial - 1, field.ndim - 1)),
    )


def taps_of(coef, at):
    return [jnp.broadcast_to(coef[k:k + 1, at], (SUBLANES, LANES)) for k in range(27)]


def tiles_of_bins(radial, body):
    for start in range(0, radial, LANES):
        body(slice(start, start + LANES))


ALL = (-1, 0, 1)


def first_level(wide, shifted, coef, centers, middle, real):
    _, cols, radial = wide.shape
    for row in sorted({row + above for row, around in centers for above in around}):
        for place, moved in enumerate(radial_shifts(wide[row])):
            shifted[place, row] = moved

    def body(at):
        taps = taps_of(coef, at)
        for place, (row, around) in enumerate(centers):
            parts = []
            for side in (slice(0, SUBLANES), slice(SUBLANES, cols)):
                sums = [None, None, None]
                for above in around:
                    window = (shifted[0, row + above, side, at], wide[row + above, side, at], shifted[1, row + above, side, at])
                    for beside in range(3):
                        for step in range(3):
                            term = taps[(above + 1) * 9 + beside * 3 + step] * window[step]
                            sums[beside] = term if sums[beside] is None else sums[beside] + term
                parts.append(sums)
            whole = [jnp.concatenate([parts[0][b], parts[1][b]], axis=0) for b in range(3)]
            value = whole[1] + pltpu.roll(whole[0], 1, 0) + pltpu.roll(whole[2], cols - 1, 0)
            if real[place] is not None:
                value = either(real[place], value, jnp.zeros_like(value))
            middle[0, 1, place, :, at] = pltpu.roll(value, 1, 0)[:SUBLANES]
            middle[1, 1, place, :, at] = value[:SUBLANES]
            middle[2, 1, place, :, at] = pltpu.roll(value, cols - 1, 0)[:SUBLANES]

    tiles_of_bins(radial, body)
    for place in range(len(centers)):
        for beside in range(3):
            for step, moved in zip((0, 2), radial_shifts(middle[beside, 1, place])):
                middle[beside, step, place] = moved


def second_level(coef, windows, radial, write):
    def body(at):
        taps = taps_of(coef, at)
        for row, around in windows.items():
            total = None
            for above, at_row in enumerate(around):
                if at_row is None:
                    continue
                buffer, place = at_row
                for beside in range(3):
                    for step in range(3):
                        term = taps[above * 9 + beside * 3 + step] * buffer[beside, step, place, :, at]
                        total = term if total is None else total + term
            write(row, at, total)

    tiles_of_bins(radial, body)


def fill_wide(wide, field, side_0, side_1, rows):
    height, width, _ = field.shape
    tiles = unpack_sides(side_0, side_1, height)
    for row in rows:
        wide[row, :width] = field[row]
        wide[row, width:] = tiles[row]


def density_inside_kernel(field, side_0, side_1, stencils, out, middle, wide, shifted):
    height, width, radial = field.shape
    fill_wide(wide, field, side_0, side_1, range(height))
    centers = [(row, ALL) for row in range(1, height - 1)]
    first_level(wide, shifted, stencils.at[0], centers, middle, [None] * len(centers))

    def write(row, at, value):
        out[row - 2, :, at] = jnp.exp(value)

    windows = {row: [(middle, row - 2 + k) for k in range(3)] for row in range(2, height - 2)}
    second_level(stencils.at[1], windows, radial, write)


def density_ends_kernel(
    field, side_0, side_1, end_1, end_0, stencils, inside, inner, behind, out, to_partner, to_outer, middle, wide, shifted
):
    height, width, radial = field.shape
    tiles = unpack_sides(side_0, side_1, height)
    lat, odd = position("lat")
    for place in range(3):
        partner, outer = end_0[place], end_1[place]
        for first, pack in ((0, either(odd, partner, outer)), (6, either(odd, outer, partner))):
            if place < 2:
                wide[first + place, :width] = pack
            else:
                wide[first, width:] = pack
                wide[first + 1, width:] = pltpu.roll(pack, 4, 0)
    for place, row in ((2, 0), (3, 1), (4, height - 2), (5, height - 1)):
        wide[place, :width] = field[row]
        wide[place, width:] = tiles[row]
    above = (lat > 0).astype(jnp.int32)
    below = (lat < lax.axis_size("lat") - 1).astype(jnp.int32)
    centers = [(row, ALL) for row in (1, 2, 5, 6)]
    first_level(wide, shifted, stencils.at[0], centers, middle, [above, None, None, below])

    def write(row, at, value):
        out[row, :, at] = jnp.exp(value)

    last = height - 3
    top = [(middle, 0), (middle, 1), (inside, 0), (inside, 1)]
    bottom = [(inside, last - 1), (inside, last), (middle, 2), (middle, 3)]
    windows = {0: top[:3], 1: top[1:], height - 2: bottom[:3], height - 1: bottom[1:]}
    second_level(stencils.at[1], windows, radial, write)
    for row in range(2, height - 2):
        out[row] = inner[row - 2]
    pack_sides([out[row] * behind[row] for row in range(height)], to_partner, to_outer)


def back_reach_kernel(field, side_1, side_0, stencils, to_partner, to_outer, middle, wide, shifted, reach):
    height, _, radial = field.shape
    last = height - 1
    fill_wide(wide, field, side_0, side_1, (0, 1, last - 1, last))
    lat, odd = position("lat")
    above = (lat > 0).astype(jnp.int32)
    below = (lat < lax.axis_size("lat") - 1).astype(jnp.int32)
    centers = [(-1, (1,)), (0, (0, 1)), (last, (-1, 0)), (last + 1, (-1,))]
    first_level(wide, shifted, stencils.at[0], centers, middle, [above, None, None, below])

    def write(row, at, value):
        reach[row, :, at] = value

    windows = {
        0: [None, None, (middle, 0)],
        1: [None, (middle, 0), (middle, 1)],
        2: [(middle, 2), (middle, 3), None],
        3: [(middle, 3), None, None],
    }
    second_level(stencils.at[1], windows, radial, write)
    for place in range(2):
        to_partner[place] = either(odd, reach[place], reach[2 + place])
        to_outer[place] = either(odd, reach[2 + place], reach[place])


def back_own_kernel(field, side_1, side_0, stencils, latent, edge, out, wide, shifted, middle):
    height, _, radial = field.shape
    fill_wide(wide, field, side_0, side_1, range(height))
    centers = [(row, ALL) for row in range(1, height - 1)]
    first_level(wide, shifted, stencils.at[0], centers, middle, [None] * len(centers))

    def write(row, at, value):
        out[row, :, at] = latent[row, :, at] + value

    line = [(edge, 0), (edge, 1)] + [(middle, place) for place in range(height - 2)] + [(edge, 2), (edge, 3)]
    second_level(stencils.at[1], {row: line[row:row + 3] for row in range(height)}, radial, write)


def close_kernel(own, end_0, end_1, out):
    height = own.shape[0]
    _, odd = position("lat")
    for row in range(2, height - 2):
        out[row] = own[row]
    for place in range(2):
        partner, outer = end_0[place], end_1[place]
        out[place] = own[place] + either(odd, partner, outer)
        out[height - 2 + place] = own[height - 2 + place] + either(odd, outer, partner)


def open_kernel(
    counts_in, offsets_in, residual_in, pixel_in, bins_in, latent_in, out, latent, to_partner, to_outer,
    counts, offsets, residual, pixel, bins, arrived,
):
    pairs = (
        (counts_in, counts), (offsets_in, offsets), (residual_in, residual), (pixel_in, pixel), (bins_in, bins),
        (latent_in, latent),
    )
    copies = [pltpu.make_async_copy(source, target, arrived.at[i]) for i, (source, target) in enumerate(pairs)]
    for copy in copies:
        copy.start()
    for copy in copies[:-1]:
        copy.wait()
    height, _, radial = latent.shape
    lane = lax.broadcasted_iota(jnp.int32, (SUBLANES, LANES), 1)
    row = lax.broadcasted_iota(jnp.int32, (SUBLANES, LANES), 0)
    slot = row * LANES + lane
    for owner in range(out.shape[0]):
        start = offsets[0, owner]
        tile = lax.shift_right_logical(start, 10)
        first = lax.bitwise_and(lax.shift_right_logical(start, 7), SUBLANES - 1)
        part = lax.bitwise_and(start, LANES - 1)
        live = slot < counts[0, owner]
        here = row < SUBLANES - first

        def window(one, two):
            up = lax.bitwise_and(SUBLANES - first, SUBLANES - 1)
            rows = jnp.where(here, pltpu.roll(one, up, 0), pltpu.roll(two, up, 0))
            turned = pltpu.roll(rows, lax.bitwise_and(LANES - part, LANES - 1), 1)
            return jnp.where(lane < LANES - part, turned, pltpu.roll(turned, SUBLANES - 1, 0))

        value = window(residual[tile], residual[tile + 1])
        cell = window(*[(pixel[at] * radial + bins[at]).astype(jnp.float32) for at in (tile, tile + 1)])
        out[owner] = jnp.where(row < RUNS, jnp.where(live, value, 0.0), pltpu.roll(jnp.where(live, cell, 0.0), RUNS, 0))

    copies[-1].wait()
    pack_sides([latent[row] for row in range(height)], to_partner, to_outer)


def behind_of(got, part, group, *, height, width, radial):
    half = radial // 2
    pixels = height * width // 2
    classes = 2 * pixels
    shards, rows, _ = got.shape
    bf16 = jnp.bfloat16
    column = lax.broadcasted_iota(jnp.int32, (classes, LANES), 0).astype(jnp.float32).astype(bf16)
    places = [
        (lax.broadcasted_iota(jnp.int32, (LANES, LANES), 1) + (first + 1)).astype(jnp.float32).astype(bf16)
        for first in range(0, half, LANES)
    ]
    zero = jnp.zeros((), bf16)

    def tall(row):
        return jnp.concatenate([jnp.broadcast_to(row, (16, LANES)).astype(bf16)] * (classes // 16), axis=0)

    tiles = got[...].reshape(shards * rows, LANES)
    cell = tiles.astype(jnp.int32)
    pixel = lax.shift_right_logical(cell, radial.bit_length() - 1)
    bins = lax.bitwise_and(cell, radial - 1)
    upper = (bins >= half).astype(jnp.int32)
    place = lax.bitwise_and(pixel + 2, width - 1)
    own = upper * pixels + lax.shift_right_logical(pixel, 3) * 4 + lax.bitwise_and(place, 3)
    label = jnp.where(lax.shift_right_logical(place, 2) == part, own, classes).astype(jnp.float32)
    lows = jnp.transpose((bins - upper * half + 1).astype(jnp.float32)).astype(bf16)
    coarse = tiles.astype(bf16).astype(jnp.float32)
    rest = tiles - coarse

    total = jnp.zeros((2 * classes, half), jnp.float32)
    for first in range(0, shards, group):
        left, right = [], []
        for run in range(group * RUNS):
            row = (first + run // RUNS) * rows + run % RUNS
            mine = tall(label[row + RUNS:row + RUNS + 1]) == column
            left.append(jnp.concatenate([
                jnp.where(mine, tall(coarse[row:row + 1]), zero), jnp.where(mine, tall(rest[row:row + 1]), zero)
            ], axis=0))
            low = jnp.broadcast_to(lows[:, row + RUNS:row + RUNS + 1], (LANES, LANES))
            right.append(jnp.concatenate([jnp.maximum(low, place) for place in places], axis=1))
        total = total + jnp.dot(
            jnp.concatenate(left, axis=1), jnp.concatenate(right, axis=0), preferred_element_type=jnp.float32
        )
    both = (total[:classes] + total[classes:]) * bin_width
    every = both[:, half - 1:] * (1.0 / half)
    lane = lax.broadcasted_iota(jnp.int32, both.shape, 1)
    at_least = jnp.where(lane == 0, every, pltpu.roll(both, 1, 1) - both + every)
    near, far = at_least[:pixels], at_least[pixels:]
    return jnp.concatenate([near + far[:, :1], far], axis=1)


def column_rows(packed, part, height):
    rows = []
    for row in range(height):
        tile = packed[row // 2 * SUBLANES:(row // 2 + 1) * SUBLANES]
        turn = row % 2 * 4 + (2 if part == 0 else SUBLANES - 2)
        rows.append(pltpu.roll(tile, (SUBLANES - turn) % SUBLANES, 0))
    return rows


def bin_sides_kernel(got, _, behind):
    height, width, radial = behind.shape
    packed = behind_of(got, 0, 1, height=height, width=width, radial=radial)
    for row, values in enumerate(column_rows(packed, 0, height)):
        behind[row] = values


def bin_rest_kernel(got, density, behind, upstream):
    height, width, radial = behind.shape
    sub = sublane(radial)
    packed = behind_of(got, 1, 4, height=height, width=width, radial=radial)
    for row, values in enumerate(column_rows(packed, 1, height)):
        upstream[row] = density[row] * jnp.where((sub < 2) | (sub >= 6), behind[row], values)


def mirror(stencils):
    turned = jnp.flip(stencils, axis=1).reshape(stencils.shape[0], 9, 3, stencils.shape[2])
    edge = jnp.zeros_like(turned[:, :, 0, :1])
    back = jnp.concatenate([edge, turned[:, :, 0, :-1]], axis=-1)
    ahead = jnp.concatenate([turned[:, :, 2, 1:], edge], axis=-1)
    return jnp.stack([back, turned[:, :, 1], ahead], axis=2).reshape(stencils.shape)


def swap(to_partner, to_outer, axis, closed, outer_first=False):
    count = lax.axis_size(axis)
    outer = [(i, (i + 1) % count) for i in range(1, count, 2) if closed or i + 1 < count]
    inner = [(i, i + 1) for i in range(0, count - 1, 2)]

    def both_ways(pairs):
        return pairs + [(j, i) for i, j in pairs]

    moves = [(to_partner, inner), (to_outer, outer)]
    got = [lax.ppermute(values, axis, both_ways(pairs)) for values, pairs in moves[::-1 if outer_first else 1]]
    return tuple(got[::-1 if outer_first else 1])


VMEM = pl.BlockSpec(memory_space=pltpu.VMEM)
HBM = pl.BlockSpec(memory_space=pltpu.HBM)
LIMIT = pltpu.CompilerParams(vmem_limit_bytes=32 * 1024 * 1024)


def on_device(residual, star_pixel, star_bin, send_counts, send_offsets, latent, stencils):
    height, width, radial = latent.shape
    shards = send_counts.shape[1]
    slots = residual.shape[0]
    f32 = jnp.float32
    i32 = jnp.int32
    tile = jax.ShapeDtypeStruct((height, width, radial), f32)
    sides = jax.ShapeDtypeStruct((height // 4, SUBLANES, radial), f32)
    ends = jax.ShapeDtypeStruct((3, SUBLANES, radial), f32)

    def table(values):
        return values.reshape(slots // (SUBLANES * LANES), SUBLANES, LANES)

    packed, latent, *to_sides = pl.pallas_call(
        open_kernel,
        out_shape=(jax.ShapeDtypeStruct((shards, 2 * RUNS, LANES), f32), tile, sides, sides),
        in_specs=[HBM] * 6,
        out_specs=(VMEM, VMEM, VMEM, VMEM),
        scratch_shapes=[pltpu.SMEM((1, shards), i32)] * 2
        + [pltpu.VMEM((slots // (SUBLANES * LANES), SUBLANES, LANES), kind) for kind in (f32, i32, i32)]
        + [pltpu.SemaphoreType.DMA((6,))],
        compiler_params=LIMIT,
        name="opening",
    )(*[
        pltpu.with_memory_space_constraint(values, pltpu.HBM)
        for values in (send_counts, send_offsets, table(residual), table(star_pixel), table(star_bin), latent)
    ])
    got = lax.all_to_all(packed, ("lat", "lon"), split_axis=0, concat_axis=0, tiled=True)

    rows = pltpu.VMEM((height, 2 * width, radial), f32)
    moved = pltpu.VMEM((2, height, 2 * width, radial), f32)
    edge = (3, 3, 4, width, radial)
    inner_rows = (3, 3, height - 2, width, radial)

    def call(kernel, name, outs, scratch, *operands):
        return pl.pallas_call(
            kernel,
            out_shape=outs,
            in_specs=[VMEM] * len(operands),
            out_specs=jax.tree.map(lambda _: VMEM, outs),
            scratch_shapes=scratch,
            compiler_params=LIMIT,
            name=name,
        )(*operands)

    def shape(*sizes):
        return jax.ShapeDtypeStruct(sizes, f32)

    beside = swap(*to_sides, "lon", True)
    to_ends = call(pack_ends_kernel, "density_pack", (ends, ends), [], latent, *beside)
    above = swap(*to_ends, "lat", False, outer_first=True)
    inner, middle = call(
        density_inside_kernel, "density_inside", (shape(height - 4, width, radial), shape(*inner_rows)), [rows, moved],
        latent, *beside, stencils,
    )
    behind = call(bin_sides_kernel, "bin_sides", tile, [], got, inner)
    density, *to_sides = call(
        density_ends_kernel, "density_ends", (tile, sides, sides), [pltpu.VMEM(edge, f32), rows, moved],
        latent, *beside, *above[::-1], stencils, middle, inner, behind,
    )
    upstream = call(bin_rest_kernel, "bin_rest", tile, [], got, density, behind)

    mirrored = mirror(stencils)[::-1]
    beside = swap(*to_sides, "lon", True, outer_first=True)
    *to_ends, middle = call(
        back_reach_kernel, "back_reach", (shape(2, width, radial), shape(2, width, radial), shape(*edge)),
        [rows, moved, pltpu.VMEM((4, width, radial), f32)], upstream, *beside[::-1], mirrored,
    )
    above = swap(*to_ends, "lat", False)
    own = call(
        back_own_kernel, "back_own", tile, [rows, moved, pltpu.VMEM(inner_rows, f32)],
        upstream, *beside[::-1], mirrored, latent, middle,
    )
    return call(close_kernel, "close", tile, [], own, *above)


def solution(mesh):
    return jax.shard_map(
        on_device,
        mesh=mesh,
        in_specs=(
            P(("lat", "lon")),
            P(("lat", "lon")),
            P(("lat", "lon")),
            P(("lat", "lon"), None),
            P(("lat", "lon"), None),
            P("lat", "lon", None),
            P(),
        ),
        out_specs=P("lat", "lon", None),
        check_vma=False,
    )
```

```python
import functools

import jax
import jax.numpy as jnp
from jax import lax
from jax.experimental import pallas as pl
from jax.experimental.pallas import tpu as pltpu
from jax.sharding import PartitionSpec as P

CAP = 512
LANES = 128
SUBLANES = 8
RUNS = CAP // LANES
bin_width = 0.0625


def position(axis):
    index = lax.axis_index(axis)
    return index, lax.bitwise_and(index, 1)


def either(flag, if_set, if_clear):
    return jnp.where(jnp.full(if_set.shape, flag, jnp.int32) > 0, if_set, if_clear)


def sublane(radial):
    return lax.broadcasted_iota(jnp.int32, (SUBLANES, radial), 0)


def pack_sides(rows, to_partner, to_outer):
    _, odd = position("lon")
    sub = sublane(rows[0].shape[1])
    for group in range(len(rows) // 4):
        before, after = rows[4 * group], rows[4 * group]
        for k in range(1, 4):
            row = rows[4 * group + k]
            pair = lax.shift_right_logical(sub, 1)
            before = jnp.where(pair == k, pltpu.roll(row, 2 * k, 0), before)
            after = jnp.where(pair == 3 - k, pltpu.roll(row, SUBLANES - 2 * k, 0), after)
        to_partner[group] = either(odd, before, after)
        to_outer[group] = either(odd, after, before)


def unpack_sides(from_partner, from_outer, height):
    _, odd = position("lon")
    sub = sublane(from_partner.shape[2])
    tiles = []
    for group in range(height // 4):
        partner, outer = from_partner[group], from_outer[group]
        before, after = either(odd, partner, outer), either(odd, outer, partner)
        for k in range(4):
            if k:
                tiles.append(jnp.where(sub < 4, pltpu.roll(after, SUBLANES - 2 * k, 0), pltpu.roll(before, 2 * k, 0)))
            else:
                tiles.append(jnp.where(sub < 4, after, before))
    return tiles


def pack_ends_kernel(field, side_0, side_1, to_partner, to_outer):
    height, _, radial = field.shape
    _, odd = position("lat")
    sub = sublane(radial)
    outside = (sub < 2) | (sub >= 6)
    tiles = unpack_sides(side_0, side_1, height)

    def ends(first):
        return (
            field[first],
            field[first + 1],
            jnp.where(outside, tiles[first], pltpu.roll(tiles[first + 1], 4, 0)),
        )

    for place, (top, bottom) in enumerate(zip(ends(0), ends(height - 2))):
        to_partner[place] = either(odd, top, bottom)
        to_outer[place] = either(odd, bottom, top)


def radial_shifts(field):
    radial = field.shape[-1]
    lane = lax.broadcasted_iota(jnp.int32, field.shape, field.ndim - 1)
    return (
        jnp.where(lane == 0, 0.0, pltpu.roll(field, 1, field.ndim - 1)),
        jnp.where(lane == radial - 1, 0.0, pltpu.roll(field, radial - 1, field.ndim - 1)),
    )


def taps_of(coef, at):
    return [jnp.broadcast_to(coef[k:k + 1, at], (SUBLANES, LANES)) for k in range(27)]


def tiles_of_bins(radial, body):
    for start in range(0, radial, LANES):
        body(slice(start, start + LANES))


ALL = (-1, 0, 1)


def first_level(wide, shifted, coef, centers, middle, real):
    _, cols, radial = wide.shape
    for row in sorted({row + above for row, around in centers for above in around}):
        for place, moved in enumerate(radial_shifts(wide[row])):
            shifted[place, row] = moved

    def body(at):
        taps = taps_of(coef, at)
        for place, (row, around) in enumerate(centers):
            parts = []
            for side in (slice(0, SUBLANES), slice(SUBLANES, cols)):
                sums = [None, None, None]
                for above in around:
                    window = (shifted[0, row + above, side, at], wide[row + above, side, at], shifted[1, row + above, side, at])
                    for beside in range(3):
                        for step in range(3):
                            term = taps[(above + 1) * 9 + beside * 3 + step] * window[step]
                            sums[beside] = term if sums[beside] is None else sums[beside] + term
                parts.append(sums)
            whole = [jnp.concatenate([parts[0][b], parts[1][b]], axis=0) for b in range(3)]
            value = whole[1] + pltpu.roll(whole[0], 1, 0) + pltpu.roll(whole[2], cols - 1, 0)
            if real[place] is not None:
                value = either(real[place], value, jnp.zeros_like(value))
            middle[0, 1, place, :, at] = pltpu.roll(value, 1, 0)[:SUBLANES]
            middle[1, 1, place, :, at] = value[:SUBLANES]
            middle[2, 1, place, :, at] = pltpu.roll(value, cols - 1, 0)[:SUBLANES]

    tiles_of_bins(radial, body)
    for place in range(len(centers)):
        for beside in range(3):
            for step, moved in zip((0, 2), radial_shifts(middle[beside, 1, place])):
                middle[beside, step, place] = moved


def second_level(coef, windows, radial, write):
    def body(at):
        taps = taps_of(coef, at)
        for row, around in windows.items():
            total = None
            for above, at_row in enumerate(around):
                if at_row is None:
                    continue
                buffer, place = at_row
                for beside in range(3):
                    for step in range(3):
                        term = taps[above * 9 + beside * 3 + step] * buffer[beside, step, place, :, at]
                        total = term if total is None else total + term
            write(row, at, total)

    tiles_of_bins(radial, body)


def fill_wide(wide, field, side_0, side_1, rows):
    height, width, _ = field.shape
    tiles = unpack_sides(side_0, side_1, height)
    for row in rows:
        wide[row, :width] = field[row]
        wide[row, width:] = tiles[row]


def density_inside_kernel(field, side_0, side_1, stencils, out, middle, wide, shifted):
    height, width, radial = field.shape
    fill_wide(wide, field, side_0, side_1, range(height))
    centers = [(row, ALL) for row in range(1, height - 1)]
    first_level(wide, shifted, stencils.at[0], centers, middle, [None] * len(centers))

    def write(row, at, value):
        out[row - 2, :, at] = jnp.exp(value)

    windows = {row: [(middle, row - 2 + k) for k in range(3)] for row in range(2, height - 2)}
    second_level(stencils.at[1], windows, radial, write)


def density_ends_kernel(
    field, side_0, side_1, end_1, end_0, stencils, inside, inner, behind, out, to_partner, to_outer, middle, wide, shifted
):
    height, width, radial = field.shape
    tiles = unpack_sides(side_0, side_1, height)
    lat, odd = position("lat")
    for place in range(3):
        partner, outer = end_0[place], end_1[place]
        for first, pack in ((0, either(odd, partner, outer)), (6, either(odd, outer, partner))):
            if place < 2:
                wide[first + place, :width] = pack
            else:
                wide[first, width:] = pack
                wide[first + 1, width:] = pltpu.roll(pack, 4, 0)
    for place, row in ((2, 0), (3, 1), (4, height - 2), (5, height - 1)):
        wide[place, :width] = field[row]
        wide[place, width:] = tiles[row]
    above = (lat > 0).astype(jnp.int32)
    below = (lat < lax.axis_size("lat") - 1).astype(jnp.int32)
    centers = [(row, ALL) for row in (1, 2, 5, 6)]
    first_level(wide, shifted, stencils.at[0], centers, middle, [above, None, None, below])

    def write(row, at, value):
        out[row, :, at] = jnp.exp(value)

    last = height - 3
    top = [(middle, 0), (middle, 1), (inside, 0), (inside, 1)]
    bottom = [(inside, last - 1), (inside, last), (middle, 2), (middle, 3)]
    windows = {0: top[:3], 1: top[1:], height - 2: bottom[:3], height - 1: bottom[1:]}
    second_level(stencils.at[1], windows, radial, write)
    for row in range(2, height - 2):
        out[row] = inner[row - 2]
    pack_sides([out[row] * behind[row] for row in range(height)], to_partner, to_outer)


def back_reach_kernel(field, side_1, side_0, stencils, to_partner, to_outer, middle, wide, shifted, reach):
    height, _, radial = field.shape
    last = height - 1
    fill_wide(wide, field, side_0, side_1, (0, 1, last - 1, last))
    lat, odd = position("lat")
    above = (lat > 0).astype(jnp.int32)
    below = (lat < lax.axis_size("lat") - 1).astype(jnp.int32)
    centers = [(-1, (1,)), (0, (0, 1)), (last, (-1, 0)), (last + 1, (-1,))]
    first_level(wide, shifted, stencils.at[0], centers, middle, [above, None, None, below])

    def write(row, at, value):
        reach[row, :, at] = value

    windows = {
        0: [None, None, (middle, 0)],
        1: [None, (middle, 0), (middle, 1)],
        2: [(middle, 2), (middle, 3), None],
        3: [(middle, 3), None, None],
    }
    second_level(stencils.at[1], windows, radial, write)
    for place in range(2):
        to_partner[place] = either(odd, reach[place], reach[2 + place])
        to_outer[place] = either(odd, reach[2 + place], reach[place])


def back_own_kernel(field, side_1, side_0, stencils, latent, edge, out, wide, shifted, middle):
    height, _, radial = field.shape
    fill_wide(wide, field, side_0, side_1, range(height))
    centers = [(row, ALL) for row in range(1, height - 1)]
    first_level(wide, shifted, stencils.at[0], centers, middle, [None] * len(centers))

    def write(row, at, value):
        out[row, :, at] = latent[row, :, at] + value

    line = [(edge, 0), (edge, 1)] + [(middle, place) for place in range(height - 2)] + [(edge, 2), (edge, 3)]
    second_level(stencils.at[1], {row: line[row:row + 3] for row in range(height)}, radial, write)


def close_kernel(own, end_0, end_1, out, top, bottom, sent):
    height = own.shape[0]
    last = height - 2
    pairs = ((own.at[2:last], out.at[2:last]), (top, out.at[:2]), (bottom, out.at[last:]))
    copies = [pltpu.make_async_copy(source, target, sent.at[i]) for i, (source, target) in enumerate(pairs)]
    copies[0].start()
    _, odd = position("lat")
    for place in range(2):
        top[place] = own[place] + either(odd, end_0[place], end_1[place])
    copies[1].start()
    for place in range(2):
        bottom[place] = own[last + place] + either(odd, end_1[place], end_0[place])
    copies[2].start()
    for copy in copies:
        copy.wait()


def open_kernel(
    counts_in, offsets_in, residual_in, pixel_in, bins_in, latent_in, out, latent, to_partner, to_outer,
    counts, offsets, residual, pixel, bins, table, arrived,
):
    pairs = (
        (counts_in, counts), (offsets_in, offsets), (residual_in, residual), (pixel_in, pixel), (bins_in, bins),
        (latent_in, latent),
    )
    copies = [pltpu.make_async_copy(source, target, arrived.at[i]) for i, (source, target) in enumerate(pairs)]
    for copy in copies:
        copy.start()
    for copy in copies[:-1]:
        copy.wait()
    height, _, radial = latent.shape
    length = residual.shape[0]
    table[pl.ds(0, length, stride=2), :] = residual[...]
    table[pl.ds(1, length, stride=2), :] = (pixel[...] * radial + bins[...]).astype(jnp.float32)

    lane = lax.broadcasted_iota(jnp.int32, (SUBLANES, LANES), 1)
    row = lax.broadcasted_iota(jnp.int32, (SUBLANES, LANES), 0)
    slot = lax.shift_right_logical(row, 1) * LANES + lane
    for owner in range(out.shape[0]):
        start = offsets[0, owner]
        first = lax.shift_right_logical(start, 7) * 2
        part = lax.bitwise_and(start, LANES - 1)
        turn = lax.bitwise_and(LANES - part, LANES - 1)
        here = pltpu.roll(table[pl.ds(first, SUBLANES), :], turn, 1)
        after = pltpu.roll(table[pl.ds(first + 2, SUBLANES), :], turn, 1)
        joined = jnp.where(lane < LANES - part, here, after)
        out[owner] = jnp.where(slot < counts[0, owner], joined, 0.0)

    copies[-1].wait()
    pack_sides([latent[row] for row in range(height)], to_partner, to_outer)


def behind_of(got, part, cuts, *, height, width, radial):
    span = radial // cuts
    pixels = height * width // 2
    classes = cuts * pixels
    shards, rows, _ = got.shape
    bf16 = jnp.bfloat16
    column = lax.broadcasted_iota(jnp.int32, (classes, LANES), 0).astype(jnp.float32).astype(bf16)
    places = [
        (lax.broadcasted_iota(jnp.int32, (LANES, LANES), 1) + (first + 1)).astype(jnp.float32).astype(bf16)
        for first in range(0, span, LANES)
    ]
    zero = jnp.zeros((), bf16)

    def tall(row):
        return jnp.concatenate([jnp.broadcast_to(row, (16, LANES)).astype(bf16)] * (classes // 16), axis=0)

    tiles = got[...].reshape(shards * rows, LANES)
    cell = tiles.astype(jnp.int32)
    pixel = lax.shift_right_logical(cell, radial.bit_length() - 1)
    bins = lax.bitwise_and(cell, radial - 1)
    cut = lax.shift_right_logical(bins, span.bit_length() - 1)
    place = lax.bitwise_and(pixel + 2, width - 1)
    own = cut * pixels + lax.shift_right_logical(pixel, 3) * 4 + lax.bitwise_and(place, 3)
    label = jnp.where(lax.shift_right_logical(place, 2) == part, own, classes).astype(jnp.float32)
    lows = jnp.transpose((lax.bitwise_and(bins, span - 1) + 1).astype(jnp.float32)).astype(bf16)
    coarse = tiles.astype(bf16).astype(jnp.float32)
    rest = tiles - coarse

    total = jnp.zeros((2 * classes, span), jnp.float32)
    for first in range(0, shards, 2):
        left, right = [], []
        for run in range(2 * RUNS):
            row = (first + run // RUNS) * rows + run % RUNS * 2
            mine = tall(label[row + 1:row + 2]) == column
            left.append(jnp.concatenate([
                jnp.where(mine, tall(coarse[row:row + 1]), zero), jnp.where(mine, tall(rest[row:row + 1]), zero)
            ], axis=0))
            low = jnp.broadcast_to(lows[:, row + 1:row + 2], (LANES, LANES))
            right.append(jnp.concatenate([jnp.maximum(low, place) for place in places], axis=1))
        total = total + jnp.dot(
            jnp.concatenate(left, axis=1), jnp.concatenate(right, axis=0), preferred_element_type=jnp.float32
        )
    both = (total[:classes] + total[classes:]) * bin_width
    every = both[:, span - 1:] * (1.0 / span)
    lane = lax.broadcasted_iota(jnp.int32, both.shape, 1)
    at_least = jnp.where(lane == 0, every, pltpu.roll(both, 1, 1) - both + every)
    ranges = [at_least[start:start + pixels] for start in range(0, classes, pixels)]
    for k in reversed(range(cuts - 1)):
        ranges[k] = ranges[k] + ranges[k + 1][:, :1]
    return jnp.concatenate(ranges, axis=1)


def column_rows(packed, part, height):
    rows = []
    for row in range(height):
        tile = packed[row // 2 * SUBLANES:(row // 2 + 1) * SUBLANES]
        turn = row % 2 * 4 + (2 if part == 0 else SUBLANES - 2)
        rows.append(pltpu.roll(tile, (SUBLANES - turn) % SUBLANES, 0))
    return rows


def bin_sides_kernel(got, _, behind):
    height, width, radial = behind.shape
    packed = behind_of(got, 0, 4, height=height, width=width, radial=radial)
    for row, values in enumerate(column_rows(packed, 0, height)):
        behind[row] = values


def bin_rest_kernel(got, density, behind, upstream):
    height, width, radial = behind.shape
    sub = sublane(radial)
    packed = behind_of(got, 1, 2, height=height, width=width, radial=radial)
    for row, values in enumerate(column_rows(packed, 1, height)):
        upstream[row] = density[row] * jnp.where((sub < 2) | (sub >= 6), behind[row], values)


def mirror(stencils):
    turned = jnp.flip(stencils, axis=1).reshape(stencils.shape[0], 9, 3, stencils.shape[2])
    edge = jnp.zeros_like(turned[:, :, 0, :1])
    back = jnp.concatenate([edge, turned[:, :, 0, :-1]], axis=-1)
    ahead = jnp.concatenate([turned[:, :, 2, 1:], edge], axis=-1)
    return jnp.stack([back, turned[:, :, 1], ahead], axis=2).reshape(stencils.shape)


def swap(to_partner, to_outer, axis, closed, outer_first=False):
    count = lax.axis_size(axis)
    outer = [(i, (i + 1) % count) for i in range(1, count, 2) if closed or i + 1 < count]
    inner = [(i, i + 1) for i in range(0, count - 1, 2)]

    def both_ways(pairs):
        return pairs + [(j, i) for i, j in pairs]

    moves = [(to_partner, inner), (to_outer, outer)]
    got = [lax.ppermute(values, axis, both_ways(pairs)) for values, pairs in moves[::-1 if outer_first else 1]]
    return tuple(got[::-1 if outer_first else 1])


VMEM = pl.BlockSpec(memory_space=pltpu.VMEM)
HBM = pl.BlockSpec(memory_space=pltpu.HBM)
LIMIT = pltpu.CompilerParams(vmem_limit_bytes=32 * 1024 * 1024)


def on_device(residual, star_pixel, star_bin, send_counts, send_offsets, latent, stencils):
    height, width, radial = latent.shape
    shards = send_counts.shape[1]
    slots = residual.shape[0]
    f32 = jnp.float32
    i32 = jnp.int32
    tile = jax.ShapeDtypeStruct((height, width, radial), f32)
    sides = jax.ShapeDtypeStruct((height // 4, SUBLANES, radial), f32)
    ends = jax.ShapeDtypeStruct((3, SUBLANES, radial), f32)

    def table(values):
        return values.reshape(slots // LANES, LANES)

    packed, latent, *to_sides = pl.pallas_call(
        open_kernel,
        out_shape=(jax.ShapeDtypeStruct((shards, 2 * RUNS, LANES), f32), tile, sides, sides),
        in_specs=[HBM] * 6,
        out_specs=(VMEM, VMEM, VMEM, VMEM),
        scratch_shapes=[pltpu.SMEM((1, shards), i32)] * 2
        + [pltpu.VMEM((slots // LANES, LANES), kind) for kind in (f32, i32, i32)]
        + [pltpu.VMEM((2 * slots // LANES, LANES), f32)]
        + [pltpu.SemaphoreType.DMA((6,))],
        compiler_params=LIMIT,
        name="opening",
    )(*[
        pltpu.with_memory_space_constraint(values, pltpu.HBM)
        for values in (send_counts, send_offsets, table(residual), table(star_pixel), table(star_bin), latent)
    ])
    got = lax.all_to_all(packed, ("lat", "lon"), split_axis=0, concat_axis=0, tiled=True)

    rows = pltpu.VMEM((height, 2 * width, radial), f32)
    moved = pltpu.VMEM((2, height, 2 * width, radial), f32)
    edge = (3, 3, 4, width, radial)
    inner_rows = (3, 3, height - 2, width, radial)

    def call(kernel, name, outs, scratch, *operands):
        return pl.pallas_call(
            kernel,
            out_shape=outs,
            in_specs=[VMEM] * len(operands),
            out_specs=jax.tree.map(lambda _: VMEM, outs),
            scratch_shapes=scratch,
            compiler_params=LIMIT,
            name=name,
        )(*operands)

    def shape(*sizes):
        return jax.ShapeDtypeStruct(sizes, f32)

    beside = swap(*to_sides, "lon", True)
    to_ends = call(pack_ends_kernel, "density_pack", (ends, ends), [], latent, *beside)
    above = swap(*to_ends, "lat", False, outer_first=True)
    inner, middle = call(
        density_inside_kernel, "density_inside", (shape(height - 4, width, radial), shape(*inner_rows)), [rows, moved],
        latent, *beside, stencils,
    )
    behind = call(bin_sides_kernel, "bin_sides", tile, [], got, inner)
    density, *to_sides = call(
        density_ends_kernel, "density_ends", (tile, sides, sides), [pltpu.VMEM(edge, f32), rows, moved],
        latent, *beside, *above[::-1], stencils, middle, inner, behind,
    )
    upstream = call(bin_rest_kernel, "bin_rest", tile, [], got, density, behind)

    mirrored = mirror(stencils)[::-1]
    beside = swap(*to_sides, "lon", True, outer_first=True)
    *to_ends, middle = call(
        back_reach_kernel, "back_reach", (shape(2, width, radial), shape(2, width, radial), shape(*edge)),
        [rows, moved, pltpu.VMEM((4, width, radial), f32)], upstream, *beside[::-1], mirrored,
    )
    above = swap(*to_ends, "lat", False)
    own = call(
        back_own_kernel, "back_own", tile, [rows, moved, pltpu.VMEM(inner_rows, f32)],
        upstream, *beside[::-1], mirrored, latent, middle,
    )
    return pl.pallas_call(
        close_kernel,
        out_shape=tile,
        in_specs=[VMEM] * 3,
        out_specs=HBM,
        scratch_shapes=[pltpu.VMEM((2, width, radial), f32)] * 2 + [pltpu.SemaphoreType.DMA((3,))],
        compiler_params=LIMIT,
        name="close",
    )(own, *above)


def solution(mesh):
    return jax.shard_map(
        on_device,
        mesh=mesh,
        in_specs=(
            P(("lat", "lon")),
            P(("lat", "lon")),
            P(("lat", "lon")),
            P(("lat", "lon"), None),
            P(("lat", "lon"), None),
            P("lat", "lon", None),
            P(),
        ),
        out_specs=P("lat", "lon", None),
        check_vma=False,
    )
```

```python
import functools

import jax
import jax.numpy as jnp
from jax import lax
from jax.experimental import pallas as pl
from jax.experimental.pallas import tpu as pltpu
from jax.sharding import PartitionSpec as P

CAP = 512
LANES = 128
SUBLANES = 8
RUNS = CAP // LANES
bin_width = 0.0625


def position(axis):
    index = lax.axis_index(axis)
    return index, lax.bitwise_and(index, 1)


def either(flag, if_set, if_clear):
    return jnp.where(jnp.full(if_set.shape, flag, jnp.int32) > 0, if_set, if_clear)


def sublane(radial):
    return lax.broadcasted_iota(jnp.int32, (SUBLANES, radial), 0)


def pack_sides(rows, to_partner, to_outer):
    _, odd = position("lon")
    sub = sublane(rows[0].shape[1])
    for group in range(len(rows) // 4):
        before, after = rows[4 * group], rows[4 * group]
        for k in range(1, 4):
            row = rows[4 * group + k]
            pair = lax.shift_right_logical(sub, 1)
            before = jnp.where(pair == k, pltpu.roll(row, 2 * k, 0), before)
            after = jnp.where(pair == 3 - k, pltpu.roll(row, SUBLANES - 2 * k, 0), after)
        to_partner[group] = either(odd, before, after)
        to_outer[group] = either(odd, after, before)


def unpack_sides(from_partner, from_outer, height):
    _, odd = position("lon")
    sub = sublane(from_partner.shape[2])
    tiles = []
    for group in range(height // 4):
        partner, outer = from_partner[group], from_outer[group]
        before, after = either(odd, partner, outer), either(odd, outer, partner)
        for k in range(4):
            if k:
                tiles.append(jnp.where(sub < 4, pltpu.roll(after, SUBLANES - 2 * k, 0), pltpu.roll(before, 2 * k, 0)))
            else:
                tiles.append(jnp.where(sub < 4, after, before))
    return tiles


def pack_ends_kernel(field, side_0, side_1, to_partner, to_outer):
    height, _, radial = field.shape
    _, odd = position("lat")
    sub = sublane(radial)
    outside = (sub < 2) | (sub >= 6)
    tiles = unpack_sides(side_0, side_1, height)

    def ends(first):
        return (
            field[first],
            field[first + 1],
            jnp.where(outside, tiles[first], pltpu.roll(tiles[first + 1], 4, 0)),
        )

    for place, (top, bottom) in enumerate(zip(ends(0), ends(height - 2))):
        to_partner[place] = either(odd, top, bottom)
        to_outer[place] = either(odd, bottom, top)


def radial_shifts(field):
    radial = field.shape[-1]
    lane = lax.broadcasted_iota(jnp.int32, field.shape, field.ndim - 1)
    return (
        jnp.where(lane == 0, 0.0, pltpu.roll(field, 1, field.ndim - 1)),
        jnp.where(lane == radial - 1, 0.0, pltpu.roll(field, radial - 1, field.ndim - 1)),
    )


def taps_of(coef, at):
    return [jnp.broadcast_to(coef[k:k + 1, at], (SUBLANES, LANES)) for k in range(27)]


def tiles_of_bins(radial, body):
    for start in range(0, radial, LANES):
        body(slice(start, start + LANES))


ALL = (-1, 0, 1)


def first_level(wide, shifted, coef, centers, middle, real):
    _, cols, radial = wide.shape
    for row in sorted({row + above for row, around in centers for above in around}):
        for place, moved in enumerate(radial_shifts(wide[row])):
            shifted[place, row] = moved

    def body(at):
        taps = taps_of(coef, at)
        for place, (row, around) in enumerate(centers):
            parts = []
            for side in (slice(0, SUBLANES), slice(SUBLANES, cols)):
                sums = [None, None, None]
                for above in around:
                    window = (shifted[0, row + above, side, at], wide[row + above, side, at], shifted[1, row + above, side, at])
                    for beside in range(3):
                        for step in range(3):
                            term = taps[(above + 1) * 9 + beside * 3 + step] * window[step]
                            sums[beside] = term if sums[beside] is None else sums[beside] + term
                parts.append(sums)
            whole = [jnp.concatenate([parts[0][b], parts[1][b]], axis=0) for b in range(3)]
            value = whole[1] + pltpu.roll(whole[0], 1, 0) + pltpu.roll(whole[2], cols - 1, 0)
            if real[place] is not None:
                value = either(real[place], value, jnp.zeros_like(value))
            middle[0, 1, place, :, at] = pltpu.roll(value, 1, 0)[:SUBLANES]
            middle[1, 1, place, :, at] = value[:SUBLANES]
            middle[2, 1, place, :, at] = pltpu.roll(value, cols - 1, 0)[:SUBLANES]

    tiles_of_bins(radial, body)
    for place in range(len(centers)):
        for beside in range(3):
            for step, moved in zip((0, 2), radial_shifts(middle[beside, 1, place])):
                middle[beside, step, place] = moved


def second_level(coef, windows, radial, write):
    def body(at):
        taps = taps_of(coef, at)
        for row, around in windows.items():
            total = None
            for above, at_row in enumerate(around):
                if at_row is None:
                    continue
                buffer, place = at_row
                for beside in range(3):
                    for step in range(3):
                        term = taps[above * 9 + beside * 3 + step] * buffer[beside, step, place, :, at]
                        total = term if total is None else total + term
            write(row, at, total)

    tiles_of_bins(radial, body)


def fill_wide(wide, field, side_0, side_1, rows):
    height, width, _ = field.shape
    tiles = unpack_sides(side_0, side_1, height)
    for row in rows:
        wide[row, :width] = field[row]
        wide[row, width:] = tiles[row]


def density_inside_kernel(field, side_0, side_1, stencils, out, middle, wide, shifted):
    height, width, radial = field.shape
    fill_wide(wide, field, side_0, side_1, range(height))
    centers = [(row, ALL) for row in range(1, height - 1)]
    first_level(wide, shifted, stencils.at[0], centers, middle, [None] * len(centers))

    def write(row, at, value):
        out[row - 2, :, at] = jnp.exp(value)

    windows = {row: [(middle, row - 2 + k) for k in range(3)] for row in range(2, height - 2)}
    second_level(stencils.at[1], windows, radial, write)


def density_ends_kernel(
    field, side_0, side_1, end_1, end_0, stencils, inside, inner, behind, out, to_partner, to_outer, middle, wide, shifted
):
    height, width, radial = field.shape
    tiles = unpack_sides(side_0, side_1, height)
    lat, odd = position("lat")
    for place in range(3):
        partner, outer = end_0[place], end_1[place]
        for first, pack in ((0, either(odd, partner, outer)), (6, either(odd, outer, partner))):
            if place < 2:
                wide[first + place, :width] = pack
            else:
                wide[first, width:] = pack
                wide[first + 1, width:] = pltpu.roll(pack, 4, 0)
    for place, row in ((2, 0), (3, 1), (4, height - 2), (5, height - 1)):
        wide[place, :width] = field[row]
        wide[place, width:] = tiles[row]
    above = (lat > 0).astype(jnp.int32)
    below = (lat < lax.axis_size("lat") - 1).astype(jnp.int32)
    centers = [(row, ALL) for row in (1, 2, 5, 6)]
    first_level(wide, shifted, stencils.at[0], centers, middle, [above, None, None, below])

    def write(row, at, value):
        out[row, :, at] = jnp.exp(value)

    last = height - 3
    top = [(middle, 0), (middle, 1), (inside, 0), (inside, 1)]
    bottom = [(inside, last - 1), (inside, last), (middle, 2), (middle, 3)]
    windows = {0: top[:3], 1: top[1:], height - 2: bottom[:3], height - 1: bottom[1:]}
    second_level(stencils.at[1], windows, radial, write)
    for row in range(2, height - 2):
        out[row] = inner[row - 2]
    pack_sides([out[row] * behind[row] for row in range(height)], to_partner, to_outer)


def back_reach_kernel(field, side_1, side_0, stencils, to_partner, to_outer, middle, wide, shifted, reach):
    height, _, radial = field.shape
    last = height - 1
    fill_wide(wide, field, side_0, side_1, (0, 1, last - 1, last))
    lat, odd = position("lat")
    above = (lat > 0).astype(jnp.int32)
    below = (lat < lax.axis_size("lat") - 1).astype(jnp.int32)
    centers = [(-1, (1,)), (0, (0, 1)), (last, (-1, 0)), (last + 1, (-1,))]
    first_level(wide, shifted, stencils.at[0], centers, middle, [above, None, None, below])

    def write(row, at, value):
        reach[row, :, at] = value

    windows = {
        0: [None, None, (middle, 0)],
        1: [None, (middle, 0), (middle, 1)],
        2: [(middle, 2), (middle, 3), None],
        3: [(middle, 3), None, None],
    }
    second_level(stencils.at[1], windows, radial, write)
    for place in range(2):
        to_partner[place] = either(odd, reach[place], reach[2 + place])
        to_outer[place] = either(odd, reach[2 + place], reach[place])


def back_own_kernel(field, side_1, side_0, stencils, latent, edge, out, wide, shifted, middle):
    height, _, radial = field.shape
    fill_wide(wide, field, side_0, side_1, range(height))
    centers = [(row, ALL) for row in range(1, height - 1)]
    first_level(wide, shifted, stencils.at[0], centers, middle, [None] * len(centers))

    def write(row, at, value):
        out[row, :, at] = latent[row, :, at] + value

    line = [(edge, 0), (edge, 1)] + [(middle, place) for place in range(height - 2)] + [(edge, 2), (edge, 3)]
    second_level(stencils.at[1], {row: line[row:row + 3] for row in range(height)}, radial, write)


def close_kernel(own, end_0, end_1, out, top, bottom, sent):
    height = own.shape[0]
    last = height - 2
    pairs = ((own.at[2:last], out.at[2:last]), (top, out.at[:2]), (bottom, out.at[last:]))
    copies = [pltpu.make_async_copy(source, target, sent.at[i]) for i, (source, target) in enumerate(pairs)]
    copies[0].start()
    _, odd = position("lat")
    for place in range(2):
        top[place] = own[place] + either(odd, end_0[place], end_1[place])
    copies[1].start()
    for place in range(2):
        bottom[place] = own[last + place] + either(odd, end_1[place], end_0[place])
    copies[2].start()
    for copy in copies:
        copy.wait()


def open_kernel(
    counts_in, offsets_in, residual_in, pixel_in, bins_in, latent_in, out, latent, to_partner, to_outer,
    counts, offsets, residual, pixel, bins, table, arrived,
):
    pairs = (
        (counts_in, counts), (offsets_in, offsets), (residual_in, residual), (pixel_in, pixel), (bins_in, bins),
        (latent_in, latent),
    )
    copies = [pltpu.make_async_copy(source, target, arrived.at[i]) for i, (source, target) in enumerate(pairs)]
    for copy in copies:
        copy.start()
    for copy in copies[:-1]:
        copy.wait()
    height, _, radial = latent.shape
    length = residual.shape[0]
    table[pl.ds(0, length, stride=2), :] = residual[...]
    table[pl.ds(1, length, stride=2), :] = (pixel[...] * radial + bins[...]).astype(jnp.float32)

    lane = lax.broadcasted_iota(jnp.int32, (SUBLANES, LANES), 1)
    row = lax.broadcasted_iota(jnp.int32, (SUBLANES, LANES), 0)
    slot = lax.shift_right_logical(row, 1) * LANES + lane
    for owner in range(out.shape[0]):
        start = offsets[0, owner]
        first = lax.shift_right_logical(start, 7) * 2
        part = lax.bitwise_and(start, LANES - 1)
        turn = lax.bitwise_and(LANES - part, LANES - 1)
        here = pltpu.roll(table[pl.ds(first, SUBLANES), :], turn, 1)
        after = pltpu.roll(table[pl.ds(first + 2, SUBLANES), :], turn, 1)
        joined = jnp.where(lane < LANES - part, here, after)
        out[owner] = jnp.where(slot < counts[0, owner], joined, 0.0)

    copies[-1].wait()
    pack_sides([latent[row] for row in range(height)], to_partner, to_outer)


def behind_of(got, part, cuts, rows_of, *, height, width, radial):
    span = radial // cuts
    pixels = height * width // 2
    classes = cuts * pixels
    shards, rows, _ = got.shape
    bf16 = jnp.bfloat16
    column = lax.broadcasted_iota(jnp.int32, (classes, LANES), 0).astype(jnp.float32).astype(bf16)
    places = [
        (lax.broadcasted_iota(jnp.int32, (LANES, LANES), 1) + (first + 1)).astype(jnp.float32).astype(bf16)
        for first in range(0, span, LANES)
    ]
    zero = jnp.zeros((), bf16)

    def tall(kind, row):
        line = jnp.broadcast_to(rows_of[kind, row:row + 1, :], (16, LANES))
        return jnp.concatenate([line.astype(bf16)] * (classes // 16), axis=0)

    tiles = got[...].reshape(shards * rows, LANES)
    cell = tiles.astype(jnp.int32)
    pixel = lax.shift_right_logical(cell, radial.bit_length() - 1)
    bins = lax.bitwise_and(cell, radial - 1)
    cut = lax.shift_right_logical(bins, span.bit_length() - 1)
    place = lax.bitwise_and(pixel + 2, width - 1)
    own = cut * pixels + lax.shift_right_logical(pixel, 3) * 4 + lax.bitwise_and(place, 3)
    rows_of[0] = jnp.where(lax.shift_right_logical(place, 2) == part, own, classes).astype(jnp.float32)
    lows = jnp.transpose((lax.bitwise_and(bins, span - 1) + 1).astype(jnp.float32)).astype(bf16)
    coarse = tiles.astype(bf16).astype(jnp.float32)
    rows_of[1] = coarse
    rows_of[2] = tiles - coarse

    total = jnp.zeros((2 * classes, span), jnp.float32)
    for first in range(0, shards, 2):
        left, right = [], []
        for run in range(2 * RUNS):
            row = (first + run // RUNS) * rows + run % RUNS * 2
            mine = tall(0, row + 1) == column
            left.append(jnp.concatenate([jnp.where(mine, tall(kind, row), zero) for kind in (1, 2)], axis=0))
            low = jnp.broadcast_to(lows[:, row + 1:row + 2], (LANES, LANES))
            right.append(jnp.concatenate([jnp.maximum(low, place) for place in places], axis=1))
        total = total + jnp.dot(
            jnp.concatenate(left, axis=1), jnp.concatenate(right, axis=0), preferred_element_type=jnp.float32
        )
    both = (total[:classes] + total[classes:]) * bin_width
    every = both[:, span - 1:] * (1.0 / span)
    lane = lax.broadcasted_iota(jnp.int32, both.shape, 1)
    at_least = jnp.where(lane == 0, every, pltpu.roll(both, 1, 1) - both + every)
    ranges = [at_least[start:start + pixels] for start in range(0, classes, pixels)]
    for k in reversed(range(cuts - 1)):
        ranges[k] = ranges[k] + ranges[k + 1][:, :1]
    return jnp.concatenate(ranges, axis=1)


def column_rows(packed, part, height):
    rows = []
    for row in range(height):
        tile = packed[row // 2 * SUBLANES:(row // 2 + 1) * SUBLANES]
        turn = row % 2 * 4 + (2 if part == 0 else SUBLANES - 2)
        rows.append(pltpu.roll(tile, (SUBLANES - turn) % SUBLANES, 0))
    return rows


def bin_sides_kernel(got, _, behind, rows_of):
    height, width, radial = behind.shape
    packed = behind_of(got, 0, 2, rows_of, height=height, width=width, radial=radial)
    for row, values in enumerate(column_rows(packed, 0, height)):
        behind[row] = values


def bin_rest_kernel(got, density, behind, upstream, rows_of):
    height, width, radial = behind.shape
    sub = sublane(radial)
    packed = behind_of(got, 1, 2, rows_of, height=height, width=width, radial=radial)
    for row, values in enumerate(column_rows(packed, 1, height)):
        upstream[row] = density[row] * jnp.where((sub < 2) | (sub >= 6), behind[row], values)


def mirror(stencils):
    turned = jnp.flip(stencils, axis=1).reshape(stencils.shape[0], 9, 3, stencils.shape[2])
    edge = jnp.zeros_like(turned[:, :, 0, :1])
    back = jnp.concatenate([edge, turned[:, :, 0, :-1]], axis=-1)
    ahead = jnp.concatenate([turned[:, :, 2, 1:], edge], axis=-1)
    return jnp.stack([back, turned[:, :, 1], ahead], axis=2).reshape(stencils.shape)


def swap(to_partner, to_outer, axis, closed, outer_first=False):
    count = lax.axis_size(axis)
    outer = [(i, (i + 1) % count) for i in range(1, count, 2) if closed or i + 1 < count]
    inner = [(i, i + 1) for i in range(0, count - 1, 2)]

    def both_ways(pairs):
        return pairs + [(j, i) for i, j in pairs]

    moves = [(to_partner, inner), (to_outer, outer)]
    got = [lax.ppermute(values, axis, both_ways(pairs)) for values, pairs in moves[::-1 if outer_first else 1]]
    return tuple(got[::-1 if outer_first else 1])


VMEM = pl.BlockSpec(memory_space=pltpu.VMEM)
HBM = pl.BlockSpec(memory_space=pltpu.HBM)
LIMIT = pltpu.CompilerParams(vmem_limit_bytes=32 * 1024 * 1024)


def on_device(residual, star_pixel, star_bin, send_counts, send_offsets, latent, stencils):
    height, width, radial = latent.shape
    shards = send_counts.shape[1]
    slots = residual.shape[0]
    f32 = jnp.float32
    i32 = jnp.int32
    tile = jax.ShapeDtypeStruct((height, width, radial), f32)
    sides = jax.ShapeDtypeStruct((height // 4, SUBLANES, radial), f32)
    ends = jax.ShapeDtypeStruct((3, SUBLANES, radial), f32)

    def table(values):
        return values.reshape(slots // LANES, LANES)

    packed, latent, *to_sides = pl.pallas_call(
        open_kernel,
        out_shape=(jax.ShapeDtypeStruct((shards, 2 * RUNS, LANES), f32), tile, sides, sides),
        in_specs=[HBM] * 6,
        out_specs=(VMEM, VMEM, VMEM, VMEM),
        scratch_shapes=[pltpu.SMEM((1, shards), i32)] * 2
        + [pltpu.VMEM((slots // LANES, LANES), kind) for kind in (f32, i32, i32)]
        + [pltpu.VMEM((2 * slots // LANES, LANES), f32)]
        + [pltpu.SemaphoreType.DMA((6,))],
        compiler_params=LIMIT,
        name="opening",
    )(*[
        pltpu.with_memory_space_constraint(values, pltpu.HBM)
        for values in (send_counts, send_offsets, table(residual), table(star_pixel), table(star_bin), latent)
    ])
    got = lax.all_to_all(packed, ("lat", "lon"), split_axis=0, concat_axis=0, tiled=True)

    rows = pltpu.VMEM((height, 2 * width, radial), f32)
    moved = pltpu.VMEM((2, height, 2 * width, radial), f32)
    edge = (3, 3, 4, width, radial)
    star_rows = pltpu.VMEM((3, shards * 2 * RUNS, LANES), f32)
    inner_rows = (3, 3, height - 2, width, radial)

    def call(kernel, name, outs, scratch, *operands):
        return pl.pallas_call(
            kernel,
            out_shape=outs,
            in_specs=[VMEM] * len(operands),
            out_specs=jax.tree.map(lambda _: VMEM, outs),
            scratch_shapes=scratch,
            compiler_params=LIMIT,
            name=name,
        )(*operands)

    def shape(*sizes):
        return jax.ShapeDtypeStruct(sizes, f32)

    beside = swap(*to_sides, "lon", True)
    to_ends = call(pack_ends_kernel, "density_pack", (ends, ends), [], latent, *beside)
    above = swap(*to_ends, "lat", False, outer_first=True)
    inner, middle = call(
        density_inside_kernel, "density_inside", (shape(height - 4, width, radial), shape(*inner_rows)), [rows, moved],
        latent, *beside, stencils,
    )
    behind = call(bin_sides_kernel, "bin_sides", tile, [star_rows], got, inner)
    density, *to_sides = call(
        density_ends_kernel, "density_ends", (tile, sides, sides), [pltpu.VMEM(edge, f32), rows, moved],
        latent, *beside, *above[::-1], stencils, middle, inner, behind,
    )
    upstream = call(bin_rest_kernel, "bin_rest", tile, [star_rows], got, density, behind)

    mirrored = mirror(stencils)[::-1]
    beside = swap(*to_sides, "lon", True, outer_first=True)
    *to_ends, middle = call(
        back_reach_kernel, "back_reach", (shape(2, width, radial), shape(2, width, radial), shape(*edge)),
        [rows, moved, pltpu.VMEM((4, width, radial), f32)], upstream, *beside[::-1], mirrored,
    )
    above = swap(*to_ends, "lat", False)
    own = call(
        back_own_kernel, "back_own", tile, [rows, moved, pltpu.VMEM(inner_rows, f32)],
        upstream, *beside[::-1], mirrored, latent, middle,
    )
    return pl.pallas_call(
        close_kernel,
        out_shape=tile,
        in_specs=[VMEM] * 3,
        out_specs=HBM,
        scratch_shapes=[pltpu.VMEM((2, width, radial), f32)] * 2 + [pltpu.SemaphoreType.DMA((3,))],
        compiler_params=LIMIT,
        name="close",
    )(own, *above)


def solution(mesh):
    return jax.shard_map(
        on_device,
        mesh=mesh,
        in_specs=(
            P(("lat", "lon")),
            P(("lat", "lon")),
            P(("lat", "lon")),
            P(("lat", "lon"), None),
            P(("lat", "lon"), None),
            P("lat", "lon", None),
            P(),
        ),
        out_specs=P("lat", "lon", None),
        check_vma=False,
    )
```

```python
import functools

import jax
import jax.numpy as jnp
from jax import lax
from jax.experimental import pallas as pl
from jax.experimental.pallas import tpu as pltpu
from jax.sharding import PartitionSpec as P

CAP = 512
LANES = 128
SUBLANES = 8
RUNS = CAP // LANES
bin_width = 0.0625


def position(axis):
    index = lax.axis_index(axis)
    return index, lax.bitwise_and(index, 1)


def either(flag, if_set, if_clear):
    return jnp.where(jnp.full(if_set.shape, flag, jnp.int32) > 0, if_set, if_clear)


def sublane(radial):
    return lax.broadcasted_iota(jnp.int32, (SUBLANES, radial), 0)


def pack_sides(rows, to_partner, to_outer):
    _, odd = position("lon")
    sub = sublane(rows[0].shape[1])
    for group in range(len(rows) // 4):
        before, after = rows[4 * group], rows[4 * group]
        for k in range(1, 4):
            row = rows[4 * group + k]
            pair = lax.shift_right_logical(sub, 1)
            before = jnp.where(pair == k, pltpu.roll(row, 2 * k, 0), before)
            after = jnp.where(pair == 3 - k, pltpu.roll(row, SUBLANES - 2 * k, 0), after)
        to_partner[group] = either(odd, before, after)
        to_outer[group] = either(odd, after, before)


def unpack_sides(from_partner, from_outer, height):
    _, odd = position("lon")
    sub = sublane(from_partner.shape[2])
    tiles = []
    for group in range(height // 4):
        partner, outer = from_partner[group], from_outer[group]
        before, after = either(odd, partner, outer), either(odd, outer, partner)
        for k in range(4):
            if k:
                tiles.append(jnp.where(sub < 4, pltpu.roll(after, SUBLANES - 2 * k, 0), pltpu.roll(before, 2 * k, 0)))
            else:
                tiles.append(jnp.where(sub < 4, after, before))
    return tiles


def pack_ends_kernel(field, side_0, side_1, to_partner, to_outer):
    height, _, radial = field.shape
    _, odd = position("lat")
    sub = sublane(radial)
    outside = (sub < 2) | (sub >= 6)
    tiles = unpack_sides(side_0, side_1, height)

    def ends(first):
        return (
            field[first],
            field[first + 1],
            jnp.where(outside, tiles[first], pltpu.roll(tiles[first + 1], 4, 0)),
        )

    for place, (top, bottom) in enumerate(zip(ends(0), ends(height - 2))):
        to_partner[place] = either(odd, top, bottom)
        to_outer[place] = either(odd, bottom, top)


def radial_shifts(field):
    radial = field.shape[-1]
    lane = lax.broadcasted_iota(jnp.int32, field.shape, field.ndim - 1)
    return (
        jnp.where(lane == 0, 0.0, pltpu.roll(field, 1, field.ndim - 1)),
        jnp.where(lane == radial - 1, 0.0, pltpu.roll(field, radial - 1, field.ndim - 1)),
    )


def taps_of(coef, at):
    return [jnp.broadcast_to(coef[k:k + 1, at], (SUBLANES, LANES)) for k in range(27)]


def tiles_of_bins(radial, body):
    for start in range(0, radial, LANES):
        body(slice(start, start + LANES))


ALL = (-1, 0, 1)


def first_level(wide, shifted, coef, centers, middle, real):
    _, cols, radial = wide.shape
    for row in sorted({row + above for row, around in centers for above in around}):
        for place, moved in enumerate(radial_shifts(wide[row])):
            shifted[place, row] = moved

    def body(at):
        taps = taps_of(coef, at)
        for place, (row, around) in enumerate(centers):
            parts = []
            for side in (slice(0, SUBLANES), slice(SUBLANES, cols)):
                sums = [None, None, None]
                for above in around:
                    window = (shifted[0, row + above, side, at], wide[row + above, side, at], shifted[1, row + above, side, at])
                    for beside in range(3):
                        for step in range(3):
                            term = taps[(above + 1) * 9 + beside * 3 + step] * window[step]
                            sums[beside] = term if sums[beside] is None else sums[beside] + term
                parts.append(sums)
            whole = [jnp.concatenate([parts[0][b], parts[1][b]], axis=0) for b in range(3)]
            value = whole[1] + pltpu.roll(whole[0], 1, 0) + pltpu.roll(whole[2], cols - 1, 0)
            if real[place] is not None:
                value = either(real[place], value, jnp.zeros_like(value))
            middle[0, 1, place, :, at] = pltpu.roll(value, 1, 0)[:SUBLANES]
            middle[1, 1, place, :, at] = value[:SUBLANES]
            middle[2, 1, place, :, at] = pltpu.roll(value, cols - 1, 0)[:SUBLANES]

    tiles_of_bins(radial, body)
    for place in range(len(centers)):
        for beside in range(3):
            for step, moved in zip((0, 2), radial_shifts(middle[beside, 1, place])):
                middle[beside, step, place] = moved


def second_level(coef, windows, radial, write):
    def body(at):
        taps = taps_of(coef, at)
        for row, around in windows.items():
            total = None
            for above, at_row in enumerate(around):
                if at_row is None:
                    continue
                buffer, place = at_row
                for beside in range(3):
                    for step in range(3):
                        term = taps[above * 9 + beside * 3 + step] * buffer[beside, step, place, :, at]
                        total = term if total is None else total + term
            write(row, at, total)

    tiles_of_bins(radial, body)


def fill_wide(wide, field, side_0, side_1, rows):
    height, width, _ = field.shape
    tiles = unpack_sides(side_0, side_1, height)
    for row in rows:
        wide[row, :width] = field[row]
        wide[row, width:] = tiles[row]


def density_inside_kernel(field, side_0, side_1, stencils, out, middle, wide, shifted):
    height, width, radial = field.shape
    fill_wide(wide, field, side_0, side_1, range(height))
    centers = [(row, ALL) for row in range(1, height - 1)]
    first_level(wide, shifted, stencils.at[0], centers, middle, [None] * len(centers))

    def write(row, at, value):
        out[row - 2, :, at] = jnp.exp(value)

    windows = {row: [(middle, row - 2 + k) for k in range(3)] for row in range(2, height - 2)}
    second_level(stencils.at[1], windows, radial, write)


def density_ends_kernel(
    field, side_0, side_1, end_1, end_0, stencils, inside, inner, behind, out, to_partner, to_outer, middle, wide, shifted
):
    height, width, radial = field.shape
    tiles = unpack_sides(side_0, side_1, height)
    lat, odd = position("lat")
    for place in range(3):
        partner, outer = end_0[place], end_1[place]
        for first, pack in ((0, either(odd, partner, outer)), (6, either(odd, outer, partner))):
            if place < 2:
                wide[first + place, :width] = pack
            else:
                wide[first, width:] = pack
                wide[first + 1, width:] = pltpu.roll(pack, 4, 0)
    for place, row in ((2, 0), (3, 1), (4, height - 2), (5, height - 1)):
        wide[place, :width] = field[row]
        wide[place, width:] = tiles[row]
    above = (lat > 0).astype(jnp.int32)
    below = (lat < lax.axis_size("lat") - 1).astype(jnp.int32)
    centers = [(row, ALL) for row in (1, 2, 5, 6)]
    first_level(wide, shifted, stencils.at[0], centers, middle, [above, None, None, below])

    def write(row, at, value):
        out[row, :, at] = jnp.exp(value)

    last = height - 3
    top = [(middle, 0), (middle, 1), (inside, 0), (inside, 1)]
    bottom = [(inside, last - 1), (inside, last), (middle, 2), (middle, 3)]
    windows = {0: top[:3], 1: top[1:], height - 2: bottom[:3], height - 1: bottom[1:]}
    second_level(stencils.at[1], windows, radial, write)
    for row in range(2, height - 2):
        out[row] = inner[row - 2]
    pack_sides([out[row] * behind[row] for row in range(height)], to_partner, to_outer)


def back_reach_kernel(field, side_1, side_0, stencils, to_partner, to_outer, middle, wide, shifted, reach):
    height, _, radial = field.shape
    last = height - 1
    fill_wide(wide, field, side_0, side_1, (0, 1, last - 1, last))
    lat, odd = position("lat")
    above = (lat > 0).astype(jnp.int32)
    below = (lat < lax.axis_size("lat") - 1).astype(jnp.int32)
    centers = [(-1, (1,)), (0, (0, 1)), (last, (-1, 0)), (last + 1, (-1,))]
    first_level(wide, shifted, stencils.at[0], centers, middle, [above, None, None, below])

    def write(row, at, value):
        reach[row, :, at] = value

    windows = {
        0: [None, None, (middle, 0)],
        1: [None, (middle, 0), (middle, 1)],
        2: [(middle, 2), (middle, 3), None],
        3: [(middle, 3), None, None],
    }
    second_level(stencils.at[1], windows, radial, write)
    for place in range(2):
        to_partner[place] = either(odd, reach[place], reach[2 + place])
        to_outer[place] = either(odd, reach[2 + place], reach[place])


def back_own_kernel(field, side_1, side_0, stencils, latent, edge, out, wide, shifted, middle):
    height, _, radial = field.shape
    fill_wide(wide, field, side_0, side_1, range(height))
    centers = [(row, ALL) for row in range(1, height - 1)]
    first_level(wide, shifted, stencils.at[0], centers, middle, [None] * len(centers))

    def write(row, at, value):
        out[row, :, at] = latent[row, :, at] + value

    line = [(edge, 0), (edge, 1)] + [(middle, place) for place in range(height - 2)] + [(edge, 2), (edge, 3)]
    second_level(stencils.at[1], {row: line[row:row + 3] for row in range(height)}, radial, write)


def close_kernel(own, end_0, end_1, out, top, bottom, sent):
    height = own.shape[0]
    last = height - 2
    pairs = ((own.at[2:last], out.at[2:last]), (top, out.at[:2]), (bottom, out.at[last:]))
    copies = [pltpu.make_async_copy(source, target, sent.at[i]) for i, (source, target) in enumerate(pairs)]
    copies[0].start()
    _, odd = position("lat")
    for place in range(2):
        top[place] = own[place] + either(odd, end_0[place], end_1[place])
    copies[1].start()
    for place in range(2):
        bottom[place] = own[last + place] + either(odd, end_1[place], end_0[place])
    copies[2].start()
    for copy in copies:
        copy.wait()


def open_kernel(
    counts_in, offsets_in, residual_in, pixel_in, bins_in, latent_in, out, latent, to_partner, to_outer,
    counts, offsets, residual, pixel, bins, table, arrived,
):
    pairs = (
        (counts_in, counts), (offsets_in, offsets), (residual_in, residual), (pixel_in, pixel), (bins_in, bins),
        (latent_in, latent),
    )
    copies = [pltpu.make_async_copy(source, target, arrived.at[i]) for i, (source, target) in enumerate(pairs)]
    for copy in copies:
        copy.start()
    for copy in copies[:-1]:
        copy.wait()
    height, _, radial = latent.shape
    length = residual.shape[0]
    table[pl.ds(0, length, stride=2), :] = residual[...]
    table[pl.ds(1, length, stride=2), :] = (pixel[...] * radial + bins[...]).astype(jnp.float32)

    lane = lax.broadcasted_iota(jnp.int32, (SUBLANES, LANES), 1)
    row = lax.broadcasted_iota(jnp.int32, (SUBLANES, LANES), 0)
    slot = lax.shift_right_logical(row, 1) * LANES + lane
    for owner in range(out.shape[0]):
        start = offsets[0, owner]
        first = lax.shift_right_logical(start, 7) * 2
        part = lax.bitwise_and(start, LANES - 1)
        turn = lax.bitwise_and(LANES - part, LANES - 1)
        here = pltpu.roll(table[pl.ds(first, SUBLANES), :], turn, 1)
        after = pltpu.roll(table[pl.ds(first + 2, SUBLANES), :], turn, 1)
        joined = jnp.where(lane < LANES - part, here, after)
        out[owner] = jnp.where(slot < counts[0, owner], joined, 0.0)

    copies[-1].wait()
    pack_sides([latent[row] for row in range(height)], to_partner, to_outer)


def behind_of(got, part, cuts, rows_of, lows, *, height, width, radial):
    span = radial // cuts
    pixels = height * width // 2
    classes = cuts * pixels
    shards, rows, _ = got.shape
    bf16 = jnp.bfloat16
    column = lax.broadcasted_iota(jnp.int32, (classes, LANES), 0).astype(jnp.float32).astype(bf16)
    places = [
        (lax.broadcasted_iota(jnp.int32, (LANES, LANES), 1) + (first + 1)).astype(jnp.float32).astype(bf16)
        for first in range(0, span, LANES)
    ]
    zero = jnp.zeros((), bf16)

    turns = lows.shape[0]
    for turn in range(turns):
        tiles = got[turn * LANES // rows:(turn + 1) * LANES // rows].reshape(LANES, LANES)
        cell = tiles.astype(jnp.int32)
        pixel = lax.shift_right_logical(cell, radial.bit_length() - 1)
        bins = lax.bitwise_and(cell, radial - 1)
        cut = lax.shift_right_logical(bins, span.bit_length() - 1)
        place = lax.bitwise_and(pixel + 2, width - 1)
        own = cut * pixels + lax.shift_right_logical(pixel, 3) * 4 + lax.bitwise_and(place, 3)
        coarse = tiles.astype(bf16).astype(jnp.float32)
        rows_of[turn, 0] = jnp.where(lax.shift_right_logical(place, 2) == part, own, classes).astype(jnp.float32)
        rows_of[turn, 1] = coarse
        rows_of[turn, 2] = tiles - coarse
        lows[turn] = jnp.transpose((lax.bitwise_and(bins, span - 1) + 1).astype(jnp.float32)).astype(bf16)

    def step(turn, total):
        def tall(kind, row):
            line = jnp.broadcast_to(rows_of[turn, kind, row:row + 1, :], (16, LANES))
            return jnp.concatenate([line.astype(bf16)] * (classes // 16), axis=0)

        for first in range(0, LANES, 2 * rows):
            left, right = [], []
            for row in range(first, first + 2 * rows, 2):
                mine = tall(0, row + 1) == column
                left.append(jnp.concatenate([jnp.where(mine, tall(kind, row), zero) for kind in (1, 2)], axis=0))
                low = jnp.broadcast_to(lows[turn, :, row + 1:row + 2], (LANES, LANES))
                right.append(jnp.concatenate([jnp.maximum(low, place) for place in places], axis=1))
            total = total + jnp.dot(
                jnp.concatenate(left, axis=1), jnp.concatenate(right, axis=0), preferred_element_type=jnp.float32
            )
        return total

    total = lax.fori_loop(0, turns, step, jnp.zeros((2 * classes, span), jnp.float32))
    both = (total[:classes] + total[classes:]) * bin_width
    every = both[:, span - 1:] * (1.0 / span)
    lane = lax.broadcasted_iota(jnp.int32, both.shape, 1)
    at_least = jnp.where(lane == 0, every, pltpu.roll(both, 1, 1) - both + every)
    ranges = [at_least[start:start + pixels] for start in range(0, classes, pixels)]
    for k in reversed(range(cuts - 1)):
        ranges[k] = ranges[k] + ranges[k + 1][:, :1]
    return jnp.concatenate(ranges, axis=1)


def column_rows(packed, part, height):
    rows = []
    for row in range(height):
        tile = packed[row // 2 * SUBLANES:(row // 2 + 1) * SUBLANES]
        turn = row % 2 * 4 + (2 if part == 0 else SUBLANES - 2)
        rows.append(pltpu.roll(tile, (SUBLANES - turn) % SUBLANES, 0))
    return rows


def bin_sides_kernel(got, _, behind, rows_of, lows):
    height, width, radial = behind.shape
    packed = behind_of(got, 0, 2, rows_of, lows, height=height, width=width, radial=radial)
    for row, values in enumerate(column_rows(packed, 0, height)):
        behind[row] = values


def bin_rest_kernel(got, density, behind, upstream, rows_of, lows):
    height, width, radial = behind.shape
    sub = sublane(radial)
    packed = behind_of(got, 1, 2, rows_of, lows, height=height, width=width, radial=radial)
    for row, values in enumerate(column_rows(packed, 1, height)):
        upstream[row] = density[row] * jnp.where((sub < 2) | (sub >= 6), behind[row], values)


def mirror(stencils):
    turned = jnp.flip(stencils, axis=1).reshape(stencils.shape[0], 9, 3, stencils.shape[2])
    edge = jnp.zeros_like(turned[:, :, 0, :1])
    back = jnp.concatenate([edge, turned[:, :, 0, :-1]], axis=-1)
    ahead = jnp.concatenate([turned[:, :, 2, 1:], edge], axis=-1)
    return jnp.stack([back, turned[:, :, 1], ahead], axis=2).reshape(stencils.shape)


def swap(to_partner, to_outer, axis, closed, outer_first=False):
    count = lax.axis_size(axis)
    outer = [(i, (i + 1) % count) for i in range(1, count, 2) if closed or i + 1 < count]
    inner = [(i, i + 1) for i in range(0, count - 1, 2)]

    def both_ways(pairs):
        return pairs + [(j, i) for i, j in pairs]

    moves = [(to_partner, inner), (to_outer, outer)]
    got = [lax.ppermute(values, axis, both_ways(pairs)) for values, pairs in moves[::-1 if outer_first else 1]]
    return tuple(got[::-1 if outer_first else 1])


VMEM = pl.BlockSpec(memory_space=pltpu.VMEM)
HBM = pl.BlockSpec(memory_space=pltpu.HBM)
LIMIT = pltpu.CompilerParams(vmem_limit_bytes=32 * 1024 * 1024)


def on_device(residual, star_pixel, star_bin, send_counts, send_offsets, latent, stencils):
    height, width, radial = latent.shape
    shards = send_counts.shape[1]
    slots = residual.shape[0]
    f32 = jnp.float32
    i32 = jnp.int32
    tile = jax.ShapeDtypeStruct((height, width, radial), f32)
    sides = jax.ShapeDtypeStruct((height // 4, SUBLANES, radial), f32)
    ends = jax.ShapeDtypeStruct((3, SUBLANES, radial), f32)

    def table(values):
        return values.reshape(slots // LANES, LANES)

    packed, latent, *to_sides = pl.pallas_call(
        open_kernel,
        out_shape=(jax.ShapeDtypeStruct((shards, 2 * RUNS, LANES), f32), tile, sides, sides),
        in_specs=[HBM] * 6,
        out_specs=(VMEM, VMEM, VMEM, VMEM),
        scratch_shapes=[pltpu.SMEM((1, shards), i32)] * 2
        + [pltpu.VMEM((slots // LANES, LANES), kind) for kind in (f32, i32, i32)]
        + [pltpu.VMEM((2 * slots // LANES, LANES), f32)]
        + [pltpu.SemaphoreType.DMA((6,))],
        compiler_params=LIMIT,
        name="opening",
    )(*[
        pltpu.with_memory_space_constraint(values, pltpu.HBM)
        for values in (send_counts, send_offsets, table(residual), table(star_pixel), table(star_bin), latent)
    ])
    got = lax.all_to_all(packed, ("lat", "lon"), split_axis=0, concat_axis=0, tiled=True)

    rows = pltpu.VMEM((height, 2 * width, radial), f32)
    moved = pltpu.VMEM((2, height, 2 * width, radial), f32)
    edge = (3, 3, 4, width, radial)
    turns = shards * 2 * RUNS // LANES
    star_rows = [pltpu.VMEM((turns, 3, LANES, LANES), f32), pltpu.VMEM((turns, LANES, LANES), jnp.bfloat16)]
    inner_rows = (3, 3, height - 2, width, radial)

    def call(kernel, name, outs, scratch, *operands):
        return pl.pallas_call(
            kernel,
            out_shape=outs,
            in_specs=[VMEM] * len(operands),
            out_specs=jax.tree.map(lambda _: VMEM, outs),
            scratch_shapes=scratch,
            compiler_params=LIMIT,
            name=name,
        )(*operands)

    def shape(*sizes):
        return jax.ShapeDtypeStruct(sizes, f32)

    beside = swap(*to_sides, "lon", True)
    to_ends = call(pack_ends_kernel, "density_pack", (ends, ends), [], latent, *beside)
    above = swap(*to_ends, "lat", False, outer_first=True)
    inner, middle = call(
        density_inside_kernel, "density_inside", (shape(height - 4, width, radial), shape(*inner_rows)), [rows, moved],
        latent, *beside, stencils,
    )
    behind = call(bin_sides_kernel, "bin_sides", tile, star_rows, got, inner)
    density, *to_sides = call(
        density_ends_kernel, "density_ends", (tile, sides, sides), [pltpu.VMEM(edge, f32), rows, moved],
        latent, *beside, *above[::-1], stencils, middle, inner, behind,
    )
    upstream = call(bin_rest_kernel, "bin_rest", tile, star_rows, got, density, behind)

    mirrored = mirror(stencils)[::-1]
    beside = swap(*to_sides, "lon", True, outer_first=True)
    *to_ends, middle = call(
        back_reach_kernel, "back_reach", (shape(2, width, radial), shape(2, width, radial), shape(*edge)),
        [rows, moved, pltpu.VMEM((4, width, radial), f32)], upstream, *beside[::-1], mirrored,
    )
    above = swap(*to_ends, "lat", False)
    own = call(
        back_own_kernel, "back_own", tile, [rows, moved, pltpu.VMEM(inner_rows, f32)],
        upstream, *beside[::-1], mirrored, latent, middle,
    )
    return pl.pallas_call(
        close_kernel,
        out_shape=tile,
        in_specs=[VMEM] * 3,
        out_specs=HBM,
        scratch_shapes=[pltpu.VMEM((2, width, radial), f32)] * 2 + [pltpu.SemaphoreType.DMA((3,))],
        compiler_params=LIMIT,
        name="close",
    )(own, *above)


def solution(mesh):
    return jax.shard_map(
        on_device,
        mesh=mesh,
        in_specs=(
            P(("lat", "lon")),
            P(("lat", "lon")),
            P(("lat", "lon")),
            P(("lat", "lon"), None),
            P(("lat", "lon"), None),
            P("lat", "lon", None),
            P(),
        ),
        out_specs=P("lat", "lon", None),
        check_vma=False,
    )
```

```python
import functools

import jax
import jax.numpy as jnp
from jax import lax
from jax.experimental import pallas as pl
from jax.experimental.pallas import tpu as pltpu
from jax.sharding import PartitionSpec as P

CAP = 512
LANES = 128
SUBLANES = 8
RUNS = CAP // LANES
bin_width = 0.0625


def position(axis):
    index = lax.axis_index(axis)
    return index, lax.bitwise_and(index, 1)


def either(flag, if_set, if_clear):
    return jnp.where(jnp.full(if_set.shape, flag, jnp.int32) > 0, if_set, if_clear)


def sublane(radial):
    return lax.broadcasted_iota(jnp.int32, (SUBLANES, radial), 0)


def pack_sides(rows, to_partner, to_outer):
    _, odd = position("lon")
    sub = sublane(rows[0].shape[1])
    for group in range(len(rows) // 4):
        before, after = rows[4 * group], rows[4 * group]
        for k in range(1, 4):
            row = rows[4 * group + k]
            pair = lax.shift_right_logical(sub, 1)
            before = jnp.where(pair == k, pltpu.roll(row, 2 * k, 0), before)
            after = jnp.where(pair == 3 - k, pltpu.roll(row, SUBLANES - 2 * k, 0), after)
        to_partner[group] = either(odd, before, after)
        to_outer[group] = either(odd, after, before)


def unpack_side(packed, before, height):
    tiles = []
    for group in range(height // 4):
        for k in range(4):
            ahead = pltpu.roll(packed[group], -2 * k % SUBLANES, 0)
            tiles.append(either(before, pltpu.roll(packed[group], 2 * k, 0), ahead))
    return tiles


def outer_place(radial):
    _, odd = position("lon")
    return lax.shift_right_logical(sublane(radial), 2) == 1 - odd


def unpack_sides(from_partner, from_outer, height):
    _, odd = position("lon")
    place = outer_place(from_partner.shape[2])
    pairs = zip(unpack_side(from_partner, odd, height), unpack_side(from_outer, 1 - odd, height))
    return [jnp.where(place, outer, partner) for partner, outer in pairs]


def pack_ends_kernel(field, side_0, side_1, to_partner, to_outer):
    height, _, radial = field.shape
    _, odd = position("lat")
    sub = sublane(radial)
    outside = (sub < 2) | (sub >= 6)
    tiles = unpack_sides(side_0, side_1, height)

    def ends(first):
        return (
            field[first],
            field[first + 1],
            jnp.where(outside, tiles[first], pltpu.roll(tiles[first + 1], 4, 0)),
        )

    for place, (top, bottom) in enumerate(zip(ends(0), ends(height - 2))):
        to_partner[place] = either(odd, top, bottom)
        to_outer[place] = either(odd, bottom, top)


def radial_shifts(field):
    radial = field.shape[-1]
    lane = lax.broadcasted_iota(jnp.int32, field.shape, field.ndim - 1)
    return (
        jnp.where(lane == 0, 0.0, pltpu.roll(field, 1, field.ndim - 1)),
        jnp.where(lane == radial - 1, 0.0, pltpu.roll(field, radial - 1, field.ndim - 1)),
    )


def taps_of(coef, at):
    return [jnp.broadcast_to(coef[k:k + 1, at], (SUBLANES, LANES)) for k in range(27)]


def tiles_of_bins(radial, body):
    for start in range(0, radial, LANES):
        body(slice(start, start + LANES))


ALL = (-1, 0, 1)


def first_level(wide, shifted, coef, centers, middle, real):
    _, cols, radial = wide.shape
    for row in sorted({row + above for row, around in centers for above in around}):
        for place, moved in enumerate(radial_shifts(wide[row])):
            shifted[place, row] = moved

    def body(at):
        taps = taps_of(coef, at)
        for place, (row, around) in enumerate(centers):
            parts = []
            for side in (slice(0, SUBLANES), slice(SUBLANES, cols)):
                sums = [None, None, None]
                for above in around:
                    window = (shifted[0, row + above, side, at], wide[row + above, side, at], shifted[1, row + above, side, at])
                    for beside in range(3):
                        for step in range(3):
                            term = taps[(above + 1) * 9 + beside * 3 + step] * window[step]
                            sums[beside] = term if sums[beside] is None else sums[beside] + term
                parts.append(sums)
            whole = [jnp.concatenate([parts[0][b], parts[1][b]], axis=0) for b in range(3)]
            value = whole[1] + pltpu.roll(whole[0], 1, 0) + pltpu.roll(whole[2], cols - 1, 0)
            if real[place] is not None:
                value = either(real[place], value, jnp.zeros_like(value))
            middle[0, 1, place, :, at] = pltpu.roll(value, 1, 0)[:SUBLANES]
            middle[1, 1, place, :, at] = value[:SUBLANES]
            middle[2, 1, place, :, at] = pltpu.roll(value, cols - 1, 0)[:SUBLANES]

    tiles_of_bins(radial, body)
    for place in range(len(centers)):
        for beside in range(3):
            for step, moved in zip((0, 2), radial_shifts(middle[beside, 1, place])):
                middle[beside, step, place] = moved


def second_level(coef, windows, radial, write):
    def body(at):
        taps = taps_of(coef, at)
        for row, around in windows.items():
            total = None
            for above, at_row in enumerate(around):
                if at_row is None:
                    continue
                buffer, place = at_row
                for beside in range(3):
                    for step in range(3):
                        term = taps[above * 9 + beside * 3 + step] * buffer[beside, step, place, :, at]
                        total = term if total is None else total + term
            write(row, at, total)

    tiles_of_bins(radial, body)


def fill_wide(wide, field, tiles, rows):
    width = field.shape[1]
    for row in rows:
        wide[row, :width] = field[row]
        wide[row, width:] = tiles[row]


def density_inside_kernel(field, side_0, side_1, stencils, out, middle, wide, shifted):
    height, width, radial = field.shape
    fill_wide(wide, field, unpack_sides(side_0, side_1, height), range(height))
    centers = [(row, ALL) for row in range(1, height - 1)]
    first_level(wide, shifted, stencils.at[0], centers, middle, [None] * len(centers))

    def write(row, at, value):
        out[row - 2, :, at] = jnp.exp(value)

    windows = {row: [(middle, row - 2 + k) for k in range(3)] for row in range(2, height - 2)}
    second_level(stencils.at[1], windows, radial, write)


def density_ends_kernel(
    field, side_0, side_1, end_1, end_0, stencils, inside, inner, behind, out, to_partner, to_outer, middle, wide, shifted
):
    height, width, radial = field.shape
    tiles = unpack_sides(side_0, side_1, height)
    lat, odd = position("lat")
    for place in range(3):
        partner, outer = end_0[place], end_1[place]
        for first, pack in ((0, either(odd, partner, outer)), (6, either(odd, outer, partner))):
            if place < 2:
                wide[first + place, :width] = pack
            else:
                wide[first, width:] = pack
                wide[first + 1, width:] = pltpu.roll(pack, 4, 0)
    for place, row in ((2, 0), (3, 1), (4, height - 2), (5, height - 1)):
        wide[place, :width] = field[row]
        wide[place, width:] = tiles[row]
    above = (lat > 0).astype(jnp.int32)
    below = (lat < lax.axis_size("lat") - 1).astype(jnp.int32)
    centers = [(row, ALL) for row in (1, 2, 5, 6)]
    first_level(wide, shifted, stencils.at[0], centers, middle, [above, None, None, below])

    def write(row, at, value):
        out[row, :, at] = jnp.exp(value)

    last = height - 3
    top = [(middle, 0), (middle, 1), (inside, 0), (inside, 1)]
    bottom = [(inside, last - 1), (inside, last), (middle, 2), (middle, 3)]
    windows = {0: top[:3], 1: top[1:], height - 2: bottom[:3], height - 1: bottom[1:]}
    second_level(stencils.at[1], windows, radial, write)
    for row in range(2, height - 2):
        out[row] = inner[row - 2]
    pack_sides([out[row] * behind[row] for row in range(height)], to_partner, to_outer)


def on_grid():
    lat, odd = position("lat")
    return odd, (lat > 0).astype(jnp.int32), (lat < lax.axis_size("lat") - 1).astype(jnp.int32)


def reach_of(wide, stencils, reach, middle, shifted):
    last, radial = wide.shape[0] - 1, wide.shape[2]
    _, above, below = on_grid()
    centers = [(-1, (1,)), (0, (0, 1)), (last, (-1, 0)), (last + 1, (-1,))]
    first_level(wide, shifted, stencils.at[0], centers, middle, [above, None, None, below])

    def write(row, at, value):
        reach[row, :, at] = value

    windows = {
        0: [None, None, (middle, 0)],
        1: [None, (middle, 0), (middle, 1)],
        2: [(middle, 2), (middle, 3), None],
        3: [(middle, 3), None, None],
    }
    second_level(stencils.at[1], windows, radial, write)


def reach_near_kernel(field, side_0, stencils, to_partner, reach, middle, wide, shifted):
    height, _, radial = field.shape
    _, odd_lon = position("lon")
    place = outer_place(radial)
    tiles = [jnp.where(place, 0.0, tile) for tile in unpack_side(side_0, odd_lon, height)]
    fill_wide(wide, field, tiles, (0, 1, height - 2, height - 1))
    reach_of(wide, stencils, reach, middle, shifted)
    odd, _, _ = on_grid()
    for row in range(2):
        to_partner[row] = either(odd, reach[row], reach[2 + row])


def reach_far_kernel(side_1, near, stencils, to_partner, to_outer, middle, wide, shifted, reach):
    height, cols, radial = wide.shape
    _, odd_lon = position("lon")
    place = outer_place(radial)
    tiles = unpack_side(side_1, 1 - odd_lon, height)
    for row in (0, 1, height - 2, height - 1):
        wide[row, :cols // 2] = jnp.zeros((cols // 2, radial), jnp.float32)
        wide[row, cols // 2:] = jnp.where(place, tiles[row], 0.0)
    reach_of(wide, stencils, reach, middle, shifted)
    odd, _, _ = on_grid()
    for row in range(2):
        to_partner[row] = either(odd, reach[row], reach[2 + row])
        to_outer[row] = either(odd, reach[2 + row] + near[2 + row], reach[row] + near[row])


def back_own_kernel(field, side_0, side_1, stencils, latent, end_0, out, wide, shifted, middle):
    height, _, radial = field.shape
    last = height - 1
    fill_wide(wide, field, unpack_sides(side_0, side_1, height), range(height))
    odd, above, below = on_grid()
    inner = [(row, ALL) for row in range(1, last)]
    centers = [(-1, (1,)), (0, (0, 1)), *inner, (last, (-1, 0)), (last + 1, (-1,))]
    first_level(wide, shifted, stencils.at[0], centers, middle, [above, *[None] * height, below])

    def write(row, at, value):
        out[row, :, at] = latent[row, :, at] + value

    windows = {row: [(middle, row + k) for k in range(3)] for row in range(height)}
    second_level(stencils.at[1], windows, radial, write)
    for row in range(2):
        part = end_0[row]
        none = jnp.zeros_like(part)
        out[row] += either(odd, part, none)
        out[last - 1 + row] += either(odd, none, part)


def close_kernel(own, end_1, end_0, out, top, bottom, sent):
    height = own.shape[0]
    last = height - 2
    pairs = ((own.at[2:last], out.at[2:last]), (top, out.at[:2]), (bottom, out.at[last:]))
    copies = [pltpu.make_async_copy(source, target, sent.at[i]) for i, (source, target) in enumerate(pairs)]
    copies[0].start()
    _, odd = position("lat")
    for place in range(2):
        top[place] = own[place] + either(odd, end_0[place], end_1[place])
    copies[1].start()
    for place in range(2):
        bottom[place] = own[last + place] + either(odd, end_1[place], end_0[place])
    copies[2].start()
    for copy in copies:
        copy.wait()


def open_kernel(
    counts_in, offsets_in, residual_in, pixel_in, bins_in, latent_in, out, latent, to_partner, to_outer,
    counts, offsets, residual, pixel, bins, table, arrived,
):
    pairs = (
        (counts_in, counts), (offsets_in, offsets), (residual_in, residual), (pixel_in, pixel), (bins_in, bins),
        (latent_in, latent),
    )
    copies = [pltpu.make_async_copy(source, target, arrived.at[i]) for i, (source, target) in enumerate(pairs)]
    for copy in copies:
        copy.start()
    for copy in copies[:-1]:
        copy.wait()
    height, _, radial = latent.shape
    length = residual.shape[0]
    table[pl.ds(0, length, stride=2), :] = residual[...]
    table[pl.ds(1, length, stride=2), :] = (pixel[...] * radial + bins[...]).astype(jnp.float32)

    lane = lax.broadcasted_iota(jnp.int32, (SUBLANES, LANES), 1)
    row = lax.broadcasted_iota(jnp.int32, (SUBLANES, LANES), 0)
    slot = lax.shift_right_logical(row, 1) * LANES + lane
    for owner in range(out.shape[0]):
        start = offsets[0, owner]
        first = lax.shift_right_logical(start, 7) * 2
        part = lax.bitwise_and(start, LANES - 1)
        turn = lax.bitwise_and(LANES - part, LANES - 1)
        here = pltpu.roll(table[pl.ds(first, SUBLANES), :], turn, 1)
        after = pltpu.roll(table[pl.ds(first + 2, SUBLANES), :], turn, 1)
        joined = jnp.where(lane < LANES - part, here, after)
        out[owner] = jnp.where(slot < counts[0, owner], joined, 0.0)

    copies[-1].wait()
    pack_sides([latent[row] for row in range(height)], to_partner, to_outer)


def behind_of(got, part, cuts, rows_of, *, height, width, radial):
    span = radial // cuts
    pixels = height * width // 2
    classes = cuts * pixels
    shards, rows, _ = got.shape
    bf16 = jnp.bfloat16
    column = lax.broadcasted_iota(jnp.int32, (classes, LANES), 0).astype(jnp.float32).astype(bf16)
    places = [
        (lax.broadcasted_iota(jnp.int32, (LANES, LANES), 1) + (first + 1)).astype(jnp.float32).astype(bf16)
        for first in range(0, span, LANES)
    ]
    zero = jnp.zeros((), bf16)

    def tall(kind, row):
        line = jnp.broadcast_to(rows_of[kind, row:row + 1, :], (16, LANES))
        return jnp.concatenate([line.astype(bf16)] * (classes // 16), axis=0)

    tiles = got[...].reshape(shards * rows, LANES)
    cell = tiles.astype(jnp.int32)
    pixel = lax.shift_right_logical(cell, radial.bit_length() - 1)
    bins = lax.bitwise_and(cell, radial - 1)
    cut = lax.shift_right_logical(bins, span.bit_length() - 1)
    place = lax.bitwise_and(pixel + 2, width - 1)
    own = cut * pixels + lax.shift_right_logical(pixel, 3) * 4 + lax.bitwise_and(place, 3)
    rows_of[0] = jnp.where(lax.shift_right_logical(place, 2) == part, own, classes).astype(jnp.float32)
    lows = jnp.transpose((lax.bitwise_and(bins, span - 1) + 1).astype(jnp.float32)).astype(bf16)
    coarse = tiles.astype(bf16).astype(jnp.float32)
    rows_of[1] = coarse
    rows_of[2] = tiles - coarse

    total = jnp.zeros((2 * classes, span), jnp.float32)
    for first in range(0, shards, 2):
        left, right = [], []
        for run in range(2 * RUNS):
            row = (first + run // RUNS) * rows + run % RUNS * 2
            mine = tall(0, row + 1) == column
            left.append(jnp.concatenate([jnp.where(mine, tall(kind, row), zero) for kind in (1, 2)], axis=0))
            low = jnp.broadcast_to(lows[:, row + 1:row + 2], (LANES, LANES))
            right.append(jnp.concatenate([jnp.maximum(low, place) for place in places], axis=1))
        total = total + jnp.dot(
            jnp.concatenate(left, axis=1), jnp.concatenate(right, axis=0), preferred_element_type=jnp.float32
        )
    both = (total[:classes] + total[classes:]) * bin_width
    every = both[:, span - 1:] * (1.0 / span)
    lane = lax.broadcasted_iota(jnp.int32, both.shape, 1)
    at_least = jnp.where(lane == 0, every, pltpu.roll(both, 1, 1) - both + every)
    ranges = [at_least[start:start + pixels] for start in range(0, classes, pixels)]
    for k in reversed(range(cuts - 1)):
        ranges[k] = ranges[k] + ranges[k + 1][:, :1]
    return jnp.concatenate(ranges, axis=1)


def column_rows(packed, part, height):
    rows = []
    for row in range(height):
        tile = packed[row // 2 * SUBLANES:(row // 2 + 1) * SUBLANES]
        turn = row % 2 * 4 + (2 if part == 0 else SUBLANES - 2)
        rows.append(pltpu.roll(tile, (SUBLANES - turn) % SUBLANES, 0))
    return rows


def bin_sides_kernel(got, _, behind, rows_of):
    height, width, radial = behind.shape
    packed = behind_of(got, 0, 2, rows_of, height=height, width=width, radial=radial)
    for row, values in enumerate(column_rows(packed, 0, height)):
        behind[row] = values


def bin_rest_kernel(got, density, behind, upstream, rows_of):
    height, width, radial = behind.shape
    sub = sublane(radial)
    packed = behind_of(got, 1, 2, rows_of, height=height, width=width, radial=radial)
    for row, values in enumerate(column_rows(packed, 1, height)):
        upstream[row] = density[row] * jnp.where((sub < 2) | (sub >= 6), behind[row], values)


def mirror(stencils):
    turned = jnp.flip(stencils, axis=1).reshape(stencils.shape[0], 9, 3, stencils.shape[2])
    edge = jnp.zeros_like(turned[:, :, 0, :1])
    back = jnp.concatenate([edge, turned[:, :, 0, :-1]], axis=-1)
    ahead = jnp.concatenate([turned[:, :, 2, 1:], edge], axis=-1)
    return jnp.stack([back, turned[:, :, 1], ahead], axis=2).reshape(stencils.shape)


def pairwise(values, axis, closed, outer):
    count = lax.axis_size(axis)
    pairs = [(i, (i + 1) % count) for i in range(int(outer), count, 2) if closed or i + 1 < count]
    return lax.ppermute(values, axis, pairs + [(j, i) for i, j in pairs])


def swap(to_partner, to_outer, axis, closed, outer_first=False):
    if outer_first:
        from_outer = pairwise(to_outer, axis, closed, True)
        return pairwise(to_partner, axis, closed, False), from_outer
    from_partner = pairwise(to_partner, axis, closed, False)
    return from_partner, pairwise(to_outer, axis, closed, True)


VMEM = pl.BlockSpec(memory_space=pltpu.VMEM)
HBM = pl.BlockSpec(memory_space=pltpu.HBM)
LIMIT = pltpu.CompilerParams(vmem_limit_bytes=32 * 1024 * 1024)


def on_device(residual, star_pixel, star_bin, send_counts, send_offsets, latent, stencils):
    height, width, radial = latent.shape
    shards = send_counts.shape[1]
    slots = residual.shape[0]
    f32 = jnp.float32
    i32 = jnp.int32
    tile = jax.ShapeDtypeStruct((height, width, radial), f32)
    sides = jax.ShapeDtypeStruct((height // 4, SUBLANES, radial), f32)
    ends = jax.ShapeDtypeStruct((3, SUBLANES, radial), f32)

    def table(values):
        return values.reshape(slots // LANES, LANES)

    packed, latent, *to_sides = pl.pallas_call(
        open_kernel,
        out_shape=(jax.ShapeDtypeStruct((shards, 2 * RUNS, LANES), f32), tile, sides, sides),
        in_specs=[HBM] * 6,
        out_specs=(VMEM, VMEM, VMEM, VMEM),
        scratch_shapes=[pltpu.SMEM((1, shards), i32)] * 2
        + [pltpu.VMEM((slots // LANES, LANES), kind) for kind in (f32, i32, i32)]
        + [pltpu.VMEM((2 * slots // LANES, LANES), f32)]
        + [pltpu.SemaphoreType.DMA((6,))],
        compiler_params=LIMIT,
        name="opening",
    )(*[
        pltpu.with_memory_space_constraint(values, pltpu.HBM)
        for values in (send_counts, send_offsets, table(residual), table(star_pixel), table(star_bin), latent)
    ])
    got = lax.all_to_all(packed, ("lat", "lon"), split_axis=0, concat_axis=0, tiled=True)

    rows = pltpu.VMEM((height, 2 * width, radial), f32)
    moved = pltpu.VMEM((2, height, 2 * width, radial), f32)
    edge = (3, 3, 4, width, radial)
    star_rows = pltpu.VMEM((3, shards * 2 * RUNS, LANES), f32)
    inner_rows = (3, 3, height - 2, width, radial)

    def call(kernel, name, outs, scratch, *operands):
        return pl.pallas_call(
            kernel,
            out_shape=outs,
            in_specs=[VMEM] * len(operands),
            out_specs=jax.tree.map(lambda _: VMEM, outs),
            scratch_shapes=scratch,
            compiler_params=LIMIT,
            name=name,
        )(*operands)

    def shape(*sizes):
        return jax.ShapeDtypeStruct(sizes, f32)

    beside = swap(*to_sides, "lon", True)
    to_ends = call(pack_ends_kernel, "density_pack", (ends, ends), [], latent, *beside)
    above = swap(*to_ends, "lat", False, outer_first=True)
    inner, middle = call(
        density_inside_kernel, "density_inside", (shape(height - 4, width, radial), shape(*inner_rows)), [rows, moved],
        latent, *beside, stencils,
    )
    behind = call(bin_sides_kernel, "bin_sides", tile, [star_rows], got, inner)
    density, *to_sides = call(
        density_ends_kernel, "density_ends", (tile, sides, sides), [pltpu.VMEM(edge, f32), rows, moved],
        latent, *beside, *above[::-1], stencils, middle, inner, behind,
    )
    upstream = call(bin_rest_kernel, "bin_rest", tile, [star_rows], got, density, behind)

    mirrored = mirror(stencils)[::-1]
    from_partner, from_outer = swap(*to_sides, "lon", True, outer_first=True)
    pair = shape(2, width, radial)
    quad = (4, width, radial)
    near_part, near = call(
        reach_near_kernel, "reach_near", (pair, shape(*quad)), [pltpu.VMEM(edge, f32), rows, moved],
        upstream, from_partner, mirrored,
    )
    first_end = pairwise(near_part, "lat", False, False)
    far_part, to_outer = call(
        reach_far_kernel, "reach_far", (pair, pair), [pltpu.VMEM(edge, f32), rows, moved, pltpu.VMEM(quad, f32)],
        from_outer, near, mirrored,
    )
    last_ends = pairwise(to_outer, "lat", False, True), pairwise(far_part, "lat", False, False)
    own = call(
        back_own_kernel, "back_own", tile, [rows, moved, pltpu.VMEM((3, 3, height + 2, width, radial), f32)],
        upstream, from_partner, from_outer, mirrored, latent, first_end,
    )
    return pl.pallas_call(
        close_kernel,
        out_shape=tile,
        in_specs=[VMEM] * 3,
        out_specs=HBM,
        scratch_shapes=[pltpu.VMEM((2, width, radial), f32)] * 2 + [pltpu.SemaphoreType.DMA((3,))],
        compiler_params=LIMIT,
        name="close",
    )(own, *last_ends)


def solution(mesh):
    return jax.shard_map(
        on_device,
        mesh=mesh,
        in_specs=(
            P(("lat", "lon")),
            P(("lat", "lon")),
            P(("lat", "lon")),
            P(("lat", "lon"), None),
            P(("lat", "lon"), None),
            P("lat", "lon", None),
            P(),
        ),
        out_specs=P("lat", "lon", None),
        check_vma=False,
    )
```

```python
import functools

import jax
import jax.numpy as jnp
from jax import lax
from jax.experimental import pallas as pl
from jax.experimental.pallas import tpu as pltpu
from jax.sharding import PartitionSpec as P

CAP = 512
LEAST = 128
LANES = 128
SUBLANES = 8
RUNS = CAP // LANES
bin_width = 0.0625


def position(axis):
    index = lax.axis_index(axis)
    return index, lax.bitwise_and(index, 1)


def either(flag, if_set, if_clear):
    return jnp.where(jnp.full(if_set.shape, flag, jnp.int32) > 0, if_set, if_clear)


def sublane(radial):
    return lax.broadcasted_iota(jnp.int32, (SUBLANES, radial), 0)


def pack_sides(rows, to_partner, to_outer):
    _, odd = position("lon")
    sub = sublane(rows[0].shape[1])
    for group in range(len(rows) // 4):
        before, after = rows[4 * group], rows[4 * group]
        for k in range(1, 4):
            row = rows[4 * group + k]
            pair = lax.shift_right_logical(sub, 1)
            before = jnp.where(pair == k, pltpu.roll(row, 2 * k, 0), before)
            after = jnp.where(pair == 3 - k, pltpu.roll(row, SUBLANES - 2 * k, 0), after)
        to_partner[group] = either(odd, before, after)
        to_outer[group] = either(odd, after, before)


def unpack_sides(from_partner, from_outer, height):
    _, odd = position("lon")
    sub = sublane(from_partner.shape[2])
    tiles = []
    for group in range(height // 4):
        partner, outer = from_partner[group], from_outer[group]
        before, after = either(odd, partner, outer), either(odd, outer, partner)
        for k in range(4):
            if k:
                tiles.append(jnp.where(sub < 4, pltpu.roll(after, SUBLANES - 2 * k, 0), pltpu.roll(before, 2 * k, 0)))
            else:
                tiles.append(jnp.where(sub < 4, after, before))
    return tiles


def pack_ends_kernel(field, side_0, side_1, to_partner, to_outer):
    height, _, radial = field.shape
    _, odd = position("lat")
    sub = sublane(radial)
    outside = (sub < 2) | (sub >= 6)
    tiles = unpack_sides(side_0, side_1, height)

    def ends(first):
        return (
            field[first],
            field[first + 1],
            jnp.where(outside, tiles[first], pltpu.roll(tiles[first + 1], 4, 0)),
        )

    for place, (top, bottom) in enumerate(zip(ends(0), ends(height - 2))):
        to_partner[place] = either(odd, top, bottom)
        to_outer[place] = either(odd, bottom, top)


def radial_shifts(field):
    radial = field.shape[-1]
    lane = lax.broadcasted_iota(jnp.int32, field.shape, field.ndim - 1)
    return (
        jnp.where(lane == 0, 0.0, pltpu.roll(field, 1, field.ndim - 1)),
        jnp.where(lane == radial - 1, 0.0, pltpu.roll(field, radial - 1, field.ndim - 1)),
    )


def taps_of(coef, at):
    return [jnp.broadcast_to(coef[k:k + 1, at], (SUBLANES, LANES)) for k in range(27)]


def tiles_of_bins(radial, body):
    for start in range(0, radial, LANES):
        body(slice(start, start + LANES))


ALL = (-1, 0, 1)


def first_level(wide, shifted, coef, centers, middle, real):
    _, cols, radial = wide.shape
    for row in sorted({row + above for row, around in centers for above in around}):
        for place, moved in enumerate(radial_shifts(wide[row])):
            shifted[place, row] = moved

    def body(at):
        taps = taps_of(coef, at)
        for place, (row, around) in enumerate(centers):
            parts = []
            for side in (slice(0, SUBLANES), slice(SUBLANES, cols)):
                sums = [None, None, None]
                for above in around:
                    window = (shifted[0, row + above, side, at], wide[row + above, side, at], shifted[1, row + above, side, at])
                    for beside in range(3):
                        for step in range(3):
                            term = taps[(above + 1) * 9 + beside * 3 + step] * window[step]
                            sums[beside] = term if sums[beside] is None else sums[beside] + term
                parts.append(sums)
            whole = [jnp.concatenate([parts[0][b], parts[1][b]], axis=0) for b in range(3)]
            value = whole[1] + pltpu.roll(whole[0], 1, 0) + pltpu.roll(whole[2], cols - 1, 0)
            if real[place] is not None:
                value = either(real[place], value, jnp.zeros_like(value))
            middle[0, 1, place, :, at] = pltpu.roll(value, 1, 0)[:SUBLANES]
            middle[1, 1, place, :, at] = value[:SUBLANES]
            middle[2, 1, place, :, at] = pltpu.roll(value, cols - 1, 0)[:SUBLANES]

    tiles_of_bins(radial, body)
    for place in range(len(centers)):
        for beside in range(3):
            for step, moved in zip((0, 2), radial_shifts(middle[beside, 1, place])):
                middle[beside, step, place] = moved


def second_level(coef, windows, radial, write):
    def body(at):
        taps = taps_of(coef, at)
        for row, around in windows.items():
            total = None
            for above, at_row in enumerate(around):
                if at_row is None:
                    continue
                buffer, place = at_row
                for beside in range(3):
                    for step in range(3):
                        term = taps[above * 9 + beside * 3 + step] * buffer[beside, step, place, :, at]
                        total = term if total is None else total + term
            write(row, at, total)

    tiles_of_bins(radial, body)


def fill_wide(wide, field, side_0, side_1, rows):
    height, width, _ = field.shape
    tiles = unpack_sides(side_0, side_1, height)
    for row in rows:
        wide[row, :width] = field[row]
        wide[row, width:] = tiles[row]


def density_inside_kernel(field, side_0, side_1, stencils, out, middle, wide, shifted):
    height, width, radial = field.shape
    fill_wide(wide, field, side_0, side_1, range(height))
    centers = [(row, ALL) for row in range(1, height - 1)]
    first_level(wide, shifted, stencils.at[0], centers, middle, [None] * len(centers))

    def write(row, at, value):
        out[row - 2, :, at] = jnp.exp(value)

    windows = {row: [(middle, row - 2 + k) for k in range(3)] for row in range(2, height - 2)}
    second_level(stencils.at[1], windows, radial, write)


def density_ends_kernel(
    field, side_0, side_1, end_1, end_0, stencils, inside, inner, behind, out, to_partner, to_outer, middle, wide, shifted
):
    height, width, radial = field.shape
    tiles = unpack_sides(side_0, side_1, height)
    lat, odd = position("lat")
    for place in range(3):
        partner, outer = end_0[place], end_1[place]
        for first, pack in ((0, either(odd, partner, outer)), (6, either(odd, outer, partner))):
            if place < 2:
                wide[first + place, :width] = pack
            else:
                wide[first, width:] = pack
                wide[first + 1, width:] = pltpu.roll(pack, 4, 0)
    for place, row in ((2, 0), (3, 1), (4, height - 2), (5, height - 1)):
        wide[place, :width] = field[row]
        wide[place, width:] = tiles[row]
    above = (lat > 0).astype(jnp.int32)
    below = (lat < lax.axis_size("lat") - 1).astype(jnp.int32)
    centers = [(row, ALL) for row in (1, 2, 5, 6)]
    first_level(wide, shifted, stencils.at[0], centers, middle, [above, None, None, below])

    def write(row, at, value):
        out[row, :, at] = jnp.exp(value)

    last = height - 3
    top = [(middle, 0), (middle, 1), (inside, 0), (inside, 1)]
    bottom = [(inside, last - 1), (inside, last), (middle, 2), (middle, 3)]
    windows = {0: top[:3], 1: top[1:], height - 2: bottom[:3], height - 1: bottom[1:]}
    second_level(stencils.at[1], windows, radial, write)
    for row in range(2, height - 2):
        out[row] = inner[row - 2]
    pack_sides([out[row] * behind[row] for row in range(height)], to_partner, to_outer)


def back_reach_kernel(field, side_1, side_0, stencils, to_partner, to_outer, middle, wide, shifted, reach):
    height, _, radial = field.shape
    last = height - 1
    fill_wide(wide, field, side_0, side_1, (0, 1, last - 1, last))
    lat, odd = position("lat")
    above = (lat > 0).astype(jnp.int32)
    below = (lat < lax.axis_size("lat") - 1).astype(jnp.int32)
    centers = [(-1, (1,)), (0, (0, 1)), (last, (-1, 0)), (last + 1, (-1,))]
    first_level(wide, shifted, stencils.at[0], centers, middle, [above, None, None, below])

    def write(row, at, value):
        reach[row, :, at] = value

    windows = {
        0: [None, None, (middle, 0)],
        1: [None, (middle, 0), (middle, 1)],
        2: [(middle, 2), (middle, 3), None],
        3: [(middle, 3), None, None],
    }
    second_level(stencils.at[1], windows, radial, write)
    for place in range(2):
        to_partner[place] = either(odd, reach[place], reach[2 + place])
        to_outer[place] = either(odd, reach[2 + place], reach[place])


def back_own_kernel(field, side_1, side_0, stencils, latent, edge, out, wide, shifted, middle):
    height, _, radial = field.shape
    fill_wide(wide, field, side_0, side_1, range(height))
    centers = [(row, ALL) for row in range(1, height - 1)]
    first_level(wide, shifted, stencils.at[0], centers, middle, [None] * len(centers))

    def write(row, at, value):
        out[row, :, at] = latent[row, :, at] + value

    line = [(edge, 0), (edge, 1)] + [(middle, place) for place in range(height - 2)] + [(edge, 2), (edge, 3)]
    second_level(stencils.at[1], {row: line[row:row + 3] for row in range(height)}, radial, write)


def close_kernel(own, end_0, end_1, out, top, bottom, sent):
    height = own.shape[0]
    last = height - 2
    pairs = ((own.at[2:last], out.at[2:last]), (top, out.at[:2]), (bottom, out.at[last:]))
    copies = [pltpu.make_async_copy(source, target, sent.at[i]) for i, (source, target) in enumerate(pairs)]
    copies[0].start()
    _, odd = position("lat")
    for place in range(2):
        top[place] = own[place] + either(odd, end_0[place], end_1[place])
    copies[1].start()
    for place in range(2):
        bottom[place] = own[last + place] + either(odd, end_1[place], end_0[place])
    copies[2].start()
    for copy in copies:
        copy.wait()


def open_kernel(
    counts_in, offsets_in, residual_in, pixel_in, bins_in, latent_in, out, latent, to_partner, to_outer,
    counts, offsets, residual, pixel, bins, table, arrived,
):
    pairs = (
        (counts_in, counts), (offsets_in, offsets), (residual_in, residual), (pixel_in, pixel), (bins_in, bins),
        (latent_in, latent),
    )
    copies = [pltpu.make_async_copy(source, target, arrived.at[i]) for i, (source, target) in enumerate(pairs)]
    for copy in copies:
        copy.start()
    for copy in copies[:-1]:
        copy.wait()
    height, _, radial = latent.shape
    length = residual.shape[0]
    table[pl.ds(0, length, stride=2), :] = residual[...]
    table[pl.ds(1, length, stride=2), :] = (pixel[...] * radial + bins[...]).astype(jnp.float32)

    lane = lax.broadcasted_iota(jnp.int32, (SUBLANES, LANES), 1)
    row = lax.broadcasted_iota(jnp.int32, (SUBLANES, LANES), 0)
    slot = lax.shift_right_logical(row, 1) * LANES + lane
    for owner in range(out.shape[0]):
        start = offsets[0, owner]
        first = lax.shift_right_logical(start, 7) * 2
        part = lax.bitwise_and(start, LANES - 1)
        turn = lax.bitwise_and(LANES - part, LANES - 1)
        here = pltpu.roll(table[pl.ds(first, SUBLANES), :], turn, 1)
        after = pltpu.roll(table[pl.ds(first + 2, SUBLANES), :], turn, 1)
        joined = jnp.where(lane < LANES - part, here, after)
        out[owner] = jnp.where(slot < counts[0, owner], joined, 0.0)

    copies[-1].wait()
    pack_sides([latent[row] for row in range(height)], to_partner, to_outer)


def behind_of(got, part, cuts, runs, rows_of, *, height, width, radial):
    span = radial // cuts
    pixels = height * width // 2
    classes = cuts * pixels
    shards, rows, _ = got.shape
    bf16 = jnp.bfloat16
    column = lax.broadcasted_iota(jnp.int32, (classes, LANES), 0).astype(jnp.float32).astype(bf16)
    places = [
        (lax.broadcasted_iota(jnp.int32, (LANES, LANES), 1) + (first + 1)).astype(jnp.float32).astype(bf16)
        for first in range(0, span, LANES)
    ]
    zero = jnp.zeros((), bf16)

    def tall(kind, row):
        line = jnp.broadcast_to(rows_of[kind, row:row + 1, :], (16, LANES))
        return jnp.concatenate([line.astype(bf16)] * (classes // 16), axis=0)

    tiles = got[...].reshape(shards * rows, LANES)
    cell = tiles.astype(jnp.int32)
    pixel = lax.shift_right_logical(cell, radial.bit_length() - 1)
    bins = lax.bitwise_and(cell, radial - 1)
    cut = lax.shift_right_logical(bins, span.bit_length() - 1)
    place = lax.bitwise_and(pixel + 2, width - 1)
    own = cut * pixels + lax.shift_right_logical(pixel, 3) * 4 + lax.bitwise_and(place, 3)
    rows_of[0] = jnp.where(lax.shift_right_logical(place, 2) == part, own, classes).astype(jnp.float32)
    lows = jnp.transpose((lax.bitwise_and(bins, span - 1) + 1).astype(jnp.float32)).astype(bf16)
    coarse = tiles.astype(bf16).astype(jnp.float32)
    rows_of[1] = coarse
    rows_of[2] = tiles - coarse

    total = jnp.zeros((2 * classes, span), jnp.float32)
    group = 2 * RUNS // runs
    for first in range(0, shards, group):
        left, right = [], []
        for run in range(group * runs):
            row = (first + run // runs) * rows + run % runs * 2
            mine = tall(0, row + 1) == column
            left.append(jnp.concatenate([jnp.where(mine, tall(kind, row), zero) for kind in (1, 2)], axis=0))
            low = jnp.broadcast_to(lows[:, row + 1:row + 2], (LANES, LANES))
            right.append(jnp.concatenate([jnp.maximum(low, place) for place in places], axis=1))
        total = total + jnp.dot(
            jnp.concatenate(left, axis=1), jnp.concatenate(right, axis=0), preferred_element_type=jnp.float32
        )
    both = (total[:classes] + total[classes:]) * bin_width
    every = both[:, span - 1:] * (1.0 / span)
    lane = lax.broadcasted_iota(jnp.int32, both.shape, 1)
    at_least = jnp.where(lane == 0, every, pltpu.roll(both, 1, 1) - both + every)
    ranges = [at_least[start:start + pixels] for start in range(0, classes, pixels)]
    for k in reversed(range(cuts - 1)):
        ranges[k] = ranges[k] + ranges[k + 1][:, :1]
    return jnp.concatenate(ranges, axis=1)


def column_rows(packed, part, height):
    rows = []
    for row in range(height):
        tile = packed[row // 2 * SUBLANES:(row // 2 + 1) * SUBLANES]
        turn = row % 2 * 4 + (2 if part == 0 else SUBLANES - 2)
        rows.append(pltpu.roll(tile, (SUBLANES - turn) % SUBLANES, 0))
    return rows


def for_load(body):
    lat, count = lax.axis_index("lat"), lax.axis_size("lat")
    middle = (lat >= count // 4) & (lat < count - count // 4)
    pl.when(middle)(lambda: body(RUNS))
    pl.when(jnp.logical_not(middle))(lambda: body(LEAST // LANES))


def bin_sides_kernel(got, _, behind, rows_of):
    height, width, radial = behind.shape

    def body(runs):
        packed = behind_of(got, 0, 2, runs, rows_of, height=height, width=width, radial=radial)
        for row, values in enumerate(column_rows(packed, 0, height)):
            behind[row] = values

    for_load(body)


def bin_rest_kernel(got, density, behind, upstream, rows_of):
    height, width, radial = behind.shape
    sub = sublane(radial)

    def body(runs):
        packed = behind_of(got, 1, 2, runs, rows_of, height=height, width=width, radial=radial)
        for row, values in enumerate(column_rows(packed, 1, height)):
            upstream[row] = density[row] * jnp.where((sub < 2) | (sub >= 6), behind[row], values)

    for_load(body)


def mirror(stencils):
    turned = jnp.flip(stencils, axis=1).reshape(stencils.shape[0], 9, 3, stencils.shape[2])
    edge = jnp.zeros_like(turned[:, :, 0, :1])
    back = jnp.concatenate([edge, turned[:, :, 0, :-1]], axis=-1)
    ahead = jnp.concatenate([turned[:, :, 2, 1:], edge], axis=-1)
    return jnp.stack([back, turned[:, :, 1], ahead], axis=2).reshape(stencils.shape)


def swap(to_partner, to_outer, axis, closed, outer_first=False):
    count = lax.axis_size(axis)
    outer = [(i, (i + 1) % count) for i in range(1, count, 2) if closed or i + 1 < count]
    inner = [(i, i + 1) for i in range(0, count - 1, 2)]

    def both_ways(pairs):
        return pairs + [(j, i) for i, j in pairs]

    moves = [(to_partner, inner), (to_outer, outer)]
    got = [lax.ppermute(values, axis, both_ways(pairs)) for values, pairs in moves[::-1 if outer_first else 1]]
    return tuple(got[::-1 if outer_first else 1])


VMEM = pl.BlockSpec(memory_space=pltpu.VMEM)
HBM = pl.BlockSpec(memory_space=pltpu.HBM)
LIMIT = pltpu.CompilerParams(vmem_limit_bytes=32 * 1024 * 1024)


def on_device(residual, star_pixel, star_bin, send_counts, send_offsets, latent, stencils):
    height, width, radial = latent.shape
    shards = send_counts.shape[1]
    slots = residual.shape[0]
    f32 = jnp.float32
    i32 = jnp.int32
    tile = jax.ShapeDtypeStruct((height, width, radial), f32)
    sides = jax.ShapeDtypeStruct((height // 4, SUBLANES, radial), f32)
    ends = jax.ShapeDtypeStruct((3, SUBLANES, radial), f32)

    def table(values):
        return values.reshape(slots // LANES, LANES)

    packed, latent, *to_sides = pl.pallas_call(
        open_kernel,
        out_shape=(jax.ShapeDtypeStruct((shards, 2 * RUNS, LANES), f32), tile, sides, sides),
        in_specs=[HBM] * 6,
        out_specs=(VMEM, VMEM, VMEM, VMEM),
        scratch_shapes=[pltpu.SMEM((1, shards), i32)] * 2
        + [pltpu.VMEM((slots // LANES, LANES), kind) for kind in (f32, i32, i32)]
        + [pltpu.VMEM((2 * slots // LANES, LANES), f32)]
        + [pltpu.SemaphoreType.DMA((6,))],
        compiler_params=LIMIT,
        name="opening",
    )(*[
        pltpu.with_memory_space_constraint(values, pltpu.HBM)
        for values in (send_counts, send_offsets, table(residual), table(star_pixel), table(star_bin), latent)
    ])
    got = lax.all_to_all(packed, ("lat", "lon"), split_axis=0, concat_axis=0, tiled=True)

    rows = pltpu.VMEM((height, 2 * width, radial), f32)
    moved = pltpu.VMEM((2, height, 2 * width, radial), f32)
    edge = (3, 3, 4, width, radial)
    star_rows = pltpu.VMEM((3, shards * 2 * RUNS, LANES), f32)
    inner_rows = (3, 3, height - 2, width, radial)

    def call(kernel, name, outs, scratch, *operands):
        return pl.pallas_call(
            kernel,
            out_shape=outs,
            in_specs=[VMEM] * len(operands),
            out_specs=jax.tree.map(lambda _: VMEM, outs),
            scratch_shapes=scratch,
            compiler_params=LIMIT,
            name=name,
        )(*operands)

    def shape(*sizes):
        return jax.ShapeDtypeStruct(sizes, f32)

    beside = swap(*to_sides, "lon", True)
    to_ends = call(pack_ends_kernel, "density_pack", (ends, ends), [], latent, *beside)
    above = swap(*to_ends, "lat", False, outer_first=True)
    inner, middle = call(
        density_inside_kernel, "density_inside", (shape(height - 4, width, radial), shape(*inner_rows)), [rows, moved],
        latent, *beside, stencils,
    )
    behind = call(bin_sides_kernel, "bin_sides", tile, [star_rows], got, inner)
    density, *to_sides = call(
        density_ends_kernel, "density_ends", (tile, sides, sides), [pltpu.VMEM(edge, f32), rows, moved],
        latent, *beside, *above[::-1], stencils, middle, inner, behind,
    )
    upstream = call(bin_rest_kernel, "bin_rest", tile, [star_rows], got, density, behind)

    mirrored = mirror(stencils)[::-1]
    beside = swap(*to_sides, "lon", True, outer_first=True)
    *to_ends, middle = call(
        back_reach_kernel, "back_reach", (shape(2, width, radial), shape(2, width, radial), shape(*edge)),
        [rows, moved, pltpu.VMEM((4, width, radial), f32)], upstream, *beside[::-1], mirrored,
    )
    above = swap(*to_ends, "lat", False)
    own = call(
        back_own_kernel, "back_own", tile, [rows, moved, pltpu.VMEM(inner_rows, f32)],
        upstream, *beside[::-1], mirrored, latent, middle,
    )
    return pl.pallas_call(
        close_kernel,
        out_shape=tile,
        in_specs=[VMEM] * 3,
        out_specs=HBM,
        scratch_shapes=[pltpu.VMEM((2, width, radial), f32)] * 2 + [pltpu.SemaphoreType.DMA((3,))],
        compiler_params=LIMIT,
        name="close",
    )(own, *above)


def solution(mesh):
    return jax.shard_map(
        on_device,
        mesh=mesh,
        in_specs=(
            P(("lat", "lon")),
            P(("lat", "lon")),
            P(("lat", "lon")),
            P(("lat", "lon"), None),
            P(("lat", "lon"), None),
            P("lat", "lon", None),
            P(),
        ),
        out_specs=P("lat", "lon", None),
        check_vma=False,
    )
```

```python
import functools

import jax
import jax.numpy as jnp
from jax import lax
from jax.experimental import pallas as pl
from jax.experimental.pallas import tpu as pltpu
from jax.sharding import PartitionSpec as P

CAP = 512
LEAST = 128
LANES = 128
SUBLANES = 8
RUNS = CAP // LANES
bin_width = 0.0625


def position(axis):
    index = lax.axis_index(axis)
    return index, lax.bitwise_and(index, 1)


def either(flag, if_set, if_clear):
    return jnp.where(jnp.full(if_set.shape, flag, jnp.int32) > 0, if_set, if_clear)


def sublane(radial):
    return lax.broadcasted_iota(jnp.int32, (SUBLANES, radial), 0)


def pack_sides(rows, to_partner, to_outer):
    _, odd = position("lon")
    sub = sublane(rows[0].shape[1])
    for group in range(len(rows) // 4):
        before, after = rows[4 * group], rows[4 * group]
        for k in range(1, 4):
            row = rows[4 * group + k]
            pair = lax.shift_right_logical(sub, 1)
            before = jnp.where(pair == k, pltpu.roll(row, 2 * k, 0), before)
            after = jnp.where(pair == 3 - k, pltpu.roll(row, SUBLANES - 2 * k, 0), after)
        to_partner[group] = either(odd, before, after)
        to_outer[group] = either(odd, after, before)


def unpack_sides(from_partner, from_outer, height):
    _, odd = position("lon")
    sub = sublane(from_partner.shape[2])
    tiles = []
    for group in range(height // 4):
        partner, outer = from_partner[group], from_outer[group]
        before, after = either(odd, partner, outer), either(odd, outer, partner)
        for k in range(4):
            if k:
                tiles.append(jnp.where(sub < 4, pltpu.roll(after, SUBLANES - 2 * k, 0), pltpu.roll(before, 2 * k, 0)))
            else:
                tiles.append(jnp.where(sub < 4, after, before))
    return tiles


def pack_four(rows, to_partner, to_outer):
    _, odd = position("lon")
    sub = sublane(rows[0].shape[1])
    for group in range(len(rows) // 2):
        one, two = rows[2 * group], pltpu.roll(rows[2 * group + 1], 4, 0)
        before, after = jnp.where(sub < 4, one, two), jnp.where(sub < 4, two, one)
        to_partner[group] = either(odd, before, after)
        to_outer[group] = either(odd, after, before)


def unpack_four(from_partner, from_outer, height):
    _, odd = position("lon")
    sub = sublane(from_partner.shape[2])
    tiles = []
    for group in range(height // 2):
        partner, outer = from_partner[group], from_outer[group]
        before, after = either(odd, partner, outer), either(odd, outer, partner)
        tiles.append(jnp.where(sub < 4, after, before))
        tiles.append(pltpu.roll(jnp.where(sub < 4, before, after), 4, 0))
    return tiles


def pack_ends_kernel(field, side_0, side_1, to_partner, to_outer):
    height = field.shape[0]
    _, odd = position("lat")
    tiles = unpack_four(side_0, side_1, height)
    top = [field[0], field[1], tiles[0], tiles[1]]
    bottom = [field[height - 2], field[height - 1], tiles[height - 2], tiles[height - 1]]
    for place, (one, two) in enumerate(zip(top, bottom)):
        to_partner[place] = either(odd, one, two)
        to_outer[place] = either(odd, two, one)


def radial_shifts(field):
    radial = field.shape[-1]
    lane = lax.broadcasted_iota(jnp.int32, field.shape, field.ndim - 1)
    return (
        jnp.where(lane == 0, 0.0, pltpu.roll(field, 1, field.ndim - 1)),
        jnp.where(lane == radial - 1, 0.0, pltpu.roll(field, radial - 1, field.ndim - 1)),
    )


def taps_of(coef, at):
    return [jnp.broadcast_to(coef[k:k + 1, at], (SUBLANES, LANES)) for k in range(27)]


def tiles_of_bins(radial, body):
    for start in range(0, radial, LANES):
        body(slice(start, start + LANES))


ALL = (-1, 0, 1)


def first_level(wide, shifted, coef, centers, middle, real):
    _, cols, radial = wide.shape
    for row in sorted({row + above for row, around in centers for above in around}):
        for place, moved in enumerate(radial_shifts(wide[row])):
            shifted[place, row] = moved

    def body(at):
        taps = taps_of(coef, at)
        for place, (row, around) in enumerate(centers):
            parts = []
            for side in (slice(0, SUBLANES), slice(SUBLANES, cols)):
                sums = [None, None, None]
                for above in around:
                    window = (shifted[0, row + above, side, at], wide[row + above, side, at], shifted[1, row + above, side, at])
                    for beside in range(3):
                        for step in range(3):
                            term = taps[(above + 1) * 9 + beside * 3 + step] * window[step]
                            sums[beside] = term if sums[beside] is None else sums[beside] + term
                parts.append(sums)
            whole = [jnp.concatenate([parts[0][b], parts[1][b]], axis=0) for b in range(3)]
            value = whole[1] + pltpu.roll(whole[0], 1, 0) + pltpu.roll(whole[2], cols - 1, 0)
            if real[place] is not None:
                value = either(real[place], value, jnp.zeros_like(value))
            kept = middle.shape[3]
            middle[0, 1, place, :, at] = pltpu.roll(value, 1, 0)[:kept]
            middle[1, 1, place, :, at] = value[:kept]
            middle[2, 1, place, :, at] = pltpu.roll(value, cols - 1, 0)[:kept]

    tiles_of_bins(radial, body)
    for place in range(len(centers)):
        for beside in range(3):
            for step, moved in zip((0, 2), radial_shifts(middle[beside, 1, place])):
                middle[beside, step, place] = moved


def second_level(coef, windows, radial, write, cols=SUBLANES):
    def body(at):
        taps = taps_of(coef, at)
        for row, around in windows.items():
            for start in range(0, cols, SUBLANES):
                side = slice(start, start + SUBLANES)
                total = None
                for above, at_row in enumerate(around):
                    if at_row is None:
                        continue
                    buffer, place = at_row
                    for beside in range(3):
                        for step in range(3):
                            term = taps[above * 9 + beside * 3 + step] * buffer[beside, step, place, side, at]
                            total = term if total is None else total + term
                write(row, side, at, total)

    tiles_of_bins(radial, body)


def fill_wide(wide, field, tiles, rows):
    width = field.shape[1]
    for row in rows:
        wide[row, :width] = field[row]
        wide[row, width:] = tiles[row]


def density_inside_kernel(field, side_0, side_1, stencils, out, middle, wide, shifted):
    height, _, radial = field.shape
    fill_wide(wide, field, unpack_four(side_0, side_1, height), range(height))
    centers = [(row, ALL) for row in range(1, height - 1)]
    first_level(wide, shifted, stencils.at[0], centers, middle, [None] * len(centers))

    def write(row, side, at, value):
        out[row - 2, side, at] = jnp.exp(value)

    windows = {row: [(middle, row - 2 + k) for k in range(3)] for row in range(2, height - 2)}
    second_level(stencils.at[1], windows, radial, write, wide.shape[1])


def density_ends_kernel(
    field, side_0, side_1, end_1, end_0, stencils, inside, inner, _, out, middle, wide, shifted
):
    height, width, radial = field.shape
    tiles = unpack_four(side_0, side_1, height)
    lat, odd = position("lat")
    for place in range(2):
        for half in range(2):
            partner, outer = end_0[2 * half + place], end_1[2 * half + place]
            at = slice(half * width, (half + 1) * width)
            wide[place, at] = either(odd, partner, outer)
            wide[6 + place, at] = either(odd, outer, partner)
    for place, row in ((2, 0), (3, 1), (4, height - 2), (5, height - 1)):
        wide[place, :width] = field[row]
        wide[place, width:] = tiles[row]
    above = (lat > 0).astype(jnp.int32)
    below = (lat < lax.axis_size("lat") - 1).astype(jnp.int32)
    centers = [(row, ALL) for row in (1, 2, 5, 6)]
    first_level(wide, shifted, stencils.at[0], centers, middle, [above, None, None, below])

    def write(row, side, at, value):
        out[row, side, at] = jnp.exp(value)

    last = height - 3
    top = [(middle, 0), (middle, 1), (inside, 0), (inside, 1)]
    bottom = [(inside, last - 1), (inside, last), (middle, 2), (middle, 3)]
    windows = {0: top[:3], 1: top[1:], height - 2: bottom[:3], height - 1: bottom[1:]}
    second_level(stencils.at[1], windows, radial, write, wide.shape[1])
    for row in range(2, height - 2):
        out[row] = inner[row - 2]


def beside_tiles(side_0, side_1, density):
    tiles = unpack_sides(side_0, side_1, density.shape[0])
    return [tile * density[row, SUBLANES:] for row, tile in enumerate(tiles)]


def back_reach_kernel(field, side_1, side_0, density, stencils, to_partner, to_outer, middle, wide, shifted, reach):
    height, _, radial = field.shape
    last = height - 1
    fill_wide(wide, field, beside_tiles(side_0, side_1, density), (0, 1, last - 1, last))
    lat, odd = position("lat")
    above = (lat > 0).astype(jnp.int32)
    below = (lat < lax.axis_size("lat") - 1).astype(jnp.int32)
    centers = [(-1, (1,)), (0, (0, 1)), (last, (-1, 0)), (last + 1, (-1,))]
    first_level(wide, shifted, stencils.at[0], centers, middle, [above, None, None, below])

    def write(row, side, at, value):
        reach[row, side, at] = value

    windows = {
        0: [None, None, (middle, 0)],
        1: [None, (middle, 0), (middle, 1)],
        2: [(middle, 2), (middle, 3), None],
        3: [(middle, 3), None, None],
    }
    second_level(stencils.at[1], windows, radial, write)
    for place in range(2):
        to_partner[place] = either(odd, reach[place], reach[2 + place])
        to_outer[place] = either(odd, reach[2 + place], reach[place])


def back_own_kernel(field, side_1, side_0, density, stencils, latent, edge, out, wide, shifted, middle):
    height, _, radial = field.shape
    fill_wide(wide, field, beside_tiles(side_0, side_1, density), range(height))
    centers = [(row, ALL) for row in range(1, height - 1)]
    first_level(wide, shifted, stencils.at[0], centers, middle, [None] * len(centers))

    def write(row, side, at, value):
        out[row, side, at] = latent[row, side, at] + value

    line = [(edge, 0), (edge, 1)] + [(middle, place) for place in range(height - 2)] + [(edge, 2), (edge, 3)]
    second_level(stencils.at[1], {row: line[row:row + 3] for row in range(height)}, radial, write)


def close_kernel(own, end_0, end_1, out, top, bottom, sent):
    height = own.shape[0]
    last = height - 2
    pairs = ((own.at[2:last], out.at[2:last]), (top, out.at[:2]), (bottom, out.at[last:]))
    copies = [pltpu.make_async_copy(source, target, sent.at[i]) for i, (source, target) in enumerate(pairs)]
    copies[0].start()
    _, odd = position("lat")
    for place in range(2):
        top[place] = own[place] + either(odd, end_0[place], end_1[place])
    copies[1].start()
    for place in range(2):
        bottom[place] = own[last + place] + either(odd, end_1[place], end_0[place])
    copies[2].start()
    for copy in copies:
        copy.wait()


def open_kernel(
    counts_in, offsets_in, residual_in, pixel_in, bins_in, latent_in, out, latent, to_partner, to_outer,
    counts, offsets, residual, pixel, bins, table, arrived,
):
    pairs = (
        (counts_in, counts), (offsets_in, offsets), (residual_in, residual), (pixel_in, pixel), (bins_in, bins),
        (latent_in, latent),
    )
    copies = [pltpu.make_async_copy(source, target, arrived.at[i]) for i, (source, target) in enumerate(pairs)]
    for copy in copies:
        copy.start()
    for copy in copies[:-1]:
        copy.wait()
    height, _, radial = latent.shape
    length = residual.shape[0]
    table[pl.ds(0, length, stride=2), :] = residual[...]
    table[pl.ds(1, length, stride=2), :] = (pixel[...] * radial + bins[...]).astype(jnp.float32)

    lane = lax.broadcasted_iota(jnp.int32, (SUBLANES, LANES), 1)
    row = lax.broadcasted_iota(jnp.int32, (SUBLANES, LANES), 0)
    slot = lax.shift_right_logical(row, 1) * LANES + lane
    for owner in range(out.shape[0]):
        start = offsets[0, owner]
        first = lax.shift_right_logical(start, 7) * 2
        part = lax.bitwise_and(start, LANES - 1)
        turn = lax.bitwise_and(LANES - part, LANES - 1)
        here = pltpu.roll(table[pl.ds(first, SUBLANES), :], turn, 1)
        after = pltpu.roll(table[pl.ds(first + 2, SUBLANES), :], turn, 1)
        joined = jnp.where(lane < LANES - part, here, after)
        out[owner] = jnp.where(slot < counts[0, owner], joined, 0.0)

    copies[-1].wait()
    pack_four([latent[row] for row in range(height)], to_partner, to_outer)


def behind_of(got, part, cuts, runs, rows_of, *, height, width, radial):
    span = radial // cuts
    pixels = height * width // 2
    classes = cuts * pixels
    shards, rows, _ = got.shape
    bf16 = jnp.bfloat16
    column = lax.broadcasted_iota(jnp.int32, (classes, LANES), 0).astype(jnp.float32).astype(bf16)
    places = [
        (lax.broadcasted_iota(jnp.int32, (LANES, LANES), 1) + (first + 1)).astype(jnp.float32).astype(bf16)
        for first in range(0, span, LANES)
    ]
    zero = jnp.zeros((), bf16)

    def tall(kind, row):
        line = jnp.broadcast_to(rows_of[kind, row:row + 1, :], (16, LANES))
        return jnp.concatenate([line.astype(bf16)] * (classes // 16), axis=0)

    tiles = got[...].reshape(shards * rows, LANES)
    cell = tiles.astype(jnp.int32)
    pixel = lax.shift_right_logical(cell, radial.bit_length() - 1)
    bins = lax.bitwise_and(cell, radial - 1)
    cut = lax.shift_right_logical(bins, span.bit_length() - 1)
    place = lax.bitwise_and(pixel + 2, width - 1)
    own = cut * pixels + lax.shift_right_logical(pixel, 3) * 4 + lax.bitwise_and(place, 3)
    rows_of[0] = jnp.where(lax.shift_right_logical(place, 2) == part, own, classes).astype(jnp.float32)
    lows = jnp.transpose((lax.bitwise_and(bins, span - 1) + 1).astype(jnp.float32)).astype(bf16)
    coarse = tiles.astype(bf16).astype(jnp.float32)
    rows_of[1] = coarse
    rows_of[2] = tiles - coarse

    total = jnp.zeros((2 * classes, span), jnp.float32)
    group = 2 * RUNS // runs
    for first in range(0, shards, group):
        left, right = [], []
        for run in range(group * runs):
            row = (first + run // runs) * rows + run % runs * 2
            mine = tall(0, row + 1) == column
            left.append(jnp.concatenate([jnp.where(mine, tall(kind, row), zero) for kind in (1, 2)], axis=0))
            low = jnp.broadcast_to(lows[:, row + 1:row + 2], (LANES, LANES))
            right.append(jnp.concatenate([jnp.maximum(low, place) for place in places], axis=1))
        total = total + jnp.dot(
            jnp.concatenate(left, axis=1), jnp.concatenate(right, axis=0), preferred_element_type=jnp.float32
        )
    both = (total[:classes] + total[classes:]) * bin_width
    every = both[:, span - 1:] * (1.0 / span)
    lane = lax.broadcasted_iota(jnp.int32, both.shape, 1)
    at_least = jnp.where(lane == 0, every, pltpu.roll(both, 1, 1) - both + every)
    ranges = [at_least[start:start + pixels] for start in range(0, classes, pixels)]
    for k in reversed(range(cuts - 1)):
        ranges[k] = ranges[k] + ranges[k + 1][:, :1]
    return jnp.concatenate(ranges, axis=1)


def column_rows(packed, part, height):
    rows = []
    for row in range(height):
        tile = packed[row // 2 * SUBLANES:(row // 2 + 1) * SUBLANES]
        turn = row % 2 * 4 + (2 if part == 0 else SUBLANES - 2)
        rows.append(pltpu.roll(tile, (SUBLANES - turn) % SUBLANES, 0))
    return rows


def for_load(body):
    lat, count = lax.axis_index("lat"), lax.axis_size("lat")
    middle = (lat >= count // 4) & (lat < count - count // 4)
    pl.when(middle)(lambda: body(RUNS))
    pl.when(jnp.logical_not(middle))(lambda: body(LEAST // LANES))


def bin_sides_kernel(got, _, behind, to_partner, to_outer, rows_of):
    height, width, radial = behind.shape

    def body(runs):
        packed = behind_of(got, 0, 2, runs, rows_of, height=height, width=width, radial=radial)
        lines = column_rows(packed, 0, height)
        for row, values in enumerate(lines):
            behind[row] = values
        pack_sides(lines, to_partner, to_outer)

    for_load(body)


def bin_rest_kernel(got, density, behind, upstream, rows_of):
    height, width, radial = behind.shape
    sub = sublane(radial)

    def body(runs):
        packed = behind_of(got, 1, 2, runs, rows_of, height=height, width=width, radial=radial)
        for row, values in enumerate(column_rows(packed, 1, height)):
            upstream[row] = density[row, :width] * jnp.where((sub < 2) | (sub >= 6), behind[row], values)

    for_load(body)


def mirror(stencils):
    turned = jnp.flip(stencils, axis=1).reshape(stencils.shape[0], 9, 3, stencils.shape[2])
    edge = jnp.zeros_like(turned[:, :, 0, :1])
    back = jnp.concatenate([edge, turned[:, :, 0, :-1]], axis=-1)
    ahead = jnp.concatenate([turned[:, :, 2, 1:], edge], axis=-1)
    return jnp.stack([back, turned[:, :, 1], ahead], axis=2).reshape(stencils.shape)


def swap(to_partner, to_outer, axis, closed, outer_first=False):
    count = lax.axis_size(axis)
    outer = [(i, (i + 1) % count) for i in range(1, count, 2) if closed or i + 1 < count]
    inner = [(i, i + 1) for i in range(0, count - 1, 2)]

    def both_ways(pairs):
        return pairs + [(j, i) for i, j in pairs]

    moves = [(to_partner, inner), (to_outer, outer)]
    got = [lax.ppermute(values, axis, both_ways(pairs)) for values, pairs in moves[::-1 if outer_first else 1]]
    return tuple(got[::-1 if outer_first else 1])


VMEM = pl.BlockSpec(memory_space=pltpu.VMEM)
HBM = pl.BlockSpec(memory_space=pltpu.HBM)
LIMIT = pltpu.CompilerParams(vmem_limit_bytes=32 * 1024 * 1024)


def on_device(residual, star_pixel, star_bin, send_counts, send_offsets, latent, stencils):
    height, width, radial = latent.shape
    shards = send_counts.shape[1]
    slots = residual.shape[0]
    f32 = jnp.float32
    i32 = jnp.int32
    tile = jax.ShapeDtypeStruct((height, width, radial), f32)
    sides = jax.ShapeDtypeStruct((height // 4, SUBLANES, radial), f32)
    ends = jax.ShapeDtypeStruct((4, SUBLANES, radial), f32)

    def table(values):
        return values.reshape(slots // LANES, LANES)

    four = jax.ShapeDtypeStruct((height // 2, SUBLANES, radial), f32)
    packed, latent, *to_sides = pl.pallas_call(
        open_kernel,
        out_shape=(jax.ShapeDtypeStruct((shards, 2 * RUNS, LANES), f32), tile, four, four),
        in_specs=[HBM] * 6,
        out_specs=(VMEM, VMEM, VMEM, VMEM),
        scratch_shapes=[pltpu.SMEM((1, shards), i32)] * 2
        + [pltpu.VMEM((slots // LANES, LANES), kind) for kind in (f32, i32, i32)]
        + [pltpu.VMEM((2 * slots // LANES, LANES), f32)]
        + [pltpu.SemaphoreType.DMA((6,))],
        compiler_params=LIMIT,
        name="opening",
    )(*[
        pltpu.with_memory_space_constraint(values, pltpu.HBM)
        for values in (send_counts, send_offsets, table(residual), table(star_pixel), table(star_bin), latent)
    ])
    got = lax.all_to_all(packed, ("lat", "lon"), split_axis=0, concat_axis=0, tiled=True)

    rows = pltpu.VMEM((height, 2 * width, radial), f32)
    moved = pltpu.VMEM((2, height, 2 * width, radial), f32)
    edge = (3, 3, 4, width, radial)
    star_rows = [pltpu.VMEM((3, shards * 2 * RUNS, LANES), f32)]
    inner_rows = (3, 3, height - 2, width, radial)

    def call(kernel, name, outs, scratch, *operands):
        return pl.pallas_call(
            kernel,
            out_shape=outs,
            in_specs=[VMEM] * len(operands),
            out_specs=jax.tree.map(lambda _: VMEM, outs),
            scratch_shapes=scratch,
            compiler_params=LIMIT,
            name=name,
        )(*operands)

    def shape(*sizes):
        return jax.ShapeDtypeStruct(sizes, f32)

    beside = swap(*to_sides, "lon", True)
    to_ends = call(pack_ends_kernel, "density_pack", (ends, ends), [], latent, *beside)
    above = swap(*to_ends, "lat", False, outer_first=True)
    broad = 2 * width
    inner, middle = call(
        density_inside_kernel, "density_inside",
        (shape(height - 4, broad, radial), shape(3, 3, height - 2, broad, radial)), [rows, moved],
        latent, *beside, stencils,
    )
    behind, *to_sides = call(bin_sides_kernel, "bin_sides", (tile, sides, sides), star_rows, got, inner)
    density = call(
        density_ends_kernel, "density_ends", shape(height, broad, radial),
        [pltpu.VMEM((3, 3, 4, broad, radial), f32), rows, moved],
        latent, *beside, *above[::-1], stencils, middle, inner, behind,
    )
    upstream = call(bin_rest_kernel, "bin_rest", tile, star_rows, got, density, behind)

    mirrored = mirror(stencils)[::-1]
    beside = swap(*to_sides, "lon", True, outer_first=True)
    *to_ends, middle = call(
        back_reach_kernel, "back_reach", (shape(2, width, radial), shape(2, width, radial), shape(*edge)),
        [rows, moved, pltpu.VMEM((4, width, radial), f32)], upstream, *beside[::-1], density, mirrored,
    )
    above = swap(*to_ends, "lat", False)
    own = call(
        back_own_kernel, "back_own", tile, [rows, moved, pltpu.VMEM(inner_rows, f32)],
        upstream, *beside[::-1], density, mirrored, latent, middle,
    )
    return pl.pallas_call(
        close_kernel,
        out_shape=tile,
        in_specs=[VMEM] * 3,
        out_specs=HBM,
        scratch_shapes=[pltpu.VMEM((2, width, radial), f32)] * 2 + [pltpu.SemaphoreType.DMA((3,))],
        compiler_params=LIMIT,
        name="close",
    )(own, *above)


def solution(mesh):
    return jax.shard_map(
        on_device,
        mesh=mesh,
        in_specs=(
            P(("lat", "lon")),
            P(("lat", "lon")),
            P(("lat", "lon")),
            P(("lat", "lon"), None),
            P(("lat", "lon"), None),
            P("lat", "lon", None),
            P(),
        ),
        out_specs=P("lat", "lon", None),
        check_vma=False,
    )
```

```python
import functools

import jax
import jax.numpy as jnp
from jax import lax
from jax.experimental import pallas as pl
from jax.experimental.pallas import tpu as pltpu
from jax.sharding import PartitionSpec as P

CAP = 512
LEAST = 128
LANES = 128
SUBLANES = 8
RUNS = CAP // LANES
bin_width = 0.0625


def position(axis):
    index = lax.axis_index(axis)
    return index, lax.bitwise_and(index, 1)


def either(flag, if_set, if_clear):
    return jnp.where(jnp.full(if_set.shape, flag, jnp.int32) > 0, if_set, if_clear)


def sublane(radial):
    return lax.broadcasted_iota(jnp.int32, (SUBLANES, radial), 0)


def pack_sides(rows, to_partner, to_outer):
    _, odd = position("lon")
    sub = sublane(rows[0].shape[1])
    for group in range(len(rows) // 4):
        before, after = rows[4 * group], rows[4 * group]
        for k in range(1, 4):
            row = rows[4 * group + k]
            pair = lax.shift_right_logical(sub, 1)
            before = jnp.where(pair == k, pltpu.roll(row, 2 * k, 0), before)
            after = jnp.where(pair == 3 - k, pltpu.roll(row, SUBLANES - 2 * k, 0), after)
        to_partner[group] = either(odd, before, after)
        to_outer[group] = either(odd, after, before)


def unpack_sides(from_partner, from_outer, height):
    _, odd = position("lon")
    sub = sublane(from_partner.shape[2])
    tiles = []
    for group in range(height // 4):
        partner, outer = from_partner[group], from_outer[group]
        before, after = either(odd, partner, outer), either(odd, outer, partner)
        for k in range(4):
            if k:
                tiles.append(jnp.where(sub < 4, pltpu.roll(after, SUBLANES - 2 * k, 0), pltpu.roll(before, 2 * k, 0)))
            else:
                tiles.append(jnp.where(sub < 4, after, before))
    return tiles


def pack_four(rows, to_partner, to_outer):
    _, odd = position("lon")
    sub = sublane(rows[0].shape[1])
    for group in range(len(rows) // 2):
        one, two = rows[2 * group], pltpu.roll(rows[2 * group + 1], 4, 0)
        before, after = jnp.where(sub < 4, one, two), jnp.where(sub < 4, two, one)
        to_partner[group] = either(odd, before, after)
        to_outer[group] = either(odd, after, before)


def unpack_four(from_partner, from_outer, height):
    _, odd = position("lon")
    sub = sublane(from_partner.shape[2])
    tiles = []
    for group in range(height // 2):
        partner, outer = from_partner[group], from_outer[group]
        before, after = either(odd, partner, outer), either(odd, outer, partner)
        tiles.append(jnp.where(sub < 4, after, before))
        tiles.append(pltpu.roll(jnp.where(sub < 4, before, after), 4, 0))
    return tiles


def pack_ends_kernel(field, side_0, side_1, to_partner, to_outer):
    height = field.shape[0]
    _, odd = position("lat")
    tiles = unpack_four(side_0, side_1, height)
    top = [field[0], field[1], tiles[0], tiles[1]]
    bottom = [field[height - 2], field[height - 1], tiles[height - 2], tiles[height - 1]]
    for place, (one, two) in enumerate(zip(top, bottom)):
        to_partner[place] = either(odd, one, two)
        to_outer[place] = either(odd, two, one)


def radial_shifts(field):
    radial = field.shape[-1]
    lane = lax.broadcasted_iota(jnp.int32, field.shape, field.ndim - 1)
    return (
        jnp.where(lane == 0, 0.0, pltpu.roll(field, 1, field.ndim - 1)),
        jnp.where(lane == radial - 1, 0.0, pltpu.roll(field, radial - 1, field.ndim - 1)),
    )


def taps_of(coef, at):
    return [jnp.broadcast_to(coef[k:k + 1, at], (SUBLANES, LANES)) for k in range(27)]


def tiles_of_bins(radial, body):
    for start in range(0, radial, LANES):
        body(slice(start, start + LANES))


ALL = (-1, 0, 1)


def first_level(wide, shifted, coef, centers, middle, real):
    _, cols, radial = wide.shape
    for row in sorted({row + above for row, around in centers for above in around}):
        for place, moved in enumerate(radial_shifts(wide[row])):
            shifted[place, row] = moved

    def body(at):
        taps = taps_of(coef, at)
        for place, (row, around) in enumerate(centers):
            parts = []
            for side in (slice(0, SUBLANES), slice(SUBLANES, cols)):
                sums = [None, None, None]
                for above in around:
                    window = (shifted[0, row + above, side, at], wide[row + above, side, at], shifted[1, row + above, side, at])
                    for beside in range(3):
                        for step in range(3):
                            term = taps[(above + 1) * 9 + beside * 3 + step] * window[step]
                            sums[beside] = term if sums[beside] is None else sums[beside] + term
                parts.append(sums)
            whole = [jnp.concatenate([parts[0][b], parts[1][b]], axis=0) for b in range(3)]
            value = whole[1] + pltpu.roll(whole[0], 1, 0) + pltpu.roll(whole[2], cols - 1, 0)
            if real[place] is not None:
                value = either(real[place], value, jnp.zeros_like(value))
            kept = middle.shape[3]
            middle[0, 1, place, :, at] = pltpu.roll(value, 1, 0)[:kept]
            middle[1, 1, place, :, at] = value[:kept]
            middle[2, 1, place, :, at] = pltpu.roll(value, cols - 1, 0)[:kept]

    tiles_of_bins(radial, body)
    for place in range(len(centers)):
        for beside in range(3):
            for step, moved in zip((0, 2), radial_shifts(middle[beside, 1, place])):
                middle[beside, step, place] = moved


def second_level(coef, windows, radial, write, cols=SUBLANES):
    def body(at):
        taps = taps_of(coef, at)
        for row, around in windows.items():
            for start in range(0, cols, SUBLANES):
                side = slice(start, start + SUBLANES)
                total = None
                for above, at_row in enumerate(around):
                    if at_row is None:
                        continue
                    buffer, place = at_row
                    for beside in range(3):
                        for step in range(3):
                            term = taps[above * 9 + beside * 3 + step] * buffer[beside, step, place, side, at]
                            total = term if total is None else total + term
                write(row, side, at, total)

    tiles_of_bins(radial, body)


def fill_wide(wide, field, tiles, rows):
    width = field.shape[1]
    for row in rows:
        wide[row, :width] = field[row]
        wide[row, width:] = tiles[row]


def density_inside_kernel(field, side_0, side_1, stencils, out, middle, wide, shifted):
    height, _, radial = field.shape
    fill_wide(wide, field, unpack_four(side_0, side_1, height), range(height))
    centers = [(row, ALL) for row in range(1, height - 1)]
    first_level(wide, shifted, stencils.at[0], centers, middle, [None] * len(centers))

    def write(row, side, at, value):
        out[row - 2, side, at] = jnp.exp(value)

    windows = {row: [(middle, row - 2 + k) for k in range(3)] for row in range(2, height - 2)}
    second_level(stencils.at[1], windows, radial, write, wide.shape[1])


def density_ends_kernel(
    field, side_0, side_1, end_1, end_0, stencils, inside, inner, _, out, middle, wide, shifted
):
    height, width, radial = field.shape
    tiles = unpack_four(side_0, side_1, height)
    lat, odd = position("lat")
    for place in range(2):
        for half in range(2):
            partner, outer = end_0[2 * half + place], end_1[2 * half + place]
            at = slice(half * width, (half + 1) * width)
            wide[place, at] = either(odd, partner, outer)
            wide[6 + place, at] = either(odd, outer, partner)
    for place, row in ((2, 0), (3, 1), (4, height - 2), (5, height - 1)):
        wide[place, :width] = field[row]
        wide[place, width:] = tiles[row]
    above = (lat > 0).astype(jnp.int32)
    below = (lat < lax.axis_size("lat") - 1).astype(jnp.int32)
    centers = [(row, ALL) for row in (1, 2, 5, 6)]
    first_level(wide, shifted, stencils.at[0], centers, middle, [above, None, None, below])

    def write(row, side, at, value):
        out[row, side, at] = jnp.exp(value)

    last = height - 3
    top = [(middle, 0), (middle, 1), (inside, 0), (inside, 1)]
    bottom = [(inside, last - 1), (inside, last), (middle, 2), (middle, 3)]
    windows = {0: top[:3], 1: top[1:], height - 2: bottom[:3], height - 1: bottom[1:]}
    second_level(stencils.at[1], windows, radial, write, wide.shape[1])
    for row in range(2, height - 2):
        out[row] = inner[row - 2]


def beside_tiles(side_0, side_1, density):
    tiles = unpack_sides(side_0, side_1, density.shape[0])
    return [tile * density[row, SUBLANES:] for row, tile in enumerate(tiles)]


def back_reach_kernel(field, side_1, side_0, density, stencils, to_partner, to_outer, middle, wide, shifted, reach):
    height, _, radial = field.shape
    last = height - 1
    fill_wide(wide, field, beside_tiles(side_0, side_1, density), (0, 1, last - 1, last))
    lat, odd = position("lat")
    above = (lat > 0).astype(jnp.int32)
    below = (lat < lax.axis_size("lat") - 1).astype(jnp.int32)
    centers = [(-1, (1,)), (0, (0, 1)), (last, (-1, 0)), (last + 1, (-1,))]
    first_level(wide, shifted, stencils.at[0], centers, middle, [above, None, None, below])

    def write(row, side, at, value):
        reach[row, side, at] = value

    windows = {
        0: [None, None, (middle, 0)],
        1: [None, (middle, 0), (middle, 1)],
        2: [(middle, 2), (middle, 3), None],
        3: [(middle, 3), None, None],
    }
    second_level(stencils.at[1], windows, radial, write)
    for place in range(2):
        to_partner[place] = either(odd, reach[place], reach[2 + place])
        to_outer[place] = either(odd, reach[2 + place], reach[place])


def back_own_kernel(field, side_1, side_0, density, stencils, latent, edge, out, wide, shifted, middle):
    height, _, radial = field.shape
    fill_wide(wide, field, beside_tiles(side_0, side_1, density), range(height))
    centers = [(row, ALL) for row in range(1, height - 1)]
    first_level(wide, shifted, stencils.at[0], centers, middle, [None] * len(centers))

    def write(row, side, at, value):
        out[row, side, at] = latent[row, side, at] + value

    line = [(edge, 0), (edge, 1)] + [(middle, place) for place in range(height - 2)] + [(edge, 2), (edge, 3)]
    second_level(stencils.at[1], {row: line[row:row + 3] for row in range(height)}, radial, write)


def close_kernel(own, end_0, end_1, out, top, bottom, sent):
    height = own.shape[0]
    last = height - 2
    pairs = ((own.at[2:last], out.at[2:last]), (top, out.at[:2]), (bottom, out.at[last:]))
    copies = [pltpu.make_async_copy(source, target, sent.at[i]) for i, (source, target) in enumerate(pairs)]
    copies[0].start()
    _, odd = position("lat")
    for place in range(2):
        top[place] = own[place] + either(odd, end_0[place], end_1[place])
    copies[1].start()
    for place in range(2):
        bottom[place] = own[last + place] + either(odd, end_1[place], end_0[place])
    copies[2].start()
    for copy in copies:
        copy.wait()


def open_kernel(
    counts_in, offsets_in, residual_in, pixel_in, bins_in, latent_in, taps_in, out, latent, to_partner, to_outer, taps,
    counts, offsets, residual, pixel, bins, table, arrived,
):
    pairs = (
        (counts_in, counts), (offsets_in, offsets), (residual_in, residual), (pixel_in, pixel), (bins_in, bins),
        (latent_in, latent), (taps_in, taps),
    )
    copies = [pltpu.make_async_copy(source, target, arrived.at[i]) for i, (source, target) in enumerate(pairs)]
    for copy in copies:
        copy.start()
    for copy in copies[:-2]:
        copy.wait()
    height, _, radial = latent.shape
    length = residual.shape[0]
    table[pl.ds(0, length, stride=2), :] = residual[...]
    table[pl.ds(1, length, stride=2), :] = (pixel[...] * radial + bins[...]).astype(jnp.float32)

    lane = lax.broadcasted_iota(jnp.int32, (SUBLANES, LANES), 1)
    row = lax.broadcasted_iota(jnp.int32, (SUBLANES, LANES), 0)
    slot = lax.shift_right_logical(row, 1) * LANES + lane
    for owner in range(out.shape[0]):
        start = offsets[0, owner]
        first = lax.shift_right_logical(start, 7) * 2
        part = lax.bitwise_and(start, LANES - 1)
        turn = lax.bitwise_and(LANES - part, LANES - 1)
        here = pltpu.roll(table[pl.ds(first, SUBLANES), :], turn, 1)
        after = pltpu.roll(table[pl.ds(first + 2, SUBLANES), :], turn, 1)
        joined = jnp.where(lane < LANES - part, here, after)
        out[owner] = jnp.where(slot < counts[0, owner], joined, 0.0)

    copies[-2].wait()
    pack_four([latent[row] for row in range(height)], to_partner, to_outer)
    copies[-1].wait()


def behind_of(got, part, cuts, runs, rows_of, *, height, width, radial):
    span = radial // cuts
    pixels = height * width // 2
    classes = cuts * pixels
    shards, rows, _ = got.shape
    bf16 = jnp.bfloat16
    column = lax.broadcasted_iota(jnp.int32, (classes, LANES), 0).astype(jnp.float32).astype(bf16)
    places = [
        (lax.broadcasted_iota(jnp.int32, (LANES, LANES), 1) + (first + 1)).astype(jnp.float32).astype(bf16)
        for first in range(0, span, LANES)
    ]
    zero = jnp.zeros((), bf16)

    def tall(kind, row):
        line = jnp.broadcast_to(rows_of[kind, row:row + 1, :], (16, LANES))
        return jnp.concatenate([line.astype(bf16)] * (classes // 16), axis=0)

    tiles = got[...].reshape(shards * rows, LANES)
    cell = tiles.astype(jnp.int32)
    pixel = lax.shift_right_logical(cell, radial.bit_length() - 1)
    bins = lax.bitwise_and(cell, radial - 1)
    cut = lax.shift_right_logical(bins, span.bit_length() - 1)
    place = lax.bitwise_and(pixel + 2, width - 1)
    own = cut * pixels + lax.shift_right_logical(pixel, 3) * 4 + lax.bitwise_and(place, 3)
    rows_of[0] = jnp.where(lax.shift_right_logical(place, 2) == part, own, classes).astype(jnp.float32)
    lows = jnp.transpose((lax.bitwise_and(bins, span - 1) + 1).astype(jnp.float32)).astype(bf16)
    coarse = tiles.astype(bf16).astype(jnp.float32)
    rows_of[1] = coarse
    rows_of[2] = tiles - coarse

    total = jnp.zeros((2 * classes, span), jnp.float32)
    group = 2 * RUNS // runs
    for first in range(0, shards, group):
        left, right = [], []
        for run in range(group * runs):
            row = (first + run // runs) * rows + run % runs * 2
            mine = tall(0, row + 1) == column
            left.append(jnp.concatenate([jnp.where(mine, tall(kind, row), zero) for kind in (1, 2)], axis=0))
            low = jnp.broadcast_to(lows[:, row + 1:row + 2], (LANES, LANES))
            right.append(jnp.concatenate([jnp.maximum(low, place) for place in places], axis=1))
        total = total + jnp.dot(
            jnp.concatenate(left, axis=1), jnp.concatenate(right, axis=0), preferred_element_type=jnp.float32
        )
    both = (total[:classes] + total[classes:]) * bin_width
    every = both[:, span - 1:] * (1.0 / span)
    lane = lax.broadcasted_iota(jnp.int32, both.shape, 1)
    at_least = jnp.where(lane == 0, every, pltpu.roll(both, 1, 1) - both + every)
    ranges = [at_least[start:start + pixels] for start in range(0, classes, pixels)]
    for k in reversed(range(cuts - 1)):
        ranges[k] = ranges[k] + ranges[k + 1][:, :1]
    return jnp.concatenate(ranges, axis=1)


def column_rows(packed, part, height):
    rows = []
    for row in range(height):
        tile = packed[row // 2 * SUBLANES:(row // 2 + 1) * SUBLANES]
        turn = row % 2 * 4 + (2 if part == 0 else SUBLANES - 2)
        rows.append(pltpu.roll(tile, (SUBLANES - turn) % SUBLANES, 0))
    return rows


def for_load(body):
    lat, count = lax.axis_index("lat"), lax.axis_size("lat")
    middle = (lat >= count // 4) & (lat < count - count // 4)
    pl.when(middle)(lambda: body(RUNS))
    pl.when(jnp.logical_not(middle))(lambda: body(LEAST // LANES))


def bin_sides_kernel(got, _, behind, to_partner, to_outer, rows_of):
    height, width, radial = behind.shape

    def body(runs):
        packed = behind_of(got, 0, 2, runs, rows_of, height=height, width=width, radial=radial)
        lines = column_rows(packed, 0, height)
        for row, values in enumerate(lines):
            behind[row] = values
        pack_sides(lines, to_partner, to_outer)

    for_load(body)


def bin_rest_kernel(got, density, behind, upstream, rows_of):
    height, width, radial = behind.shape
    sub = sublane(radial)

    def body(runs):
        packed = behind_of(got, 1, 2, runs, rows_of, height=height, width=width, radial=radial)
        for row, values in enumerate(column_rows(packed, 1, height)):
            upstream[row] = density[row, :width] * jnp.where((sub < 2) | (sub >= 6), behind[row], values)

    for_load(body)


def tables_kernel(taps, stencils, mirrored):
    count, levels, _ = taps.shape
    for level in range(levels):
        for tap in range(count):
            row = taps[tap, level:level + 1, :]
            stencils[level, tap:tap + 1, :] = row
            turned = count - 1 - tap
            if turned % 3 != 1:
                row = radial_shifts(row)[turned % 3 // 2]
            mirrored[levels - 1 - level, turned:turned + 1, :] = row


def swap(to_partner, to_outer, axis, closed, outer_first=False):
    count = lax.axis_size(axis)
    outer = [(i, (i + 1) % count) for i in range(1, count, 2) if closed or i + 1 < count]
    inner = [(i, i + 1) for i in range(0, count - 1, 2)]

    def both_ways(pairs):
        return pairs + [(j, i) for i, j in pairs]

    moves = [(to_partner, inner), (to_outer, outer)]
    got = [lax.ppermute(values, axis, both_ways(pairs)) for values, pairs in moves[::-1 if outer_first else 1]]
    return tuple(got[::-1 if outer_first else 1])


VMEM = pl.BlockSpec(memory_space=pltpu.VMEM)
HBM = pl.BlockSpec(memory_space=pltpu.HBM)
LIMIT = pltpu.CompilerParams(vmem_limit_bytes=32 * 1024 * 1024)


def on_device(residual, star_pixel, star_bin, send_counts, send_offsets, latent, stencils):
    height, width, radial = latent.shape
    shards = send_counts.shape[1]
    slots = residual.shape[0]
    f32 = jnp.float32
    i32 = jnp.int32
    tile = jax.ShapeDtypeStruct((height, width, radial), f32)
    sides = jax.ShapeDtypeStruct((height // 4, SUBLANES, radial), f32)
    ends = jax.ShapeDtypeStruct((4, SUBLANES, radial), f32)

    def table(values):
        return values.reshape(slots // LANES, LANES)

    four = jax.ShapeDtypeStruct((height // 2, SUBLANES, radial), f32)
    taps = jax.ShapeDtypeStruct((stencils.shape[1], stencils.shape[0], radial), f32)
    packed, latent, *to_sides, taps = pl.pallas_call(
        open_kernel,
        out_shape=(jax.ShapeDtypeStruct((shards, 2 * RUNS, LANES), f32), tile, four, four, taps),
        in_specs=[HBM] * 7,
        out_specs=(VMEM,) * 5,
        scratch_shapes=[pltpu.SMEM((1, shards), i32)] * 2
        + [pltpu.VMEM((slots // LANES, LANES), kind) for kind in (f32, i32, i32)]
        + [pltpu.VMEM((2 * slots // LANES, LANES), f32)]
        + [pltpu.SemaphoreType.DMA((7,))],
        compiler_params=LIMIT,
        name="opening",
    )(*[
        pltpu.with_memory_space_constraint(values, pltpu.HBM)
        for values in (send_counts, send_offsets, table(residual), table(star_pixel), table(star_bin), latent, stencils.transpose(1, 0, 2))
    ])
    got = lax.all_to_all(packed, ("lat", "lon"), split_axis=0, concat_axis=0, tiled=True)

    rows = pltpu.VMEM((height, 2 * width, radial), f32)
    moved = pltpu.VMEM((2, height, 2 * width, radial), f32)
    edge = (3, 3, 4, width, radial)
    star_rows = [pltpu.VMEM((3, shards * 2 * RUNS, LANES), f32)]
    inner_rows = (3, 3, height - 2, width, radial)

    def call(kernel, name, outs, scratch, *operands):
        return pl.pallas_call(
            kernel,
            out_shape=outs,
            in_specs=[VMEM] * len(operands),
            out_specs=jax.tree.map(lambda _: VMEM, outs),
            scratch_shapes=scratch,
            compiler_params=LIMIT,
            name=name,
        )(*operands)

    def shape(*sizes):
        return jax.ShapeDtypeStruct(sizes, f32)

    beside = swap(*to_sides, "lon", True)
    to_ends = call(pack_ends_kernel, "density_pack", (ends, ends), [], latent, *beside)
    above = swap(*to_ends, "lat", False, outer_first=True)
    broad = 2 * width
    coefs = jax.ShapeDtypeStruct(stencils.shape, f32)
    stencils, mirrored = call(tables_kernel, "tables", (coefs, coefs), [], taps)
    inner, middle = call(
        density_inside_kernel, "density_inside",
        (shape(height - 4, broad, radial), shape(3, 3, height - 2, broad, radial)), [rows, moved],
        latent, *beside, stencils,
    )
    behind, *to_sides = call(bin_sides_kernel, "bin_sides", (tile, sides, sides), star_rows, got, inner)
    density = call(
        density_ends_kernel, "density_ends", shape(height, broad, radial),
        [pltpu.VMEM((3, 3, 4, broad, radial), f32), rows, moved],
        latent, *beside, *above[::-1], stencils, middle, inner, behind,
    )
    upstream = call(bin_rest_kernel, "bin_rest", tile, star_rows, got, density, behind)

    beside = swap(*to_sides, "lon", True, outer_first=True)
    *to_ends, middle = call(
        back_reach_kernel, "back_reach", (shape(2, width, radial), shape(2, width, radial), shape(*edge)),
        [rows, moved, pltpu.VMEM((4, width, radial), f32)], upstream, *beside[::-1], density, mirrored,
    )
    above = swap(*to_ends, "lat", False)
    own = call(
        back_own_kernel, "back_own", tile, [rows, moved, pltpu.VMEM(inner_rows, f32)],
        upstream, *beside[::-1], density, mirrored, latent, middle,
    )
    return pl.pallas_call(
        close_kernel,
        out_shape=tile,
        in_specs=[VMEM] * 3,
        out_specs=HBM,
        scratch_shapes=[pltpu.VMEM((2, width, radial), f32)] * 2 + [pltpu.SemaphoreType.DMA((3,))],
        compiler_params=LIMIT,
        name="close",
    )(own, *above)


def solution(mesh):
    return jax.shard_map(
        on_device,
        mesh=mesh,
        in_specs=(
            P(("lat", "lon")),
            P(("lat", "lon")),
            P(("lat", "lon")),
            P(("lat", "lon"), None),
            P(("lat", "lon"), None),
            P("lat", "lon", None),
            P(),
        ),
        out_specs=P("lat", "lon", None),
        check_vma=False,
    )
```

```python
import functools

import jax
import jax.numpy as jnp
from jax import lax
from jax.experimental import pallas as pl
from jax.experimental.pallas import tpu as pltpu
from jax.sharding import PartitionSpec as P

CAP = 512
LEAST = 128
LANES = 128
SUBLANES = 8
RUNS = CAP // LANES
bin_width = 0.0625


def position(axis):
    index = lax.axis_index(axis)
    return index, lax.bitwise_and(index, 1)


def either(flag, if_set, if_clear):
    return jnp.where(jnp.full(if_set.shape, flag, jnp.int32) > 0, if_set, if_clear)


def sublane(radial):
    return lax.broadcasted_iota(jnp.int32, (SUBLANES, radial), 0)


def pack_sides(rows, to_partner, to_outer):
    _, odd = position("lon")
    sub = sublane(rows[0].shape[1])
    for group in range(len(rows) // 4):
        before, after = rows[4 * group], rows[4 * group]
        for k in range(1, 4):
            row = rows[4 * group + k]
            pair = lax.shift_right_logical(sub, 1)
            before = jnp.where(pair == k, pltpu.roll(row, 2 * k, 0), before)
            after = jnp.where(pair == 3 - k, pltpu.roll(row, SUBLANES - 2 * k, 0), after)
        to_partner[group] = either(odd, before, after)
        to_outer[group] = either(odd, after, before)


def unpack_sides(from_partner, from_outer, height):
    _, odd = position("lon")
    sub = sublane(from_partner.shape[2])
    tiles = []
    for group in range(height // 4):
        partner, outer = from_partner[group], from_outer[group]
        before, after = either(odd, partner, outer), either(odd, outer, partner)
        for k in range(4):
            if k:
                tiles.append(jnp.where(sub < 4, pltpu.roll(after, SUBLANES - 2 * k, 0), pltpu.roll(before, 2 * k, 0)))
            else:
                tiles.append(jnp.where(sub < 4, after, before))
    return tiles


def pack_four(rows, to_partner, to_outer):
    _, odd = position("lon")
    sub = sublane(rows[0].shape[1])
    for group in range(len(rows) // 2):
        one, two = rows[2 * group], pltpu.roll(rows[2 * group + 1], 4, 0)
        before, after = jnp.where(sub < 4, one, two), jnp.where(sub < 4, two, one)
        to_partner[group] = either(odd, before, after)
        to_outer[group] = either(odd, after, before)


def unpack_four(from_partner, from_outer, height):
    _, odd = position("lon")
    sub = sublane(from_partner.shape[2])
    tiles = []
    for group in range(height // 2):
        partner, outer = from_partner[group], from_outer[group]
        before, after = either(odd, partner, outer), either(odd, outer, partner)
        tiles.append(jnp.where(sub < 4, after, before))
        tiles.append(pltpu.roll(jnp.where(sub < 4, before, after), 4, 0))
    return tiles


def pack_ends_kernel(field, side_0, side_1, to_partner, to_outer):
    height = field.shape[0]
    _, odd = position("lat")
    tiles = unpack_four(side_0, side_1, height)
    top = [field[0], field[1], tiles[0], tiles[1]]
    bottom = [field[height - 2], field[height - 1], tiles[height - 2], tiles[height - 1]]
    for place, (one, two) in enumerate(zip(top, bottom)):
        to_partner[place] = either(odd, one, two)
        to_outer[place] = either(odd, two, one)


def radial_shifts(field):
    radial = field.shape[-1]
    lane = lax.broadcasted_iota(jnp.int32, field.shape, field.ndim - 1)
    return (
        jnp.where(lane == 0, 0.0, pltpu.roll(field, 1, field.ndim - 1)),
        jnp.where(lane == radial - 1, 0.0, pltpu.roll(field, radial - 1, field.ndim - 1)),
    )


def taps_of(coef, at):
    return [jnp.broadcast_to(coef[k:k + 1, at], (SUBLANES, LANES)) for k in range(27)]


def tiles_of_bins(radial, body):
    for start in range(0, radial, LANES):
        body(slice(start, start + LANES))


ALL = (-1, 0, 1)


def first_level(wide, shifted, coef, centers, middle, real):
    _, cols, radial = wide.shape
    for row in sorted({row + above for row, around in centers for above in around}):
        for place, moved in enumerate(radial_shifts(wide[row])):
            shifted[place, row] = moved

    def body(at):
        taps = taps_of(coef, at)
        for place, (row, around) in enumerate(centers):
            parts = []
            for side in (slice(0, SUBLANES), slice(SUBLANES, cols)):
                sums = [None, None, None]
                for above in around:
                    window = (shifted[0, row + above, side, at], wide[row + above, side, at], shifted[1, row + above, side, at])
                    for beside in range(3):
                        for step in range(3):
                            term = taps[(above + 1) * 9 + beside * 3 + step] * window[step]
                            sums[beside] = term if sums[beside] is None else sums[beside] + term
                parts.append(sums)
            whole = [jnp.concatenate([parts[0][b], parts[1][b]], axis=0) for b in range(3)]
            value = whole[1] + pltpu.roll(whole[0], 1, 0) + pltpu.roll(whole[2], cols - 1, 0)
            if real[place] is not None:
                value = either(real[place], value, jnp.zeros_like(value))
            kept = middle.shape[3]
            middle[0, 1, place, :, at] = pltpu.roll(value, 1, 0)[:kept]
            middle[1, 1, place, :, at] = value[:kept]
            middle[2, 1, place, :, at] = pltpu.roll(value, cols - 1, 0)[:kept]

    tiles_of_bins(radial, body)
    for place in range(len(centers)):
        for beside in range(3):
            for step, moved in zip((0, 2), radial_shifts(middle[beside, 1, place])):
                middle[beside, step, place] = moved


def second_level(coef, windows, radial, write, cols=SUBLANES):
    def body(at):
        taps = taps_of(coef, at)
        for row, around in windows.items():
            for start in range(0, cols, SUBLANES):
                side = slice(start, start + SUBLANES)
                total = None
                for above, at_row in enumerate(around):
                    if at_row is None:
                        continue
                    buffer, place = at_row
                    for beside in range(3):
                        for step in range(3):
                            term = taps[above * 9 + beside * 3 + step] * buffer[beside, step, place, side, at]
                            total = term if total is None else total + term
                write(row, side, at, total)

    tiles_of_bins(radial, body)


def fill_wide(wide, field, tiles, rows):
    width = field.shape[1]
    for row in rows:
        wide[row, :width] = field[row]
        wide[row, width:] = tiles[row]


def density_inside_kernel(field, side_0, side_1, stencils, out, middle, wide, shifted):
    height, _, radial = field.shape
    fill_wide(wide, field, unpack_four(side_0, side_1, height), range(height))
    centers = [(row, ALL) for row in range(1, height - 1)]
    first_level(wide, shifted, stencils.at[0], centers, middle, [None] * len(centers))

    def write(row, side, at, value):
        out[row - 2, side, at] = jnp.exp(value)

    windows = {row: [(middle, row - 2 + k) for k in range(3)] for row in range(2, height - 2)}
    second_level(stencils.at[1], windows, radial, write, wide.shape[1])


def density_ends_kernel(
    field, side_0, side_1, end_1, end_0, stencils, inside, inner, _, out, middle, wide, shifted
):
    height, width, radial = field.shape
    tiles = unpack_four(side_0, side_1, height)
    lat, odd = position("lat")
    for place in range(2):
        for half in range(2):
            partner, outer = end_0[2 * half + place], end_1[2 * half + place]
            at = slice(half * width, (half + 1) * width)
            wide[place, at] = either(odd, partner, outer)
            wide[6 + place, at] = either(odd, outer, partner)
    for place, row in ((2, 0), (3, 1), (4, height - 2), (5, height - 1)):
        wide[place, :width] = field[row]
        wide[place, width:] = tiles[row]
    above = (lat > 0).astype(jnp.int32)
    below = (lat < lax.axis_size("lat") - 1).astype(jnp.int32)
    centers = [(row, ALL) for row in (1, 2, 5, 6)]
    first_level(wide, shifted, stencils.at[0], centers, middle, [above, None, None, below])

    def write(row, side, at, value):
        out[row, side, at] = jnp.exp(value)

    last = height - 3
    top = [(middle, 0), (middle, 1), (inside, 0), (inside, 1)]
    bottom = [(inside, last - 1), (inside, last), (middle, 2), (middle, 3)]
    windows = {0: top[:3], 1: top[1:], height - 2: bottom[:3], height - 1: bottom[1:]}
    second_level(stencils.at[1], windows, radial, write, wide.shape[1])
    for row in range(2, height - 2):
        out[row] = inner[row - 2]


def beside_tiles(side_0, side_1, density):
    tiles = unpack_sides(side_0, side_1, density.shape[0])
    return [tile * density[row, SUBLANES:] for row, tile in enumerate(tiles)]


def back_reach_kernel(field, side_1, side_0, density, stencils, to_partner, to_outer, middle, wide, shifted, reach):
    height, _, radial = field.shape
    last = height - 1
    fill_wide(wide, field, beside_tiles(side_0, side_1, density), (0, 1, last - 1, last))
    lat, odd = position("lat")
    above = (lat > 0).astype(jnp.int32)
    below = (lat < lax.axis_size("lat") - 1).astype(jnp.int32)
    centers = [(-1, (1,)), (0, (0, 1)), (last, (-1, 0)), (last + 1, (-1,))]
    first_level(wide, shifted, stencils.at[0], centers, middle, [above, None, None, below])

    def write(row, side, at, value):
        reach[row, side, at] = value

    windows = {
        0: [None, None, (middle, 0)],
        1: [None, (middle, 0), (middle, 1)],
        2: [(middle, 2), (middle, 3), None],
        3: [(middle, 3), None, None],
    }
    second_level(stencils.at[1], windows, radial, write)
    for place in range(2):
        to_partner[place] = either(odd, reach[place], reach[2 + place])
        to_outer[place] = either(odd, reach[2 + place], reach[place])


def back_own_kernel(field, side_1, side_0, density, stencils, latent, edge, out, wide, shifted, middle):
    height, _, radial = field.shape
    fill_wide(wide, field, beside_tiles(side_0, side_1, density), range(height))
    centers = [(row, ALL) for row in range(1, height - 1)]
    first_level(wide, shifted, stencils.at[0], centers, middle, [None] * len(centers))

    def write(row, side, at, value):
        out[row, side, at] = latent[row, side, at] + value

    line = [(edge, 0), (edge, 1)] + [(middle, place) for place in range(height - 2)] + [(edge, 2), (edge, 3)]
    second_level(stencils.at[1], {row: line[row:row + 3] for row in range(height)}, radial, write)


def close_kernel(own, end_0, end_1, out, top, bottom, sent):
    height = own.shape[0]
    last = height - 2
    pairs = ((own.at[2:last], out.at[2:last]), (top, out.at[:2]), (bottom, out.at[last:]))
    copies = [pltpu.make_async_copy(source, target, sent.at[i]) for i, (source, target) in enumerate(pairs)]
    copies[0].start()
    _, odd = position("lat")
    for place in range(2):
        top[place] = own[place] + either(odd, end_0[place], end_1[place])
    copies[1].start()
    for place in range(2):
        bottom[place] = own[last + place] + either(odd, end_1[place], end_0[place])
    copies[2].start()
    for copy in copies:
        copy.wait()


def open_kernel(
    counts_in, offsets_in, residual_in, pixel_in, bins_in, latent_in, taps_in, out, latent, to_partner, to_outer, taps,
    counts, offsets, residual, pixel, bins, table, arrived,
):
    pairs = (
        (counts_in, counts), (offsets_in, offsets), (residual_in, residual), (pixel_in, pixel), (bins_in, bins),
        (latent_in, latent), (taps_in, taps),
    )
    copies = [pltpu.make_async_copy(source, target, arrived.at[i]) for i, (source, target) in enumerate(pairs)]
    for copy in copies:
        copy.start()
    for copy in copies[:-2]:
        copy.wait()
    height, _, radial = latent.shape
    length = residual.shape[0]
    table[pl.ds(0, length, stride=2), :] = residual[...]
    table[pl.ds(1, length, stride=2), :] = (pixel[...] * radial + bins[...]).astype(jnp.float32)

    lane = lax.broadcasted_iota(jnp.int32, (SUBLANES, LANES), 1)
    row = lax.broadcasted_iota(jnp.int32, (SUBLANES, LANES), 0)
    slot = lax.shift_right_logical(row, 1) * LANES + lane
    for owner in range(out.shape[0]):
        start = offsets[0, owner]
        first = lax.shift_right_logical(start, 7) * 2
        part = lax.bitwise_and(start, LANES - 1)
        turn = lax.bitwise_and(LANES - part, LANES - 1)
        here = pltpu.roll(table[pl.ds(first, SUBLANES), :], turn, 1)
        after = pltpu.roll(table[pl.ds(first + 2, SUBLANES), :], turn, 1)
        joined = jnp.where(lane < LANES - part, here, after)
        out[owner] = jnp.where(slot < counts[0, owner], joined, 0.0)

    copies[-2].wait()
    pack_four([latent[row] for row in range(height)], to_partner, to_outer)
    copies[-1].wait()


def behind_of(got, part, cuts, runs, rows_of, *, height, width, radial):
    span = radial // cuts
    pixels = height * width // 2
    classes = cuts * pixels
    shards, rows, _ = got.shape
    bf16 = jnp.bfloat16
    column = lax.broadcasted_iota(jnp.int32, (classes, LANES), 0).astype(jnp.float32).astype(bf16)
    places = [
        (lax.broadcasted_iota(jnp.int32, (LANES, LANES), 1) + (first + 1)).astype(jnp.float32).astype(bf16)
        for first in range(0, span, LANES)
    ]
    zero = jnp.zeros((), bf16)

    def tall(kind, row):
        line = jnp.broadcast_to(rows_of[kind, row:row + 1, :], (16, LANES))
        return jnp.concatenate([line.astype(bf16)] * (classes // 16), axis=0)

    tiles = got[...].reshape(shards * rows, LANES)
    cell = tiles.astype(jnp.int32)
    pixel = lax.shift_right_logical(cell, radial.bit_length() - 1)
    bins = lax.bitwise_and(cell, radial - 1)
    cut = lax.shift_right_logical(bins, span.bit_length() - 1)
    place = lax.bitwise_and(pixel + 2, width - 1)
    own = cut * pixels + lax.shift_right_logical(pixel, 3) * 4 + lax.bitwise_and(place, 3)
    rows_of[0] = jnp.where(lax.shift_right_logical(place, 2) == part, own, classes).astype(jnp.float32)
    lows = jnp.transpose((lax.bitwise_and(bins, span - 1) + 1).astype(jnp.float32)).astype(bf16)
    coarse = tiles.astype(bf16).astype(jnp.float32)
    rows_of[1] = coarse
    rows_of[2] = tiles - coarse

    total = jnp.zeros((2 * classes, span), jnp.float32)
    group = 2 * RUNS // runs
    for first in range(0, shards, group):
        left, right = [], []
        for run in range(group * runs):
            row = (first + run // runs) * rows + run % runs * 2
            mine = tall(0, row + 1) == column
            left.append(jnp.concatenate([jnp.where(mine, tall(kind, row), zero) for kind in (1, 2)], axis=0))
            low = jnp.broadcast_to(lows[:, row + 1:row + 2], (LANES, LANES))
            right.append(jnp.concatenate([jnp.maximum(low, place) for place in places], axis=1))
        total = total + jnp.dot(
            jnp.concatenate(left, axis=1), jnp.concatenate(right, axis=0), preferred_element_type=jnp.float32
        )
    both = (total[:classes] + total[classes:]) * bin_width
    every = both[:, span - 1:] * (1.0 / span)
    lane = lax.broadcasted_iota(jnp.int32, both.shape, 1)
    at_least = jnp.where(lane == 0, every, pltpu.roll(both, 1, 1) - both + every)
    ranges = [at_least[start:start + pixels] for start in range(0, classes, pixels)]
    for k in reversed(range(cuts - 1)):
        ranges[k] = ranges[k] + ranges[k + 1][:, :1]
    return jnp.concatenate(ranges, axis=1)


def column_rows(packed, part, height):
    rows = []
    for row in range(height):
        tile = packed[row // 2 * SUBLANES:(row // 2 + 1) * SUBLANES]
        turn = row % 2 * 4 + (2 if part == 0 else SUBLANES - 2)
        rows.append(pltpu.roll(tile, (SUBLANES - turn) % SUBLANES, 0))
    return rows


def for_load(body):
    lat, count = lax.axis_index("lat"), lax.axis_size("lat")
    middle = (lat >= count // 4) & (lat < count - count // 4)
    pl.when(middle)(lambda: body(RUNS))
    pl.when(jnp.logical_not(middle))(lambda: body(LEAST // LANES))


def bin_sides_kernel(got, _, behind, to_partner, to_outer, rows_of):
    height, width, radial = behind.shape

    def body(runs):
        packed = behind_of(got, 0, 2, runs, rows_of, height=height, width=width, radial=radial)
        lines = column_rows(packed, 0, height)
        for row, values in enumerate(lines):
            behind[row] = values
        pack_sides(lines, to_partner, to_outer)

    for_load(body)


def bin_rest_kernel(got, density, behind, upstream, rows_of):
    height, width, radial = behind.shape
    sub = sublane(radial)

    def body(runs):
        packed = behind_of(got, 1, 2, runs, rows_of, height=height, width=width, radial=radial)
        for row, values in enumerate(column_rows(packed, 1, height)):
            upstream[row] = density[row, :width] * jnp.where((sub < 2) | (sub >= 6), behind[row], values)

    for_load(body)


def mirror(stencils):
    turned = jnp.flip(stencils, axis=1).reshape(stencils.shape[0], 9, 3, stencils.shape[2])
    edge = jnp.zeros_like(turned[:, :, 0, :1])
    back = jnp.concatenate([edge, turned[:, :, 0, :-1]], axis=-1)
    ahead = jnp.concatenate([turned[:, :, 2, 1:], edge], axis=-1)
    return jnp.stack([back, turned[:, :, 1], ahead], axis=2).reshape(stencils.shape)


def swap(to_partner, to_outer, axis, closed, outer_first=False):
    count = lax.axis_size(axis)
    outer = [(i, (i + 1) % count) for i in range(1, count, 2) if closed or i + 1 < count]
    inner = [(i, i + 1) for i in range(0, count - 1, 2)]

    def both_ways(pairs):
        return pairs + [(j, i) for i, j in pairs]

    moves = [(to_partner, inner), (to_outer, outer)]
    got = [lax.ppermute(values, axis, both_ways(pairs)) for values, pairs in moves[::-1 if outer_first else 1]]
    return tuple(got[::-1 if outer_first else 1])


VMEM = pl.BlockSpec(memory_space=pltpu.VMEM)
HBM = pl.BlockSpec(memory_space=pltpu.HBM)
LIMIT = pltpu.CompilerParams(vmem_limit_bytes=32 * 1024 * 1024)


def on_device(residual, star_pixel, star_bin, send_counts, send_offsets, latent, stencils):
    height, width, radial = latent.shape
    shards = send_counts.shape[1]
    slots = residual.shape[0]
    f32 = jnp.float32
    i32 = jnp.int32
    tile = jax.ShapeDtypeStruct((height, width, radial), f32)
    sides = jax.ShapeDtypeStruct((height // 4, SUBLANES, radial), f32)
    ends = jax.ShapeDtypeStruct((4, SUBLANES, radial), f32)

    def table(values):
        return values.reshape(slots // LANES, LANES)

    four = jax.ShapeDtypeStruct((height // 2, SUBLANES, radial), f32)
    taps = jax.ShapeDtypeStruct((stencils.shape[1], stencils.shape[0], radial), f32)
    packed, latent, *to_sides, taps = pl.pallas_call(
        open_kernel,
        out_shape=(jax.ShapeDtypeStruct((shards, 2 * RUNS, LANES), f32), tile, four, four, taps),
        in_specs=[HBM] * 7,
        out_specs=(VMEM,) * 5,
        scratch_shapes=[pltpu.SMEM((1, shards), i32)] * 2
        + [pltpu.VMEM((slots // LANES, LANES), kind) for kind in (f32, i32, i32)]
        + [pltpu.VMEM((2 * slots // LANES, LANES), f32)]
        + [pltpu.SemaphoreType.DMA((7,))],
        compiler_params=LIMIT,
        name="opening",
    )(*[
        pltpu.with_memory_space_constraint(values, pltpu.HBM)
        for values in (send_counts, send_offsets, table(residual), table(star_pixel), table(star_bin), latent, stencils.transpose(1, 0, 2))
    ])
    got = lax.all_to_all(packed, ("lat", "lon"), split_axis=0, concat_axis=0, tiled=True)

    rows = pltpu.VMEM((height, 2 * width, radial), f32)
    moved = pltpu.VMEM((2, height, 2 * width, radial), f32)
    edge = (3, 3, 4, width, radial)
    star_rows = [pltpu.VMEM((3, shards * 2 * RUNS, LANES), f32)]
    inner_rows = (3, 3, height - 2, width, radial)

    def call(kernel, name, outs, scratch, *operands):
        return pl.pallas_call(
            kernel,
            out_shape=outs,
            in_specs=[VMEM] * len(operands),
            out_specs=jax.tree.map(lambda _: VMEM, outs),
            scratch_shapes=scratch,
            compiler_params=LIMIT,
            name=name,
        )(*operands)

    def shape(*sizes):
        return jax.ShapeDtypeStruct(sizes, f32)

    beside = swap(*to_sides, "lon", True)
    to_ends = call(pack_ends_kernel, "density_pack", (ends, ends), [], latent, *beside)
    above = swap(*to_ends, "lat", False, outer_first=True)
    broad = 2 * width
    stencils = taps.transpose(1, 0, 2)
    mirrored = mirror(stencils)[::-1]
    inner, middle = call(
        density_inside_kernel, "density_inside",
        (shape(height - 4, broad, radial), shape(3, 3, height - 2, broad, radial)), [rows, moved],
        latent, *beside, stencils,
    )
    behind, *to_sides = call(bin_sides_kernel, "bin_sides", (tile, sides, sides), star_rows, got, inner)
    density = call(
        density_ends_kernel, "density_ends", shape(height, broad, radial),
        [pltpu.VMEM((3, 3, 4, broad, radial), f32), rows, moved],
        latent, *beside, *above[::-1], stencils, middle, inner, behind,
    )
    upstream = call(bin_rest_kernel, "bin_rest", tile, star_rows, got, density, behind)

    beside = swap(*to_sides, "lon", True, outer_first=True)
    *to_ends, middle = call(
        back_reach_kernel, "back_reach", (shape(2, width, radial), shape(2, width, radial), shape(*edge)),
        [rows, moved, pltpu.VMEM((4, width, radial), f32)], upstream, *beside[::-1], density, mirrored,
    )
    above = swap(*to_ends, "lat", False)
    own = call(
        back_own_kernel, "back_own", tile, [rows, moved, pltpu.VMEM(inner_rows, f32)],
        upstream, *beside[::-1], density, mirrored, latent, middle,
    )
    return pl.pallas_call(
        close_kernel,
        out_shape=tile,
        in_specs=[VMEM] * 3,
        out_specs=HBM,
        scratch_shapes=[pltpu.VMEM((2, width, radial), f32)] * 2 + [pltpu.SemaphoreType.DMA((3,))],
        compiler_params=LIMIT,
        name="close",
    )(own, *above)


def solution(mesh):
    return jax.shard_map(
        on_device,
        mesh=mesh,
        in_specs=(
            P(("lat", "lon")),
            P(("lat", "lon")),
            P(("lat", "lon")),
            P(("lat", "lon"), None),
            P(("lat", "lon"), None),
            P("lat", "lon", None),
            P(),
        ),
        out_specs=P("lat", "lon", None),
        check_vma=False,
    )
```

```python
import functools

import jax
import jax.numpy as jnp
from jax import lax
from jax.experimental import pallas as pl
from jax.experimental.pallas import tpu as pltpu
from jax.sharding import PartitionSpec as P

CAP = 512
LEAST = 128
LANES = 128
SUBLANES = 8
RUNS = CAP // LANES
bin_width = 0.0625


def position(axis):
    index = lax.axis_index(axis)
    return index, lax.bitwise_and(index, 1)


def either(flag, if_set, if_clear):
    return jnp.where(jnp.full(if_set.shape, flag, jnp.int32) > 0, if_set, if_clear)


def sublane(radial):
    return lax.broadcasted_iota(jnp.int32, (SUBLANES, radial), 0)


def pack_sides(rows, to_partner, to_outer):
    _, odd = position("lon")
    sub = sublane(rows[0].shape[1])
    for group in range(len(rows) // 4):
        before, after = rows[4 * group], rows[4 * group]
        for k in range(1, 4):
            row = rows[4 * group + k]
            pair = lax.shift_right_logical(sub, 1)
            before = jnp.where(pair == k, pltpu.roll(row, 2 * k, 0), before)
            after = jnp.where(pair == 3 - k, pltpu.roll(row, SUBLANES - 2 * k, 0), after)
        to_partner[group] = either(odd, before, after)
        to_outer[group] = either(odd, after, before)


def unpack_sides(from_partner, from_outer, height):
    _, odd = position("lon")
    sub = sublane(from_partner.shape[2])
    tiles = []
    for group in range(height // 4):
        partner, outer = from_partner[group], from_outer[group]
        before, after = either(odd, partner, outer), either(odd, outer, partner)
        for k in range(4):
            if k:
                tiles.append(jnp.where(sub < 4, pltpu.roll(after, SUBLANES - 2 * k, 0), pltpu.roll(before, 2 * k, 0)))
            else:
                tiles.append(jnp.where(sub < 4, after, before))
    return tiles


def pack_four(rows, to_partner, to_outer):
    _, odd = position("lon")
    sub = sublane(rows[0].shape[1])
    for group in range(len(rows) // 2):
        one, two = rows[2 * group], pltpu.roll(rows[2 * group + 1], 4, 0)
        before, after = jnp.where(sub < 4, one, two), jnp.where(sub < 4, two, one)
        to_partner[group] = either(odd, before, after)
        to_outer[group] = either(odd, after, before)


def unpack_four(from_partner, from_outer, height):
    _, odd = position("lon")
    sub = sublane(from_partner.shape[2])
    tiles = []
    for group in range(height // 2):
        partner, outer = from_partner[group], from_outer[group]
        before, after = either(odd, partner, outer), either(odd, outer, partner)
        tiles.append(jnp.where(sub < 4, after, before))
        tiles.append(pltpu.roll(jnp.where(sub < 4, before, after), 4, 0))
    return tiles


def pack_ends_kernel(field, side_0, side_1, to_partner, to_outer):
    height = field.shape[0]
    _, odd = position("lat")
    tiles = unpack_four(side_0, side_1, height)
    top = [field[0], field[1], tiles[0], tiles[1]]
    bottom = [field[height - 2], field[height - 1], tiles[height - 2], tiles[height - 1]]
    for place, (one, two) in enumerate(zip(top, bottom)):
        to_partner[place] = either(odd, one, two)
        to_outer[place] = either(odd, two, one)


def radial_shifts(field):
    radial = field.shape[-1]
    lane = lax.broadcasted_iota(jnp.int32, field.shape, field.ndim - 1)
    return (
        jnp.where(lane == 0, 0.0, pltpu.roll(field, 1, field.ndim - 1)),
        jnp.where(lane == radial - 1, 0.0, pltpu.roll(field, radial - 1, field.ndim - 1)),
    )


def taps_of(coef, at):
    return [jnp.broadcast_to(coef[k:k + 1, at], (SUBLANES, LANES)) for k in range(27)]


def tiles_of_bins(radial, body):
    for start in range(0, radial, LANES):
        body(slice(start, start + LANES))


ALL = (-1, 0, 1)


def first_level(wide, shifted, coef, centers, middle, real):
    _, cols, radial = wide.shape
    for row in sorted({row + above for row, around in centers for above in around}):
        for place, moved in enumerate(radial_shifts(wide[row])):
            shifted[place, row] = moved

    def body(at):
        taps = taps_of(coef, at)
        for place, (row, around) in enumerate(centers):
            parts = []
            for side in (slice(0, SUBLANES), slice(SUBLANES, cols)):
                sums = [None, None, None]
                for above in around:
                    window = (shifted[0, row + above, side, at], wide[row + above, side, at], shifted[1, row + above, side, at])
                    for beside in range(3):
                        for step in range(3):
                            term = taps[(above + 1) * 9 + beside * 3 + step] * window[step]
                            sums[beside] = term if sums[beside] is None else sums[beside] + term
                parts.append(sums)
            whole = [jnp.concatenate([parts[0][b], parts[1][b]], axis=0) for b in range(3)]
            value = whole[1] + pltpu.roll(whole[0], 1, 0) + pltpu.roll(whole[2], cols - 1, 0)
            if real[place] is not None:
                value = either(real[place], value, jnp.zeros_like(value))
            kept = middle.shape[3]
            middle[0, 1, place, :, at] = pltpu.roll(value, 1, 0)[:kept]
            middle[1, 1, place, :, at] = value[:kept]
            middle[2, 1, place, :, at] = pltpu.roll(value, cols - 1, 0)[:kept]

    tiles_of_bins(radial, body)
    for place in range(len(centers)):
        for beside in range(3):
            for step, moved in zip((0, 2), radial_shifts(middle[beside, 1, place])):
                middle[beside, step, place] = moved


def second_level(coef, windows, radial, write, cols=SUBLANES):
    def body(at):
        taps = taps_of(coef, at)
        for row, around in windows.items():
            for start in range(0, cols, SUBLANES):
                side = slice(start, start + SUBLANES)
                total = None
                for above, at_row in enumerate(around):
                    if at_row is None:
                        continue
                    buffer, place = at_row
                    for beside in range(3):
                        for step in range(3):
                            term = taps[above * 9 + beside * 3 + step] * buffer[beside, step, place, side, at]
                            total = term if total is None else total + term
                write(row, side, at, total)

    tiles_of_bins(radial, body)


def fill_wide(wide, field, tiles, rows):
    width = field.shape[1]
    for row in rows:
        wide[row, :width] = field[row]
        wide[row, width:] = tiles[row]


def density_inside_kernel(field, side_0, side_1, stencils, out, middle, wide, shifted):
    height, _, radial = field.shape
    fill_wide(wide, field, unpack_four(side_0, side_1, height), range(height))
    centers = [(row, ALL) for row in range(1, height - 1)]
    first_level(wide, shifted, stencils.at[0], centers, middle, [None] * len(centers))

    def write(row, side, at, value):
        out[row - 2, side, at] = jnp.exp(value)

    windows = {row: [(middle, row - 2 + k) for k in range(3)] for row in range(2, height - 2)}
    second_level(stencils.at[1], windows, radial, write, wide.shape[1])


def density_ends_kernel(
    field, side_0, side_1, end_1, end_0, stencils, inside, inner, _, out, middle, wide, shifted
):
    height, width, radial = field.shape
    tiles = unpack_four(side_0, side_1, height)
    lat, odd = position("lat")
    for place in range(2):
        for half in range(2):
            partner, outer = end_0[2 * half + place], end_1[2 * half + place]
            at = slice(half * width, (half + 1) * width)
            wide[place, at] = either(odd, partner, outer)
            wide[6 + place, at] = either(odd, outer, partner)
    for place, row in ((2, 0), (3, 1), (4, height - 2), (5, height - 1)):
        wide[place, :width] = field[row]
        wide[place, width:] = tiles[row]
    above = (lat > 0).astype(jnp.int32)
    below = (lat < lax.axis_size("lat") - 1).astype(jnp.int32)
    centers = [(row, ALL) for row in (1, 2, 5, 6)]
    first_level(wide, shifted, stencils.at[0], centers, middle, [above, None, None, below])

    def write(row, side, at, value):
        out[row, side, at] = jnp.exp(value)

    last = height - 3
    top = [(middle, 0), (middle, 1), (inside, 0), (inside, 1)]
    bottom = [(inside, last - 1), (inside, last), (middle, 2), (middle, 3)]
    windows = {0: top[:3], 1: top[1:], height - 2: bottom[:3], height - 1: bottom[1:]}
    second_level(stencils.at[1], windows, radial, write, wide.shape[1])
    for row in range(2, height - 2):
        out[row] = inner[row - 2]


def beside_tiles(side_0, side_1, density):
    tiles = unpack_sides(side_0, side_1, density.shape[0])
    return [tile * density[row, SUBLANES:] for row, tile in enumerate(tiles)]


def back_reach_kernel(field, side_1, side_0, density, stencils, to_partner, to_outer, middle, wide, shifted, reach):
    height, _, radial = field.shape
    last = height - 1
    fill_wide(wide, field, beside_tiles(side_0, side_1, density), (0, 1, last - 1, last))
    lat, odd = position("lat")
    above = (lat > 0).astype(jnp.int32)
    below = (lat < lax.axis_size("lat") - 1).astype(jnp.int32)
    centers = [(-1, (1,)), (0, (0, 1)), (last, (-1, 0)), (last + 1, (-1,))]
    first_level(wide, shifted, stencils.at[0], centers, middle, [above, None, None, below])

    def write(row, side, at, value):
        reach[row, side, at] = value

    windows = {
        0: [None, None, (middle, 0)],
        1: [None, (middle, 0), (middle, 1)],
        2: [(middle, 2), (middle, 3), None],
        3: [(middle, 3), None, None],
    }
    second_level(stencils.at[1], windows, radial, write)
    for place in range(2):
        to_partner[place] = either(odd, reach[place], reach[2 + place])
        to_outer[place] = either(odd, reach[2 + place], reach[place])


def back_own_kernel(field, side_1, side_0, density, stencils, latent, edge, out, wide, shifted, middle):
    height, _, radial = field.shape
    fill_wide(wide, field, beside_tiles(side_0, side_1, density), range(height))
    centers = [(row, ALL) for row in range(1, height - 1)]
    first_level(wide, shifted, stencils.at[0], centers, middle, [None] * len(centers))

    def write(row, side, at, value):
        out[row, side, at] = latent[row, side, at] + value

    line = [(edge, 0), (edge, 1)] + [(middle, place) for place in range(height - 2)] + [(edge, 2), (edge, 3)]
    second_level(stencils.at[1], {row: line[row:row + 3] for row in range(height)}, radial, write)


def close_kernel(own, end_0, end_1, out, top, bottom, sent):
    height = own.shape[0]
    last = height - 2
    pairs = ((own.at[2:last], out.at[2:last]), (top, out.at[:2]), (bottom, out.at[last:]))
    copies = [pltpu.make_async_copy(source, target, sent.at[i]) for i, (source, target) in enumerate(pairs)]
    copies[0].start()
    _, odd = position("lat")
    for place in range(2):
        top[place] = own[place] + either(odd, end_0[place], end_1[place])
    copies[1].start()
    for place in range(2):
        bottom[place] = own[last + place] + either(odd, end_1[place], end_0[place])
    copies[2].start()
    for copy in copies:
        copy.wait()


def open_kernel(
    counts_in, offsets_in, residual_in, pixel_in, bins_in, latent_in, taps_in, out, latent, to_partner, to_outer, taps,
    counts, offsets, residual, pixel, bins, table, arrived,
):
    pairs = (
        (counts_in, counts), (offsets_in, offsets), (residual_in, residual), (pixel_in, pixel), (bins_in, bins),
        (latent_in, latent), (taps_in, taps),
    )
    copies = [pltpu.make_async_copy(source, target, arrived.at[i]) for i, (source, target) in enumerate(pairs)]
    for copy in copies:
        copy.start()
    for copy in copies[:-2]:
        copy.wait()
    height, _, radial = latent.shape
    length = residual.shape[0]
    table[pl.ds(0, length, stride=2), :] = residual[...]
    table[pl.ds(1, length, stride=2), :] = (pixel[...] * radial + bins[...]).astype(jnp.float32)

    lane = lax.broadcasted_iota(jnp.int32, (SUBLANES, LANES), 1)
    row = lax.broadcasted_iota(jnp.int32, (SUBLANES, LANES), 0)
    slot = lax.shift_right_logical(row, 1) * LANES + lane
    for owner in range(out.shape[0]):
        start = offsets[0, owner]
        first = lax.shift_right_logical(start, 7) * 2
        part = lax.bitwise_and(start, LANES - 1)
        turn = lax.bitwise_and(LANES - part, LANES - 1)
        here = pltpu.roll(table[pl.ds(first, SUBLANES), :], turn, 1)
        after = pltpu.roll(table[pl.ds(first + 2, SUBLANES), :], turn, 1)
        joined = jnp.where(lane < LANES - part, here, after)
        out[owner] = jnp.where(slot < counts[0, owner], joined, 0.0)

    copies[-2].wait()
    pack_four([latent[row] for row in range(height)], to_partner, to_outer)
    copies[-1].wait()


def behind_of(got, part, cuts, runs, rows_of, *, height, width, radial):
    span = radial // cuts
    pixels = height * width // 2
    classes = cuts * pixels
    shards, rows, _ = got.shape
    bf16 = jnp.bfloat16
    column = lax.broadcasted_iota(jnp.int32, (classes, LANES), 0).astype(jnp.float32).astype(bf16)
    places = [
        (lax.broadcasted_iota(jnp.int32, (LANES, LANES), 1) + (first + 1)).astype(jnp.float32).astype(bf16)
        for first in range(0, span, LANES)
    ]
    zero = jnp.zeros((), bf16)

    def tall(kind, row):
        line = jnp.broadcast_to(rows_of[kind, row:row + 1, :], (16, LANES))
        return jnp.concatenate([line.astype(bf16)] * (classes // 16), axis=0)

    tiles = got[...].reshape(shards * rows, LANES)
    cell = tiles.astype(jnp.int32)
    pixel = lax.shift_right_logical(cell, radial.bit_length() - 1)
    bins = lax.bitwise_and(cell, radial - 1)
    cut = lax.shift_right_logical(bins, span.bit_length() - 1)
    place = lax.bitwise_and(pixel + 2, width - 1)
    own = cut * pixels + lax.shift_right_logical(pixel, 3) * 4 + lax.bitwise_and(place, 3)
    rows_of[0] = jnp.where(lax.shift_right_logical(place, 2) == part, own, classes).astype(jnp.float32)
    lows = jnp.transpose((lax.bitwise_and(bins, span - 1) + 1).astype(jnp.float32)).astype(bf16)
    coarse = tiles.astype(bf16).astype(jnp.float32)
    rows_of[1] = coarse
    rows_of[2] = tiles - coarse

    sums = [jnp.zeros((2 * classes, span), jnp.float32) for _ in range(2)]
    group = 2 * RUNS // runs
    for turn, first in enumerate(range(0, shards, group)):
        left, right = [], []
        for run in range(group * runs):
            row = (first + run // runs) * rows + run % runs * 2
            mine = tall(0, row + 1) == column
            left.append(jnp.concatenate([jnp.where(mine, tall(kind, row), zero) for kind in (1, 2)], axis=0))
            low = jnp.broadcast_to(lows[:, row + 1:row + 2], (LANES, LANES))
            right.append(jnp.concatenate([jnp.maximum(low, place) for place in places], axis=1))
        sums[turn % 2] = sums[turn % 2] + jnp.dot(
            jnp.concatenate(left, axis=1), jnp.concatenate(right, axis=0), preferred_element_type=jnp.float32
        )
    total = sums[0] + sums[1]
    both = (total[:classes] + total[classes:]) * bin_width
    every = both[:, span - 1:] * (1.0 / span)
    lane = lax.broadcasted_iota(jnp.int32, both.shape, 1)
    at_least = jnp.where(lane == 0, every, pltpu.roll(both, 1, 1) - both + every)
    ranges = [at_least[start:start + pixels] for start in range(0, classes, pixels)]
    for k in reversed(range(cuts - 1)):
        ranges[k] = ranges[k] + ranges[k + 1][:, :1]
    return jnp.concatenate(ranges, axis=1)


def column_rows(packed, part, height):
    rows = []
    for row in range(height):
        tile = packed[row // 2 * SUBLANES:(row // 2 + 1) * SUBLANES]
        turn = row % 2 * 4 + (2 if part == 0 else SUBLANES - 2)
        rows.append(pltpu.roll(tile, (SUBLANES - turn) % SUBLANES, 0))
    return rows


def for_load(body):
    lat, count = lax.axis_index("lat"), lax.axis_size("lat")
    middle = (lat >= count // 4) & (lat < count - count // 4)
    pl.when(middle)(lambda: body(RUNS))
    pl.when(jnp.logical_not(middle))(lambda: body(LEAST // LANES))


def bin_sides_kernel(got, _, behind, to_partner, to_outer, rows_of):
    height, width, radial = behind.shape

    def body(runs):
        packed = behind_of(got, 0, 2, runs, rows_of, height=height, width=width, radial=radial)
        lines = column_rows(packed, 0, height)
        for row, values in enumerate(lines):
            behind[row] = values
        pack_sides(lines, to_partner, to_outer)

    for_load(body)


def bin_rest_kernel(got, density, behind, upstream, rows_of):
    height, width, radial = behind.shape
    sub = sublane(radial)

    def body(runs):
        packed = behind_of(got, 1, 2, runs, rows_of, height=height, width=width, radial=radial)
        for row, values in enumerate(column_rows(packed, 1, height)):
            upstream[row] = density[row, :width] * jnp.where((sub < 2) | (sub >= 6), behind[row], values)

    for_load(body)


def mirror(stencils):
    turned = jnp.flip(stencils, axis=1).reshape(stencils.shape[0], 9, 3, stencils.shape[2])
    edge = jnp.zeros_like(turned[:, :, 0, :1])
    back = jnp.concatenate([edge, turned[:, :, 0, :-1]], axis=-1)
    ahead = jnp.concatenate([turned[:, :, 2, 1:], edge], axis=-1)
    return jnp.stack([back, turned[:, :, 1], ahead], axis=2).reshape(stencils.shape)


def swap(to_partner, to_outer, axis, closed, outer_first=False):
    count = lax.axis_size(axis)
    outer = [(i, (i + 1) % count) for i in range(1, count, 2) if closed or i + 1 < count]
    inner = [(i, i + 1) for i in range(0, count - 1, 2)]

    def both_ways(pairs):
        return pairs + [(j, i) for i, j in pairs]

    moves = [(to_partner, inner), (to_outer, outer)]
    got = [lax.ppermute(values, axis, both_ways(pairs)) for values, pairs in moves[::-1 if outer_first else 1]]
    return tuple(got[::-1 if outer_first else 1])


VMEM = pl.BlockSpec(memory_space=pltpu.VMEM)
HBM = pl.BlockSpec(memory_space=pltpu.HBM)
LIMIT = pltpu.CompilerParams(vmem_limit_bytes=32 * 1024 * 1024)


def on_device(residual, star_pixel, star_bin, send_counts, send_offsets, latent, stencils):
    height, width, radial = latent.shape
    shards = send_counts.shape[1]
    slots = residual.shape[0]
    f32 = jnp.float32
    i32 = jnp.int32
    tile = jax.ShapeDtypeStruct((height, width, radial), f32)
    sides = jax.ShapeDtypeStruct((height // 4, SUBLANES, radial), f32)
    ends = jax.ShapeDtypeStruct((4, SUBLANES, radial), f32)

    def table(values):
        return values.reshape(slots // LANES, LANES)

    four = jax.ShapeDtypeStruct((height // 2, SUBLANES, radial), f32)
    taps = jax.ShapeDtypeStruct((stencils.shape[1], stencils.shape[0], radial), f32)
    packed, latent, *to_sides, taps = pl.pallas_call(
        open_kernel,
        out_shape=(jax.ShapeDtypeStruct((shards, 2 * RUNS, LANES), f32), tile, four, four, taps),
        in_specs=[HBM] * 7,
        out_specs=(VMEM,) * 5,
        scratch_shapes=[pltpu.SMEM((1, shards), i32)] * 2
        + [pltpu.VMEM((slots // LANES, LANES), kind) for kind in (f32, i32, i32)]
        + [pltpu.VMEM((2 * slots // LANES, LANES), f32)]
        + [pltpu.SemaphoreType.DMA((7,))],
        compiler_params=LIMIT,
        name="opening",
    )(*[
        pltpu.with_memory_space_constraint(values, pltpu.HBM)
        for values in (send_counts, send_offsets, table(residual), table(star_pixel), table(star_bin), latent, stencils.transpose(1, 0, 2))
    ])
    got = lax.all_to_all(packed, ("lat", "lon"), split_axis=0, concat_axis=0, tiled=True)

    rows = pltpu.VMEM((height, 2 * width, radial), f32)
    moved = pltpu.VMEM((2, height, 2 * width, radial), f32)
    edge = (3, 3, 4, width, radial)
    star_rows = [pltpu.VMEM((3, shards * 2 * RUNS, LANES), f32)]
    inner_rows = (3, 3, height - 2, width, radial)

    def call(kernel, name, outs, scratch, *operands):
        return pl.pallas_call(
            kernel,
            out_shape=outs,
            in_specs=[VMEM] * len(operands),
            out_specs=jax.tree.map(lambda _: VMEM, outs),
            scratch_shapes=scratch,
            compiler_params=LIMIT,
            name=name,
        )(*operands)

    def shape(*sizes):
        return jax.ShapeDtypeStruct(sizes, f32)

    beside = swap(*to_sides, "lon", True)
    to_ends = call(pack_ends_kernel, "density_pack", (ends, ends), [], latent, *beside)
    above = swap(*to_ends, "lat", False, outer_first=True)
    broad = 2 * width
    stencils = taps.transpose(1, 0, 2)
    mirrored = mirror(stencils)[::-1]
    inner, middle = call(
        density_inside_kernel, "density_inside",
        (shape(height - 4, broad, radial), shape(3, 3, height - 2, broad, radial)), [rows, moved],
        latent, *beside, stencils,
    )
    behind, *to_sides = call(bin_sides_kernel, "bin_sides", (tile, sides, sides), star_rows, got, inner)
    density = call(
        density_ends_kernel, "density_ends", shape(height, broad, radial),
        [pltpu.VMEM((3, 3, 4, broad, radial), f32), rows, moved],
        latent, *beside, *above[::-1], stencils, middle, inner, behind,
    )
    upstream = call(bin_rest_kernel, "bin_rest", tile, star_rows, got, density, behind)

    beside = swap(*to_sides, "lon", True, outer_first=True)
    *to_ends, middle = call(
        back_reach_kernel, "back_reach", (shape(2, width, radial), shape(2, width, radial), shape(*edge)),
        [rows, moved, pltpu.VMEM((4, width, radial), f32)], upstream, *beside[::-1], density, mirrored,
    )
    above = swap(*to_ends, "lat", False)
    own = call(
        back_own_kernel, "back_own", tile, [rows, moved, pltpu.VMEM(inner_rows, f32)],
        upstream, *beside[::-1], density, mirrored, latent, middle,
    )
    return pl.pallas_call(
        close_kernel,
        out_shape=tile,
        in_specs=[VMEM] * 3,
        out_specs=HBM,
        scratch_shapes=[pltpu.VMEM((2, width, radial), f32)] * 2 + [pltpu.SemaphoreType.DMA((3,))],
        compiler_params=LIMIT,
        name="close",
    )(own, *above)


def solution(mesh):
    return jax.shard_map(
        on_device,
        mesh=mesh,
        in_specs=(
            P(("lat", "lon")),
            P(("lat", "lon")),
            P(("lat", "lon")),
            P(("lat", "lon"), None),
            P(("lat", "lon"), None),
            P("lat", "lon", None),
            P(),
        ),
        out_specs=P("lat", "lon", None),
        check_vma=False,
    )
```

```python
import functools

import jax
import jax.numpy as jnp
from jax import lax
from jax.experimental import pallas as pl
from jax.experimental.pallas import tpu as pltpu
from jax.sharding import PartitionSpec as P

CAP = 512
LEAST = 128
LANES = 128
SUBLANES = 8
RUNS = CAP // LANES
bin_width = 0.0625


def position(axis):
    index = lax.axis_index(axis)
    return index, lax.bitwise_and(index, 1)


def either(flag, if_set, if_clear):
    return jnp.where(jnp.full(if_set.shape, flag, jnp.int32) > 0, if_set, if_clear)


def sublane(radial):
    return lax.broadcasted_iota(jnp.int32, (SUBLANES, radial), 0)


def unpack_sides(from_partner, from_outer, height):
    _, odd = position("lon")
    sub = sublane(from_partner.shape[2])
    tiles = []
    for group in range(height // 4):
        partner, outer = from_partner[group], from_outer[group]
        before, after = either(odd, partner, outer), either(odd, outer, partner)
        for k in range(4):
            ahead = pltpu.roll(after, -2 * k % SUBLANES, 0)
            tiles.append(jnp.where(sub < 4, ahead, pltpu.roll(before, SUBLANES - 2 - 2 * k, 0)))
    return tiles


def pack_four(rows, to_partner, to_outer):
    _, odd = position("lon")
    sub = sublane(rows[0].shape[1])
    for group in range(len(rows) // 2):
        one, two = rows[2 * group], pltpu.roll(rows[2 * group + 1], 4, 0)
        before, after = jnp.where(sub < 4, one, two), jnp.where(sub < 4, two, one)
        to_partner[group] = either(odd, before, after)
        to_outer[group] = either(odd, after, before)


def unpack_four(from_partner, from_outer, height):
    _, odd = position("lon")
    sub = sublane(from_partner.shape[2])
    tiles = []
    for group in range(height // 2):
        partner, outer = from_partner[group], from_outer[group]
        before, after = either(odd, partner, outer), either(odd, outer, partner)
        tiles.append(jnp.where(sub < 4, after, before))
        tiles.append(pltpu.roll(jnp.where(sub < 4, before, after), 4, 0))
    return tiles


def pack_ends_kernel(field, side_0, side_1, to_partner, to_outer):
    height = field.shape[0]
    _, odd = position("lat")
    tiles = unpack_four(side_0, side_1, height)
    top = [field[0], field[1], tiles[0], tiles[1]]
    bottom = [field[height - 2], field[height - 1], tiles[height - 2], tiles[height - 1]]
    for place, (one, two) in enumerate(zip(top, bottom)):
        to_partner[place] = either(odd, one, two)
        to_outer[place] = either(odd, two, one)


def radial_shifts(field):
    radial = field.shape[-1]
    lane = lax.broadcasted_iota(jnp.int32, field.shape, field.ndim - 1)
    return (
        jnp.where(lane == 0, 0.0, pltpu.roll(field, 1, field.ndim - 1)),
        jnp.where(lane == radial - 1, 0.0, pltpu.roll(field, radial - 1, field.ndim - 1)),
    )


def taps_of(coef, at):
    return [jnp.broadcast_to(coef[k:k + 1, at], (SUBLANES, LANES)) for k in range(27)]


def tiles_of_bins(radial, body):
    for start in range(0, radial, LANES):
        body(slice(start, start + LANES))


ALL = (-1, 0, 1)


def first_level(wide, shifted, coef, centers, middle, real):
    _, cols, radial = wide.shape
    for row in sorted({row + above for row, around in centers for above in around}):
        for place, moved in enumerate(radial_shifts(wide[row])):
            shifted[place, row] = moved

    def body(at):
        taps = taps_of(coef, at)
        for place, (row, around) in enumerate(centers):
            parts = []
            for side in (slice(0, SUBLANES), slice(SUBLANES, cols)):
                sums = [None, None, None]
                for above in around:
                    window = (shifted[0, row + above, side, at], wide[row + above, side, at], shifted[1, row + above, side, at])
                    for beside in range(3):
                        for step in range(3):
                            term = taps[(above + 1) * 9 + beside * 3 + step] * window[step]
                            sums[beside] = term if sums[beside] is None else sums[beside] + term
                parts.append(sums)
            whole = [jnp.concatenate([parts[0][b], parts[1][b]], axis=0) for b in range(3)]
            value = whole[1] + pltpu.roll(whole[0], 1, 0) + pltpu.roll(whole[2], cols - 1, 0)
            if real[place] is not None:
                value = either(real[place], value, jnp.zeros_like(value))
            kept = middle.shape[3]
            middle[0, 1, place, :, at] = pltpu.roll(value, 1, 0)[:kept]
            middle[1, 1, place, :, at] = value[:kept]
            middle[2, 1, place, :, at] = pltpu.roll(value, cols - 1, 0)[:kept]

    tiles_of_bins(radial, body)
    for place in range(len(centers)):
        for beside in range(3):
            for step, moved in zip((0, 2), radial_shifts(middle[beside, 1, place])):
                middle[beside, step, place] = moved


def second_level(coef, windows, radial, write, cols=SUBLANES):
    def body(at):
        taps = taps_of(coef, at)
        for row, around in windows.items():
            for start in range(0, cols, SUBLANES):
                side = slice(start, start + SUBLANES)
                total = None
                for above, at_row in enumerate(around):
                    if at_row is None:
                        continue
                    buffer, place = at_row
                    for beside in range(3):
                        for step in range(3):
                            term = taps[above * 9 + beside * 3 + step] * buffer[beside, step, place, side, at]
                            total = term if total is None else total + term
                write(row, side, at, total)

    tiles_of_bins(radial, body)


def fill_wide(wide, field, tiles, rows):
    width = field.shape[1]
    for row in rows:
        wide[row, :width] = field[row]
        wide[row, width:] = tiles[row]


def density_inside_kernel(field, side_0, side_1, stencils, out, middle, wide, shifted):
    height, _, radial = field.shape
    fill_wide(wide, field, unpack_four(side_0, side_1, height), range(height))
    centers = [(row, ALL) for row in range(1, height - 1)]
    first_level(wide, shifted, stencils.at[0], centers, middle, [None] * len(centers))

    def write(row, side, at, value):
        out[row - 2, side, at] = jnp.exp(value)

    windows = {row: [(middle, row - 2 + k) for k in range(3)] for row in range(2, height - 2)}
    second_level(stencils.at[1], windows, radial, write, wide.shape[1])


def density_ends_kernel(
    field, side_0, side_1, end_1, end_0, stencils, inside, inner, _, out, middle, wide, shifted
):
    height, width, radial = field.shape
    tiles = unpack_four(side_0, side_1, height)
    lat, odd = position("lat")
    for place in range(2):
        for half in range(2):
            partner, outer = end_0[2 * half + place], end_1[2 * half + place]
            at = slice(half * width, (half + 1) * width)
            wide[place, at] = either(odd, partner, outer)
            wide[6 + place, at] = either(odd, outer, partner)
    for place, row in ((2, 0), (3, 1), (4, height - 2), (5, height - 1)):
        wide[place, :width] = field[row]
        wide[place, width:] = tiles[row]
    above = (lat > 0).astype(jnp.int32)
    below = (lat < lax.axis_size("lat") - 1).astype(jnp.int32)
    centers = [(row, ALL) for row in (1, 2, 5, 6)]
    first_level(wide, shifted, stencils.at[0], centers, middle, [above, None, None, below])

    def write(row, side, at, value):
        out[row, side, at] = jnp.exp(value)

    last = height - 3
    top = [(middle, 0), (middle, 1), (inside, 0), (inside, 1)]
    bottom = [(inside, last - 1), (inside, last), (middle, 2), (middle, 3)]
    windows = {0: top[:3], 1: top[1:], height - 2: bottom[:3], height - 1: bottom[1:]}
    second_level(stencils.at[1], windows, radial, write, wide.shape[1])
    for row in range(2, height - 2):
        out[row] = inner[row - 2]


def beside_tiles(side_0, side_1, density):
    tiles = unpack_sides(side_0, side_1, density.shape[0])
    return [tile * density[row, SUBLANES:] for row, tile in enumerate(tiles)]


def back_reach_kernel(field, side_1, side_0, density, stencils, to_partner, to_outer, middle, wide, shifted, reach):
    height, _, radial = field.shape
    last = height - 1
    fill_wide(wide, field, beside_tiles(side_0, side_1, density), (0, 1, last - 1, last))
    lat, odd = position("lat")
    above = (lat > 0).astype(jnp.int32)
    below = (lat < lax.axis_size("lat") - 1).astype(jnp.int32)
    centers = [(-1, (1,)), (0, (0, 1)), (last, (-1, 0)), (last + 1, (-1,))]
    first_level(wide, shifted, stencils.at[0], centers, middle, [above, None, None, below])

    def write(row, side, at, value):
        reach[row, side, at] = value

    windows = {
        0: [None, None, (middle, 0)],
        1: [None, (middle, 0), (middle, 1)],
        2: [(middle, 2), (middle, 3), None],
        3: [(middle, 3), None, None],
    }
    second_level(stencils.at[1], windows, radial, write)
    for place in range(2):
        to_partner[place] = either(odd, reach[place], reach[2 + place])
        to_outer[place] = either(odd, reach[2 + place], reach[place])


def back_own_kernel(field, side_1, side_0, density, stencils, latent, edge, out, wide, shifted, middle):
    height, _, radial = field.shape
    fill_wide(wide, field, beside_tiles(side_0, side_1, density), range(height))
    centers = [(row, ALL) for row in range(1, height - 1)]
    first_level(wide, shifted, stencils.at[0], centers, middle, [None] * len(centers))

    def write(row, side, at, value):
        out[row, side, at] = latent[row, side, at] + value

    line = [(edge, 0), (edge, 1)] + [(middle, place) for place in range(height - 2)] + [(edge, 2), (edge, 3)]
    second_level(stencils.at[1], {row: line[row:row + 3] for row in range(height)}, radial, write)


def close_kernel(own, end_0, end_1, out, top, bottom, sent):
    height = own.shape[0]
    last = height - 2
    pairs = ((own.at[2:last], out.at[2:last]), (top, out.at[:2]), (bottom, out.at[last:]))
    copies = [pltpu.make_async_copy(source, target, sent.at[i]) for i, (source, target) in enumerate(pairs)]
    copies[0].start()
    _, odd = position("lat")
    for place in range(2):
        top[place] = own[place] + either(odd, end_0[place], end_1[place])
    copies[1].start()
    for place in range(2):
        bottom[place] = own[last + place] + either(odd, end_1[place], end_0[place])
    copies[2].start()
    for copy in copies:
        copy.wait()


def open_kernel(
    counts_in, offsets_in, residual_in, pixel_in, bins_in, latent_in, taps_in, out, latent, to_partner, to_outer, taps,
    counts, offsets, residual, pixel, bins, table, arrived,
):
    pairs = (
        (counts_in, counts), (offsets_in, offsets), (residual_in, residual), (pixel_in, pixel), (bins_in, bins),
        (latent_in, latent), (taps_in, taps),
    )
    copies = [pltpu.make_async_copy(source, target, arrived.at[i]) for i, (source, target) in enumerate(pairs)]
    for copy in copies:
        copy.start()
    for copy in copies[:-2]:
        copy.wait()
    height, _, radial = latent.shape
    length = residual.shape[0]
    table[pl.ds(0, length, stride=2), :] = residual[...]
    table[pl.ds(1, length, stride=2), :] = (pixel[...] * radial + bins[...]).astype(jnp.float32)

    lane = lax.broadcasted_iota(jnp.int32, (SUBLANES, LANES), 1)
    row = lax.broadcasted_iota(jnp.int32, (SUBLANES, LANES), 0)
    slot = lax.shift_right_logical(row, 1) * LANES + lane
    for owner in range(out.shape[0]):
        start = offsets[0, owner]
        first = lax.shift_right_logical(start, 7) * 2
        part = lax.bitwise_and(start, LANES - 1)
        turn = lax.bitwise_and(LANES - part, LANES - 1)
        here = pltpu.roll(table[pl.ds(first, SUBLANES), :], turn, 1)
        after = pltpu.roll(table[pl.ds(first + 2, SUBLANES), :], turn, 1)
        joined = jnp.where(lane < LANES - part, here, after)
        out[owner] = jnp.where(slot < counts[0, owner], joined, 0.0)

    copies[-2].wait()
    pack_four([latent[row] for row in range(height)], to_partner, to_outer)
    copies[-1].wait()


def behind_of(got, index_of, pixels, runs, rows_of, *, width, radial):
    span = radial // 2
    classes = 2 * pixels
    shards, rows, _ = got.shape
    bf16 = jnp.bfloat16
    column = lax.broadcasted_iota(jnp.int32, (classes, LANES), 0).astype(jnp.float32).astype(bf16)
    places = [
        (lax.broadcasted_iota(jnp.int32, (LANES, LANES), 1) + first).astype(jnp.float32).astype(bf16)
        for first in range(0, span, LANES)
    ]
    zero = jnp.zeros((), bf16)
    one = jnp.ones((), bf16)

    def tall(kind, row):
        line = jnp.broadcast_to(rows_of[kind, row:row + 1, :], (16, LANES))
        return jnp.concatenate([line.astype(bf16)] * (classes // 16), axis=0)

    tiles = got[...].reshape(shards * rows, LANES)
    cell = tiles.astype(jnp.int32)
    pixel = lax.shift_right_logical(cell, radial.bit_length() - 1)
    bins = lax.bitwise_and(cell, radial - 1)
    upper = lax.shift_right_logical(bins, span.bit_length() - 1)
    index = index_of(lax.shift_right_logical(pixel, width.bit_length() - 1), lax.bitwise_and(pixel, width - 1))
    rows_of[0] = jnp.where(index < pixels, upper * pixels + index, classes).astype(jnp.float32)
    lows = jnp.transpose(lax.bitwise_and(bins, span - 1).astype(jnp.float32)).astype(bf16)
    coarse = tiles.astype(bf16).astype(jnp.float32)
    rows_of[1] = coarse
    rows_of[2] = tiles - coarse

    total = jnp.zeros((2 * classes, span), jnp.float32)
    group = 2 * RUNS // runs
    for first in range(0, shards, group):
        left, right = [], []
        for run in range(group * runs):
            row = (first + run // runs) * rows + run % runs * 2
            mine = tall(0, row + 1) == column
            left.append(jnp.concatenate([jnp.where(mine, tall(kind, row), zero) for kind in (1, 2)], axis=0))
            low = jnp.broadcast_to(lows[:, row + 1:row + 2], (LANES, LANES))
            right.append(jnp.concatenate([jnp.where(low >= place, one, zero) for place in places], axis=1))
        total = total + jnp.dot(
            jnp.concatenate(left, axis=1), jnp.concatenate(right, axis=0), preferred_element_type=jnp.float32
        )
    both = (total[:classes] + total[classes:]) * bin_width
    near, far = both[:pixels], both[pixels:]
    return jnp.concatenate([near + far[:, :1], far], axis=1)


def for_load(body):
    lat, count = lax.axis_index("lat"), lax.axis_size("lat")
    middle = (lat >= count // 4) & (lat < count - count // 4)
    pl.when(middle)(lambda: body(RUNS))
    pl.when(jnp.logical_not(middle))(lambda: body(LEAST // LANES))


def bin_sides_kernel(got, _, to_partner, to_outer, rows_of):
    _, odd = position("lon")

    def index_of(row, col):
        side = lax.bitwise_xor(lax.shift_right_logical(col, 2), odd)
        return jnp.where((col < 2) | (col >= 6), side * 16 + row * 2 + lax.bitwise_and(col, 1), 32)

    def body(runs):
        packed = behind_of(got, index_of, 32, runs, rows_of, width=SUBLANES, radial=to_outer.shape[2])
        for place in range(2):
            to_outer[place] = packed[place * SUBLANES:(place + 1) * SUBLANES]
            to_partner[place] = packed[(2 + place) * SUBLANES:(3 + place) * SUBLANES]

    for_load(body)


def bin_rest_kernel(got, density, to_partner, to_outer, upstream, rows_of):
    height, width, radial = upstream.shape
    _, odd = position("lon")
    sub = sublane(radial)

    def body(runs):
        packed = behind_of(
            got, lambda row, col: jnp.where((col >= 2) & (col < 6), row * 4 + col - 2, 32), 32, runs, rows_of,
            width=width, radial=radial,
        )
        for row in range(height):
            group, k = row // 4, row % 4
            partner, outer = to_partner[group], to_outer[group]
            first, last = either(odd, partner, outer), either(odd, outer, partner)
            first = pltpu.roll(first, -2 * k % SUBLANES, 0)
            last = pltpu.roll(last, SUBLANES - 2 - 2 * k, 0)
            inner = packed[row // 2 * SUBLANES:(row // 2 + 1) * SUBLANES]
            inner = pltpu.roll(inner, 6 if row % 2 else 2, 0)
            mine = jnp.where(sub < 2, first, jnp.where(sub < 6, inner, last))
            upstream[row] = density[row, :width] * mine

    for_load(body)


def mirror(stencils):
    turned = jnp.flip(stencils, axis=1).reshape(stencils.shape[0], 9, 3, stencils.shape[2])
    edge = jnp.zeros_like(turned[:, :, 0, :1])
    back = jnp.concatenate([edge, turned[:, :, 0, :-1]], axis=-1)
    ahead = jnp.concatenate([turned[:, :, 2, 1:], edge], axis=-1)
    return jnp.stack([back, turned[:, :, 1], ahead], axis=2).reshape(stencils.shape)


def swap(to_partner, to_outer, axis, closed, outer_first=False):
    count = lax.axis_size(axis)
    outer = [(i, (i + 1) % count) for i in range(1, count, 2) if closed or i + 1 < count]
    inner = [(i, i + 1) for i in range(0, count - 1, 2)]

    def both_ways(pairs):
        return pairs + [(j, i) for i, j in pairs]

    moves = [(to_partner, inner), (to_outer, outer)]
    got = [lax.ppermute(values, axis, both_ways(pairs)) for values, pairs in moves[::-1 if outer_first else 1]]
    return tuple(got[::-1 if outer_first else 1])


VMEM = pl.BlockSpec(memory_space=pltpu.VMEM)
HBM = pl.BlockSpec(memory_space=pltpu.HBM)
LIMIT = pltpu.CompilerParams(vmem_limit_bytes=32 * 1024 * 1024)


def on_device(residual, star_pixel, star_bin, send_counts, send_offsets, latent, stencils):
    height, width, radial = latent.shape
    shards = send_counts.shape[1]
    slots = residual.shape[0]
    f32 = jnp.float32
    i32 = jnp.int32
    tile = jax.ShapeDtypeStruct((height, width, radial), f32)
    sides = jax.ShapeDtypeStruct((height // 4, SUBLANES, radial), f32)
    ends = jax.ShapeDtypeStruct((4, SUBLANES, radial), f32)

    def table(values):
        return values.reshape(slots // LANES, LANES)

    four = jax.ShapeDtypeStruct((height // 2, SUBLANES, radial), f32)
    taps = jax.ShapeDtypeStruct((stencils.shape[1], stencils.shape[0], radial), f32)
    packed, latent, *to_sides, taps = pl.pallas_call(
        open_kernel,
        out_shape=(jax.ShapeDtypeStruct((shards, 2 * RUNS, LANES), f32), tile, four, four, taps),
        in_specs=[HBM] * 7,
        out_specs=(VMEM,) * 5,
        scratch_shapes=[pltpu.SMEM((1, shards), i32)] * 2
        + [pltpu.VMEM((slots // LANES, LANES), kind) for kind in (f32, i32, i32)]
        + [pltpu.VMEM((2 * slots // LANES, LANES), f32)]
        + [pltpu.SemaphoreType.DMA((7,))],
        compiler_params=LIMIT,
        name="opening",
    )(*[
        pltpu.with_memory_space_constraint(values, pltpu.HBM)
        for values in (send_counts, send_offsets, table(residual), table(star_pixel), table(star_bin), latent, stencils.transpose(1, 0, 2))
    ])
    got = lax.all_to_all(packed, ("lat", "lon"), split_axis=0, concat_axis=0, tiled=True)

    rows = pltpu.VMEM((height, 2 * width, radial), f32)
    moved = pltpu.VMEM((2, height, 2 * width, radial), f32)
    edge = (3, 3, 4, width, radial)
    star_rows = [pltpu.VMEM((3, shards * 2 * RUNS, LANES), f32)]
    inner_rows = (3, 3, height - 2, width, radial)

    def call(kernel, name, outs, scratch, *operands):
        return pl.pallas_call(
            kernel,
            out_shape=outs,
            in_specs=[VMEM] * len(operands),
            out_specs=jax.tree.map(lambda _: VMEM, outs),
            scratch_shapes=scratch,
            compiler_params=LIMIT,
            name=name,
        )(*operands)

    def shape(*sizes):
        return jax.ShapeDtypeStruct(sizes, f32)

    beside = swap(*to_sides, "lon", True)
    to_ends = call(pack_ends_kernel, "density_pack", (ends, ends), [], latent, *beside)
    above = swap(*to_ends, "lat", False, outer_first=True)
    broad = 2 * width
    stencils = taps.transpose(1, 0, 2)
    mirrored = mirror(stencils)[::-1]
    inner, middle = call(
        density_inside_kernel, "density_inside",
        (shape(height - 4, broad, radial), shape(3, 3, height - 2, broad, radial)), [rows, moved],
        latent, *beside, stencils,
    )
    to_sides = call(bin_sides_kernel, "bin_sides", (sides, sides), star_rows, got, inner)
    density = call(
        density_ends_kernel, "density_ends", shape(height, broad, radial),
        [pltpu.VMEM((3, 3, 4, broad, radial), f32), rows, moved],
        latent, *beside, *above[::-1], stencils, middle, inner, to_sides[1],
    )
    upstream = call(bin_rest_kernel, "bin_rest", tile, star_rows, got, density, *to_sides)

    beside = swap(*to_sides, "lon", True, outer_first=True)
    *to_ends, middle = call(
        back_reach_kernel, "back_reach", (shape(2, width, radial), shape(2, width, radial), shape(*edge)),
        [rows, moved, pltpu.VMEM((4, width, radial), f32)], upstream, *beside[::-1], density, mirrored,
    )
    above = swap(*to_ends, "lat", False)
    own = call(
        back_own_kernel, "back_own", tile, [rows, moved, pltpu.VMEM(inner_rows, f32)],
        upstream, *beside[::-1], density, mirrored, latent, middle,
    )
    return pl.pallas_call(
        close_kernel,
        out_shape=tile,
        in_specs=[VMEM] * 3,
        out_specs=HBM,
        scratch_shapes=[pltpu.VMEM((2, width, radial), f32)] * 2 + [pltpu.SemaphoreType.DMA((3,))],
        compiler_params=LIMIT,
        name="close",
    )(own, *above)


def solution(mesh):
    return jax.shard_map(
        on_device,
        mesh=mesh,
        in_specs=(
            P(("lat", "lon")),
            P(("lat", "lon")),
            P(("lat", "lon")),
            P(("lat", "lon"), None),
            P(("lat", "lon"), None),
            P("lat", "lon", None),
            P(),
        ),
        out_specs=P("lat", "lon", None),
        check_vma=False,
    )
```

```python
import functools

import jax
import jax.numpy as jnp
from jax import lax
from jax.experimental import pallas as pl
from jax.experimental.pallas import tpu as pltpu
from jax.sharding import PartitionSpec as P

CAP = 512
LEAST = 128
LANES = 128
SUBLANES = 8
RUNS = CAP // LANES
bin_width = 0.0625


def position(axis):
    index = lax.axis_index(axis)
    return index, lax.bitwise_and(index, 1)


def either(flag, if_set, if_clear):
    return jnp.where(jnp.full(if_set.shape, flag, jnp.int32) > 0, if_set, if_clear)


def sublane(radial):
    return lax.broadcasted_iota(jnp.int32, (SUBLANES, radial), 0)


def unpack_sides(from_partner, from_outer, height):
    _, odd = position("lon")
    sub = sublane(from_outer.shape[2])
    tiles = []
    for group in range(height // 4):
        partner, outer = from_partner[group], from_outer[group]
        before, after = either(odd, partner, outer), either(odd, outer, partner)
        for k in range(4):
            ahead = pltpu.roll(after, -2 * k % SUBLANES, 0)
            tiles.append(jnp.where(sub < 4, ahead, pltpu.roll(before, SUBLANES - 2 - 2 * k, 0)))
    return tiles


def pack_four(rows, to_partner, to_outer):
    _, odd = position("lon")
    sub = sublane(rows[0].shape[1])
    for group in range(len(rows) // 2):
        one, two = rows[2 * group], pltpu.roll(rows[2 * group + 1], 4, 0)
        before, after = jnp.where(sub < 4, one, two), jnp.where(sub < 4, two, one)
        to_partner[group] = either(odd, before, after)
        to_outer[group] = either(odd, after, before)


def unpack_four(from_partner, from_outer, height):
    _, odd = position("lon")
    sub = sublane(from_partner.shape[2])
    tiles = []
    for group in range(height // 2):
        partner, outer = from_partner[group], from_outer[group]
        before, after = either(odd, partner, outer), either(odd, outer, partner)
        tiles.append(jnp.where(sub < 4, after, before))
        tiles.append(pltpu.roll(jnp.where(sub < 4, before, after), 4, 0))
    return tiles


def pack_ends_kernel(field, side_0, side_1, to_partner, to_outer):
    height = field.shape[0]
    _, odd = position("lat")
    tiles = unpack_four(side_0, side_1, height)
    top = [field[0], field[1], tiles[0], tiles[1]]
    bottom = [field[height - 2], field[height - 1], tiles[height - 2], tiles[height - 1]]
    for place, (one, two) in enumerate(zip(top, bottom)):
        to_partner[place] = either(odd, one, two)
        to_outer[place] = either(odd, two, one)


def radial_shifts(field):
    radial = field.shape[-1]
    lane = lax.broadcasted_iota(jnp.int32, field.shape, field.ndim - 1)
    return (
        jnp.where(lane == 0, 0.0, pltpu.roll(field, 1, field.ndim - 1)),
        jnp.where(lane == radial - 1, 0.0, pltpu.roll(field, radial - 1, field.ndim - 1)),
    )


def taps_of(coef, at):
    return [jnp.broadcast_to(coef[k:k + 1, at], (SUBLANES, LANES)) for k in range(27)]


def tiles_of_bins(radial, body):
    for start in range(0, radial, LANES):
        body(slice(start, start + LANES))


ALL = (-1, 0, 1)


def first_level(wide, shifted, coef, centers, middle, real):
    _, cols, radial = wide.shape
    for row in sorted({row + above for row, around in centers for above in around}):
        for place, moved in enumerate(radial_shifts(wide[row])):
            shifted[place, row] = moved

    def body(at):
        taps = taps_of(coef, at)
        for place, (row, around) in enumerate(centers):
            parts = []
            for side in (slice(0, SUBLANES), slice(SUBLANES, cols)):
                sums = [None, None, None]
                for above in around:
                    window = (shifted[0, row + above, side, at], wide[row + above, side, at], shifted[1, row + above, side, at])
                    for beside in range(3):
                        for step in range(3):
                            term = taps[(above + 1) * 9 + beside * 3 + step] * window[step]
                            sums[beside] = term if sums[beside] is None else sums[beside] + term
                parts.append(sums)
            whole = [jnp.concatenate([parts[0][b], parts[1][b]], axis=0) for b in range(3)]
            value = whole[1] + pltpu.roll(whole[0], 1, 0) + pltpu.roll(whole[2], cols - 1, 0)
            if real[place] is not None:
                value = either(real[place], value, jnp.zeros_like(value))
            kept = middle.shape[3]
            middle[0, 1, place, :, at] = pltpu.roll(value, 1, 0)[:kept]
            middle[1, 1, place, :, at] = value[:kept]
            middle[2, 1, place, :, at] = pltpu.roll(value, cols - 1, 0)[:kept]

    tiles_of_bins(radial, body)
    for place in range(len(centers)):
        for beside in range(3):
            for step, moved in zip((0, 2), radial_shifts(middle[beside, 1, place])):
                middle[beside, step, place] = moved


def second_level(coef, windows, radial, write, cols=SUBLANES):
    def body(at):
        taps = taps_of(coef, at)
        for row, around in windows.items():
            for start in range(0, cols, SUBLANES):
                side = slice(start, start + SUBLANES)
                total = None
                for above, at_row in enumerate(around):
                    if at_row is None:
                        continue
                    buffer, place = at_row
                    for beside in range(3):
                        for step in range(3):
                            term = taps[above * 9 + beside * 3 + step] * buffer[beside, step, place, side, at]
                            total = term if total is None else total + term
                write(row, side, at, total)

    tiles_of_bins(radial, body)


def fill_wide(wide, field, tiles, rows):
    width = field.shape[1]
    for row in rows:
        wide[row, :width] = field[row]
        wide[row, width:] = tiles[row]


def density_inside_kernel(field, side_0, side_1, stencils, out, middle, wide, shifted):
    height, _, radial = field.shape
    fill_wide(wide, field, unpack_four(side_0, side_1, height), range(height))
    centers = [(row, ALL) for row in range(1, height - 1)]
    first_level(wide, shifted, stencils.at[0], centers, middle, [None] * len(centers))

    def write(row, side, at, value):
        out[row - 2, side, at] = jnp.exp(value)

    windows = {row: [(middle, row - 2 + k) for k in range(3)] for row in range(2, height - 2)}
    second_level(stencils.at[1], windows, radial, write, wide.shape[1])


def density_ends_kernel(
    field, side_0, side_1, end_1, end_0, stencils, inside, inner, _, out, middle, wide, shifted
):
    height, width, radial = field.shape
    tiles = unpack_four(side_0, side_1, height)
    lat, odd = position("lat")
    for place in range(2):
        for half in range(2):
            partner, outer = end_0[2 * half + place], end_1[2 * half + place]
            at = slice(half * width, (half + 1) * width)
            wide[place, at] = either(odd, partner, outer)
            wide[6 + place, at] = either(odd, outer, partner)
    for place, row in ((2, 0), (3, 1), (4, height - 2), (5, height - 1)):
        wide[place, :width] = field[row]
        wide[place, width:] = tiles[row]
    above = (lat > 0).astype(jnp.int32)
    below = (lat < lax.axis_size("lat") - 1).astype(jnp.int32)
    centers = [(row, ALL) for row in (1, 2, 5, 6)]
    first_level(wide, shifted, stencils.at[0], centers, middle, [above, None, None, below])

    def write(row, side, at, value):
        out[row, side, at] = jnp.exp(value)

    last = height - 3
    top = [(middle, 0), (middle, 1), (inside, 0), (inside, 1)]
    bottom = [(inside, last - 1), (inside, last), (middle, 2), (middle, 3)]
    windows = {0: top[:3], 1: top[1:], height - 2: bottom[:3], height - 1: bottom[1:]}
    second_level(stencils.at[1], windows, radial, write, wide.shape[1])
    for row in range(2, height - 2):
        out[row] = inner[row - 2]


def beside_tiles(pair, side_1, density):
    _, odd = position("lon")
    side_0 = [either(odd, pair[0, group], pair[1, group]) for group in range(2)]
    tiles = unpack_sides(side_0, side_1, density.shape[0])
    return [tile * density[row, SUBLANES:] for row, tile in enumerate(tiles)]


def back_reach_kernel(field, side_1, pair, density, stencils, to_partner, to_outer, middle, wide, shifted, reach):
    height, _, radial = field.shape
    last = height - 1
    fill_wide(wide, field, beside_tiles(pair, side_1, density), (0, 1, last - 1, last))
    lat, odd = position("lat")
    above = (lat > 0).astype(jnp.int32)
    below = (lat < lax.axis_size("lat") - 1).astype(jnp.int32)
    centers = [(-1, (1,)), (0, (0, 1)), (last, (-1, 0)), (last + 1, (-1,))]
    first_level(wide, shifted, stencils.at[0], centers, middle, [above, None, None, below])

    def write(row, side, at, value):
        reach[row, side, at] = value

    windows = {
        0: [None, None, (middle, 0)],
        1: [None, (middle, 0), (middle, 1)],
        2: [(middle, 2), (middle, 3), None],
        3: [(middle, 3), None, None],
    }
    second_level(stencils.at[1], windows, radial, write)
    for place in range(2):
        to_partner[place] = either(odd, reach[place], reach[2 + place])
        to_outer[place] = either(odd, reach[2 + place], reach[place])


def back_own_kernel(field, side_1, pair, density, stencils, latent, edge, out, wide, shifted, middle):
    height, _, radial = field.shape
    fill_wide(wide, field, beside_tiles(pair, side_1, density), range(height))
    centers = [(row, ALL) for row in range(1, height - 1)]
    first_level(wide, shifted, stencils.at[0], centers, middle, [None] * len(centers))

    def write(row, side, at, value):
        out[row, side, at] = latent[row, side, at] + value

    line = [(edge, 0), (edge, 1)] + [(middle, place) for place in range(height - 2)] + [(edge, 2), (edge, 3)]
    second_level(stencils.at[1], {row: line[row:row + 3] for row in range(height)}, radial, write)


def close_kernel(own, end_0, end_1, out, top, bottom, sent):
    height = own.shape[0]
    last = height - 2
    pairs = ((own.at[2:last], out.at[2:last]), (top, out.at[:2]), (bottom, out.at[last:]))
    copies = [pltpu.make_async_copy(source, target, sent.at[i]) for i, (source, target) in enumerate(pairs)]
    copies[0].start()
    _, odd = position("lat")
    for place in range(2):
        top[place] = own[place] + either(odd, end_0[place], end_1[place])
    copies[1].start()
    for place in range(2):
        bottom[place] = own[last + place] + either(odd, end_1[place], end_0[place])
    copies[2].start()
    for copy in copies:
        copy.wait()


def open_kernel(
    counts_in, offsets_in, residual_in, pixel_in, bins_in, latent_in, taps_in, out, latent, to_partner, to_outer, taps,
    counts, offsets, residual, pixel, bins, table, arrived,
):
    pairs = (
        (counts_in, counts), (offsets_in, offsets), (residual_in, residual), (pixel_in, pixel), (bins_in, bins),
        (latent_in, latent), (taps_in, taps),
    )
    copies = [pltpu.make_async_copy(source, target, arrived.at[i]) for i, (source, target) in enumerate(pairs)]
    for copy in copies:
        copy.start()
    for copy in copies[:-2]:
        copy.wait()
    height, _, radial = latent.shape
    length = residual.shape[0]
    table[pl.ds(0, length, stride=2), :] = residual[...]
    table[pl.ds(1, length, stride=2), :] = (pixel[...] * radial + bins[...]).astype(jnp.float32)

    lane = lax.broadcasted_iota(jnp.int32, (SUBLANES, LANES), 1)
    row = lax.broadcasted_iota(jnp.int32, (SUBLANES, LANES), 0)
    slot = lax.shift_right_logical(row, 1) * LANES + lane
    for owner in range(out.shape[0]):
        start = offsets[0, owner]
        first = lax.shift_right_logical(start, 7) * 2
        part = lax.bitwise_and(start, LANES - 1)
        turn = lax.bitwise_and(LANES - part, LANES - 1)
        here = pltpu.roll(table[pl.ds(first, SUBLANES), :], turn, 1)
        after = pltpu.roll(table[pl.ds(first + 2, SUBLANES), :], turn, 1)
        joined = jnp.where(lane < LANES - part, here, after)
        out[owner] = jnp.where(slot < counts[0, owner], joined, 0.0)

    copies[-2].wait()
    pack_four([latent[row] for row in range(height)], to_partner, to_outer)
    copies[-1].wait()


def behind_of(got, index_of, pixels, runs, rows_of, *, width, radial):
    span = radial // 2
    classes = 2 * pixels
    shards, rows, _ = got.shape
    bf16 = jnp.bfloat16
    column = lax.broadcasted_iota(jnp.int32, (classes, LANES), 0).astype(jnp.float32).astype(bf16)
    places = [
        (lax.broadcasted_iota(jnp.int32, (LANES, LANES), 1) + first).astype(jnp.float32).astype(bf16)
        for first in range(0, span, LANES)
    ]
    zero = jnp.zeros((), bf16)
    one = jnp.ones((), bf16)

    def tall(kind, row):
        line = jnp.broadcast_to(rows_of[kind, row:row + 1, :], (16, LANES))
        return jnp.concatenate([line.astype(bf16)] * (classes // 16), axis=0)

    tiles = got[...].reshape(shards * rows, LANES)
    cell = tiles.astype(jnp.int32)
    pixel = lax.shift_right_logical(cell, radial.bit_length() - 1)
    bins = lax.bitwise_and(cell, radial - 1)
    upper = lax.shift_right_logical(bins, span.bit_length() - 1)
    index = index_of(lax.shift_right_logical(pixel, width.bit_length() - 1), lax.bitwise_and(pixel, width - 1))
    rows_of[0] = jnp.where(index < pixels, upper * pixels + index, classes).astype(jnp.float32)
    lows = jnp.transpose(lax.bitwise_and(bins, span - 1).astype(jnp.float32)).astype(bf16)
    coarse = tiles.astype(bf16).astype(jnp.float32)
    rows_of[1] = coarse
    rows_of[2] = tiles - coarse

    total = jnp.zeros((2 * classes, span), jnp.float32)
    group = 2 * RUNS // runs
    for first in range(0, shards, group):
        left, right = [], []
        for run in range(group * runs):
            row = (first + run // runs) * rows + run % runs * 2
            mine = tall(0, row + 1) == column
            left.append(jnp.concatenate([jnp.where(mine, tall(kind, row), zero) for kind in (1, 2)], axis=0))
            low = jnp.broadcast_to(lows[:, row + 1:row + 2], (LANES, LANES))
            right.append(jnp.concatenate([jnp.where(low >= place, one, zero) for place in places], axis=1))
        total = total + jnp.dot(
            jnp.concatenate(left, axis=1), jnp.concatenate(right, axis=0), preferred_element_type=jnp.float32
        )
    both = (total[:classes] + total[classes:]) * bin_width
    near, far = both[:pixels], both[pixels:]
    return jnp.concatenate([near + far[:, :1], far], axis=1)


def for_load(body):
    lat, count = lax.axis_index("lat"), lax.axis_size("lat")
    middle = (lat >= count // 4) & (lat < count - count // 4)
    pl.when(middle)(lambda: body(RUNS))
    pl.when(jnp.logical_not(middle))(lambda: body(LEAST // LANES))


def bin_outer_kernel(got, _, to_outer, rows_of):
    _, odd = position("lon")

    def index_of(row, col):
        return jnp.where(lax.shift_right_logical(col, 1) == 3 * odd, row * 2 + lax.bitwise_and(col, 1), 16)

    def body(runs):
        packed = behind_of(got, index_of, 16, runs, rows_of, width=SUBLANES, radial=to_outer.shape[2])
        for place in range(2):
            to_outer[place] = packed[place * SUBLANES:(place + 1) * SUBLANES]

    for_load(body)


def bin_rest_kernel(got, density, to_outer, upstream, to_pair, rows_of):
    height, width, radial = upstream.shape
    _, odd = position("lon")
    pair = lax.shift_right_logical(sublane(radial), 1)

    def index_of(row, col):
        place = lax.bitwise_and(col + 2 * odd, width - 1) - 2
        return jnp.where(place >= 0, lax.shift_right_logical(place, 1) * 16 + row * 2 + lax.bitwise_and(place, 1), 48)

    def body(runs):
        packed = behind_of(got, index_of, 48, runs, rows_of, width=width, radial=radial)

        def part(step, group):
            at = (2 * step + group) * SUBLANES
            return packed[at:at + SUBLANES]

        for row in range(height):
            group, k = row // 4, row % 4
            mine = pltpu.roll(to_outer[group], -2 * k % SUBLANES, 0)
            for step in range(3):
                mine = jnp.where(pair == step + 1, pltpu.roll(part(step, group), (2 * (step + 1 - k)) % SUBLANES, 0), mine)
            upstream[row] = density[row, :width] * either(odd, pltpu.roll(mine, SUBLANES - 2, 0), mine)
        for group in range(2):
            side = either(odd, part(0, group), part(2, group))
            to_pair[0, group] = side
            to_pair[1, group] = side

    for_load(body)


def mirror(stencils):
    turned = jnp.flip(stencils, axis=1).reshape(stencils.shape[0], 9, 3, stencils.shape[2])
    edge = jnp.zeros_like(turned[:, :, 0, :1])
    back = jnp.concatenate([edge, turned[:, :, 0, :-1]], axis=-1)
    ahead = jnp.concatenate([turned[:, :, 2, 1:], edge], axis=-1)
    return jnp.stack([back, turned[:, :, 1], ahead], axis=2).reshape(stencils.shape)


def swap(to_partner, to_outer, axis, closed, outer_first=False):
    count = lax.axis_size(axis)
    outer = [(i, (i + 1) % count) for i in range(1, count, 2) if closed or i + 1 < count]
    inner = [(i, i + 1) for i in range(0, count - 1, 2)]

    def both_ways(pairs):
        return pairs + [(j, i) for i, j in pairs]

    moves = [(to_partner, inner), (to_outer, outer)]
    got = [lax.ppermute(values, axis, both_ways(pairs)) for values, pairs in moves[::-1 if outer_first else 1]]
    return tuple(got[::-1 if outer_first else 1])


VMEM = pl.BlockSpec(memory_space=pltpu.VMEM)
HBM = pl.BlockSpec(memory_space=pltpu.HBM)
LIMIT = pltpu.CompilerParams(vmem_limit_bytes=32 * 1024 * 1024)


def on_device(residual, star_pixel, star_bin, send_counts, send_offsets, latent, stencils):
    height, width, radial = latent.shape
    shards = send_counts.shape[1]
    slots = residual.shape[0]
    f32 = jnp.float32
    i32 = jnp.int32
    tile = jax.ShapeDtypeStruct((height, width, radial), f32)
    sides = jax.ShapeDtypeStruct((height // 4, SUBLANES, radial), f32)
    ends = jax.ShapeDtypeStruct((4, SUBLANES, radial), f32)

    def table(values):
        return values.reshape(slots // LANES, LANES)

    four = jax.ShapeDtypeStruct((height // 2, SUBLANES, radial), f32)
    taps = jax.ShapeDtypeStruct((stencils.shape[1], stencils.shape[0], radial), f32)
    packed, latent, *to_sides, taps = pl.pallas_call(
        open_kernel,
        out_shape=(jax.ShapeDtypeStruct((shards, 2 * RUNS, LANES), f32), tile, four, four, taps),
        in_specs=[HBM] * 7,
        out_specs=(VMEM,) * 5,
        scratch_shapes=[pltpu.SMEM((1, shards), i32)] * 2
        + [pltpu.VMEM((slots // LANES, LANES), kind) for kind in (f32, i32, i32)]
        + [pltpu.VMEM((2 * slots // LANES, LANES), f32)]
        + [pltpu.SemaphoreType.DMA((7,))],
        compiler_params=LIMIT,
        name="opening",
    )(*[
        pltpu.with_memory_space_constraint(values, pltpu.HBM)
        for values in (send_counts, send_offsets, table(residual), table(star_pixel), table(star_bin), latent, stencils.transpose(1, 0, 2))
    ])
    got = lax.all_to_all(packed, ("lat", "lon"), split_axis=0, concat_axis=0, tiled=True)

    rows = pltpu.VMEM((height, 2 * width, radial), f32)
    moved = pltpu.VMEM((2, height, 2 * width, radial), f32)
    edge = (3, 3, 4, width, radial)
    star_rows = [pltpu.VMEM((3, shards * 2 * RUNS, LANES), f32)]
    inner_rows = (3, 3, height - 2, width, radial)

    def call(kernel, name, outs, scratch, *operands):
        return pl.pallas_call(
            kernel,
            out_shape=outs,
            in_specs=[VMEM] * len(operands),
            out_specs=jax.tree.map(lambda _: VMEM, outs),
            scratch_shapes=scratch,
            compiler_params=LIMIT,
            name=name,
        )(*operands)

    def shape(*sizes):
        return jax.ShapeDtypeStruct(sizes, f32)

    beside = swap(*to_sides, "lon", True)
    to_ends = call(pack_ends_kernel, "density_pack", (ends, ends), [], latent, *beside)
    above = swap(*to_ends, "lat", False, outer_first=True)
    broad = 2 * width
    stencils = taps.transpose(1, 0, 2)
    mirrored = mirror(stencils)[::-1]
    inner, middle = call(
        density_inside_kernel, "density_inside",
        (shape(height - 4, broad, radial), shape(3, 3, height - 2, broad, radial)), [rows, moved],
        latent, *beside, stencils,
    )
    to_outer = call(bin_outer_kernel, "bin_outer", sides, star_rows, got, inner)
    density = call(
        density_ends_kernel, "density_ends", shape(height, broad, radial),
        [pltpu.VMEM((3, 3, 4, broad, radial), f32), rows, moved],
        latent, *beside, *above[::-1], stencils, middle, inner, to_outer,
    )
    upstream, to_pair = call(
        bin_rest_kernel, "bin_rest", (tile, shape(2, 2, SUBLANES, radial)), star_rows, got, density, to_outer
    )

    count = lax.axis_size("lon")
    from_outer = lax.ppermute(
        to_outer, "lon", [(i, (i + 1) % count) for i in range(1, count, 2)] + [((i + 1) % count, i) for i in range(1, count, 2)]
    )
    pair = lax.all_to_all(
        to_pair, "lon", 0, 0, axis_index_groups=[[i, i + 1] for i in range(0, count, 2)], tiled=True
    )
    *to_ends, middle = call(
        back_reach_kernel, "back_reach", (shape(2, width, radial), shape(2, width, radial), shape(*edge)),
        [rows, moved, pltpu.VMEM((4, width, radial), f32)], upstream, from_outer, pair, density, mirrored,
    )
    above = swap(*to_ends, "lat", False)
    own = call(
        back_own_kernel, "back_own", tile, [rows, moved, pltpu.VMEM(inner_rows, f32)],
        upstream, from_outer, pair, density, mirrored, latent, middle,
    )
    return pl.pallas_call(
        close_kernel,
        out_shape=tile,
        in_specs=[VMEM] * 3,
        out_specs=HBM,
        scratch_shapes=[pltpu.VMEM((2, width, radial), f32)] * 2 + [pltpu.SemaphoreType.DMA((3,))],
        compiler_params=LIMIT,
        name="close",
    )(own, *above)


def solution(mesh):
    return jax.shard_map(
        on_device,
        mesh=mesh,
        in_specs=(
            P(("lat", "lon")),
            P(("lat", "lon")),
            P(("lat", "lon")),
            P(("lat", "lon"), None),
            P(("lat", "lon"), None),
            P("lat", "lon", None),
            P(),
        ),
        out_specs=P("lat", "lon", None),
        check_vma=False,
    )
```

```python
import functools

import jax
import jax.numpy as jnp
from jax import lax
from jax.experimental import pallas as pl
from jax.experimental.pallas import tpu as pltpu
from jax.sharding import PartitionSpec as P

CAP = 512
LEAST = 128
LANES = 128
SUBLANES = 8
RUNS = CAP // LANES
bin_width = 0.0625


def position(axis):
    index = lax.axis_index(axis)
    return index, lax.bitwise_and(index, 1)


def either(flag, if_set, if_clear):
    return jnp.where(jnp.full(if_set.shape, flag, jnp.int32) > 0, if_set, if_clear)


def sublane(radial):
    return lax.broadcasted_iota(jnp.int32, (SUBLANES, radial), 0)


def unpack_sides(from_partner, from_outer, height):
    _, odd = position("lon")
    sub = sublane(from_partner.shape[2])
    tiles = []
    for group in range(height // 4):
        partner, outer = from_partner[group], from_outer[group]
        before, after = either(odd, partner, outer), either(odd, outer, partner)
        for k in range(4):
            ahead = pltpu.roll(after, -2 * k % SUBLANES, 0)
            tiles.append(jnp.where(sub < 4, ahead, pltpu.roll(before, SUBLANES - 2 - 2 * k, 0)))
    return tiles


def pack_four(rows, to_partner, to_outer):
    _, odd = position("lon")
    sub = sublane(rows[0].shape[1])
    for group in range(len(rows) // 2):
        one, two = rows[2 * group], pltpu.roll(rows[2 * group + 1], 4, 0)
        before, after = jnp.where(sub < 4, one, two), jnp.where(sub < 4, two, one)
        to_partner[group] = either(odd, before, after)
        to_outer[group] = either(odd, after, before)


def unpack_four(from_partner, from_outer, height):
    _, odd = position("lon")
    sub = sublane(from_partner.shape[2])
    tiles = []
    for group in range(height // 2):
        partner, outer = from_partner[group], from_outer[group]
        before, after = either(odd, partner, outer), either(odd, outer, partner)
        tiles.append(jnp.where(sub < 4, after, before))
        tiles.append(pltpu.roll(jnp.where(sub < 4, before, after), 4, 0))
    return tiles


def pack_ends_kernel(field, side_0, side_1, to_partner, to_outer):
    height = field.shape[0]
    _, odd = position("lat")
    tiles = unpack_four(side_0, side_1, height)
    top = [field[0], field[1], tiles[0], tiles[1]]
    bottom = [field[height - 2], field[height - 1], tiles[height - 2], tiles[height - 1]]
    for place, (one, two) in enumerate(zip(top, bottom)):
        to_partner[place] = either(odd, one, two)
        to_outer[place] = either(odd, two, one)


def radial_shifts(field):
    radial = field.shape[-1]
    lane = lax.broadcasted_iota(jnp.int32, field.shape, field.ndim - 1)
    return (
        jnp.where(lane == 0, 0.0, pltpu.roll(field, 1, field.ndim - 1)),
        jnp.where(lane == radial - 1, 0.0, pltpu.roll(field, radial - 1, field.ndim - 1)),
    )


def taps_of(coef, at):
    return [jnp.broadcast_to(coef[k:k + 1, at], (SUBLANES, LANES)) for k in range(27)]


def tiles_of_bins(radial, body):
    for start in range(0, radial, LANES):
        body(slice(start, start + LANES))


ALL = (-1, 0, 1)


def first_level(wide, shifted, coef, centers, middle, real):
    _, cols, radial = wide.shape
    for row in sorted({row + above for row, around in centers for above in around}):
        for place, moved in enumerate(radial_shifts(wide[row])):
            shifted[place, row] = moved

    def body(at):
        taps = taps_of(coef, at)
        for place, (row, around) in enumerate(centers):
            parts = []
            for side in (slice(0, SUBLANES), slice(SUBLANES, cols)):
                sums = [None, None, None]
                for above in around:
                    window = (shifted[0, row + above, side, at], wide[row + above, side, at], shifted[1, row + above, side, at])
                    for beside in range(3):
                        for step in range(3):
                            term = taps[(above + 1) * 9 + beside * 3 + step] * window[step]
                            sums[beside] = term if sums[beside] is None else sums[beside] + term
                parts.append(sums)
            whole = [jnp.concatenate([parts[0][b], parts[1][b]], axis=0) for b in range(3)]
            value = whole[1] + pltpu.roll(whole[0], 1, 0) + pltpu.roll(whole[2], cols - 1, 0)
            if real[place] is not None:
                value = either(real[place], value, jnp.zeros_like(value))
            kept = middle.shape[3]
            middle[0, 1, place, :, at] = pltpu.roll(value, 1, 0)[:kept]
            middle[1, 1, place, :, at] = value[:kept]
            middle[2, 1, place, :, at] = pltpu.roll(value, cols - 1, 0)[:kept]

    tiles_of_bins(radial, body)
    for place in range(len(centers)):
        for beside in range(3):
            for step, moved in zip((0, 2), radial_shifts(middle[beside, 1, place])):
                middle[beside, step, place] = moved


def second_level(coef, windows, radial, write, cols=SUBLANES):
    def body(at):
        taps = taps_of(coef, at)
        for row, around in windows.items():
            for start in range(0, cols, SUBLANES):
                side = slice(start, start + SUBLANES)
                total = None
                for above, at_row in enumerate(around):
                    if at_row is None:
                        continue
                    buffer, place = at_row
                    for beside in range(3):
                        for step in range(3):
                            term = taps[above * 9 + beside * 3 + step] * buffer[beside, step, place, side, at]
                            total = term if total is None else total + term
                write(row, side, at, total)

    tiles_of_bins(radial, body)


def fill_wide(wide, field, tiles, rows):
    width = field.shape[1]
    for row in rows:
        wide[row, :width] = field[row]
        wide[row, width:] = tiles[row]


def density_inside_kernel(field, side_0, side_1, stencils, out, middle, wide, shifted):
    height, _, radial = field.shape
    fill_wide(wide, field, unpack_four(side_0, side_1, height), range(height))
    centers = [(row, ALL) for row in range(1, height - 1)]
    first_level(wide, shifted, stencils.at[0], centers, middle, [None] * len(centers))

    def write(row, side, at, value):
        out[row - 2, side, at] = jnp.exp(value)

    windows = {row: [(middle, row - 2 + k) for k in range(3)] for row in range(2, height - 2)}
    second_level(stencils.at[1], windows, radial, write, wide.shape[1])


def density_ends_kernel(
    field, side_0, side_1, end_1, end_0, stencils, inside, inner, _, out, middle, wide, shifted
):
    height, width, radial = field.shape
    tiles = unpack_four(side_0, side_1, height)
    lat, odd = position("lat")
    for place in range(2):
        for half in range(2):
            partner, outer = end_0[2 * half + place], end_1[2 * half + place]
            at = slice(half * width, (half + 1) * width)
            wide[place, at] = either(odd, partner, outer)
            wide[6 + place, at] = either(odd, outer, partner)
    for place, row in ((2, 0), (3, 1), (4, height - 2), (5, height - 1)):
        wide[place, :width] = field[row]
        wide[place, width:] = tiles[row]
    above = (lat > 0).astype(jnp.int32)
    below = (lat < lax.axis_size("lat") - 1).astype(jnp.int32)
    centers = [(row, ALL) for row in (1, 2, 5, 6)]
    first_level(wide, shifted, stencils.at[0], centers, middle, [above, None, None, below])

    def write(row, side, at, value):
        out[row, side, at] = jnp.exp(value)

    last = height - 3
    top = [(middle, 0), (middle, 1), (inside, 0), (inside, 1)]
    bottom = [(inside, last - 1), (inside, last), (middle, 2), (middle, 3)]
    windows = {0: top[:3], 1: top[1:], height - 2: bottom[:3], height - 1: bottom[1:]}
    second_level(stencils.at[1], windows, radial, write, wide.shape[1])
    for row in range(2, height - 2):
        out[row] = inner[row - 2]


def beside_tiles(side_0, side_1, density):
    tiles = unpack_sides(side_0, side_1, density.shape[0])
    return [tile * density[row, SUBLANES:] for row, tile in enumerate(tiles)]


def back_reach_kernel(field, side_1, side_0, density, stencils, to_partner, to_outer, middle, wide, shifted, reach):
    height, _, radial = field.shape
    last = height - 1
    fill_wide(wide, field, beside_tiles(side_0, side_1, density), (0, 1, last - 1, last))
    lat, odd = position("lat")
    above = (lat > 0).astype(jnp.int32)
    below = (lat < lax.axis_size("lat") - 1).astype(jnp.int32)
    centers = [(-1, (1,)), (0, (0, 1)), (last, (-1, 0)), (last + 1, (-1,))]
    first_level(wide, shifted, stencils.at[0], centers, middle, [above, None, None, below])

    def write(row, side, at, value):
        reach[row, side, at] = value

    windows = {
        0: [None, None, (middle, 0)],
        1: [None, (middle, 0), (middle, 1)],
        2: [(middle, 2), (middle, 3), None],
        3: [(middle, 3), None, None],
    }
    second_level(stencils.at[1], windows, radial, write)
    for place in range(2):
        to_partner[place] = either(odd, reach[place], reach[2 + place])
        to_outer[place] = either(odd, reach[2 + place], reach[place])


def back_own_kernel(field, side_1, side_0, density, stencils, latent, edge, out, wide, shifted, middle):
    height, _, radial = field.shape
    fill_wide(wide, field, beside_tiles(side_0, side_1, density), range(height))
    centers = [(row, ALL) for row in range(1, height - 1)]
    first_level(wide, shifted, stencils.at[0], centers, middle, [None] * len(centers))

    def write(row, side, at, value):
        out[row, side, at] = latent[row, side, at] + value

    line = [(edge, 0), (edge, 1)] + [(middle, place) for place in range(height - 2)] + [(edge, 2), (edge, 3)]
    second_level(stencils.at[1], {row: line[row:row + 3] for row in range(height)}, radial, write)


def close_kernel(own, end_0, end_1, out, top, bottom, sent):
    height = own.shape[0]
    last = height - 2
    pairs = ((own.at[2:last], out.at[2:last]), (top, out.at[:2]), (bottom, out.at[last:]))
    copies = [pltpu.make_async_copy(source, target, sent.at[i]) for i, (source, target) in enumerate(pairs)]
    copies[0].start()
    _, odd = position("lat")
    for place in range(2):
        top[place] = own[place] + either(odd, end_0[place], end_1[place])
    copies[1].start()
    for place in range(2):
        bottom[place] = own[last + place] + either(odd, end_1[place], end_0[place])
    copies[2].start()
    for copy in copies:
        copy.wait()


def open_kernel(
    counts_in, offsets_in, residual_in, pixel_in, bins_in, latent_in, taps_in, out, latent, to_partner, to_outer, taps,
    counts, offsets, residual, pixel, bins, table, arrived,
):
    pairs = (
        (counts_in, counts), (offsets_in, offsets), (residual_in, residual), (pixel_in, pixel), (bins_in, bins),
        (latent_in, latent), (taps_in, taps),
    )
    copies = [pltpu.make_async_copy(source, target, arrived.at[i]) for i, (source, target) in enumerate(pairs)]
    for copy in copies:
        copy.start()
    for copy in copies[:-2]:
        copy.wait()
    height, _, radial = latent.shape
    length = residual.shape[0]
    table[pl.ds(0, length, stride=2), :] = residual[...]
    table[pl.ds(1, length, stride=2), :] = (pixel[...] * radial + bins[...]).astype(jnp.float32)

    lane = lax.broadcasted_iota(jnp.int32, (SUBLANES, LANES), 1)
    row = lax.broadcasted_iota(jnp.int32, (SUBLANES, LANES), 0)
    slot = lax.shift_right_logical(row, 1) * LANES + lane
    for owner in range(out.shape[0]):
        start = offsets[0, owner]
        first = lax.shift_right_logical(start, 7) * 2
        part = lax.bitwise_and(start, LANES - 1)
        turn = lax.bitwise_and(LANES - part, LANES - 1)
        here = pltpu.roll(table[pl.ds(first, SUBLANES), :], turn, 1)
        after = pltpu.roll(table[pl.ds(first + 2, SUBLANES), :], turn, 1)
        joined = jnp.where(lane < LANES - part, here, after)
        out[owner] = jnp.where(slot < counts[0, owner], joined, 0.0)

    copies[-2].wait()
    pack_four([latent[row] for row in range(height)], to_partner, to_outer)
    copies[-1].wait()


def behind_of(got, index_of, pixels, runs, rows_of, *, width, radial):
    span = radial // 2
    classes = 2 * pixels
    shards, rows, _ = got.shape
    bf16 = jnp.bfloat16
    column = lax.broadcasted_iota(jnp.int32, (classes, LANES), 0).astype(jnp.float32).astype(bf16)
    places = [
        (lax.broadcasted_iota(jnp.int32, (LANES, LANES), 1) + first).astype(jnp.float32).astype(bf16)
        for first in range(0, span, LANES)
    ]
    zero = jnp.zeros((), bf16)
    one = jnp.ones((), bf16)

    def tall(kind, row):
        line = jnp.broadcast_to(rows_of[kind, row:row + 1, :], (16, LANES))
        return jnp.concatenate([line.astype(bf16)] * (classes // 16), axis=0)

    total = jnp.zeros((2 * classes, span), jnp.float32)
    group = 2 * RUNS // runs
    block = LANES // rows
    for start in range(0, shards, block):
        tiles = got[start:start + block].reshape(LANES, LANES)
        cell = tiles.astype(jnp.int32)
        pixel = lax.shift_right_logical(cell, radial.bit_length() - 1)
        bins = lax.bitwise_and(cell, radial - 1)
        upper = lax.shift_right_logical(bins, span.bit_length() - 1)
        index = index_of(lax.shift_right_logical(pixel, width.bit_length() - 1), lax.bitwise_and(pixel, width - 1))
        at = slice(start * rows, start * rows + LANES)
        lows = jnp.transpose(lax.bitwise_and(bins, span - 1).astype(jnp.float32)).astype(bf16)
        coarse = tiles.astype(bf16).astype(jnp.float32)
        rows_of[0, at] = jnp.where(index < pixels, upper * pixels + index, classes).astype(jnp.float32)
        rows_of[1, at] = coarse
        rows_of[2, at] = tiles - coarse
        for first in range(0, block, group):
            left, right = [], []
            for run in range(group * runs):
                here = (first + run // runs) * rows + run % runs * 2
                row = start * rows + here
                mine = tall(0, row + 1) == column
                left.append(jnp.concatenate([jnp.where(mine, tall(kind, row), zero) for kind in (1, 2)], axis=0))
                low = jnp.broadcast_to(lows[:, here + 1:here + 2], (LANES, LANES))
                right.append(jnp.concatenate([jnp.where(low >= place, one, zero) for place in places], axis=1))
            total = total + jnp.dot(
                jnp.concatenate(left, axis=1), jnp.concatenate(right, axis=0), preferred_element_type=jnp.float32
            )
    both = (total[:classes] + total[classes:]) * bin_width
    near, far = both[:pixels], both[pixels:]
    return jnp.concatenate([near + far[:, :1], far], axis=1)


def for_load(body):
    lat, count = lax.axis_index("lat"), lax.axis_size("lat")
    middle = (lat >= count // 4) & (lat < count - count // 4)
    pl.when(middle)(lambda: body(RUNS))
    pl.when(jnp.logical_not(middle))(lambda: body(LEAST // LANES))


def bin_sides_kernel(got, _, to_partner, to_outer, rows_of):
    _, odd = position("lon")

    def index_of(row, col):
        side = lax.bitwise_xor(lax.shift_right_logical(col, 2), odd)
        return jnp.where((col < 2) | (col >= 6), side * 16 + row * 2 + lax.bitwise_and(col, 1), 32)

    def body(runs):
        packed = behind_of(got, index_of, 32, runs, rows_of, width=SUBLANES, radial=to_outer.shape[2])
        for place in range(2):
            to_outer[place] = packed[place * SUBLANES:(place + 1) * SUBLANES]
            to_partner[place] = packed[(2 + place) * SUBLANES:(3 + place) * SUBLANES]

    for_load(body)


def bin_rest_kernel(got, density, to_partner, to_outer, upstream, rows_of):
    height, width, radial = upstream.shape
    _, odd = position("lon")
    sub = sublane(radial)

    def body(runs):
        packed = behind_of(
            got, lambda row, col: jnp.where((col >= 2) & (col < 6), row * 4 + col - 2, 32), 32, runs, rows_of,
            width=width, radial=radial,
        )
        for row in range(height):
            group, k = row // 4, row % 4
            partner, outer = to_partner[group], to_outer[group]
            first, last = either(odd, partner, outer), either(odd, outer, partner)
            first = pltpu.roll(first, -2 * k % SUBLANES, 0)
            last = pltpu.roll(last, SUBLANES - 2 - 2 * k, 0)
            inner = packed[row // 2 * SUBLANES:(row // 2 + 1) * SUBLANES]
            inner = pltpu.roll(inner, 6 if row % 2 else 2, 0)
            mine = jnp.where(sub < 2, first, jnp.where(sub < 6, inner, last))
            upstream[row] = density[row, :width] * mine

    for_load(body)


def mirror(stencils):
    turned = jnp.flip(stencils, axis=1).reshape(stencils.shape[0], 9, 3, stencils.shape[2])
    edge = jnp.zeros_like(turned[:, :, 0, :1])
    back = jnp.concatenate([edge, turned[:, :, 0, :-1]], axis=-1)
    ahead = jnp.concatenate([turned[:, :, 2, 1:], edge], axis=-1)
    return jnp.stack([back, turned[:, :, 1], ahead], axis=2).reshape(stencils.shape)


def swap(to_partner, to_outer, axis, closed, outer_first=False):
    count = lax.axis_size(axis)
    outer = [(i, (i + 1) % count) for i in range(1, count, 2) if closed or i + 1 < count]
    inner = [(i, i + 1) for i in range(0, count - 1, 2)]

    def both_ways(pairs):
        return pairs + [(j, i) for i, j in pairs]

    moves = [(to_partner, inner), (to_outer, outer)]
    got = [lax.ppermute(values, axis, both_ways(pairs)) for values, pairs in moves[::-1 if outer_first else 1]]
    return tuple(got[::-1 if outer_first else 1])


VMEM = pl.BlockSpec(memory_space=pltpu.VMEM)
HBM = pl.BlockSpec(memory_space=pltpu.HBM)
LIMIT = pltpu.CompilerParams(vmem_limit_bytes=32 * 1024 * 1024)


def on_device(residual, star_pixel, star_bin, send_counts, send_offsets, latent, stencils):
    height, width, radial = latent.shape
    shards = send_counts.shape[1]
    slots = residual.shape[0]
    f32 = jnp.float32
    i32 = jnp.int32
    tile = jax.ShapeDtypeStruct((height, width, radial), f32)
    sides = jax.ShapeDtypeStruct((height // 4, SUBLANES, radial), f32)
    ends = jax.ShapeDtypeStruct((4, SUBLANES, radial), f32)

    def table(values):
        return values.reshape(slots // LANES, LANES)

    four = jax.ShapeDtypeStruct((height // 2, SUBLANES, radial), f32)
    taps = jax.ShapeDtypeStruct((stencils.shape[1], stencils.shape[0], radial), f32)
    packed, latent, *to_sides, taps = pl.pallas_call(
        open_kernel,
        out_shape=(jax.ShapeDtypeStruct((shards, 2 * RUNS, LANES), f32), tile, four, four, taps),
        in_specs=[HBM] * 7,
        out_specs=(VMEM,) * 5,
        scratch_shapes=[pltpu.SMEM((1, shards), i32)] * 2
        + [pltpu.VMEM((slots // LANES, LANES), kind) for kind in (f32, i32, i32)]
        + [pltpu.VMEM((2 * slots // LANES, LANES), f32)]
        + [pltpu.SemaphoreType.DMA((7,))],
        compiler_params=LIMIT,
        name="opening",
    )(*[
        pltpu.with_memory_space_constraint(values, pltpu.HBM)
        for values in (send_counts, send_offsets, table(residual), table(star_pixel), table(star_bin), latent, stencils.transpose(1, 0, 2))
    ])
    got = lax.all_to_all(packed, ("lat", "lon"), split_axis=0, concat_axis=0, tiled=True)

    rows = pltpu.VMEM((height, 2 * width, radial), f32)
    moved = pltpu.VMEM((2, height, 2 * width, radial), f32)
    edge = (3, 3, 4, width, radial)
    star_rows = [pltpu.VMEM((3, shards * 2 * RUNS, LANES), f32)]
    inner_rows = (3, 3, height - 2, width, radial)

    def call(kernel, name, outs, scratch, *operands):
        return pl.pallas_call(
            kernel,
            out_shape=outs,
            in_specs=[VMEM] * len(operands),
            out_specs=jax.tree.map(lambda _: VMEM, outs),
            scratch_shapes=scratch,
            compiler_params=LIMIT,
            name=name,
        )(*operands)

    def shape(*sizes):
        return jax.ShapeDtypeStruct(sizes, f32)

    beside = swap(*to_sides, "lon", True)
    to_ends = call(pack_ends_kernel, "density_pack", (ends, ends), [], latent, *beside)
    above = swap(*to_ends, "lat", False, outer_first=True)
    broad = 2 * width
    stencils = taps.transpose(1, 0, 2)
    mirrored = mirror(stencils)[::-1]
    inner, middle = call(
        density_inside_kernel, "density_inside",
        (shape(height - 4, broad, radial), shape(3, 3, height - 2, broad, radial)), [rows, moved],
        latent, *beside, stencils,
    )
    to_sides = call(bin_sides_kernel, "bin_sides", (sides, sides), star_rows, got, inner)
    density = call(
        density_ends_kernel, "density_ends", shape(height, broad, radial),
        [pltpu.VMEM((3, 3, 4, broad, radial), f32), rows, moved],
        latent, *beside, *above[::-1], stencils, middle, inner, to_sides[1],
    )
    upstream = call(bin_rest_kernel, "bin_rest", tile, star_rows, got, density, *to_sides)

    beside = swap(*to_sides, "lon", True, outer_first=True)
    *to_ends, middle = call(
        back_reach_kernel, "back_reach", (shape(2, width, radial), shape(2, width, radial), shape(*edge)),
        [rows, moved, pltpu.VMEM((4, width, radial), f32)], upstream, *beside[::-1], density, mirrored,
    )
    above = swap(*to_ends, "lat", False)
    own = call(
        back_own_kernel, "back_own", tile, [rows, moved, pltpu.VMEM(inner_rows, f32)],
        upstream, *beside[::-1], density, mirrored, latent, middle,
    )
    return pl.pallas_call(
        close_kernel,
        out_shape=tile,
        in_specs=[VMEM] * 3,
        out_specs=HBM,
        scratch_shapes=[pltpu.VMEM((2, width, radial), f32)] * 2 + [pltpu.SemaphoreType.DMA((3,))],
        compiler_params=LIMIT,
        name="close",
    )(own, *above)


def solution(mesh):
    return jax.shard_map(
        on_device,
        mesh=mesh,
        in_specs=(
            P(("lat", "lon")),
            P(("lat", "lon")),
            P(("lat", "lon")),
            P(("lat", "lon"), None),
            P(("lat", "lon"), None),
            P("lat", "lon", None),
            P(),
        ),
        out_specs=P("lat", "lon", None),
        check_vma=False,
    )
```

```python
import functools

import jax
import jax.numpy as jnp
from jax import lax
from jax.experimental import pallas as pl
from jax.experimental.pallas import tpu as pltpu
from jax.sharding import PartitionSpec as P

CAP = 512
LEAST = 128
LANES = 128
SUBLANES = 8
RUNS = CAP // LANES
bin_width = 0.0625


def position(axis):
    index = lax.axis_index(axis)
    return index, lax.bitwise_and(index, 1)


def either(flag, if_set, if_clear):
    return jnp.where(jnp.full(if_set.shape, flag, jnp.int32) > 0, if_set, if_clear)


def sublane(radial):
    return lax.broadcasted_iota(jnp.int32, (SUBLANES, radial), 0)


def unpack_sides(from_partner, from_outer, height):
    _, odd = position("lon")
    sub = sublane(from_partner.shape[2])
    tiles = []
    for group in range(height // 4):
        partner, outer = from_partner[group], from_outer[group]
        before, after = either(odd, partner, outer), either(odd, outer, partner)
        for k in range(4):
            ahead = pltpu.roll(after, -2 * k % SUBLANES, 0)
            tiles.append(jnp.where(sub < 4, ahead, pltpu.roll(before, SUBLANES - 2 - 2 * k, 0)))
    return tiles


def pack_four(rows, to_partner, to_outer):
    _, odd = position("lon")
    sub = sublane(rows[0].shape[1])
    for group in range(len(rows) // 2):
        one, two = rows[2 * group], pltpu.roll(rows[2 * group + 1], 4, 0)
        before, after = jnp.where(sub < 4, one, two), jnp.where(sub < 4, two, one)
        to_partner[group] = either(odd, before, after)
        to_outer[group] = either(odd, after, before)


def unpack_four(from_partner, from_outer, height):
    _, odd = position("lon")
    sub = sublane(from_partner.shape[2])
    tiles = []
    for group in range(height // 2):
        partner, outer = from_partner[group], from_outer[group]
        before, after = either(odd, partner, outer), either(odd, outer, partner)
        tiles.append(jnp.where(sub < 4, after, before))
        tiles.append(pltpu.roll(jnp.where(sub < 4, before, after), 4, 0))
    return tiles


def pack_ends_kernel(field, side_0, side_1, to_partner, to_outer):
    height = field.shape[0]
    _, odd = position("lat")
    tiles = unpack_four(side_0, side_1, height)
    top = [field[0], field[1], tiles[0], tiles[1]]
    bottom = [field[height - 2], field[height - 1], tiles[height - 2], tiles[height - 1]]
    for place, (one, two) in enumerate(zip(top, bottom)):
        to_partner[place] = either(odd, one, two)
        to_outer[place] = either(odd, two, one)


def radial_shifts(field):
    radial = field.shape[-1]
    lane = lax.broadcasted_iota(jnp.int32, field.shape, field.ndim - 1)
    return (
        jnp.where(lane == 0, 0.0, pltpu.roll(field, 1, field.ndim - 1)),
        jnp.where(lane == radial - 1, 0.0, pltpu.roll(field, radial - 1, field.ndim - 1)),
    )


def taps_of(coef, at):
    return [jnp.broadcast_to(coef[k:k + 1, at], (SUBLANES, LANES)) for k in range(27)]


def tiles_of_bins(radial, body):
    for start in range(0, radial, LANES):
        body(slice(start, start + LANES))


ALL = (-1, 0, 1)


def first_level(wide, shifted, coef, centers, middle, real):
    _, cols, radial = wide.shape
    for row in sorted({row + above for row, around in centers for above in around}):
        for place, moved in enumerate(radial_shifts(wide[row])):
            shifted[place, row] = moved

    def body(at):
        taps = taps_of(coef, at)
        for place, (row, around) in enumerate(centers):
            parts = []
            for side in (slice(0, SUBLANES), slice(SUBLANES, cols)):
                sums = [None, None, None]
                for above in around:
                    window = (shifted[0, row + above, side, at], wide[row + above, side, at], shifted[1, row + above, side, at])
                    for beside in range(3):
                        for step in range(3):
                            term = taps[(above + 1) * 9 + beside * 3 + step] * window[step]
                            sums[beside] = term if sums[beside] is None else sums[beside] + term
                parts.append(sums)
            whole = [jnp.concatenate([parts[0][b], parts[1][b]], axis=0) for b in range(3)]
            value = whole[1] + pltpu.roll(whole[0], 1, 0) + pltpu.roll(whole[2], cols - 1, 0)
            if real[place] is not None:
                value = either(real[place], value, jnp.zeros_like(value))
            kept = middle.shape[3]
            middle[0, 1, place, :, at] = pltpu.roll(value, 1, 0)[:kept]
            middle[1, 1, place, :, at] = value[:kept]
            middle[2, 1, place, :, at] = pltpu.roll(value, cols - 1, 0)[:kept]

    tiles_of_bins(radial, body)
    for place in range(len(centers)):
        for beside in range(3):
            for step, moved in zip((0, 2), radial_shifts(middle[beside, 1, place])):
                middle[beside, step, place] = moved


def second_level(coef, windows, radial, write, cols=SUBLANES):
    def body(at):
        taps = taps_of(coef, at)
        for row, around in windows.items():
            for start in range(0, cols, SUBLANES):
                side = slice(start, start + SUBLANES)
                total = None
                for above, at_row in enumerate(around):
                    if at_row is None:
                        continue
                    buffer, place = at_row
                    for beside in range(3):
                        for step in range(3):
                            term = taps[above * 9 + beside * 3 + step] * buffer[beside, step, place, side, at]
                            total = term if total is None else total + term
                write(row, side, at, total)

    tiles_of_bins(radial, body)


def fill_wide(wide, field, tiles, rows):
    width = field.shape[1]
    for row in rows:
        wide[row, :width] = field[row]
        wide[row, width:] = tiles[row]


def density_inside_kernel(field, side_0, side_1, stencils, out, middle, wide, shifted):
    height, _, radial = field.shape
    fill_wide(wide, field, unpack_four(side_0, side_1, height), range(height))
    centers = [(row, ALL) for row in range(1, height - 1)]
    first_level(wide, shifted, stencils.at[0], centers, middle, [None] * len(centers))

    def write(row, side, at, value):
        out[row - 2, side, at] = jnp.exp(value)

    windows = {row: [(middle, row - 2 + k) for k in range(3)] for row in range(2, height - 2)}
    second_level(stencils.at[1], windows, radial, write, wide.shape[1])


def density_ends_kernel(
    field, side_0, side_1, end_1, end_0, stencils, inside, inner, _, out, middle, wide, shifted
):
    height, width, radial = field.shape
    tiles = unpack_four(side_0, side_1, height)
    lat, odd = position("lat")
    for place in range(2):
        for half in range(2):
            partner, outer = end_0[2 * half + place], end_1[2 * half + place]
            at = slice(half * width, (half + 1) * width)
            wide[place, at] = either(odd, partner, outer)
            wide[6 + place, at] = either(odd, outer, partner)
    for place, row in ((2, 0), (3, 1), (4, height - 2), (5, height - 1)):
        wide[place, :width] = field[row]
        wide[place, width:] = tiles[row]
    above = (lat > 0).astype(jnp.int32)
    below = (lat < lax.axis_size("lat") - 1).astype(jnp.int32)
    centers = [(row, ALL) for row in (1, 2, 5, 6)]
    first_level(wide, shifted, stencils.at[0], centers, middle, [above, None, None, below])

    def write(row, side, at, value):
        out[row, side, at] = jnp.exp(value)

    last = height - 3
    top = [(middle, 0), (middle, 1), (inside, 0), (inside, 1)]
    bottom = [(inside, last - 1), (inside, last), (middle, 2), (middle, 3)]
    windows = {0: top[:3], 1: top[1:], height - 2: bottom[:3], height - 1: bottom[1:]}
    second_level(stencils.at[1], windows, radial, write, wide.shape[1])
    for row in range(2, height - 2):
        out[row] = inner[row - 2]


def beside_tiles(side_0, side_1, density):
    tiles = unpack_sides(side_0, side_1, density.shape[0])
    return [tile * density[row, SUBLANES:] for row, tile in enumerate(tiles)]


def back_reach_kernel(field, side_1, side_0, density, stencils, to_partner, to_outer, middle, wide, shifted, reach):
    height, _, radial = field.shape
    last = height - 1
    fill_wide(wide, field, beside_tiles(side_0, side_1, density), (0, 1, last - 1, last))
    lat, odd = position("lat")
    above = (lat > 0).astype(jnp.int32)
    below = (lat < lax.axis_size("lat") - 1).astype(jnp.int32)
    centers = [(-1, (1,)), (0, (0, 1)), (last, (-1, 0)), (last + 1, (-1,))]
    first_level(wide, shifted, stencils.at[0], centers, middle, [above, None, None, below])

    def write(row, side, at, value):
        reach[row, side, at] = value

    windows = {
        0: [None, None, (middle, 0)],
        1: [None, (middle, 0), (middle, 1)],
        2: [(middle, 2), (middle, 3), None],
        3: [(middle, 3), None, None],
    }
    second_level(stencils.at[1], windows, radial, write)
    for place in range(2):
        to_partner[place] = either(odd, reach[place], reach[2 + place])
        to_outer[place] = either(odd, reach[2 + place], reach[place])


def back_own_kernel(field, side_1, side_0, density, stencils, latent, edge, out, wide, shifted, middle):
    height, _, radial = field.shape
    fill_wide(wide, field, beside_tiles(side_0, side_1, density), range(height))
    centers = [(row, ALL) for row in range(1, height - 1)]
    first_level(wide, shifted, stencils.at[0], centers, middle, [None] * len(centers))

    def write(row, side, at, value):
        out[row, side, at] = latent[row, side, at] + value

    line = [(edge, 0), (edge, 1)] + [(middle, place) for place in range(height - 2)] + [(edge, 2), (edge, 3)]
    second_level(stencils.at[1], {row: line[row:row + 3] for row in range(height)}, radial, write)


def close_kernel(own, end_0, end_1, out, top, bottom, sent):
    height = own.shape[0]
    last = height - 2
    pairs = ((own.at[2:last], out.at[2:last]), (top, out.at[:2]), (bottom, out.at[last:]))
    copies = [pltpu.make_async_copy(source, target, sent.at[i]) for i, (source, target) in enumerate(pairs)]
    copies[0].start()
    _, odd = position("lat")
    for place in range(2):
        top[place] = own[place] + either(odd, end_0[place], end_1[place])
    copies[1].start()
    for place in range(2):
        bottom[place] = own[last + place] + either(odd, end_1[place], end_0[place])
    copies[2].start()
    for copy in copies:
        copy.wait()


def open_kernel(
    counts_in, offsets_in, residual_in, pixel_in, bins_in, latent_in, taps_in, out, latent, to_partner, to_outer, taps,
    counts, offsets, residual, pixel, bins, table, arrived,
):
    pairs = (
        (counts_in, counts), (offsets_in, offsets),
        *((source.at[:target.shape[0]], target) for source, target in ((residual_in, residual), (pixel_in, pixel), (bins_in, bins))),
        (latent_in, latent), (taps_in, taps),
    )
    copies = [pltpu.make_async_copy(source, target, arrived.at[i]) for i, (source, target) in enumerate(pairs)]
    for copy in copies:
        copy.start()
    for copy in copies[:-2]:
        copy.wait()
    height, _, radial = latent.shape
    length = residual.shape[0]
    table[pl.ds(0, length, stride=2), :] = residual[...]
    table[pl.ds(1, length, stride=2), :] = (pixel[...] * radial + bins[...]).astype(jnp.float32)

    lane = lax.broadcasted_iota(jnp.int32, (SUBLANES, LANES), 1)
    row = lax.broadcasted_iota(jnp.int32, (SUBLANES, LANES), 0)
    slot = lax.shift_right_logical(row, 1) * LANES + lane
    for owner in range(out.shape[0]):
        start = offsets[0, owner]
        first = lax.shift_right_logical(start, 7) * 2
        part = lax.bitwise_and(start, LANES - 1)
        turn = lax.bitwise_and(LANES - part, LANES - 1)
        here = pltpu.roll(table[pl.ds(first, SUBLANES), :], turn, 1)
        after = pltpu.roll(table[pl.ds(first + 2, SUBLANES), :], turn, 1)
        joined = jnp.where(lane < LANES - part, here, after)
        out[owner] = jnp.where(slot < counts[0, owner], joined, 0.0)

    copies[-2].wait()
    pack_four([latent[row] for row in range(height)], to_partner, to_outer)
    copies[-1].wait()


def behind_of(got, index_of, pixels, runs, rows_of, *, width, radial):
    span = radial // 2
    classes = 2 * pixels
    shards, rows, _ = got.shape
    bf16 = jnp.bfloat16
    column = lax.broadcasted_iota(jnp.int32, (classes, LANES), 0).astype(jnp.float32).astype(bf16)
    places = [
        (lax.broadcasted_iota(jnp.int32, (LANES, LANES), 1) + first).astype(jnp.float32).astype(bf16)
        for first in range(0, span, LANES)
    ]
    zero = jnp.zeros((), bf16)
    one = jnp.ones((), bf16)

    def tall(kind, row):
        line = jnp.broadcast_to(rows_of[kind, row:row + 1, :], (16, LANES))
        return jnp.concatenate([line.astype(bf16)] * (classes // 16), axis=0)

    total = jnp.zeros((2 * classes, span), jnp.float32)
    group = 2 * RUNS // runs
    block = LANES // rows
    for start in range(0, shards, block):
        tiles = got[start:start + block].reshape(LANES, LANES)
        cell = tiles.astype(jnp.int32)
        pixel = lax.shift_right_logical(cell, radial.bit_length() - 1)
        bins = lax.bitwise_and(cell, radial - 1)
        upper = lax.shift_right_logical(bins, span.bit_length() - 1)
        index = index_of(lax.shift_right_logical(pixel, width.bit_length() - 1), lax.bitwise_and(pixel, width - 1))
        at = slice(start * rows, start * rows + LANES)
        lows = jnp.transpose(lax.bitwise_and(bins, span - 1).astype(jnp.float32)).astype(bf16)
        coarse = tiles.astype(bf16).astype(jnp.float32)
        rows_of[0, at] = jnp.where(index < pixels, upper * pixels + index, classes).astype(jnp.float32)
        rows_of[1, at] = coarse
        rows_of[2, at] = tiles - coarse
        for first in range(0, block, group):
            left, right = [], []
            for run in range(group * runs):
                here = (first + run // runs) * rows + run % runs * 2
                row = start * rows + here
                mine = tall(0, row + 1) == column
                left.append(jnp.concatenate([jnp.where(mine, tall(kind, row), zero) for kind in (1, 2)], axis=0))
                low = jnp.broadcast_to(lows[:, here + 1:here + 2], (LANES, LANES))
                right.append(jnp.concatenate([jnp.where(low >= place, one, zero) for place in places], axis=1))
            total = total + jnp.dot(
                jnp.concatenate(left, axis=1), jnp.concatenate(right, axis=0), preferred_element_type=jnp.float32
            )
    both = (total[:classes] + total[classes:]) * bin_width
    near, far = both[:pixels], both[pixels:]
    return jnp.concatenate([near + far[:, :1], far], axis=1)


def for_load(body):
    lat, count = lax.axis_index("lat"), lax.axis_size("lat")
    middle = (lat >= count // 4) & (lat < count - count // 4)
    pl.when(middle)(lambda: body(RUNS))
    pl.when(jnp.logical_not(middle))(lambda: body(LEAST // LANES))


def bin_sides_kernel(got, _, to_partner, to_outer, rows_of):
    _, odd = position("lon")

    def index_of(row, col):
        side = lax.bitwise_xor(lax.shift_right_logical(col, 2), odd)
        return jnp.where((col < 2) | (col >= 6), side * 16 + row * 2 + lax.bitwise_and(col, 1), 32)

    def body(runs):
        packed = behind_of(got, index_of, 32, runs, rows_of, width=SUBLANES, radial=to_outer.shape[2])
        for place in range(2):
            to_outer[place] = packed[place * SUBLANES:(place + 1) * SUBLANES]
            to_partner[place] = packed[(2 + place) * SUBLANES:(3 + place) * SUBLANES]

    for_load(body)


def bin_rest_kernel(got, density, to_partner, to_outer, upstream, rows_of):
    height, width, radial = upstream.shape
    _, odd = position("lon")
    sub = sublane(radial)

    def body(runs):
        packed = behind_of(
            got, lambda row, col: jnp.where((col >= 2) & (col < 6), row * 4 + col - 2, 32), 32, runs, rows_of,
            width=width, radial=radial,
        )
        for row in range(height):
            group, k = row // 4, row % 4
            partner, outer = to_partner[group], to_outer[group]
            first, last = either(odd, partner, outer), either(odd, outer, partner)
            first = pltpu.roll(first, -2 * k % SUBLANES, 0)
            last = pltpu.roll(last, SUBLANES - 2 - 2 * k, 0)
            inner = packed[row // 2 * SUBLANES:(row // 2 + 1) * SUBLANES]
            inner = pltpu.roll(inner, 6 if row % 2 else 2, 0)
            mine = jnp.where(sub < 2, first, jnp.where(sub < 6, inner, last))
            upstream[row] = density[row, :width] * mine

    for_load(body)


def mirror(stencils):
    turned = jnp.flip(stencils, axis=1).reshape(stencils.shape[0], 9, 3, stencils.shape[2])
    edge = jnp.zeros_like(turned[:, :, 0, :1])
    back = jnp.concatenate([edge, turned[:, :, 0, :-1]], axis=-1)
    ahead = jnp.concatenate([turned[:, :, 2, 1:], edge], axis=-1)
    return jnp.stack([back, turned[:, :, 1], ahead], axis=2).reshape(stencils.shape)


def swap(to_partner, to_outer, axis, closed, outer_first=False):
    count = lax.axis_size(axis)
    outer = [(i, (i + 1) % count) for i in range(1, count, 2) if closed or i + 1 < count]
    inner = [(i, i + 1) for i in range(0, count - 1, 2)]

    def both_ways(pairs):
        return pairs + [(j, i) for i, j in pairs]

    moves = [(to_partner, inner), (to_outer, outer)]
    got = [lax.ppermute(values, axis, both_ways(pairs)) for values, pairs in moves[::-1 if outer_first else 1]]
    return tuple(got[::-1 if outer_first else 1])


VMEM = pl.BlockSpec(memory_space=pltpu.VMEM)
HBM = pl.BlockSpec(memory_space=pltpu.HBM)
LIMIT = pltpu.CompilerParams(vmem_limit_bytes=32 * 1024 * 1024)


def on_device(residual, star_pixel, star_bin, send_counts, send_offsets, latent, stencils):
    height, width, radial = latent.shape
    shards = send_counts.shape[1]
    slots = residual.shape[0]
    filled = min(slots // LANES, shards // 2 * (CAP + LEAST) // LANES + SUBLANES)
    f32 = jnp.float32
    i32 = jnp.int32
    tile = jax.ShapeDtypeStruct((height, width, radial), f32)
    sides = jax.ShapeDtypeStruct((height // 4, SUBLANES, radial), f32)
    ends = jax.ShapeDtypeStruct((4, SUBLANES, radial), f32)

    def table(values):
        return values.reshape(slots // LANES, LANES)

    four = jax.ShapeDtypeStruct((height // 2, SUBLANES, radial), f32)
    taps = jax.ShapeDtypeStruct((stencils.shape[1], stencils.shape[0], radial), f32)
    packed, latent, *to_sides, taps = pl.pallas_call(
        open_kernel,
        out_shape=(jax.ShapeDtypeStruct((shards, 2 * RUNS, LANES), f32), tile, four, four, taps),
        in_specs=[HBM] * 7,
        out_specs=(VMEM,) * 5,
        scratch_shapes=[pltpu.SMEM((1, shards), i32)] * 2
        + [pltpu.VMEM((filled, LANES), kind) for kind in (f32, i32, i32)]
        + [pltpu.VMEM((2 * filled, LANES), f32)]
        + [pltpu.SemaphoreType.DMA((7,))],
        compiler_params=LIMIT,
        name="opening",
    )(*[
        pltpu.with_memory_space_constraint(values, pltpu.HBM)
        for values in (send_counts, send_offsets, table(residual), table(star_pixel), table(star_bin), latent, stencils.transpose(1, 0, 2))
    ])
    got = lax.all_to_all(packed, ("lat", "lon"), split_axis=0, concat_axis=0, tiled=True)

    rows = pltpu.VMEM((height, 2 * width, radial), f32)
    moved = pltpu.VMEM((2, height, 2 * width, radial), f32)
    edge = (3, 3, 4, width, radial)
    star_rows = [pltpu.VMEM((3, shards * 2 * RUNS, LANES), f32)]
    inner_rows = (3, 3, height - 2, width, radial)

    def call(kernel, name, outs, scratch, *operands):
        return pl.pallas_call(
            kernel,
            out_shape=outs,
            in_specs=[VMEM] * len(operands),
            out_specs=jax.tree.map(lambda _: VMEM, outs),
            scratch_shapes=scratch,
            compiler_params=LIMIT,
            name=name,
        )(*operands)

    def shape(*sizes):
        return jax.ShapeDtypeStruct(sizes, f32)

    beside = swap(*to_sides, "lon", True)
    to_ends = call(pack_ends_kernel, "density_pack", (ends, ends), [], latent, *beside)
    above = swap(*to_ends, "lat", False, outer_first=True)
    broad = 2 * width
    stencils = taps.transpose(1, 0, 2)
    mirrored = mirror(stencils)[::-1]
    inner, middle = call(
        density_inside_kernel, "density_inside",
        (shape(height - 4, broad, radial), shape(3, 3, height - 2, broad, radial)), [rows, moved],
        latent, *beside, stencils,
    )
    to_sides = call(bin_sides_kernel, "bin_sides", (sides, sides), star_rows, got, inner)
    density = call(
        density_ends_kernel, "density_ends", shape(height, broad, radial),
        [pltpu.VMEM((3, 3, 4, broad, radial), f32), rows, moved],
        latent, *beside, *above[::-1], stencils, middle, inner, to_sides[1],
    )
    upstream = call(bin_rest_kernel, "bin_rest", tile, star_rows, got, density, *to_sides)

    beside = swap(*to_sides, "lon", True, outer_first=True)
    *to_ends, middle = call(
        back_reach_kernel, "back_reach", (shape(2, width, radial), shape(2, width, radial), shape(*edge)),
        [rows, moved, pltpu.VMEM((4, width, radial), f32)], upstream, *beside[::-1], density, mirrored,
    )
    above = swap(*to_ends, "lat", False)
    own = call(
        back_own_kernel, "back_own", tile, [rows, moved, pltpu.VMEM(inner_rows, f32)],
        upstream, *beside[::-1], density, mirrored, latent, middle,
    )
    return pl.pallas_call(
        close_kernel,
        out_shape=tile,
        in_specs=[VMEM] * 3,
        out_specs=HBM,
        scratch_shapes=[pltpu.VMEM((2, width, radial), f32)] * 2 + [pltpu.SemaphoreType.DMA((3,))],
        compiler_params=LIMIT,
        name="close",
    )(own, *above)


def solution(mesh):
    return jax.shard_map(
        on_device,
        mesh=mesh,
        in_specs=(
            P(("lat", "lon")),
            P(("lat", "lon")),
            P(("lat", "lon")),
            P(("lat", "lon"), None),
            P(("lat", "lon"), None),
            P("lat", "lon", None),
            P(),
        ),
        out_specs=P("lat", "lon", None),
        check_vma=False,
    )
```
